512 devices in a mesh: gx: 8 (over z), gy: 64 (over y, x, core).
Axes of the slice: x: 4, y: 8, z: 8, core: 2. Of those that a mesh axis runs over, the one named last changes fastest.
Arguments:
- level_set: float32 [64, 2048, 128], P('gx', 'gy'), may hold values from -3 to 3
- velocity: float32 [3, 64, 2048, 128], P(None, 'gx', 'gy'), may hold values from -5 to 5
- source: float32 [64, 2048, 128], P('gx', 'gy'), may hold values from -6 to 6
- wick_solid: int32 [8, 256, 16], P('gx', 'gy'), may hold values 0 or 1
Outputs:
- level_new: float32 [64, 2048, 128], P('gx', 'gy')
- pressure: float32 [64, 2048, 128], P('gx', 'gy')
The draws below stay inside these ranges and needn't reach their ends.
All inputs are finite; a program needn't handle non-finite values. No bound on the sum of `wick_solid` on one device may be relied on, other than what follows from the above.
Results may differ from the reference program's by a relative error of at most 0.00055.
Values sent between devices are 32-bit elements; how exact they have to be, the bound alone decides.
No kernel may reach another device: no remote copies, remote signals or barrier semaphores. Data moves between devices by JAX's collectives and lax.ppermute only.
A program may use at most 64 MiB of HBM per device.

```python
import jax
import jax.numpy as jnp
import numpy as np
from jax import lax

EZ = 1
EY = 4
EX = 16
ITERS = 2
NZ = 64
NY = 2048
NX = 128
N_GX = 8
N_GY = 64


def touch_ends(entries, rng, low, top_value):
    longest = entries.shape.index(max(entries.shape))
    spots = []
    for shift in (0, 1):
        where = [jax.random.randint(jax.random.fold_in(rng, axis), (), 0, length) for axis, length in enumerate(entries.shape)]
        where[longest] = (where[longest] + shift) % entries.shape[longest]
        spots.append(tuple(where))
    return entries.at[spots[0]].set(low).at[spots[1]].set(top_value)


def block_levels(rng, dims, cuts, least, high):
    factor_of = 1.0
    for axis_at, blocks in cuts:
        heights = jax.random.uniform(jax.random.fold_in(jax.random.fold_in(rng, 6), axis_at), (blocks,), jnp.float32, least / len(cuts), high / len(cuts))
        factor_of = factor_of * jnp.repeat(jnp.exp(heights), dims[axis_at] // blocks).reshape((-1,) + (1,) * (len(dims) - 1 - axis_at))
    return factor_of


def normal_values(own_key, shape, width, reach, pieces=(), kind=jnp.bfloat16):
    values = width * jax.random.normal(own_key, shape, jnp.float32)
    if pieces:
        values = values * block_levels(own_key, shape, pieces, -0.22, 0.18)
    return jnp.clip(values, -reach, reach).astype(kind)


def setup_inputs(seed: int = 0) -> dict:
    splits = jax.random.split(jax.random.key(seed), 5)
    level_set = normal_values(splits[0], (NZ, NY, NX), 0.5, 3.0, ((0, 8), (1, 64)), jnp.float32)
    velocity = normal_values(splits[1], (3, NZ, NY, NX), 1.0, 5.0, ((1, 8), (2, 64)), jnp.float32)
    source = normal_values(splits[2], (NZ, NY, NX), 1.0, 6.0, ((0, 8), (1, 64)), jnp.float32)
    wick_solid = touch_ends((jax.random.randint(splits[3], (EZ * N_GX, EY * N_GY, EX), 0, 3) < 1).astype(jnp.int32), jax.random.fold_in(splits[3], 1), 0, 1)
    return {"level_set": level_set, "velocity": velocity, "source": source, "wick_solid": wick_solid}


TIME_STEP = 0.02
HELM_COEF = 0.25
LEVEL_WIDTH = 0.25
GAS_RATIO = 10.0
SOLID_FACTOR = 0.25
SCHWARZ_SCALE = 0.5
SCHWARZ_SHIFT = 0.05

def gll_tables():
    gll_nodes = np.array([-1.0, -0.8717401485096066, -0.5917001814331423, -0.2092992179024789, 0.2092992179024789, 0.5917001814331423, 0.8717401485096066, 1.0])
    weight_np = np.array([1.0 / 28.0, 0.21070422714350603, 0.3411226924835044, 0.4124587946587038, 0.4124587946587038, 0.3411226924835044, 0.21070422714350603, 1.0 / 28.0])
    bary_weights = np.array([1.0 / np.prod([gll_nodes[i] - gll_nodes[j] for j in range(8) if j != i]) for i in range(8)])
    derivative = np.zeros((8, 8))
    for i in range(8):
        for j in range(8):
            if i != j:
                derivative[i, j] = bary_weights[j] / bary_weights[i] / (gll_nodes[i] - gll_nodes[j])
        derivative[i, i] = -np.sum(derivative[i])
    return (weight_np, derivative)

def sine_tables():
    indices = np.arange(10) + 1.0
    sine_basis = np.sqrt(2.0 / 11.0) * np.sin(np.pi * np.outer(indices, indices) / 11.0)
    eigen_vals = 2.0 - 2.0 * np.cos(np.pi * indices / 11.0)
    return (sine_basis, eigen_vals)

def apply_blocks(values, matrix, axis_id):
    block_size = matrix.shape[0]
    dim_shape = values.shape
    if axis_id == 2:
        big_table = jnp.kron(jnp.eye(dim_shape[2] // block_size, dtype=jnp.float32), matrix.T)
        return jnp.dot(values, big_table, precision=lax.Precision.HIGHEST)
    if axis_id == 0:
        parted = values.reshape(dim_shape[0] // block_size, block_size, dim_shape[1], dim_shape[2])
        return jnp.einsum('ij,ajyx->aiyx', matrix, parted, precision=lax.Precision.HIGHEST).reshape(dim_shape)
    parted = values.reshape(dim_shape[0], dim_shape[1] // block_size, block_size, dim_shape[2])
    return jnp.einsum('ij,zajx->zaix', matrix, parted, precision=lax.Precision.HIGHEST).reshape(dim_shape)

def node_weights(weight_np, grid_shape):
    weight_row = jnp.asarray(weight_np, dtype=jnp.float32)
    along_z = jnp.tile(weight_row, grid_shape[0] // 8)
    along_y = jnp.tile(weight_row, grid_shape[1] // 8)
    along_x = jnp.tile(weight_row, grid_shape[2] // 8)
    return along_z[:, None, None] * along_y[None, :, None] * along_x[None, None, :]

def axis_count(length, start, total):
    position = jnp.arange(length) + start
    node_pos = jnp.arange(length) % 8
    inner_lo = jnp.logical_and(node_pos == 0, position > 0).astype(jnp.float32)
    inner_hi = jnp.logical_and(node_pos == 7, position < total - 1).astype(jnp.float32)
    return 1.0 + inner_lo + inner_hi

def fold_axis(padded, axis_id):
    length = padded.shape[axis_id] - 2
    node_pos = jnp.arange(length) % 8
    mask_shape = [1, 1, 1]
    mask_shape[axis_id] = length
    first_mask = (node_pos == 0).astype(jnp.float32).reshape(mask_shape)
    last_mask = (node_pos == 7).astype(jnp.float32).reshape(mask_shape)
    middle = lax.slice_in_dim(padded, 1, length + 1, axis=axis_id)
    lower_rim = lax.slice_in_dim(padded, 0, length, axis=axis_id)
    upper_rim = lax.slice_in_dim(padded, 2, length + 2, axis=axis_id)
    return middle + first_mask * lower_rim + last_mask * upper_rim

def fold_all(padded):
    summed = fold_axis(padded, 1)
    summed = fold_axis(summed, 0)
    summed = jnp.pad(summed, ((0, 0), (0, 0), (1, 1)))
    return fold_axis(summed, 2)

def extend_axis(padded, axis_id):
    length = padded.shape[axis_id] - 4
    blocks = length // 8
    dim_shape = list(padded.shape)
    part_shape = dim_shape[:axis_id] + [blocks, 8] + dim_shape[axis_id + 1:]
    center_part = lax.slice_in_dim(padded, 2, length + 2, axis=axis_id).reshape(part_shape)
    lower_part = lax.slice_in_dim(padded, 0, length, axis=axis_id).reshape(part_shape)
    upper_part = lax.slice_in_dim(padded, 4, length + 4, axis=axis_id).reshape(part_shape)
    lower_rim = lax.slice_in_dim(lower_part, 0, 1, axis=axis_id + 1)
    upper_rim = lax.slice_in_dim(upper_part, 7, 8, axis=axis_id + 1)
    joined = jnp.concatenate([lower_rim, center_part, upper_rim], axis=axis_id + 1)
    return joined.reshape(dim_shape[:axis_id] + [blocks * 10] + dim_shape[axis_id + 1:])

def extend_all(padded):
    widened = extend_axis(padded, 1)
    widened = extend_axis(widened, 0)
    widened = jnp.pad(widened, ((0, 0), (0, 0), (2, 2)))
    return extend_axis(widened, 2)

def inner_axis(values, axis_id):
    dim_shape = list(values.shape)
    blocks = dim_shape[axis_id] // 10
    parted = values.reshape(dim_shape[:axis_id] + [blocks, 10] + dim_shape[axis_id + 1:])
    kept_nodes = lax.slice_in_dim(parted, 1, 9, axis=axis_id + 1)
    return kept_nodes.reshape(dim_shape[:axis_id] + [blocks * 8] + dim_shape[axis_id + 1:])

def schwarz_solve(widened, sine_basis, eigen_vals):
    spectral = apply_blocks(apply_blocks(apply_blocks(widened, sine_basis, 0), sine_basis, 1), sine_basis, 2)
    lam_z = jnp.tile(eigen_vals, widened.shape[0] // 10)
    lam_y = jnp.tile(eigen_vals, widened.shape[1] // 10)
    lam_x = jnp.tile(eigen_vals, widened.shape[2] // 10)
    denominator = SCHWARZ_SCALE * (lam_z[:, None, None] + lam_y[None, :, None] + lam_x[None, None, :]) + SCHWARZ_SHIFT
    spectral = spectral / denominator
    restored = apply_blocks(apply_blocks(apply_blocks(spectral, sine_basis, 0), sine_basis, 1), sine_basis, 2)
    return inner_axis(inner_axis(inner_axis(restored, 0), 1), 2)

def coarse_matrix(kbar):
    rows_gx, rows_gy = kbar.shape
    along_z = 2.0 * kbar[:-1] * kbar[1:] / (kbar[:-1] + kbar[1:]) * (EY * EX / EZ)
    along_y = 2.0 * kbar[:, :-1] * kbar[:, 1:] / (kbar[:, :-1] + kbar[:, 1:]) * (EZ * EX / EY)
    diagonal = HELM_COEF * EZ * EY * EX + jnp.pad(along_z, ((1, 0), (0, 0))) + jnp.pad(along_z, ((0, 1), (0, 0)))
    diagonal = diagonal + jnp.pad(along_y, ((0, 0), (1, 0))) + jnp.pad(along_y, ((0, 0), (0, 1)))
    total = rows_gx * rows_gy
    z_links = jnp.pad(along_z, ((0, 1), (0, 0))).reshape(total)[:total - rows_gy]
    y_links = jnp.pad(along_y, ((0, 0), (0, 1))).reshape(total)[:total - 1]
    matrix = jnp.diag(diagonal.reshape(total)) - jnp.diag(z_links, rows_gy) - jnp.diag(z_links, -rows_gy)
    return matrix - jnp.diag(y_links, 1) - jnp.diag(y_links, -1)

def chol_solve(factor, rhs_vec):
    column = rhs_vec.reshape(-1, 1)
    middle = lax.linalg.triangular_solve(factor, column, left_side=True, lower=True)
    return lax.linalg.triangular_solve(factor, middle, left_side=True, lower=True, transpose_a=True).reshape(-1)

def reference(level_set, velocity, source, wick_solid):
    weight_np, deriv_np = gll_tables()
    deriv = jnp.asarray(deriv_np, dtype=jnp.float32)
    deriv_t = jnp.asarray(deriv_np.T, dtype=jnp.float32)
    basis_np, eigen_np = sine_tables()
    sine_basis = jnp.asarray(basis_np, dtype=jnp.float32)
    eigen_vals = jnp.asarray(eigen_np, dtype=jnp.float32)
    grid_shape = level_set.shape
    node_w = node_weights(weight_np, grid_shape)
    mass_w = 0.125 * node_w
    mult = axis_count(grid_shape[0], 0, grid_shape[0])[:, None, None] * axis_count(grid_shape[1], 0, grid_shape[1])[None, :, None] * axis_count(grid_shape[2], 0, grid_shape[2])[None, None, :]
    inv_mult = 1.0 / mult

    def assemble(values):
        return fold_all(jnp.pad(values, ((1, 1), (1, 1), (0, 0))))
    advect = velocity[0] * 2.0 * apply_blocks(level_set, deriv, 0)
    advect = advect + velocity[1] * 2.0 * apply_blocks(level_set, deriv, 1)
    advect = advect + velocity[2] * 2.0 * apply_blocks(level_set, deriv, 2)
    moved = level_set - TIME_STEP * advect
    level_new = assemble(mass_w * moved) / (mass_w * mult)
    heavi = jax.nn.sigmoid(level_new / LEVEL_WIDTH)
    solid_pts = jnp.repeat(jnp.repeat(jnp.repeat(wick_solid, 8, axis=0), 8, axis=1), 8, axis=2).astype(jnp.float32)
    coef = (GAS_RATIO - (GAS_RATIO - 1.0) * heavi) * (1.0 - (1.0 - SOLID_FACTOR) * solid_pts)
    flux_w = 0.5 * coef * node_w

    def helm(values):
        result = HELM_COEF * mass_w * values
        for axis_id in range(3):
            result = result + apply_blocks(flux_w * apply_blocks(values, deriv, axis_id), deriv_t, axis_id)
        return assemble(result)
    diverge = 2.0 * (apply_blocks(velocity[0], deriv, 0) + apply_blocks(velocity[1], deriv, 1) + apply_blocks(velocity[2], deriv, 2))
    rhs = assemble(mass_w * (source - TIME_STEP * diverge))
    slab_rows = EZ * 8
    col_rows = EY * 8
    kbar = lax.optimization_barrier(jnp.mean(coef.reshape(N_GX, slab_rows, N_GY, col_rows, grid_shape[2]), axis=(1, 3, 4)))
    factor = jnp.linalg.cholesky(coarse_matrix(kbar))

    def coarse_field(residual):
        totals = lax.optimization_barrier(jnp.sum((residual * inv_mult).reshape(N_GX, slab_rows, N_GY, col_rows, grid_shape[2]), axis=(1, 3, 4)))
        solved = chol_solve(factor, totals.reshape(-1)).reshape(N_GX, N_GY)
        return jnp.repeat(jnp.repeat(solved, slab_rows, axis=0), col_rows, axis=1)[:, :, None]

    def precond(residual):
        widened = extend_all(jnp.pad(residual, ((2, 2), (2, 2), (0, 0))))
        local = schwarz_solve(widened, sine_basis, eigen_vals)
        return assemble(inv_mult * (local + coarse_field(residual)))

    def inner(left, right):
        return jnp.sum(left * right * inv_mult)
    pressure = jnp.zeros_like(rhs)
    residual = rhs
    precon = precond(residual)
    rz_now = inner(residual, precon)
    search = precon
    for sweep_id in range(ITERS):
        applied = helm(search)
        step_len = rz_now / inner(search, applied)
        pressure = pressure + step_len * search
        residual = residual - step_len * applied
        if sweep_id + 1 < ITERS:
            precon = precond(residual)
            rz_next = inner(residual, precon)
            search = precon + rz_next / rz_now * search
            rz_now = rz_next
    return (level_new, pressure)
```

```python
import functools

import jax
import jax.numpy as jnp
import numpy as np
from jax import lax
from jax.experimental import pallas as pl
from jax.experimental.pallas import tpu as pltpu
from jax.sharding import PartitionSpec as P

EZ = 1
EY = 4
EX = 16
ROWS = 8 * EY
LANES = 8 * EX

TIME_STEP = 0.02
HELM_COEF = 0.25
LEVEL_WIDTH = 0.25
GAS_RATIO = 10.0
SOLID_FACTOR = 0.25
SCHWARZ_SCALE = 0.5
SCHWARZ_SHIFT = 0.05

F32 = jnp.float32
BF16 = jnp.bfloat16
VMEM = pltpu.VMEM
SMEM = pltpu.SMEM
LIMIT = 24 * 1024 * 1024
PAIRS = ((0, 0), (0, 1), (0, 2), (1, 1), (1, 2), (2, 2))


def gll_tables():
    gll_nodes = np.array(
        [
            -1.0,
            -0.8717401485096066,
            -0.5917001814331423,
            -0.2092992179024789,
            0.2092992179024789,
            0.5917001814331423,
            0.8717401485096066,
            1.0,
        ]
    )
    weight_np = np.array(
        [
            1.0 / 28.0,
            0.21070422714350603,
            0.3411226924835044,
            0.4124587946587038,
            0.4124587946587038,
            0.3411226924835044,
            0.21070422714350603,
            1.0 / 28.0,
        ]
    )
    bary_weights = np.array(
        [1.0 / np.prod([gll_nodes[i] - gll_nodes[j] for j in range(8) if j != i]) for i in range(8)]
    )
    derivative = np.zeros((8, 8))
    for i in range(8):
        for j in range(8):
            if i != j:
                derivative[i, j] = bary_weights[j] / bary_weights[i] / (gll_nodes[i] - gll_nodes[j])
        derivative[i, i] = -np.sum(derivative[i])
    return (weight_np, derivative)


def sine_tables():
    indices = np.arange(10) + 1.0
    sine_basis = np.sqrt(2.0 / 11.0) * np.sin(np.pi * np.outer(indices, indices) / 11.0)
    eigen_vals = 2.0 - 2.0 * np.cos(np.pi * indices / 11.0)
    return (sine_basis, eigen_vals)


WEIGHT, DERIV = gll_tables()
SINE, EIGEN = sine_tables()


def split_const(matrix):
    single = matrix.astype(np.float32)
    high = single.astype(jnp.bfloat16)
    low = (single - high.astype(np.float32)).astype(jnp.bfloat16)
    return high, low


def line_maps(count):
    length = 8 * count
    total = length + 4

    def column(position):
        if 0 <= position < length:
            return position
        return {-2: length, -1: length + 1, length: length + 2, length + 1: length + 3}[position]

    assembled = {}
    for position in range(-2, length + 2):
        row = np.zeros(total)
        row[column(position)] = 1.0
        if 0 <= position < length:
            if position % 8 == 0:
                row[column(position - 1)] += 1.0
            if position % 8 == 7:
                row[column(position + 1)] += 1.0
        assembled[position] = row
    forward = np.zeros((10 * count, total))
    for element in range(count):
        places = [8 * element - 2] + list(range(8 * element, 8 * element + 8)) + [8 * element + 9]
        forward[10 * element : 10 * element + 10] = SINE @ np.stack([assembled[p] for p in places])
    backward = np.zeros((length, 10 * count))
    for element in range(count):
        backward[8 * element : 8 * element + 8, 10 * element : 10 * element + 10] = SINE[1:9]
    for element in range(count - 1):
        first, second = 8 * element + 7, 8 * element + 8
        mean = 0.5 * (backward[first] + backward[second])
        backward[first] = mean
        backward[second] = mean
    return forward, backward


FZ, BZ = line_maps(1)
FY, BY = line_maps(EY)
FY = np.pad(FY, ((0, 0), (0, 4)))
FX, BX = line_maps(EX)
FX = FX[:, :LANES]


def denominators():
    lam_y = np.tile(EIGEN, EY)
    lam_x = np.tile(EIGEN, EX)
    total = EIGEN[:, None, None] + lam_y[None, :, None] + lam_x[None, None, :]
    return (1.0 / (SCHWARZ_SCALE * total + SCHWARZ_SHIFT)).astype(np.float32)


INV_DEN = denominators()
DX_H, DX_L = split_const(np.kron(np.eye(EX), DERIV.T))
DXT_H, DXT_L = split_const(np.kron(np.eye(EX), DERIV))
FY_H, FY_L = split_const(FY)
BY_H, BY_L = split_const(BY)
FX_H, FX_L = split_const(FX.T.copy())
BX_H, BX_L = split_const(BX.T.copy())


def roll_table():
    table = np.zeros((2, 8, 8, LANES), np.float32)
    for kind, matrix in enumerate((DERIV, DERIV.T)):
        for k in range(8):
            for i in range(8):
                table[kind, k, i, :] = matrix[i, (i + k) % 8]
    return table


ROLLS = roll_table()
WY = np.tile(WEIGHT, EY)
WX = np.tile(WEIGHT, EX)
PLANE_W = (WY[:, None] * WX[None, :]).astype(np.float32)


def inner_count(count):
    mult = np.ones(8 * count)
    position = np.arange(8 * count)
    mult[(position % 8 == 0) & (position > 0)] += 1.0
    mult[(position % 8 == 7) & (position < 8 * count - 1)] += 1.0
    return mult


INV_MASS = (8.0 / (WY * inner_count(EY))[:, None] / (WX * inner_count(EX))[None, :]).astype(
    np.float32
)
SPREAD = np.kron(np.eye(EX), np.ones((1, 8))).astype(jnp.bfloat16)


def shape_functions(count, has_low, has_high):
    length = 8 * count
    pieces = np.zeros((3, length))
    pieces[1] = 1.0
    if has_low:
        pieces[0, 0] = 0.5
        pieces[1, 0] = 0.5
    if has_high:
        pieces[2, -1] = 0.5
        pieces[1, -1] = 0.5
    slopes = np.stack([np.kron(np.eye(count), DERIV) @ piece for piece in pieces])
    return pieces, slopes


CASES = ((False, True), (True, True), (True, False))


def z_table():
    table = np.zeros((3, 16, 8))
    for case, (low, high) in enumerate(CASES):
        pieces, slopes = shape_functions(1, low, high)
        for index, (first, second) in enumerate(PAIRS):
            table[case, index] = slopes[first] * slopes[second]
            table[case, 6 + index] = pieces[first] * pieces[second]
            mass = np.sum(WEIGHT * pieces[first] * pieces[second])
            table[case, 15, index] = HELM_COEF / 8.0 * np.sum(WX) * mass
        table[case, 12:15] = pieces
    return table.astype(np.float32)


def y_table():
    table = np.zeros((3, 3, ROWS, LANES))
    for case, (low, high) in enumerate(CASES):
        pieces, slopes = shape_functions(EY, low, high)
        for first in range(3):
            table[case, 2, :, first] = pieces[first]
            for second in range(3):
                table[case, 0, :, 3 * first + second] = pieces[first] * pieces[second]
                table[case, 1, :, 3 * first + second] = slopes[first] * slopes[second]
    return table.astype(np.float32)


Z_TABLE = z_table()
Y_TABLE = y_table()


def parts(values):
    high = values.astype(BF16)
    low = (values - high.astype(F32)).astype(BF16)
    return high, low


def dot(left, right):
    return jnp.dot(left, right, preferred_element_type=F32)


def left_table(table, values):
    high, low = parts(values)
    return dot(table[0][...], high) + dot(table[0][...], low) + dot(table[1][...], high)


def right_table(values, table):
    high, low = parts(values)
    return dot(high, table[0][...]) + dot(low, table[0][...]) + dot(high, table[1][...])


def along_z(values, matrix):
    rows = []
    for i in range(matrix.shape[0]):
        total = None
        for j in range(matrix.shape[1]):
            if matrix[i, j] == 0.0:
                continue
            term = float(matrix[i, j]) * values[j]
            total = term if total is None else total + term
        rows.append(total)
    return rows


def along_y(values, rolls, kind):
    grouped = values.reshape(8 * EY, 8, LANES)
    total = rolls[kind, 0][None] * grouped
    for k in range(1, 8):
        total = total + rolls[kind, k][None] * pltpu.roll(grouped, 8 - k, 1)
    return total.reshape(8, ROWS, LANES)


def along_x(values, table):
    return right_table(values.reshape(8 * ROWS, LANES), table).reshape(8, ROWS, LANES)


def stack(planes):
    return jnp.concatenate([plane[None] for plane in planes], axis=0)


def edge_rows(rows, low, high):
    position = lax.broadcasted_iota(jnp.int32, (rows, LANES), 0)
    return jnp.where(position == 0, low, jnp.where(position == rows - 1, high, 1.0))


def local_operator(values, flux, plane_w, rolls, dx, dxt):
    gz = along_z([values[i] for i in range(8)], DERIV)
    fz = along_z([flux[i] * gz[i] for i in range(8)], DERIV.T)
    total = along_y(flux * along_y(values, rolls, 0), rolls, 1)
    total = total + along_x(flux * along_x(values, dx), dxt)
    planes = [
        total[i] + fz[i] + (HELM_COEF * 0.125 * float(WEIGHT[i])) * (plane_w * values[i])
        for i in range(8)
    ]
    return stack(planes)


def add_faces(own, low_z, high_z, low_y, high_y):
    row = lax.broadcasted_iota(jnp.int32, (ROWS, LANES), 0)
    planes = []
    for i in range(8):
        plane = own[i]
        first = low_y[i : i + 1]
        last = high_y[i : i + 1]
        if i == 0:
            plane = plane + low_z
            first = first + low_y[8:9]
            last = last + high_y[8:9]
        if i == 7:
            plane = plane + high_z
            first = first + low_y[9:10]
            last = last + high_y[9:10]
        plane = plane + jnp.where(row == 0, first, jnp.where(row == ROWS - 1, last, 0.0))
        planes.append(plane)
    return stack(planes)


def schwarz(ext, tables, inv_den, near, out_ref, low_ref, high_ref):
    fy, fx, bx, by = tables
    spectral = along_z([ext[i] for i in range(12)], FZ)
    spectral = [left_table(fy, plane) for plane in spectral]
    wide = right_table(jnp.concatenate(spectral, axis=0), fx)
    wide = wide * inv_den[...].reshape(10 * 10 * EY, 10 * EX)
    back = right_table(wide, bx)
    step = 10 * EY
    back = [left_table(by, back[step * i : step * (i + 1)]) for i in range(10)]
    planes = along_z(back, BZ)
    edge = edge_rows(ROWS, near[2], near[3])
    planes = [plane * edge for plane in planes]
    planes[0] = planes[0] * near[0]
    planes[7] = planes[7] * near[1]
    for i in range(8):
        out_ref[i] = planes[i]
    low_ref[...] = planes[0]
    high_ref[...] = planes[7]


def fill_ext(ext, own, low_z, high_z, low_y, high_y):
    for i in range(8):
        ext[i, 0:ROWS] = own[i]
    for i in range(2):
        ext[8 + i, 0:ROWS] = low_z[i]
        ext[10 + i, 0:ROWS] = high_z[i]
    zeros = jnp.zeros((4, LANES), F32)
    for i in range(12):
        ext[i, ROWS : ROWS + 8] = jnp.concatenate(
            [low_y[2 * i : 2 * i + 2], high_y[2 * i : 2 * i + 2], zeros], axis=0
        )


def partition_total(ext, near):
    total = near[0] * ext[0] + near[1] * ext[7] + 0.5 * (ext[9] + ext[10])
    for i in range(1, 7):
        total = total + ext[i]
    row = lax.broadcasted_iota(jnp.int32, (ROWS + 8, LANES), 0)
    weight = jnp.where(row < ROWS, 1.0, 0.0)
    weight = jnp.where(row == 0, near[2], weight)
    weight = jnp.where(row == ROWS - 1, near[3], weight)
    weight = jnp.where((row == ROWS + 1) | (row == ROWS + 2), 0.5, weight)
    return jnp.sum(total * weight)


def lane_row(entries):
    lane = lax.broadcasted_iota(jnp.int32, (1, LANES), 1)
    row = jnp.zeros((1, LANES), F32)
    for index, value in enumerate(entries):
        row = jnp.where(lane == index, value, row)
    return row


def advect_kernel(lev, vel, src, plane_w, rolls, dxh, dxl, b_ref, l_ref, zlo, zhi):
    dx = (dxh, dxl)
    level = lev[...]
    v0, v1, v2 = vel[0], vel[1], vel[2]
    gz = stack(along_z([level[i] for i in range(8)], DERIV))
    advect = v0 * gz + v1 * along_y(level, rolls, 0) + v2 * along_x(level, dx)
    moved = level - (2.0 * TIME_STEP) * advect
    diverge = stack(along_z([v0[i] for i in range(8)], DERIV))
    diverge = diverge + along_y(v1, rolls, 0) + along_x(v2, dx)
    force = src[...] - (2.0 * TIME_STEP) * diverge
    weights = plane_w[...]
    for i in range(8):
        mass = (0.125 * float(WEIGHT[i])) * weights
        term = mass * force[i]
        moved_i = mass * moved[i]
        b_ref[i] = term
        l_ref[i] = moved_i
        if i < 2:
            zlo[i] = term
        if i == 0:
            zlo[2] = moved_i
        if i > 5:
            zhi[i - 6] = term
        if i == 7:
            zhi[2] = moved_i


def rim_kernel(kinds, *refs):
    count = len(kinds)
    own = refs[:count]
    low_z, high_z, low_y, high_y = refs[count:]
    at = 0
    for (width, start), array in zip(kinds, own, strict=True):
        for i in range(8):
            low_y[at : at + width] = array[i, 0:width]
            high_y[at : at + width] = array[i, ROWS - width : ROWS]
            at += width
        for planes in (low_z, high_z):
            for i in range(width):
                low_y[at : at + width] = planes[start + i, 0:width]
                high_y[at : at + width] = planes[start + i, ROWS - width : ROWS]
                at += width
    rest = low_y.shape[0] - at
    if rest:
        low_y[at : at + rest] = jnp.zeros((rest, LANES), F32)
        high_y[at : at + rest] = jnp.zeros((rest, LANES), F32)


def level_kernel(
    near, solid, spread, inv_mass, plane_w, inv_den, fyh, fyl, fxh, fxl, bxh, bxl, byh, byl,
    b, l, zlo, zhi, ylo, yhi, level_ref, flux_ref, w_ref, wlo, whi, stat, ext,
):
    own = add_faces(
        l[...], zlo[2], zhi[2], ylo[24:34], yhi[24:34]
    )
    row = lax.broadcasted_iota(jnp.int32, (8, ROWS, LANES), 1)
    lane = lax.broadcasted_iota(jnp.int32, (8, ROWS, LANES), 2)
    before = jnp.where((row % 8 == 0) & (row > 0), pltpu.roll(own, 1, 1), 0.0)
    after = jnp.where((row % 8 == 7) & (row < ROWS - 1), pltpu.roll(own, ROWS - 1, 1), 0.0)
    own = own + before + after
    before = jnp.where((lane % 8 == 0) & (lane > 0), pltpu.roll(own, 1, 2), 0.0)
    after = jnp.where((lane % 8 == 7) & (lane < LANES - 1), pltpu.roll(own, LANES - 1, 2), 0.0)
    own = own + before + after
    inverse = inv_mass[...] * edge_rows(ROWS, near[2], near[3])
    in_solid = dot(solid[...].astype(BF16), spread[...])
    open_part = jnp.concatenate(
        [jnp.broadcast_to(1.0 - (1.0 - SOLID_FACTOR) * in_solid[e : e + 1], (8, LANES)) for e in range(EY)],
        axis=0,
    )
    total = jnp.zeros((ROWS, LANES), F32)
    for i in range(8):
        scale = 1.0 / float(WEIGHT[i])
        plane = own[i] * (inverse * scale)
        if i == 0:
            plane = plane * near[0]
        if i == 7:
            plane = plane * near[1]
        level_ref[i] = plane
        liquid = jax.nn.sigmoid(plane * (1.0 / LEVEL_WIDTH))
        coef = (GAS_RATIO - (GAS_RATIO - 1.0) * liquid) * open_part
        total = total + coef
        flux_ref[i] = (0.5 * float(WEIGHT[i])) * (coef * plane_w[...])
    kbar = jnp.sum(total) * (1.0 / (8 * ROWS * LANES))
    fill_ext(ext, b, zlo, zhi, ylo, yhi)
    stat[...] = lane_row([kbar, partition_total(ext, near)])
    schwarz(ext, ((fyh, fyl), (fxh, fxl), (bxh, bxl), (byh, byl)), inv_den, near, w_ref, wlo, whi)


def schwarz_kernel(
    near, inv_den, fyh, fyl, fxh, fxl, bxh, bxl, byh, byl, b, zlo, zhi, ylo, yhi,
    w_ref, wlo, whi, ext,
):
    fill_ext(ext, b, zlo, zhi, ylo, yhi)
    schwarz(ext, ((fyh, fyl), (fxh, fxl), (bxh, bxl), (byh, byl)), inv_den, near, w_ref, wlo, whi)


def galerkin_kernel(
    zt, yt, wy, plane_w, rolls, dxh, dxl, dxth, dxtl, stat_in, flux, w, zlo, zhi, ylo, yhi,
    zl_ref, stat,
):
    local = add_faces(w[...], zlo[...], zhi[...], ylo[...], yhi[...])
    zl_ref[...] = local
    fluxes = flux[...]
    applied = local_operator(local, fluxes, plane_w[...], rolls, (dxh, dxl), (dxth, dxtl))

    def combine(index, planes):
        total = zt[index, 0] * planes[0]
        for i in range(1, 8):
            total = total + zt[index, i] * planes[i]
        return jnp.sum(total, axis=1, keepdims=True)

    total = jnp.zeros((ROWS, LANES), F32)
    for a in range(3):
        placed = pltpu.roll(yt[2], 2 + 3 * a, 1)
        total = total + combine(12 + a, applied) * placed
    for index in range(6):
        shift = 11 + 9 * index
        slope_z = combine(index, fluxes) + zt[15, index] * wy[...]
        slope_y = combine(6 + index, fluxes)
        total = total + slope_z * pltpu.roll(yt[0], shift, 1)
        total = total + slope_y * pltpu.roll(yt[1], shift, 1)
    stat[...] = stat_in[...] + jnp.sum(total, axis=0, keepdims=True)


def invert(blocks, sub):
    for k in range(8):
        pivot = 1.0 / blocks[k][k : k + 1]
        scaled = jnp.where(sub == k, pivot, blocks[k] * pivot)
        rows = []
        for r in range(8):
            if r == k:
                rows.append(scaled)
            else:
                rest = jnp.where(sub == k, 0.0, blocks[r])
                rows.append(rest - blocks[r][k : k + 1] * scaled)
        blocks = rows
    return blocks


def multiply(left, right):
    rows = []
    for r in range(8):
        total = left[r][0:1] * right[0]
        for k in range(1, 8):
            total = total + left[r][k : k + 1] * right[k]
        rows.append(total)
    return rows


def matvec(terms, sub):
    result = jnp.zeros_like(terms[0][1])
    for r in range(8):
        product = terms[0][0][r] * terms[0][1]
        for blocks, column in terms[1:]:
            product = product + blocks[r] * column
        result = jnp.where(sub == r, jnp.sum(product, axis=0, keepdims=True), result)
    return result


def coarse_kernel(count, place, gathered, out_ref, wide, values):
    lanes = LANES
    wide[...] = jnp.zeros((LANES, LANES), F32)
    for i in range(8):
        wide[0:count] = gathered[:, i, :]
        values[i] = wide[...].T
    sub = lax.broadcasted_iota(jnp.int32, (8, lanes), 0)
    lane = lax.broadcasted_iota(jnp.int32, (8, lanes), 1)

    def value(index):
        return jnp.concatenate([values[i, index : index + 1] for i in range(8)], axis=0)

    def move(array, dz, dy):
        if dz:
            array = pltpu.roll(array, (-dz) % 8, 0)
        if dy:
            array = pltpu.roll(array, (-dy) % lanes, 1)
        return array

    kbar = jnp.where(lane < count, value(0), 1.0)
    above = move(kbar, 1, 0)
    link_z = jnp.where(sub < 7, 2.0 * kbar * above / (kbar + above) * (EY * EX / EZ), 0.0)
    link_z = jnp.where(lane < count, link_z, 0.0)
    beside = move(kbar, 0, 1)
    link_y = 2.0 * kbar * beside / (kbar + beside) * (EZ * EX / EY)
    link_y = jnp.where(lane < count - 1, link_y, 0.0)
    back_z = move(link_z, -1, 0)
    back_y = move(link_y, 0, -1)
    diagonal = HELM_COEF * EZ * EY * EX + link_z + back_z + link_y + back_y
    blocks, lower, upper = [], [], []
    for r in range(8):
        row = jnp.where(sub == r, diagonal, 0.0)
        row = jnp.where(sub == r + 1, -back_z, row)
        row = jnp.where(sub == r - 1, -link_z, row)
        blocks.append(row)
        lower.append(jnp.where(sub == r, -back_y, 0.0))
        upper.append(jnp.where(sub == r, -link_y, 0.0))
    levels = []
    step = 1
    while step < count:
        inverse = invert(blocks, sub)
        down = multiply(lower, [move(row, 0, -step) for row in inverse])
        up = multiply(upper, [move(row, 0, step) for row in inverse])
        levels.append((step, down, up))
        before_u = multiply(down, [move(row, 0, -step) for row in upper])
        after_l = multiply(up, [move(row, 0, step) for row in lower])
        if 2 * step < count:
            new_lower = multiply(down, [move(row, 0, -step) for row in lower])
            new_upper = multiply(up, [move(row, 0, step) for row in upper])
            lower = [-row for row in new_lower]
            upper = [-row for row in new_upper]
        blocks = [blocks[r] - before_u[r] - after_l[r] for r in range(8)]
        step *= 2
    inverse = invert(blocks, sub)

    def solve(column):
        for distance, down, up in levels:
            pulled = matvec(
                [(down, move(column, 0, -distance)), (up, move(column, 0, distance))], sub
            )
            column = column - pulled
        return matvec([(inverse, column)], sub)

    offsets = [(a - 1, b - 1) for a in range(3) for b in range(3)]
    first = solve(value(1))
    near_first = [move(first, dz, dy) for dz, dy in offsets]
    totals = jnp.zeros((8, lanes), F32)
    for d, (dz, dy) in enumerate(offsets):
        term = value(2 + d)
        for e in range(9):
            a, b, c, f = d // 3, d % 3, e // 3, e % 3
            if a > c:
                a, b, c, f = c, f, a, b
            term = term + value(11 + 9 * PAIRS.index((a, c)) + 3 * b + f) * near_first[e]
        totals = totals + move(term, -dz, -dy)
    totals = jnp.where(lane < count, totals, 0.0)
    second = solve(totals)
    near_second = [move(second, dz, dy) for dz, dy in offsets]
    mine = (sub == place[0]) & (lane == place[1])
    for d in range(9):
        out_ref[d : d + 1] = jnp.full((1, lanes), jnp.sum(jnp.where(mine, near_first[d], 0.0)))
        out_ref[16 + d : 17 + d] = jnp.full(
            (1, lanes), jnp.sum(jnp.where(mine, near_second[d], 0.0))
        )


def add_coarse(local, zt, yt, coarse, start):
    columns = []
    for a in range(3):
        total = yt[2, :, 0:1] * coarse[start + 3 * a : start + 3 * a + 1]
        for b in range(1, 3):
            total = total + yt[2, :, b : b + 1] * coarse[start + 3 * a + b : start + 3 * a + b + 1]
        columns.append(total)
    planes = []
    for i in range(8):
        plane = local[i] + zt[13, i] * columns[1]
        if i == 0:
            plane = plane + zt[12, i] * columns[0]
        if i == 7:
            plane = plane + zt[14, i] * columns[2]
        planes.append(plane)
    return stack(planes)


def apply_kernel(
    zt, yt, plane_w, rolls, dxh, dxl, dxth, dxtl, coarse, flux, b, zl,
    z_ref, y_ref, ylo, yhi, stat,
):
    field = add_coarse(zl[...], zt, yt, coarse, 0)
    z_ref[...] = field
    applied = local_operator(field, flux[...], plane_w[...], rolls, (dxh, dxl), (dxth, dxtl))
    y_ref[...] = applied
    ylo[...] = applied[0:2]
    yhi[...] = applied[6:8]
    stat[...] = lane_row([jnp.sum(b[...] * field), jnp.sum(field * applied)])


def second_kernel(
    zt, yt, plane_w, rolls, dxh, dxl, dxth, dxtl, coarse, flux, b, y, w, zlo, zhi, ylo, yhi,
    stat_in, q_ref, stat,
):
    local = add_faces(w[...], zlo[...], zhi[...], ylo[...], yhi[...])
    field = add_coarse(local, zt, yt, coarse, 16)
    q_ref[...] = field
    applied = local_operator(field, flux[...], plane_w[...], rolls, (dxh, dxl), (dxth, dxtl))
    sums = [0.0, 0.0, jnp.sum(b[...] * field), jnp.sum(y[...] * field), jnp.sum(field * applied)]
    stat[...] = stat_in[...] + lane_row(sums)


def combine_kernel(sums, z, q, p_ref):
    total = jnp.sum(sums[...], axis=0, keepdims=True)
    rz, pap, rq, aq, qhq = (total[:, k : k + 1] for k in range(5))
    step = rz / pap
    rz_next = step * (step * aq - rq)
    beta = rz_next / rz
    grown = 1.0 + beta
    curved = grown * grown * pap - 2.0 * step * grown * aq + step * step * qhq
    step_next = rz_next / curved
    on_z = step + step_next * grown
    on_q = step_next * step
    p_ref[...] = on_z.reshape(1, 1, 1) * z[...] - on_q.reshape(1, 1, 1) * q[...]


def call(kernel, outs, specs, args, scratch=(), flops=1000000):
    nbytes = sum(4 * int(np.prod(out)) for out in outs) * 2
    return pl.pallas_call(
        kernel,
        out_shape=[jax.ShapeDtypeStruct(out, F32) for out in outs],
        in_specs=[pl.BlockSpec(memory_space=SMEM if spec else VMEM) for spec in specs],
        out_specs=[pl.BlockSpec(memory_space=VMEM) for _ in outs],
        scratch_shapes=list(scratch),
        compiler_params=pltpu.CompilerParams(vmem_limit_bytes=LIMIT),
        cost_estimate=pl.CostEstimate(flops=flops, bytes_accessed=nbytes, transcendentals=0),
    )(*args)


def run(kernel, outs, smem, args, scratch=(), flops=1000000):
    specs = [True] * len(smem) + [False] * len(args)
    return call(kernel, outs, specs, list(smem) + list(args), scratch, flops)


def shift(axis, low_face, high_face):
    count = lax.axis_size(axis)
    forward = [(i, i + 1) for i in range(count - 1)]
    backward = [(target, source) for source, target in forward]
    return lax.ppermute(high_face, axis, forward), lax.ppermute(low_face, axis, backward)


def gather_tiles(row, count_gx, count_gy):
    tile = jnp.broadcast_to(row, (count_gx, LANES))
    tile = lax.all_to_all(tile, "gx", 0, 0, tiled=True)
    wide = jnp.broadcast_to(tile[None], (count_gy, count_gx, LANES))
    return lax.all_to_all(wide, "gy", 0, 0, tiled=True)


def body(level_set, velocity, source, wick_solid):
    block = level_set.shape
    count_gx = lax.axis_size("gx")
    count_gy = lax.axis_size("gy")
    index_gx = lax.axis_index("gx")
    index_gy = lax.axis_index("gy")

    def ends(index, count):
        return [jnp.where(index > 0, 0.5, 1.0), jnp.where(index < count - 1, 0.5, 1.0)]

    def case(index, count):
        return jnp.where(index == 0, 0, jnp.where(index == count - 1, 2, 1))

    near = jnp.stack(ends(index_gx, count_gx) + ends(index_gy, count_gy)).astype(F32)
    zt = lax.dynamic_index_in_dim(jnp.asarray(Z_TABLE), case(index_gx, count_gx), 0, False)
    yt = lax.dynamic_index_in_dim(jnp.asarray(Y_TABLE), case(index_gy, count_gy), 0, False)
    place = jnp.stack([index_gx, index_gy]).astype(jnp.int32)
    plane_w = jnp.asarray(PLANE_W)
    rolls = jnp.asarray(ROLLS)
    dx = (jnp.asarray(DX_H), jnp.asarray(DX_L))
    dxt = (jnp.asarray(DXT_H), jnp.asarray(DXT_L))
    wy = jnp.asarray(WY.astype(np.float32)[:, None])
    operator = (plane_w, rolls, *dx, *dxt)
    solver = (INV_DEN, FY_H, FY_L, FX_H, FX_L, BX_H, BX_L, BY_H, BY_L)
    solver = tuple(jnp.asarray(table) for table in solver)
    face = (ROWS, LANES)
    ext = VMEM((12, ROWS + 8, LANES), F32)
    solid = wick_solid.reshape(EY, EX).astype(F32)

    b, l, zlo, zhi = run(
        advect_kernel,
        [block, block, (3, *face), (3, *face)],
        [],
        [level_set, velocity, source, plane_w, rolls, *dx],
    )
    zlo, zhi = shift("gx", zlo, zhi)
    ylo, yhi = run(
        functools.partial(rim_kernel, ((2, 0), (1, 2))), [(40, LANES)] * 2, [], [b, l, zlo, zhi]
    )
    ylo, yhi = shift("gy", ylo, yhi)
    level_new, flux, w, wlo, whi, stat = run(
        level_kernel,
        [block, block, block, face, face, (1, LANES)],
        [near],
        [
            solid, jnp.asarray(SPREAD), jnp.asarray(INV_MASS), plane_w, *solver,
            b, l, zlo, zhi, ylo, yhi,
        ],
        [ext],
    )

    def exchange_one(w, wlo, whi):
        zlo, zhi = shift("gx", wlo, whi)
        ylo, yhi = run(
            functools.partial(rim_kernel, ((1, 0),)), [(16, LANES)] * 2, [],
            [w, zlo[None], zhi[None]],
        )
        ylo, yhi = shift("gy", ylo, yhi)
        return zlo, zhi, ylo, yhi

    faces = exchange_one(w, wlo, whi)
    zl, stat = run(
        galerkin_kernel,
        [block, (1, LANES)],
        [zt],
        [yt, wy, *operator, stat, flux, w, *faces],
    )
    gathered = gather_tiles(stat, count_gx, count_gy)
    (coarse,) = run(
        functools.partial(coarse_kernel, count_gy),
        [(32, LANES)],
        [place],
        [gathered],
        [VMEM((LANES, LANES), F32), VMEM((8, LANES, LANES), F32)],
    )
    z, y, zlo, zhi, sums = run(
        apply_kernel,
        [block, block, (2, *face), (2, *face), (1, LANES)],
        [zt],
        [yt, *operator, coarse, flux, b, zl],
    )
    zlo, zhi = shift("gx", zlo, zhi)
    ylo, yhi = run(
        functools.partial(rim_kernel, ((2, 0),)), [(24, LANES)] * 2, [], [y, zlo, zhi]
    )
    ylo, yhi = shift("gy", ylo, yhi)
    w, wlo, whi = run(
        schwarz_kernel,
        [block, face, face],
        [near],
        [*solver, y, zlo, zhi, ylo, yhi],
        [ext],
    )
    faces = exchange_one(w, wlo, whi)
    q, sums = run(
        second_kernel,
        [block, (1, LANES)],
        [zt],
        [yt, *operator, coarse, flux, b, y, w, *faces, sums],
    )
    tile = jnp.broadcast_to(sums, (count_gx, LANES))
    tile = lax.all_to_all(tile, "gx", 0, 0, tiled=True)
    wide = jnp.broadcast_to(jnp.sum(tile, axis=0, keepdims=True), (count_gy, LANES))
    wide = lax.all_to_all(wide, "gy", 0, 0, tiled=True)
    (pressure,) = run(combine_kernel, [block], [], [wide, z, q])
    return (level_new, pressure)


def solution(mesh):
    placed = (
        P("gx", "gy", None),
        P(None, "gx", "gy", None),
        P("gx", "gy", None),
        P("gx", "gy", None),
    )
    return jax.shard_map(
        body,
        mesh=mesh,
        in_specs=placed,
        out_specs=(P("gx", "gy", None), P("gx", "gy", None)),
        check_vma=False,
    )
```

```python
import functools

import jax
import jax.numpy as jnp
import numpy as np
from jax import lax
from jax.experimental import pallas as pl
from jax.experimental.pallas import tpu as pltpu
from jax.sharding import PartitionSpec as P

EZ = 1
EY = 4
EX = 16
ROWS = 8 * EY
LANES = 8 * EX

TIME_STEP = 0.02
HELM_COEF = 0.25
LEVEL_WIDTH = 0.25
GAS_RATIO = 10.0
SOLID_FACTOR = 0.25
SCHWARZ_SCALE = 0.5
SCHWARZ_SHIFT = 0.05

F32 = jnp.float32
BF16 = jnp.bfloat16
VMEM = pltpu.VMEM
SMEM = pltpu.SMEM
LIMIT = 24 * 1024 * 1024
PAIRS = ((0, 0), (0, 1), (0, 2), (1, 1), (1, 2), (2, 2))


def gll_tables():
    gll_nodes = np.array(
        [
            -1.0,
            -0.8717401485096066,
            -0.5917001814331423,
            -0.2092992179024789,
            0.2092992179024789,
            0.5917001814331423,
            0.8717401485096066,
            1.0,
        ]
    )
    weight_np = np.array(
        [
            1.0 / 28.0,
            0.21070422714350603,
            0.3411226924835044,
            0.4124587946587038,
            0.4124587946587038,
            0.3411226924835044,
            0.21070422714350603,
            1.0 / 28.0,
        ]
    )
    bary_weights = np.array(
        [1.0 / np.prod([gll_nodes[i] - gll_nodes[j] for j in range(8) if j != i]) for i in range(8)]
    )
    derivative = np.zeros((8, 8))
    for i in range(8):
        for j in range(8):
            if i != j:
                derivative[i, j] = bary_weights[j] / bary_weights[i] / (gll_nodes[i] - gll_nodes[j])
        derivative[i, i] = -np.sum(derivative[i])
    return (weight_np, derivative)


def sine_tables():
    indices = np.arange(10) + 1.0
    sine_basis = np.sqrt(2.0 / 11.0) * np.sin(np.pi * np.outer(indices, indices) / 11.0)
    eigen_vals = 2.0 - 2.0 * np.cos(np.pi * indices / 11.0)
    return (sine_basis, eigen_vals)


WEIGHT, DERIV = gll_tables()
SINE, EIGEN = sine_tables()


def split_const(matrix):
    single = matrix.astype(np.float32)
    high = single.astype(jnp.bfloat16)
    low = (single - high.astype(np.float32)).astype(jnp.bfloat16)
    return high, low


def line_maps(count):
    length = 8 * count
    total = length + 4

    def column(position):
        if 0 <= position < length:
            return position
        return {-2: length, -1: length + 1, length: length + 2, length + 1: length + 3}[position]

    assembled = {}
    for position in range(-2, length + 2):
        row = np.zeros(total)
        row[column(position)] = 1.0
        if 0 <= position < length:
            if position % 8 == 0:
                row[column(position - 1)] += 1.0
            if position % 8 == 7:
                row[column(position + 1)] += 1.0
        assembled[position] = row
    forward = np.zeros((10 * count, total))
    for element in range(count):
        places = [8 * element - 2] + list(range(8 * element, 8 * element + 8)) + [8 * element + 9]
        forward[10 * element : 10 * element + 10] = SINE @ np.stack([assembled[p] for p in places])
    backward = np.zeros((length, 10 * count))
    for element in range(count):
        backward[8 * element : 8 * element + 8, 10 * element : 10 * element + 10] = SINE[1:9]
    for element in range(count - 1):
        first, second = 8 * element + 7, 8 * element + 8
        mean = 0.5 * (backward[first] + backward[second])
        backward[first] = mean
        backward[second] = mean
    return forward, backward


def wide_maps():
    count = EY + 2
    forward, backward = line_maps(count)
    length = 8 * count
    columns = np.zeros((10 * count, ROWS + 2 * TILE))
    columns[:, :ROWS] = forward[:, 8 : 8 + ROWS]
    columns[:, ROWS : ROWS + 2] = forward[:, length : length + 2]
    columns[:, ROWS + 2 : ROWS + 10] = forward[:, :8]
    columns[:, ROWS + TILE : ROWS + TILE + 8] = forward[:, length - 8 : length]
    columns[:, ROWS + TILE + 8 : ROWS + TILE + 10] = forward[:, length + 2 : length + 4]
    _, own = line_maps(EY)
    rows = np.zeros((ROWS + 8, 10 * count))
    rows[:ROWS, 10 : 10 + 10 * EY] = own
    rows[ROWS, :10] = SINE[8]
    rows[ROWS + 1, 10 + 10 * EY :] = SINE[1]
    return columns, rows


TILE = 16
FZ, BZ = line_maps(1)
FY, BY = wide_maps()
FX, BX = line_maps(EX)
FX = FX[:, :LANES]


def denominators():
    lam_y = np.tile(EIGEN, EY + 2)
    lam_x = np.tile(EIGEN, EX)
    total = EIGEN[:, None, None] + lam_y[None, :, None] + lam_x[None, None, :]
    return (1.0 / (SCHWARZ_SCALE * total + SCHWARZ_SHIFT)).astype(np.float32)


INV_DEN = denominators()
FY_H, FY_L = split_const(FY)
BY_H, BY_L = split_const(BY)
FX_H, FX_L = split_const(FX.T.copy())
BX_H, BX_L = split_const(BX.T.copy())


def roll_table():
    table = np.zeros((2, 8, 8, LANES))
    for kind, matrix in enumerate((DERIV, DERIV.T)):
        for k in range(8):
            for i in range(8):
                table[kind, k, i, :] = matrix[i, (i + k) % 8]
    return table.reshape(2 * 64, LANES)


WY = np.tile(WEIGHT, EY)
WX = np.tile(WEIGHT, EX)
AT_ROLLS = ROWS
AT_DX = AT_ROLLS + 128
AT_DXT = AT_DX + LANES
PACKED = np.concatenate(
    [
        WY[:, None] * WX[None, :],
        roll_table(),
        np.kron(np.eye(EX), DERIV.T),
        np.kron(np.eye(EX), DERIV),
    ]
).astype(np.float32)


def inner_count(count):
    mult = np.ones(8 * count)
    position = np.arange(8 * count)
    mult[(position % 8 == 0) & (position > 0)] += 1.0
    mult[(position % 8 == 7) & (position < 8 * count - 1)] += 1.0
    return mult


INV_MASS = (8.0 / (WY * inner_count(EY))[:, None] / (WX * inner_count(EX))[None, :]).astype(
    np.float32
)
SPREAD = np.kron(np.eye(EX), np.ones((1, 8))).astype(jnp.bfloat16)


def shape_functions(count, has_low, has_high):
    length = 8 * count
    pieces = np.zeros((3, length))
    pieces[1] = 1.0
    if has_low:
        pieces[0, 0] = 0.5
        pieces[1, 0] = 0.5
    if has_high:
        pieces[2, -1] = 0.5
        pieces[1, -1] = 0.5
    slopes = np.stack([np.kron(np.eye(count), DERIV) @ piece for piece in pieces])
    return pieces, slopes


CASES = ((False, True), (True, True), (True, False))


def z_table():
    table = np.zeros((3, 16, 8))
    for case, (low, high) in enumerate(CASES):
        pieces, slopes = shape_functions(1, low, high)
        for index, (first, second) in enumerate(PAIRS):
            table[case, index] = slopes[first] * slopes[second]
            table[case, 6 + index] = pieces[first] * pieces[second]
            mass = np.sum(WEIGHT * pieces[first] * pieces[second])
            table[case, 15, index] = HELM_COEF / 8.0 * np.sum(WX) * mass
        table[case, 12:15] = pieces
    return table.astype(np.float32)


def y_table():
    table = np.zeros((3, 3, ROWS, LANES))
    for case, (low, high) in enumerate(CASES):
        pieces, slopes = shape_functions(EY, low, high)
        for first in range(3):
            table[case, 2, :, first] = pieces[first]
            for second in range(3):
                table[case, 0, :, 3 * first + second] = pieces[first] * pieces[second]
                table[case, 1, :, 3 * first + second] = slopes[first] * slopes[second]
    return table.astype(np.float32)


Z_TABLE = z_table()
Y_TABLE = y_table()


def parts(values):
    high = values.astype(BF16)
    low = (values - high.astype(F32)).astype(BF16)
    return high, low


def dot(left, right):
    return jnp.dot(left, right, preferred_element_type=F32)


def left_table(table, values):
    high, low = parts(values)
    return dot(table[0][...], high) + dot(table[0][...], low) + dot(table[1][...], high)


def right_table(values, table):
    high, low = parts(values)
    return dot(high, table[0][...]) + dot(low, table[0][...]) + dot(high, table[1][...])


def along_z(values, matrix):
    rows = []
    for i in range(matrix.shape[0]):
        total = None
        for j in range(matrix.shape[1]):
            if matrix[i, j] == 0.0:
                continue
            term = float(matrix[i, j]) * values[j]
            total = term if total is None else total + term
        rows.append(total)
    return rows


def along_y(values, packed, kind):
    grouped = values.reshape(8 * EY, 8, LANES)
    start = AT_ROLLS + 64 * kind
    total = packed[start : start + 8][None] * grouped
    for k in range(1, 8):
        total = total + packed[start + 8 * k : start + 8 * k + 8][None] * pltpu.roll(grouped, 8 - k, 1)
    return total.reshape(8, ROWS, LANES)


def along_x(values, packed, kind):
    start = AT_DXT if kind else AT_DX
    high, low = parts(packed[start : start + LANES])
    first, rest = parts(values.reshape(8 * ROWS, LANES))
    total = dot(first, high) + dot(rest, high) + dot(first, low)
    return total.reshape(8, ROWS, LANES)


def stack(planes):
    return jnp.concatenate([plane[None] for plane in planes], axis=0)


def edge_rows(rows, low, high):
    position = lax.broadcasted_iota(jnp.int32, (rows, LANES), 0)
    return jnp.where(position == 0, low, jnp.where(position == rows - 1, high, 1.0))


def local_operator(values, flux, packed):
    plane_w = packed[0:ROWS]
    gz = along_z([values[i] for i in range(8)], DERIV)
    fz = along_z([flux[i] * gz[i] for i in range(8)], DERIV.T)
    total = along_y(flux * along_y(values, packed, 0), packed, 1)
    total = total + along_x(flux * along_x(values, packed, 0), packed, 1)
    planes = [
        total[i] + fz[i] + (HELM_COEF * 0.125 * float(WEIGHT[i])) * (plane_w * values[i])
        for i in range(8)
    ]
    return stack(planes)


def add_planes(own, low_z, high_z):
    planes = [own[i] for i in range(8)]
    planes[0] = planes[0] + low_z
    planes[7] = planes[7] + high_z
    return stack(planes)


def schwarz(own, low_z, high_z, low_y, high_y, tables, inv_den, near, out_ref, low_ref, high_ref):
    fy, fx, bx, by = tables
    middle = along_z([own[i] for i in range(8)] + [low_z[0], low_z[1], high_z[0], high_z[1]], FZ)
    below = along_z([low_y[i] for i in range(12)], FZ)
    above = along_z([high_y[i] for i in range(12)], FZ)
    spectral = [
        left_table(fy, jnp.concatenate([middle[i], below[i], above[i]], axis=0)) for i in range(10)
    ]
    step = 10 * (EY + 2)
    wide = right_table(jnp.concatenate(spectral, axis=0), fx)
    wide = wide * inv_den[...].reshape(10 * step, 10 * EX)
    back = right_table(wide, bx)
    back = [left_table(by, back[step * i : step * (i + 1)]) for i in range(10)]
    planes = along_z(back, BZ)
    edge = edge_rows(ROWS, near[2], near[3])
    row = lax.broadcasted_iota(jnp.int32, (ROWS, LANES), 0)
    for i in range(8):
        first = (1.0 - near[2]) * planes[i][ROWS : ROWS + 1]
        last = (1.0 - near[3]) * planes[i][ROWS + 1 : ROWS + 2]
        other = jnp.where(row == 0, first, jnp.where(row == ROWS - 1, last, 0.0))
        planes[i] = planes[i][0:ROWS] * edge + other
    planes[0] = planes[0] * near[0]
    planes[7] = planes[7] * near[1]
    for i in range(8):
        out_ref[i] = planes[i]
    low_ref[...] = planes[0]
    high_ref[...] = planes[7]


def partition_total(own, low_z, high_z, low_y, high_y, near):
    def planes(array):
        total = near[0] * array[0] + near[1] * array[7]
        for i in range(1, 7):
            total = total + array[i]
        return total

    total = planes(own) + 0.5 * (low_z[1] + high_z[0])
    below = planes(low_y) + 0.5 * (low_y[9] + low_y[10])
    above = planes(high_y) + 0.5 * (high_y[9] + high_y[10])
    faces = 0.5 * (below[9:10] + above[0:1])
    return jnp.sum(total * edge_rows(ROWS, near[2], near[3])) + jnp.sum(faces)


def lane_row(entries):
    lane = lax.broadcasted_iota(jnp.int32, (1, LANES), 1)
    row = jnp.zeros((1, LANES), F32)
    for index, value in enumerate(entries):
        row = jnp.where(lane == index, value, row)
    return row


def advect_kernel(lev, vel, src, packed, b_ref, l_ref, zlo, zhi):
    level = lev[...]
    v0, v1, v2 = vel[0], vel[1], vel[2]
    gz = stack(along_z([level[i] for i in range(8)], DERIV))
    advect = v0 * gz + v1 * along_y(level, packed, 0) + v2 * along_x(level, packed, 0)
    moved = level - (2.0 * TIME_STEP) * advect
    diverge = stack(along_z([v0[i] for i in range(8)], DERIV))
    diverge = diverge + along_y(v1, packed, 0) + along_x(v2, packed, 0)
    force = src[...] - (2.0 * TIME_STEP) * diverge
    weights = packed[0:ROWS]
    for i in range(8):
        mass = (0.125 * float(WEIGHT[i])) * weights
        term = mass * force[i]
        moved_i = mass * moved[i]
        b_ref[i] = term
        l_ref[i] = moved_i
        if i < 2:
            zlo[i] = term
        if i == 0:
            zlo[2] = moved_i
        if i > 5:
            zhi[i - 6] = term
        if i == 7:
            zhi[2] = moved_i


def rim_kernel(count, *refs):
    own = refs[:count]
    low_z, high_z, low_y, high_y = refs[count:]
    zeros = jnp.zeros((TILE - 10 - (count - 1), LANES), F32)

    def rows(planes, level, at, far):
        pieces = [planes[at, ROWS - 10 : ROWS] if far else planes[at, 0:10]]
        if count == 2:
            if level is None:
                pieces.append(jnp.zeros((1, LANES), F32))
            else:
                array, index = level
                pieces.append(array[index, ROWS - 1 : ROWS] if far else array[index, 0:1])
        return jnp.concatenate(pieces + [zeros], axis=0)

    for far, out in ((False, low_y), (True, high_y)):
        for i in range(8):
            out[i] = rows(own[0], (own[-1], i), i, far)
        for i in range(2):
            out[8 + i] = rows(low_z, (low_z, 2) if i == 1 else None, i, far)
            out[10 + i] = rows(high_z, (high_z, 2) if i == 0 else None, i, far)


def level_kernel(
    near, solid, spread, inv_mass, packed, inv_den, fyh, fyl, fxh, fxl, bxh, bxl, byh, byl,
    b, l, zlo, zhi, ylo, yhi, level_ref, flux_ref, w_ref, wlo, whi, stat,
):
    row = lax.broadcasted_iota(jnp.int32, (ROWS, LANES), 0)
    planes = []
    for i in range(8):
        plane = l[i]
        first = ylo[i, 10:11]
        last = yhi[i, 10:11]
        if i == 0:
            plane = plane + zlo[2]
            first = first + ylo[9, 10:11]
            last = last + yhi[9, 10:11]
        if i == 7:
            plane = plane + zhi[2]
            first = first + ylo[10, 10:11]
            last = last + yhi[10, 10:11]
        planes.append(plane + jnp.where(row == 0, first, jnp.where(row == ROWS - 1, last, 0.0)))
    own = stack(planes)
    row = lax.broadcasted_iota(jnp.int32, (8, ROWS, LANES), 1)
    lane = lax.broadcasted_iota(jnp.int32, (8, ROWS, LANES), 2)
    before = jnp.where((row % 8 == 0) & (row > 0), pltpu.roll(own, 1, 1), 0.0)
    after = jnp.where((row % 8 == 7) & (row < ROWS - 1), pltpu.roll(own, ROWS - 1, 1), 0.0)
    own = own + before + after
    before = jnp.where((lane % 8 == 0) & (lane > 0), pltpu.roll(own, 1, 2), 0.0)
    after = jnp.where((lane % 8 == 7) & (lane < LANES - 1), pltpu.roll(own, LANES - 1, 2), 0.0)
    own = own + before + after
    inverse = inv_mass[...] * edge_rows(ROWS, near[2], near[3])
    in_solid = dot(solid[...].astype(BF16), spread[...])
    open_part = jnp.concatenate(
        [jnp.broadcast_to(1.0 - (1.0 - SOLID_FACTOR) * in_solid[e : e + 1], (8, LANES)) for e in range(EY)],
        axis=0,
    )
    plane_w = packed[0:ROWS]
    total = jnp.zeros((ROWS, LANES), F32)
    for i in range(8):
        scale = 1.0 / float(WEIGHT[i])
        plane = own[i] * (inverse * scale)
        if i == 0:
            plane = plane * near[0]
        if i == 7:
            plane = plane * near[1]
        level_ref[i] = plane
        liquid = jax.nn.sigmoid(plane * (1.0 / LEVEL_WIDTH))
        coef = (GAS_RATIO - (GAS_RATIO - 1.0) * liquid) * open_part
        total = total + coef
        flux_ref[i] = (0.5 * float(WEIGHT[i])) * (coef * plane_w)
    kbar = jnp.sum(total) * (1.0 / (8 * ROWS * LANES))
    stat[...] = lane_row([kbar, partition_total(b, zlo, zhi, ylo, yhi, near)])
    tables = ((fyh, fyl), (fxh, fxl), (bxh, bxl), (byh, byl))
    schwarz(b, zlo, zhi, ylo, yhi, tables, inv_den, near, w_ref, wlo, whi)


def schwarz_kernel(
    near, inv_den, fyh, fyl, fxh, fxl, bxh, bxl, byh, byl, b, zlo, zhi, ylo, yhi,
    w_ref, wlo, whi,
):
    tables = ((fyh, fyl), (fxh, fxl), (bxh, bxl), (byh, byl))
    schwarz(b, zlo, zhi, ylo, yhi, tables, inv_den, near, w_ref, wlo, whi)


def galerkin_kernel(zt, yt, wy, packed, stat_in, flux, w, zlo, zhi, zl_ref, stat):
    local = add_planes(w, zlo[...], zhi[...])
    zl_ref[...] = local
    fluxes = flux[...]
    applied = local_operator(local, fluxes, packed)

    def combine(index, planes):
        total = zt[index, 0] * planes[0]
        for i in range(1, 8):
            total = total + zt[index, i] * planes[i]
        return jnp.sum(total, axis=1, keepdims=True)

    total = jnp.zeros((ROWS, LANES), F32)
    for a in range(3):
        placed = pltpu.roll(yt[2], 2 + 3 * a, 1)
        total = total + combine(12 + a, applied) * placed
    for index in range(6):
        shift = 11 + 9 * index
        slope_z = combine(index, fluxes) + zt[15, index] * wy[...]
        slope_y = combine(6 + index, fluxes)
        total = total + slope_z * pltpu.roll(yt[0], shift, 1)
        total = total + slope_y * pltpu.roll(yt[1], shift, 1)
    stat[...] = stat_in[...] + jnp.sum(total, axis=0, keepdims=True)


def invert(blocks, sub):
    for k in range(8):
        pivot = 1.0 / blocks[k][k : k + 1]
        scaled = jnp.where(sub == k, pivot, blocks[k] * pivot)
        rows = []
        for r in range(8):
            if r == k:
                rows.append(scaled)
            else:
                rest = jnp.where(sub == k, 0.0, blocks[r])
                rows.append(rest - blocks[r][k : k + 1] * scaled)
        blocks = rows
    return blocks


def multiply(left, right):
    rows = []
    for r in range(8):
        total = left[r][0:1] * right[0]
        for k in range(1, 8):
            total = total + left[r][k : k + 1] * right[k]
        rows.append(total)
    return rows


def matvec(terms, sub):
    result = jnp.zeros_like(terms[0][1])
    for r in range(8):
        product = terms[0][0][r] * terms[0][1]
        for blocks, column in terms[1:]:
            product = product + blocks[r] * column
        result = jnp.where(sub == r, jnp.sum(product, axis=0, keepdims=True), result)
    return result


def coarse_kernel(count, place, gathered, out_ref, wide, values):
    lanes = LANES
    wide[...] = jnp.zeros((LANES, LANES), F32)
    for i in range(8):
        wide[0:count] = gathered[count * i : count * (i + 1)]
        values[i] = wide[...].T
    sub = lax.broadcasted_iota(jnp.int32, (8, lanes), 0)
    lane = lax.broadcasted_iota(jnp.int32, (8, lanes), 1)

    def value(index):
        return jnp.concatenate([values[i, index : index + 1] for i in range(8)], axis=0)

    def move(array, dz, dy):
        if dz:
            array = pltpu.roll(array, (-dz) % 8, 0)
        if dy:
            array = pltpu.roll(array, (-dy) % lanes, 1)
        return array

    kbar = jnp.where(lane < count, value(0), 1.0)
    above = move(kbar, 1, 0)
    link_z = jnp.where(sub < 7, 2.0 * kbar * above / (kbar + above) * (EY * EX / EZ), 0.0)
    link_z = jnp.where(lane < count, link_z, 0.0)
    beside = move(kbar, 0, 1)
    link_y = 2.0 * kbar * beside / (kbar + beside) * (EZ * EX / EY)
    link_y = jnp.where(lane < count - 1, link_y, 0.0)
    back_z = move(link_z, -1, 0)
    back_y = move(link_y, 0, -1)
    diagonal = HELM_COEF * EZ * EY * EX + link_z + back_z + link_y + back_y
    blocks, lower, upper = [], [], []
    for r in range(8):
        row = jnp.where(sub == r, diagonal, 0.0)
        row = jnp.where(sub == r + 1, -back_z, row)
        row = jnp.where(sub == r - 1, -link_z, row)
        blocks.append(row)
        lower.append(jnp.where(sub == r, -back_y, 0.0))
        upper.append(jnp.where(sub == r, -link_y, 0.0))
    levels = []
    step = 1
    while step < count:
        inverse = invert(blocks, sub)
        down = multiply(lower, [move(row, 0, -step) for row in inverse])
        up = multiply(upper, [move(row, 0, step) for row in inverse])
        levels.append((step, down, up))
        before_u = multiply(down, [move(row, 0, -step) for row in upper])
        after_l = multiply(up, [move(row, 0, step) for row in lower])
        if 2 * step < count:
            new_lower = multiply(down, [move(row, 0, -step) for row in lower])
            new_upper = multiply(up, [move(row, 0, step) for row in upper])
            lower = [-row for row in new_lower]
            upper = [-row for row in new_upper]
        blocks = [blocks[r] - before_u[r] - after_l[r] for r in range(8)]
        step *= 2
    inverse = invert(blocks, sub)

    def solve(column):
        for distance, down, up in levels:
            pulled = matvec(
                [(down, move(column, 0, -distance)), (up, move(column, 0, distance))], sub
            )
            column = column - pulled
        return matvec([(inverse, column)], sub)

    offsets = [(a - 1, b - 1) for a in range(3) for b in range(3)]
    first = solve(value(1))
    near_first = [move(first, dz, dy) for dz, dy in offsets]
    totals = jnp.zeros((8, lanes), F32)
    for d, (dz, dy) in enumerate(offsets):
        term = value(2 + d)
        for e in range(9):
            a, b, c, f = d // 3, d % 3, e // 3, e % 3
            if a > c:
                a, b, c, f = c, f, a, b
            term = term + value(11 + 9 * PAIRS.index((a, c)) + 3 * b + f) * near_first[e]
        totals = totals + move(term, -dz, -dy)
    totals = jnp.where(lane < count, totals, 0.0)
    second = solve(totals)
    near_second = [move(second, dz, dy) for dz, dy in offsets]
    mine = (sub == place[0]) & (lane == place[1])
    for d in range(9):
        out_ref[d : d + 1] = jnp.full((1, lanes), jnp.sum(jnp.where(mine, near_first[d], 0.0)))
        out_ref[16 + d : 17 + d] = jnp.full(
            (1, lanes), jnp.sum(jnp.where(mine, near_second[d], 0.0))
        )


def add_coarse(local, zt, yt, coarse, start):
    columns = []
    for a in range(3):
        total = yt[2, :, 0:1] * coarse[start + 3 * a : start + 3 * a + 1]
        for b in range(1, 3):
            total = total + yt[2, :, b : b + 1] * coarse[start + 3 * a + b : start + 3 * a + b + 1]
        columns.append(total)
    planes = []
    for i in range(8):
        plane = local[i] + zt[13, i] * columns[1]
        if i == 0:
            plane = plane + zt[12, i] * columns[0]
        if i == 7:
            plane = plane + zt[14, i] * columns[2]
        planes.append(plane)
    return stack(planes)


def apply_kernel(
    zt, yt, packed, coarse, flux, b, zl,
    z_ref, y_ref, ylo, yhi, stat,
):
    field = add_coarse(zl[...], zt, yt, coarse, 0)
    z_ref[...] = field
    applied = local_operator(field, flux[...], packed)
    y_ref[...] = applied
    ylo[...] = applied[0:2]
    yhi[...] = applied[6:8]
    stat[...] = lane_row([jnp.sum(b[...] * field), jnp.sum(field * applied)])


def second_kernel(
    zt, yt, packed, coarse, flux, b, y, w, zlo, zhi,
    stat_in, q_ref, stat,
):
    local = add_planes(w, zlo[...], zhi[...])
    field = add_coarse(local, zt, yt, coarse, 16)
    q_ref[...] = field
    applied = local_operator(field, flux[...], packed)
    sums = [0.0, 0.0, jnp.sum(b[...] * field), jnp.sum(y[...] * field), jnp.sum(field * applied)]
    stat[...] = stat_in[...] + lane_row(sums)


def combine_kernel(sums, z, q, p_ref):
    total = jnp.sum(sums[...], axis=0, keepdims=True)
    rz, pap, rq, aq, qhq = (total[:, k : k + 1] for k in range(5))
    step = rz / pap
    rz_next = step * (step * aq - rq)
    beta = rz_next / rz
    grown = 1.0 + beta
    curved = grown * grown * pap - 2.0 * step * grown * aq + step * step * qhq
    step_next = rz_next / curved
    on_z = step + step_next * grown
    on_q = step_next * step
    p_ref[...] = on_z.reshape(1, 1, 1) * z[...] - on_q.reshape(1, 1, 1) * q[...]


def call(kernel, outs, specs, args, scratch=(), flops=1000000):
    nbytes = sum(4 * int(np.prod(out)) for out in outs) * 2
    return pl.pallas_call(
        kernel,
        out_shape=[jax.ShapeDtypeStruct(out, F32) for out in outs],
        in_specs=[pl.BlockSpec(memory_space=SMEM if spec else VMEM) for spec in specs],
        out_specs=[pl.BlockSpec(memory_space=VMEM) for _ in outs],
        scratch_shapes=list(scratch),
        compiler_params=pltpu.CompilerParams(vmem_limit_bytes=LIMIT),
        cost_estimate=pl.CostEstimate(flops=flops, bytes_accessed=nbytes, transcendentals=0),
    )(*args)


def run(kernel, outs, smem, args, scratch=(), flops=1000000):
    specs = [True] * len(smem) + [False] * len(args)
    return call(kernel, outs, specs, list(smem) + list(args), scratch, flops)


def shift(axis, low_face, high_face):
    count = lax.axis_size(axis)
    forward = [(i, i + 1) for i in range(count - 1)]
    backward = [(target, source) for source, target in forward]
    return lax.ppermute(high_face, axis, forward), lax.ppermute(low_face, axis, backward)


def body(level_set, velocity, source, wick_solid):
    block = level_set.shape
    count_gx = lax.axis_size("gx")
    count_gy = lax.axis_size("gy")
    index_gx = lax.axis_index("gx")
    index_gy = lax.axis_index("gy")

    def ends(index, count):
        return [jnp.where(index > 0, 0.5, 1.0), jnp.where(index < count - 1, 0.5, 1.0)]

    def case(index, count):
        return jnp.where(index == 0, 0, jnp.where(index == count - 1, 2, 1))

    near = jnp.stack(ends(index_gx, count_gx) + ends(index_gy, count_gy)).astype(F32)
    zt = lax.dynamic_index_in_dim(jnp.asarray(Z_TABLE), case(index_gx, count_gx), 0, False)
    yt = lax.dynamic_index_in_dim(jnp.asarray(Y_TABLE), case(index_gy, count_gy), 0, False)
    place = jnp.stack([index_gx, index_gy]).astype(jnp.int32)
    packed = jnp.asarray(PACKED)
    wy = jnp.asarray(WY.astype(np.float32)[:, None])
    solver = (INV_DEN, FY_H, FY_L, FX_H, FX_L, BX_H, BX_L, BY_H, BY_L)
    solver = tuple(jnp.asarray(table) for table in solver)
    face = (ROWS, LANES)
    rim = (12, TILE, LANES)
    solid = wick_solid.reshape(EY, EX).astype(F32)

    b, l, zlo, zhi = run(
        advect_kernel,
        [block, block, (3, *face), (3, *face)],
        [],
        [level_set, velocity, source, packed],
    )
    zlo, zhi = shift("gx", zlo, zhi)
    ylo, yhi = run(functools.partial(rim_kernel, 2), [rim, rim], [], [b, l, zlo, zhi])
    ylo, yhi = shift("gy", ylo, yhi)
    level_new, flux, w, wlo, whi, stat = run(
        level_kernel,
        [block, block, block, face, face, (1, LANES)],
        [near],
        [
            solid, jnp.asarray(SPREAD), jnp.asarray(INV_MASS), packed, *solver,
            b, l, zlo, zhi, ylo, yhi,
        ],
    )
    zlo, zhi = shift("gx", wlo, whi)
    zl, stat = run(
        galerkin_kernel,
        [block, (1, LANES)],
        [zt],
        [yt, wy, packed, stat, flux, w, zlo, zhi],
    )
    wide = jnp.broadcast_to(stat, (count_gx * count_gy, LANES))
    gathered = lax.all_to_all(wide, ("gx", "gy"), 0, 0, tiled=True)
    (coarse,) = run(
        functools.partial(coarse_kernel, count_gy),
        [(32, LANES)],
        [place],
        [gathered],
        [VMEM((LANES, LANES), F32), VMEM((8, LANES, LANES), F32)],
    )
    z, y, zlo, zhi, sums = run(
        apply_kernel,
        [block, block, (2, *face), (2, *face), (1, LANES)],
        [zt],
        [yt, packed, coarse, flux, b, zl],
    )
    zlo, zhi = shift("gx", zlo, zhi)
    ylo, yhi = run(functools.partial(rim_kernel, 1), [rim, rim], [], [y, zlo, zhi])
    ylo, yhi = shift("gy", ylo, yhi)
    w, wlo, whi = run(
        schwarz_kernel,
        [block, face, face],
        [near],
        [*solver, y, zlo, zhi, ylo, yhi],
    )
    zlo, zhi = shift("gx", wlo, whi)
    q, sums = run(
        second_kernel,
        [block, (1, LANES)],
        [zt],
        [yt, packed, coarse, flux, b, y, w, zlo, zhi, sums],
    )
    tile = jnp.broadcast_to(sums, (count_gx, LANES))
    tile = lax.all_to_all(tile, "gx", 0, 0, tiled=True)
    wide = jnp.broadcast_to(jnp.sum(tile, axis=0, keepdims=True), (count_gy, LANES))
    wide = lax.all_to_all(wide, "gy", 0, 0, tiled=True)
    (pressure,) = run(combine_kernel, [block], [], [wide, z, q])
    return (level_new, pressure)


def solution(mesh):
    placed = (
        P("gx", "gy", None),
        P(None, "gx", "gy", None),
        P("gx", "gy", None),
        P("gx", "gy", None),
    )
    return jax.shard_map(
        body,
        mesh=mesh,
        in_specs=placed,
        out_specs=(P("gx", "gy", None), P("gx", "gy", None)),
        check_vma=False,
    )
```

```python
import functools

import jax
import jax.numpy as jnp
import numpy as np
from jax import lax
from jax.experimental import pallas as pl
from jax.experimental.pallas import tpu as pltpu
from jax.sharding import PartitionSpec as P

EZ = 1
EY = 4
EX = 16
ROWS = 8 * EY
LANES = 8 * EX

TIME_STEP = 0.02
HELM_COEF = 0.25
LEVEL_WIDTH = 0.25
GAS_RATIO = 10.0
SOLID_FACTOR = 0.25
SCHWARZ_SCALE = 0.5
SCHWARZ_SHIFT = 0.05

F32 = jnp.float32
BF16 = jnp.bfloat16
VMEM = pltpu.VMEM
SMEM = pltpu.SMEM
LIMIT = 24 * 1024 * 1024


def gll_tables():
    gll_nodes = np.array(
        [
            -1.0,
            -0.8717401485096066,
            -0.5917001814331423,
            -0.2092992179024789,
            0.2092992179024789,
            0.5917001814331423,
            0.8717401485096066,
            1.0,
        ]
    )
    weight_np = np.array(
        [
            1.0 / 28.0,
            0.21070422714350603,
            0.3411226924835044,
            0.4124587946587038,
            0.4124587946587038,
            0.3411226924835044,
            0.21070422714350603,
            1.0 / 28.0,
        ]
    )
    bary_weights = np.array(
        [1.0 / np.prod([gll_nodes[i] - gll_nodes[j] for j in range(8) if j != i]) for i in range(8)]
    )
    derivative = np.zeros((8, 8))
    for i in range(8):
        for j in range(8):
            if i != j:
                derivative[i, j] = bary_weights[j] / bary_weights[i] / (gll_nodes[i] - gll_nodes[j])
        derivative[i, i] = -np.sum(derivative[i])
    return (weight_np, derivative)


def sine_tables():
    indices = np.arange(10) + 1.0
    sine_basis = np.sqrt(2.0 / 11.0) * np.sin(np.pi * np.outer(indices, indices) / 11.0)
    eigen_vals = 2.0 - 2.0 * np.cos(np.pi * indices / 11.0)
    return (sine_basis, eigen_vals)


WEIGHT, DERIV = gll_tables()
SINE, EIGEN = sine_tables()


def split_const(matrix):
    single = matrix.astype(np.float32)
    high = single.astype(jnp.bfloat16)
    low = (single - high.astype(np.float32)).astype(jnp.bfloat16)
    return high, low


def line_maps(count):
    length = 8 * count
    total = length + 4

    def column(position):
        if 0 <= position < length:
            return position
        return {-2: length, -1: length + 1, length: length + 2, length + 1: length + 3}[position]

    assembled = {}
    for position in range(-2, length + 2):
        row = np.zeros(total)
        row[column(position)] = 1.0
        if 0 <= position < length:
            if position % 8 == 0:
                row[column(position - 1)] += 1.0
            if position % 8 == 7:
                row[column(position + 1)] += 1.0
        assembled[position] = row
    forward = np.zeros((10 * count, total))
    for element in range(count):
        places = [8 * element - 2] + list(range(8 * element, 8 * element + 8)) + [8 * element + 9]
        forward[10 * element : 10 * element + 10] = SINE @ np.stack([assembled[p] for p in places])
    backward = np.zeros((length, 10 * count))
    for element in range(count):
        backward[8 * element : 8 * element + 8, 10 * element : 10 * element + 10] = SINE[1:9]
    for element in range(count - 1):
        first, second = 8 * element + 7, 8 * element + 8
        mean = 0.5 * (backward[first] + backward[second])
        backward[first] = mean
        backward[second] = mean
    return forward, backward


def wide_maps():
    count = EY + 2
    forward, backward = line_maps(count)
    length = 8 * count
    columns = np.zeros((10 * count, ROWS + 2 * TILE))
    columns[:, :ROWS] = forward[:, 8 : 8 + ROWS]
    columns[:, ROWS : ROWS + 2] = forward[:, length : length + 2]
    columns[:, ROWS + 2 : ROWS + 10] = forward[:, :8]
    columns[:, ROWS + TILE : ROWS + TILE + 8] = forward[:, length - 8 : length]
    columns[:, ROWS + TILE + 8 : ROWS + TILE + 10] = forward[:, length + 2 : length + 4]
    _, own = line_maps(EY)
    rows = np.zeros((ROWS + 8, 10 * count))
    rows[:ROWS, 10 : 10 + 10 * EY] = own
    rows[ROWS, :10] = SINE[8]
    rows[ROWS + 1, 10 + 10 * EY :] = SINE[1]
    return columns, rows


TILE = 16
FZ, BZ = line_maps(1)
FY, BY = wide_maps()
FX, BX = line_maps(EX)
FX = FX[:, :LANES]


def denominators():
    lam_y = np.tile(EIGEN, EY + 2)
    lam_x = np.tile(EIGEN, EX)
    total = EIGEN[:, None, None] + lam_y[None, :, None] + lam_x[None, None, :]
    return (1.0 / (SCHWARZ_SCALE * total + SCHWARZ_SHIFT)).astype(np.float32)


INV_DEN = denominators()
FY_H, FY_L = split_const(FY)
BY_H, BY_L = split_const(BY)
FX_H, FX_L = split_const(FX.T.copy())
BX_H, BX_L = split_const(BX.T.copy())


def roll_table():
    table = np.zeros((2, 8, 8, LANES))
    for kind, matrix in enumerate((DERIV, DERIV.T)):
        for k in range(8):
            for i in range(8):
                table[kind, k, i, :] = matrix[i, (i + k) % 8]
    return table.reshape(2 * 64, LANES)


WY = np.tile(WEIGHT, EY)
WX = np.tile(WEIGHT, EX)
AT_ROLLS = ROWS
AT_DX = AT_ROLLS + 128
AT_DXT = AT_DX + LANES
AT_SQUARE = AT_DXT + LANES
PACKED = np.concatenate(
    [
        WY[:, None] * WX[None, :],
        roll_table(),
        np.kron(np.eye(EX), DERIV.T),
        np.kron(np.eye(EX), DERIV),
        np.repeat(DERIV[:, :1] ** 2, LANES, axis=1),
        np.repeat(DERIV[:, 7:] ** 2, LANES, axis=1),
    ]
).astype(np.float32)


def inner_count(count):
    mult = np.ones(8 * count)
    position = np.arange(8 * count)
    mult[(position % 8 == 0) & (position > 0)] += 1.0
    mult[(position % 8 == 7) & (position < 8 * count - 1)] += 1.0
    return mult


INV_MASS = (8.0 / (WY * inner_count(EY))[:, None] / (WX * inner_count(EX))[None, :]).astype(
    np.float32
)
SPREAD = np.kron(np.eye(EX), np.ones((1, 8))).astype(jnp.bfloat16)


def parts(values):
    high = values.astype(BF16)
    low = (values - high.astype(F32)).astype(BF16)
    return high, low


def dot(left, right):
    return jnp.dot(left, right, preferred_element_type=F32)


def left_table(table, values):
    high, low = parts(values)
    return dot(table[0][...], high) + dot(table[0][...], low) + dot(table[1][...], high)


def right_table(values, table):
    high, low = parts(values)
    return dot(high, table[0][...]) + dot(low, table[0][...]) + dot(high, table[1][...])


def along_z(values, matrix):
    rows = []
    for i in range(matrix.shape[0]):
        total = None
        for j in range(matrix.shape[1]):
            if matrix[i, j] == 0.0:
                continue
            term = float(matrix[i, j]) * values[j]
            total = term if total is None else total + term
        rows.append(total)
    return rows


def along_y(values, packed, kind):
    grouped = values.reshape(8 * EY, 8, LANES)
    start = AT_ROLLS + 64 * kind
    total = packed[start : start + 8][None] * grouped
    for k in range(1, 8):
        total = total + packed[start + 8 * k : start + 8 * k + 8][None] * pltpu.roll(grouped, 8 - k, 1)
    return total.reshape(8, ROWS, LANES)


def along_x(values, packed, kind):
    start = AT_DXT if kind else AT_DX
    high, low = parts(packed[start : start + LANES])
    first, rest = parts(values.reshape(8 * ROWS, LANES))
    total = dot(first, high) + dot(rest, high) + dot(first, low)
    return total.reshape(8, ROWS, LANES)


def stack(planes):
    return jnp.concatenate([plane[None] for plane in planes], axis=0)


def edge_rows(rows, low, high):
    position = lax.broadcasted_iota(jnp.int32, (rows, LANES), 0)
    return jnp.where(position == 0, low, jnp.where(position == rows - 1, high, 1.0))


def local_operator(values, flux, packed):
    plane_w = packed[0:ROWS]
    gz = along_z([values[i] for i in range(8)], DERIV)
    fz = along_z([flux[i] * gz[i] for i in range(8)], DERIV.T)
    total = along_y(flux * along_y(values, packed, 0), packed, 1)
    total = total + along_x(flux * along_x(values, packed, 0), packed, 1)
    planes = [
        total[i] + fz[i] + (HELM_COEF * 0.125 * float(WEIGHT[i])) * (plane_w * values[i])
        for i in range(8)
    ]
    return stack(planes)


def add_planes(own, low_z, high_z):
    planes = [own[i] for i in range(8)]
    planes[0] = planes[0] + low_z
    planes[7] = planes[7] + high_z
    return stack(planes)


def schwarz(own, low_z, high_z, low_y, high_y, tables, inv_den, near, out_ref, low_ref, high_ref):
    fy, fx, bx, by = tables
    middle = along_z([own[i] for i in range(8)] + [low_z[0], low_z[1], high_z[0], high_z[1]], FZ)
    below = along_z([low_y[i] for i in range(12)], FZ)
    above = along_z([high_y[i] for i in range(12)], FZ)
    spectral = [
        left_table(fy, jnp.concatenate([middle[i], below[i], above[i]], axis=0)) for i in range(10)
    ]
    step = 10 * (EY + 2)
    wide = right_table(jnp.concatenate(spectral, axis=0), fx)
    wide = wide * inv_den[...].reshape(10 * step, 10 * EX)
    back = right_table(wide, bx)
    back = [left_table(by, back[step * i : step * (i + 1)]) for i in range(10)]
    planes = along_z(back, BZ)
    edge = edge_rows(ROWS, near[2], near[3])
    row = lax.broadcasted_iota(jnp.int32, (ROWS, LANES), 0)
    for i in range(8):
        first = (1.0 - near[2]) * planes[i][ROWS : ROWS + 1]
        last = (1.0 - near[3]) * planes[i][ROWS + 1 : ROWS + 2]
        other = jnp.where(row == 0, first, jnp.where(row == ROWS - 1, last, 0.0))
        planes[i] = planes[i][0:ROWS] * edge + other
    planes[0] = planes[0] * near[0]
    planes[7] = planes[7] * near[1]
    for i in range(8):
        out_ref[i] = planes[i]
    low_ref[...] = planes[0]
    high_ref[...] = planes[7]


def partition_total(own, low_z, high_z, low_y, high_y, near):
    def planes(array):
        total = near[0] * array[0] + near[1] * array[7]
        for i in range(1, 7):
            total = total + array[i]
        return total

    total = planes(own) + 0.5 * (low_z[1] + high_z[0])
    below = planes(low_y) + 0.5 * (low_y[9] + low_y[10])
    above = planes(high_y) + 0.5 * (high_y[9] + high_y[10])
    faces = 0.5 * (below[9:10] + above[0:1])
    return jnp.sum(total * edge_rows(ROWS, near[2], near[3])) + jnp.sum(faces)


def lane_row(entries):
    lane = lax.broadcasted_iota(jnp.int32, (1, LANES), 1)
    row = jnp.zeros((1, LANES), F32)
    for index, value in enumerate(entries):
        row = jnp.where(lane == index, value, row)
    return row


def advect_kernel(
    lev_in, vel_in, src_in, packed_in, b_ref, l_ref, zlo, zhi, lev, vel, src, packed, sems
):
    copies = [
        pltpu.make_async_copy(source, target, sems.at[index])
        for index, (source, target) in enumerate(
            ((vel_in, vel), (lev_in, lev), (packed_in, packed), (src_in, src))
        )
    ]
    for copy in copies:
        copy.start()
    for copy in copies:
        copy.wait()
    level = lev[...]
    v0, v1, v2 = vel[0], vel[1], vel[2]
    gz = stack(along_z([level[i] for i in range(8)], DERIV))
    advect = v0 * gz + v1 * along_y(level, packed, 0) + v2 * along_x(level, packed, 0)
    moved = level - (2.0 * TIME_STEP) * advect
    diverge = stack(along_z([v0[i] for i in range(8)], DERIV))
    diverge = diverge + along_y(v1, packed, 0) + along_x(v2, packed, 0)
    force = src[...] - (2.0 * TIME_STEP) * diverge
    weights = packed[0:ROWS]
    for i in range(8):
        mass = (0.125 * float(WEIGHT[i])) * weights
        term = mass * force[i]
        moved_i = mass * moved[i]
        b_ref[i] = term
        l_ref[i] = moved_i
        if i < 2:
            zlo[i] = term
        if i == 0:
            zlo[2] = moved_i
        if i > 5:
            zhi[i - 6] = term
        if i == 7:
            zhi[2] = moved_i


def rim_kernel(count, *refs):
    own = refs[:count]
    low_z, high_z, low_y, high_y = refs[count:]
    zeros = jnp.zeros((TILE - 10 - (count - 1), LANES), F32)

    def rows(planes, level, at, far):
        pieces = [planes[at, ROWS - 10 : ROWS] if far else planes[at, 0:10]]
        if count == 2:
            if level is None:
                pieces.append(jnp.zeros((1, LANES), F32))
            else:
                array, index = level
                pieces.append(array[index, ROWS - 1 : ROWS] if far else array[index, 0:1])
        return jnp.concatenate(pieces + [zeros], axis=0)

    for far, out in ((False, low_y), (True, high_y)):
        for i in range(8):
            out[i] = rows(own[0], (own[-1], i), i, far)
        for i in range(2):
            out[8 + i] = rows(low_z, (low_z, 2) if i == 1 else None, i, far)
            out[10 + i] = rows(high_z, (high_z, 2) if i == 0 else None, i, far)


def level_kernel(
    near, solid, spread, inv_mass, packed, b, l, zlo, zhi, ylo, yhi, level_ref, flux_ref, stat
):
    row = lax.broadcasted_iota(jnp.int32, (ROWS, LANES), 0)
    planes = []
    for i in range(8):
        plane = l[i]
        first = ylo[i, 10:11]
        last = yhi[i, 10:11]
        if i == 0:
            plane = plane + zlo[2]
            first = first + ylo[9, 10:11]
            last = last + yhi[9, 10:11]
        if i == 7:
            plane = plane + zhi[2]
            first = first + ylo[10, 10:11]
            last = last + yhi[10, 10:11]
        planes.append(plane + jnp.where(row == 0, first, jnp.where(row == ROWS - 1, last, 0.0)))
    own = stack(planes)
    row = lax.broadcasted_iota(jnp.int32, (8, ROWS, LANES), 1)
    lane = lax.broadcasted_iota(jnp.int32, (8, ROWS, LANES), 2)
    before = jnp.where((row % 8 == 0) & (row > 0), pltpu.roll(own, 1, 1), 0.0)
    after = jnp.where((row % 8 == 7) & (row < ROWS - 1), pltpu.roll(own, ROWS - 1, 1), 0.0)
    own = own + before + after
    before = jnp.where((lane % 8 == 0) & (lane > 0), pltpu.roll(own, 1, 2), 0.0)
    after = jnp.where((lane % 8 == 7) & (lane < LANES - 1), pltpu.roll(own, LANES - 1, 2), 0.0)
    own = own + before + after
    inverse = inv_mass[...] * edge_rows(ROWS, near[2], near[3])
    in_solid = dot(solid[...].astype(BF16), spread[...])
    open_part = jnp.concatenate(
        [jnp.broadcast_to(1.0 - (1.0 - SOLID_FACTOR) * in_solid[e : e + 1], (8, LANES)) for e in range(EY)],
        axis=0,
    )
    plane_w = packed[0:ROWS]
    total = jnp.zeros((ROWS, LANES), F32)
    fluxes = []
    for i in range(8):
        scale = 1.0 / float(WEIGHT[i])
        plane = own[i] * (inverse * scale)
        if i == 0:
            plane = plane * near[0]
        if i == 7:
            plane = plane * near[1]
        level_ref[i] = plane
        liquid = jax.nn.sigmoid(plane * (1.0 / LEVEL_WIDTH))
        coef = (GAS_RATIO - (GAS_RATIO - 1.0) * liquid) * open_part
        total = total + coef
        flux = (0.5 * float(WEIGHT[i])) * (coef * plane_w)
        flux_ref[i] = flux
        fluxes.append(flux)
    kbar = jnp.sum(total) * (1.0 / (8 * ROWS * LANES))
    entries = [kbar, partition_total(b, zlo, zhi, ylo, yhi, near)] + [0.0] * 9
    for first, second in ((0, 0), (0, 7), (7, 7)):
        slopes = along_z(fluxes, (DERIV[:, first] * DERIV[:, second])[None, :])[0]
        column = jnp.sum(slopes, axis=1, keepdims=True)
        entries += [jnp.sum(column, axis=0, keepdims=True), column[0:1], column[ROWS - 1 : ROWS]]
    inner = fluxes[0] + fluxes[1]
    for i in range(2, 8):
        inner = inner + fluxes[i]
    for at, start in ((0, 0), (ROWS - 8, 8)):
        square = packed[AT_SQUARE + start : AT_SQUARE + start + 8]
        entries += [jnp.sum(square * plane[at : at + 8]) for plane in (inner, fluxes[0], fluxes[7])]
    stat[...] = lane_row(entries)


def schwarz_kernel(
    near, inv_den, fyh, fyl, fxh, fxl, bxh, bxl, byh, byl, b, zlo, zhi, ylo, yhi,
    w_ref, wlo, whi,
):
    tables = ((fyh, fyl), (fxh, fxl), (bxh, bxl), (byh, byl))
    schwarz(b, zlo, zhi, ylo, yhi, tables, inv_den, near, w_ref, wlo, whi)


def galerkin_kernel(near, packed, stat_in, flux, w, zlo, zhi, zl_ref, stat):
    local = add_planes(w, zlo[...], zhi[...])
    zl_ref[...] = local
    applied = local_operator(local, flux[...], packed)
    inner = near[0] * applied[0] + near[1] * applied[7]
    for i in range(1, 7):
        inner = inner + applied[i]
    edge = edge_rows(ROWS, near[2], near[3])
    entries = [0.0, 0.0]
    for plane in ((1.0 - near[0]) * applied[0], inner, (1.0 - near[1]) * applied[7]):
        entries += [
            (1.0 - near[2]) * jnp.sum(plane[0:1]),
            jnp.sum(edge * plane),
            (1.0 - near[3]) * jnp.sum(plane[ROWS - 1 : ROWS]),
        ]
    stat[...] = jnp.broadcast_to(stat_in[...] + lane_row(entries), stat.shape)


def turn_kernel(gathered, out_ref, wide):
    count = gathered.shape[0]
    wide[...] = jnp.zeros((LANES, LANES), F32)
    wide[0:count] = gathered[...]
    turned = wide[...].T
    tile = turned[0:16] + pltpu.roll(turned[16:32], LANES // 2, 1)
    for i in range(out_ref.shape[0]):
        out_ref[i] = tile


def invert(blocks, sub):
    for k in range(8):
        pivot = 1.0 / blocks[k][k : k + 1]
        scaled = jnp.where(sub == k, pivot, blocks[k] * pivot)
        rows = []
        for r in range(8):
            if r == k:
                rows.append(scaled)
            else:
                rest = jnp.where(sub == k, 0.0, blocks[r])
                rows.append(rest - blocks[r][k : k + 1] * scaled)
        blocks = rows
    return blocks


def multiply(left, right):
    rows = []
    for r in range(8):
        total = left[r][0:1] * right[0]
        for k in range(1, 8):
            total = total + left[r][k : k + 1] * right[k]
        rows.append(total)
    return rows


def matvec(terms, sub):
    result = jnp.zeros_like(terms[0][1])
    for r in range(8):
        product = terms[0][0][r] * terms[0][1]
        for blocks, column in terms[1:]:
            product = product + blocks[r] * column
        result = jnp.where(sub == r, jnp.sum(product, axis=0, keepdims=True), result)
    return result


def coarse_operator(c, sums_z, sums_y, low_z, high_z, low_y, high_y):
    result = [[None] * 3 for _ in range(3)]

    def ends(values, low, high):
        inside = values[1]
        first = (1.0 - low) * inside + low * values[0]
        last = (1.0 - high) * inside + high * values[2]
        return inside, first, last

    def tested(inside, first, last, low, high):
        return (low * first, inside + (1.0 - low) * first + (1.0 - high) * last, high * last)

    by_b = []
    for b in range(3):
        inside, first, last = ends([c[a][b] for a in range(3)], low_z, high_z)
        end = float(WEIGHT[0])
        by_b.append(tested((2.0 - 2.0 * end) * inside, end * first, end * last, low_z, high_z))
    scale = HELM_COEF / 8.0 * float(np.sum(WX))
    for a in range(3):
        inside, first, last = ends([by_b[b][a] for b in range(3)], low_y, high_y)
        end = scale * float(WEIGHT[0])
        middle = scale * (2.0 * EY - 2.0 * float(WEIGHT[0]))
        result[a] = list(tested(middle * inside, end * first, end * last, low_y, high_y))

    slopes = []
    for outer, factor in ((0, low_z), (2, high_z)):
        slopes.append(ends([factor * (c[outer][b] - c[1][b]) for b in range(3)], low_y, high_y))
    for s, (outer, factor) in enumerate(((0, low_z), (2, high_z))):
        parts_y = []
        for place in range(3):
            total = None
            for t in range(2):
                whole, first, last = sums_z[s + t]
                weight = (whole - first - last, first, last)[place]
                term = weight * slopes[t][place]
                total = term if total is None else total + term
            parts_y.append(total)
        for b, value in enumerate(tested(*parts_y, low_y, high_y)):
            result[outer][b] = result[outer][b] + factor * value
            result[1][b] = result[1][b] - factor * value

    for s, (outer, factor) in enumerate(((0, low_y), (2, high_y))):
        slope = ends([factor * (c[a][outer] - c[a][1]) for a in range(3)], low_z, high_z)
        whole, first, last = sums_y[s]
        pieces = ((whole - first - last) * slope[0], first * slope[1], last * slope[2])
        for a, value in enumerate(tested(*pieces, low_z, high_z)):
            result[a][outer] = result[a][outer] + factor * value
            result[a][1] = result[a][1] - factor * value
    return result


def coarse_kernel(count, place, gathered, out_ref):
    lanes = LANES
    sub = lax.broadcasted_iota(jnp.int32, (8, lanes), 0)
    lane = lax.broadcasted_iota(jnp.int32, (8, lanes), 1)

    def value(index):
        row = index % 16
        array = jnp.concatenate([gathered[i, row : row + 1] for i in range(8)], axis=0)
        if index >= 16:
            array = pltpu.roll(array, lanes // 2, 1)
        return jnp.where(lane < count, array, 0.0)

    def move(array, dz, dy):
        if dz:
            array = pltpu.roll(array, (-dz) % 8, 0)
        if dy:
            array = pltpu.roll(array, (-dy) % lanes, 1)
        return array

    kbar = jnp.where(lane < count, value(0), 1.0)
    above = move(kbar, 1, 0)
    link_z = jnp.where(sub < 7, 2.0 * kbar * above / (kbar + above) * (EY * EX / EZ), 0.0)
    link_z = jnp.where(lane < count, link_z, 0.0)
    beside = move(kbar, 0, 1)
    link_y = 2.0 * kbar * beside / (kbar + beside) * (EZ * EX / EY)
    link_y = jnp.where(lane < count - 1, link_y, 0.0)
    back_z = move(link_z, -1, 0)
    back_y = move(link_y, 0, -1)
    diagonal = HELM_COEF * EZ * EY * EX + link_z + back_z + link_y + back_y
    blocks, lower, upper = [], [], []
    for r in range(8):
        row = jnp.where(sub == r, diagonal, 0.0)
        row = jnp.where(sub == r + 1, -back_z, row)
        row = jnp.where(sub == r - 1, -link_z, row)
        blocks.append(row)
        lower.append(jnp.where(sub == r, -back_y, 0.0))
        upper.append(jnp.where(sub == r, -link_y, 0.0))
    levels = []
    step = 1
    while step < count:
        inverse = invert(blocks, sub)
        down = multiply(lower, [move(row, 0, -step) for row in inverse])
        up = multiply(upper, [move(row, 0, step) for row in inverse])
        levels.append((step, down, up))
        before_u = multiply(down, [move(row, 0, -step) for row in upper])
        after_l = multiply(up, [move(row, 0, step) for row in lower])
        if 2 * step < count:
            new_lower = multiply(down, [move(row, 0, -step) for row in lower])
            new_upper = multiply(up, [move(row, 0, step) for row in upper])
            lower = [-row for row in new_lower]
            upper = [-row for row in new_upper]
        blocks = [blocks[r] - before_u[r] - after_l[r] for r in range(8)]
        step *= 2
    inverse = invert(blocks, sub)

    def solve(column):
        for distance, down, up in levels:
            pulled = matvec(
                [(down, move(column, 0, -distance)), (up, move(column, 0, distance))], sub
            )
            column = column - pulled
        return matvec([(inverse, column)], sub)

    offsets = [(a - 1, b - 1) for a in range(3) for b in range(3)]
    first = solve(value(1))
    near_first = [move(first, dz, dy) for dz, dy in offsets]
    low_z = jnp.where(sub > 0, 0.5, 0.0)
    high_z = jnp.where(sub < 7, 0.5, 0.0)
    low_y = jnp.where(lane > 0, 0.5, 0.0)
    high_y = jnp.where(lane < count - 1, 0.5, 0.0)
    sums_z = [[value(11 + 3 * k + j) for j in range(3)] for k in range(3)]
    sums_y = [[value(20 + 3 * k + j) for j in range(3)] for k in range(2)]
    values = [near_first[0:3], near_first[3:6], near_first[6:9]]
    tested = coarse_operator(values, sums_z, sums_y, low_z, high_z, low_y, high_y)
    totals = jnp.zeros((8, lanes), F32)
    for d, (dz, dy) in enumerate(offsets):
        term = jnp.where(lane < count, value(2 + d) + tested[d // 3][d % 3], 0.0)
        totals = totals + move(term, -dz, -dy)
    totals = jnp.where(lane < count, totals, 0.0)
    second = solve(totals)
    near_second = [move(second, dz, dy) for dz, dy in offsets]
    mine = (sub == place[0]) & (lane == place[1])
    for d in range(9):
        out_ref[d : d + 1] = jnp.full((1, lanes), jnp.sum(jnp.where(mine, near_first[d], 0.0)))
        out_ref[16 + d : 17 + d] = jnp.full(
            (1, lanes), jnp.sum(jnp.where(mine, near_second[d], 0.0))
        )


def add_coarse(local, near, coarse, start):
    row = lax.broadcasted_iota(jnp.int32, (ROWS, LANES), 0)
    edge = edge_rows(ROWS, near[2], near[3])
    below = jnp.where(row == 0, 1.0 - near[2], 0.0)
    above = jnp.where(row == ROWS - 1, 1.0 - near[3], 0.0)
    columns = []
    for a in range(3):
        at = start + 3 * a
        columns.append(
            below * coarse[at : at + 1] + edge * coarse[at + 1 : at + 2] + above * coarse[at + 2 : at + 3]
        )
    planes = [local[i] + columns[1] for i in range(8)]
    planes[0] = planes[0] + (1.0 - near[0]) * (columns[0] - columns[1])
    planes[7] = planes[7] + (1.0 - near[1]) * (columns[2] - columns[1])
    return stack(planes)


def apply_kernel(near, packed, coarse, flux, b, zl, z_ref, y_ref, ylo, yhi, stat):
    field = add_coarse(zl[...], near, coarse, 0)
    z_ref[...] = field
    applied = local_operator(field, flux[...], packed)
    y_ref[...] = applied
    ylo[...] = applied[0:2]
    yhi[...] = applied[6:8]
    stat[...] = lane_row([jnp.sum(b[...] * field), jnp.sum(field * applied)])


def second_kernel(near, packed, coarse, flux, b, y, w, zlo, zhi, stat_in, q_ref, stat):
    local = add_planes(w, zlo[...], zhi[...])
    field = add_coarse(local, near, coarse, 16)
    q_ref[...] = field
    applied = local_operator(field, flux[...], packed)
    sums = [0.0, 0.0, jnp.sum(b[...] * field), jnp.sum(y[...] * field), jnp.sum(field * applied)]
    stat[...] = jnp.broadcast_to(stat_in[...] + lane_row(sums), stat.shape)


def combine_kernel(sums, z, q, p_ref):
    total = jnp.sum(sums[...], axis=0, keepdims=True)
    rz, pap, rq, aq, qhq = (total[:, k : k + 1] for k in range(5))
    step = rz / pap
    rz_next = step * (step * aq - rq)
    beta = rz_next / rz
    grown = 1.0 + beta
    curved = grown * grown * pap - 2.0 * step * grown * aq + step * step * qhq
    step_next = rz_next / curved
    on_z = step + step_next * grown
    on_q = step_next * step
    p_ref[...] = on_z.reshape(1, 1, 1) * z[...] - on_q.reshape(1, 1, 1) * q[...]


def run(kernel, outs, smem, args, scratch=(), flops=1000000, place=VMEM, limit=LIMIT):
    nbytes = sum(4 * int(np.prod(out)) for out in outs) * 2
    return pl.pallas_call(
        kernel,
        out_shape=[jax.ShapeDtypeStruct(out, F32) for out in outs],
        in_specs=[pl.BlockSpec(memory_space=SMEM) for _ in smem]
        + [pl.BlockSpec(memory_space=place) for _ in args],
        out_specs=[pl.BlockSpec(memory_space=VMEM) for _ in outs],
        scratch_shapes=list(scratch),
        compiler_params=pltpu.CompilerParams(vmem_limit_bytes=limit),
        cost_estimate=pl.CostEstimate(flops=flops, bytes_accessed=nbytes, transcendentals=0),
    )(*smem, *args)


def shift(axis, low_face, high_face):
    count = lax.axis_size(axis)
    forward = [(i, i + 1) for i in range(count - 1)]
    backward = [(target, source) for source, target in forward]
    return lax.ppermute(high_face, axis, forward), lax.ppermute(low_face, axis, backward)


def body(level_set, velocity, source, wick_solid):
    block = level_set.shape
    count_gx = lax.axis_size("gx")
    count_gy = lax.axis_size("gy")
    index_gx = lax.axis_index("gx")
    index_gy = lax.axis_index("gy")

    def ends(index, count):
        return [jnp.where(index > 0, 0.5, 1.0), jnp.where(index < count - 1, 0.5, 1.0)]

    near = jnp.stack(ends(index_gx, count_gx) + ends(index_gy, count_gy)).astype(F32)
    place = jnp.stack([index_gx, index_gy]).astype(jnp.int32)
    packed = jnp.asarray(PACKED)
    solver = (INV_DEN, FY_H, FY_L, FX_H, FX_L, BX_H, BX_L, BY_H, BY_L)
    solver = tuple(jnp.asarray(table) for table in solver)
    face = (ROWS, LANES)
    rim = (12, TILE, LANES)
    solid = wick_solid.reshape(EY, EX).astype(F32)

    b, l, zlo, zhi = run(
        advect_kernel,
        [block, block, (3, *face), (3, *face)],
        [],
        [level_set, velocity, source, packed],
        [VMEM(block, F32), VMEM((3, *block), F32), VMEM(block, F32), VMEM(PACKED.shape, F32)]
        + [pltpu.SemaphoreType.DMA((4,))],
        place=pl.ANY,
        limit=56 * 1024 * 1024,
    )
    zlo, zhi = shift("gx", zlo, zhi)
    ylo, yhi = run(functools.partial(rim_kernel, 2), [rim, rim], [], [b, l, zlo, zhi])
    ylo, yhi = shift("gy", ylo, yhi)
    w, wlo, whi = run(
        schwarz_kernel, [block, face, face], [near], [*solver, b, zlo, zhi, ylo, yhi]
    )
    wlo, whi = shift("gx", wlo, whi)
    level_new, flux, stat = run(
        level_kernel,
        [block, block, (1, LANES)],
        [near],
        [
            solid, jnp.asarray(SPREAD), jnp.asarray(INV_MASS), packed,
            b, l, zlo, zhi, ylo, yhi,
        ],
        flops=20000000,
    )
    zl, stat = run(
        galerkin_kernel,
        [block, (count_gy, LANES)],
        [near],
        [packed, stat, flux, w, wlo, whi],
    )
    gathered = lax.all_to_all(stat, "gy", 0, 0, tiled=True)
    (turned,) = run(
        turn_kernel, [(count_gx, TILE, LANES)], [], [gathered], [VMEM((LANES, LANES), F32)]
    )
    gathered = lax.all_to_all(turned, "gx", 0, 0, tiled=True)
    (coarse,) = run(
        functools.partial(coarse_kernel, count_gy), [(32, LANES)], [place], [gathered]
    )
    z, y, zlo, zhi, sums = run(
        apply_kernel,
        [block, block, (2, *face), (2, *face), (1, LANES)],
        [near],
        [packed, coarse, flux, b, zl],
    )
    zlo, zhi = shift("gx", zlo, zhi)
    ylo, yhi = run(functools.partial(rim_kernel, 1), [rim, rim], [], [y, zlo, zhi])
    ylo, yhi = shift("gy", ylo, yhi)
    w, wlo, whi = run(
        schwarz_kernel, [block, face, face], [near], [*solver, y, zlo, zhi, ylo, yhi]
    )
    zlo, zhi = shift("gx", wlo, whi)
    q, sums = run(
        second_kernel,
        [block, (count_gx, LANES)],
        [near],
        [packed, coarse, flux, b, y, w, zlo, zhi, sums],
    )
    tile = lax.all_to_all(sums, "gx", 0, 0, tiled=True)
    wide = jnp.broadcast_to(jnp.sum(tile, axis=0, keepdims=True), (count_gy, LANES))
    wide = lax.all_to_all(wide, "gy", 0, 0, tiled=True)
    (pressure,) = run(combine_kernel, [block], [], [wide, z, q])
    return (level_new, pressure)


def solution(mesh):
    placed = (
        P("gx", "gy", None),
        P(None, "gx", "gy", None),
        P("gx", "gy", None),
        P("gx", "gy", None),
    )
    return jax.shard_map(
        body,
        mesh=mesh,
        in_specs=placed,
        out_specs=(P("gx", "gy", None), P("gx", "gy", None)),
        check_vma=False,
    )
```

```python
import functools

import jax
import jax.numpy as jnp
import numpy as np
from jax import lax
from jax.experimental import pallas as pl
from jax.experimental.pallas import tpu as pltpu
from jax.sharding import PartitionSpec as P

EZ = 1
EY = 4
EX = 16
ROWS = 8 * EY
LANES = 8 * EX

TIME_STEP = 0.02
HELM_COEF = 0.25
LEVEL_WIDTH = 0.25
GAS_RATIO = 10.0
SOLID_FACTOR = 0.25
SCHWARZ_SCALE = 0.5
SCHWARZ_SHIFT = 0.05

F32 = jnp.float32
BF16 = jnp.bfloat16
VMEM = pltpu.VMEM
SMEM = pltpu.SMEM
LIMIT = 24 * 1024 * 1024


def gll_tables():
    gll_nodes = np.array(
        [
            -1.0,
            -0.8717401485096066,
            -0.5917001814331423,
            -0.2092992179024789,
            0.2092992179024789,
            0.5917001814331423,
            0.8717401485096066,
            1.0,
        ]
    )
    weight_np = np.array(
        [
            1.0 / 28.0,
            0.21070422714350603,
            0.3411226924835044,
            0.4124587946587038,
            0.4124587946587038,
            0.3411226924835044,
            0.21070422714350603,
            1.0 / 28.0,
        ]
    )
    bary_weights = np.array(
        [1.0 / np.prod([gll_nodes[i] - gll_nodes[j] for j in range(8) if j != i]) for i in range(8)]
    )
    derivative = np.zeros((8, 8))
    for i in range(8):
        for j in range(8):
            if i != j:
                derivative[i, j] = bary_weights[j] / bary_weights[i] / (gll_nodes[i] - gll_nodes[j])
        derivative[i, i] = -np.sum(derivative[i])
    return (weight_np, derivative)


def sine_tables():
    indices = np.arange(10) + 1.0
    sine_basis = np.sqrt(2.0 / 11.0) * np.sin(np.pi * np.outer(indices, indices) / 11.0)
    eigen_vals = 2.0 - 2.0 * np.cos(np.pi * indices / 11.0)
    return (sine_basis, eigen_vals)


WEIGHT, DERIV = gll_tables()
SINE, EIGEN = sine_tables()


def split_const(matrix):
    single = matrix.astype(np.float32)
    high = single.astype(jnp.bfloat16)
    low = (single - high.astype(np.float32)).astype(jnp.bfloat16)
    return high, low


def line_maps(count):
    length = 8 * count
    total = length + 4

    def column(position):
        if 0 <= position < length:
            return position
        return {-2: length, -1: length + 1, length: length + 2, length + 1: length + 3}[position]

    assembled = {}
    for position in range(-2, length + 2):
        row = np.zeros(total)
        row[column(position)] = 1.0
        if 0 <= position < length:
            if position % 8 == 0:
                row[column(position - 1)] += 1.0
            if position % 8 == 7:
                row[column(position + 1)] += 1.0
        assembled[position] = row
    forward = np.zeros((10 * count, total))
    for element in range(count):
        places = [8 * element - 2] + list(range(8 * element, 8 * element + 8)) + [8 * element + 9]
        forward[10 * element : 10 * element + 10] = SINE @ np.stack([assembled[p] for p in places])
    backward = np.zeros((length, 10 * count))
    for element in range(count):
        backward[8 * element : 8 * element + 8, 10 * element : 10 * element + 10] = SINE[1:9]
    for element in range(count - 1):
        first, second = 8 * element + 7, 8 * element + 8
        mean = 0.5 * (backward[first] + backward[second])
        backward[first] = mean
        backward[second] = mean
    return forward, backward


def wide_maps():
    count = EY + 2
    forward, backward = line_maps(count)
    length = 8 * count
    columns = np.zeros((10 * count, ROWS + 2 * TILE))
    columns[:, :ROWS] = forward[:, 8 : 8 + ROWS]
    columns[:, ROWS : ROWS + 2] = forward[:, length : length + 2]
    columns[:, ROWS + 2 : ROWS + 10] = forward[:, :8]
    columns[:, ROWS + TILE : ROWS + TILE + 8] = forward[:, length - 8 : length]
    columns[:, ROWS + TILE + 8 : ROWS + TILE + 10] = forward[:, length + 2 : length + 4]
    _, own = line_maps(EY)
    rows = np.zeros((ROWS + 8, 10 * count))
    rows[:ROWS, 10 : 10 + 10 * EY] = own
    rows[ROWS, :10] = SINE[8]
    rows[ROWS + 1, 10 + 10 * EY :] = SINE[1]
    return columns, rows


TILE = 16
FZ, BZ = line_maps(1)
FY, BY = wide_maps()
SPECTRAL_Y = 64
FY = np.pad(FY, ((0, SPECTRAL_Y - FY.shape[0]), (0, 0)))
BY = np.pad(BY, ((0, 0), (0, SPECTRAL_Y - BY.shape[1])))
FX, BX = line_maps(EX)
FX = FX[:, :LANES]


def denominators():
    lam_y = np.tile(EIGEN, EY + 2)
    lam_x = np.tile(EIGEN, EX)
    total = EIGEN[:, None, None] + lam_y[None, :, None] + lam_x[None, None, :]
    inverse = 1.0 / (SCHWARZ_SCALE * total + SCHWARZ_SHIFT)
    inverse = np.pad(inverse, ((0, 0), (0, SPECTRAL_Y - inverse.shape[1]), (0, 0)))
    return inverse.reshape(10 * SPECTRAL_Y, 10 * EX).astype(np.float32)


INV_DEN = denominators()
FX_H, FX_L = split_const(FX.T.copy())
BX_H, BX_L = split_const(BX.T.copy())


def wide_const(table):
    high, low = split_const(table)
    return np.concatenate([high, high, low], axis=1)


FY_W = wide_const(FY)
BY_W = wide_const(BY)
FX_HH = np.concatenate([FX_H, FX_H], axis=0)


def roll_table():
    table = np.zeros((2, 8, 8, LANES))
    for kind, matrix in enumerate((DERIV, DERIV.T)):
        for k in range(8):
            for i in range(8):
                table[kind, k, i, :] = matrix[i, (i + k) % 8]
    return table.reshape(2 * 64, LANES)


WY = np.tile(WEIGHT, EY)
WX = np.tile(WEIGHT, EX)
AT_ROLLS = ROWS
AT_DX = AT_ROLLS + 128
AT_DXT = AT_DX + LANES
AT_SQUARE = AT_DXT + LANES
PACKED = np.concatenate(
    [
        WY[:, None] * WX[None, :],
        roll_table(),
        np.kron(np.eye(EX), DERIV.T),
        np.kron(np.eye(EX), DERIV),
        np.repeat(DERIV[:, :1] ** 2, LANES, axis=1),
        np.repeat(DERIV[:, 7:] ** 2, LANES, axis=1),
    ]
).astype(np.float32)


def inner_count(count):
    mult = np.ones(8 * count)
    position = np.arange(8 * count)
    mult[(position % 8 == 0) & (position > 0)] += 1.0
    mult[(position % 8 == 7) & (position < 8 * count - 1)] += 1.0
    return mult


INV_MASS = (8.0 / (WY * inner_count(EY))[:, None] / (WX * inner_count(EX))[None, :]).astype(
    np.float32
)
SPREAD = np.kron(np.eye(EX), np.ones((1, 8))).astype(jnp.bfloat16)


def parts(values):
    high = values.astype(BF16)
    low = (values - high.astype(F32)).astype(BF16)
    return high, low


def dot(left, right):
    return jnp.dot(left, right, preferred_element_type=F32)


def left_pairs(table, planes):
    results = []
    for i in range(0, len(planes), 2):
        high, low = parts(jnp.concatenate([planes[i], planes[i + 1]], axis=1))
        both = dot(table[...], jnp.concatenate([high, low, high], axis=0))
        results += [both[:, 0:LANES], both[:, LANES : 2 * LANES]]
    return results


def along_z(values, matrix):
    rows = []
    for i in range(matrix.shape[0]):
        total = None
        for j in range(matrix.shape[1]):
            if matrix[i, j] == 0.0:
                continue
            term = float(matrix[i, j]) * values[j]
            total = term if total is None else total + term
        rows.append(total)
    return rows


def along_y(values, packed, kind):
    count = values.shape[0]
    grouped = values.reshape(count * EY, 8, LANES)
    start = AT_ROLLS + 64 * kind
    total = packed[start : start + 8][None] * grouped
    for k in range(1, 8):
        total = total + packed[start + 8 * k : start + 8 * k + 8][None] * pltpu.roll(grouped, 8 - k, 1)
    return total.reshape(count, ROWS, LANES)


def along_x(values, packed, kind):
    start = AT_DXT if kind else AT_DX
    high, low = parts(packed[start : start + LANES])
    first, rest = parts(values.reshape(8 * ROWS, LANES))
    total = dot(
        jnp.concatenate([first, rest], axis=1), jnp.concatenate([high, high], axis=0)
    ) + dot(first, low)
    return total.reshape(8, ROWS, LANES)


def stack(planes):
    return jnp.concatenate([plane[None] for plane in planes], axis=0)


def edge_rows(rows, low, high):
    position = lax.broadcasted_iota(jnp.int32, (rows, LANES), 0)
    return jnp.where(position == 0, low, jnp.where(position == rows - 1, high, 1.0))


def local_operator(values, flux, packed):
    plane_w = packed[0:ROWS]
    gz = along_z([values[i] for i in range(8)], DERIV)
    fz = along_z([flux[i] * gz[i] for i in range(8)], DERIV.T)
    total = along_y(flux * along_y(values, packed, 0), packed, 1)
    total = total + along_x(flux * along_x(values, packed, 0), packed, 1)
    planes = [
        total[i] + fz[i] + (HELM_COEF * 0.125 * float(WEIGHT[i])) * (plane_w * values[i])
        for i in range(8)
    ]
    return stack(planes)


def add_planes(own, low_z, high_z):
    planes = [own[i] for i in range(8)]
    planes[0] = planes[0] + low_z
    planes[7] = planes[7] + high_z
    return stack(planes)


def schwarz(own, low_z, high_z, low_y, high_y, tables, inv_den, near, out_ref, low_ref, high_ref):
    fy, fxhh, fxl, bxh, bxl, by = tables
    middle = along_z([own[i] for i in range(8)] + [low_z[0], low_z[1], high_z[0], high_z[1]], FZ)
    below = along_z([low_y[i] for i in range(12)], FZ)
    above = along_z([high_y[i] for i in range(12)], FZ)
    spectral = left_pairs(
        fy, [jnp.concatenate([middle[i], below[i], above[i]], axis=0) for i in range(10)]
    )
    high, low = parts(jnp.concatenate(spectral, axis=0))
    wide = dot(jnp.concatenate([high, low], axis=1), fxhh[...]) + dot(high, fxl[...])
    high, low = parts(wide * inv_den[...])
    back = dot(high, bxh[...]) + dot(low, bxh[...]) + dot(high, bxl[...])
    step = SPECTRAL_Y
    back = left_pairs(by, [back[step * i : step * (i + 1)] for i in range(10)])
    planes = along_z(back, BZ)
    edge = edge_rows(ROWS, near[2], near[3])
    row = lax.broadcasted_iota(jnp.int32, (ROWS, LANES), 0)
    for i in range(8):
        first = (1.0 - near[2]) * planes[i][ROWS : ROWS + 1]
        last = (1.0 - near[3]) * planes[i][ROWS + 1 : ROWS + 2]
        other = jnp.where(row == 0, first, jnp.where(row == ROWS - 1, last, 0.0))
        planes[i] = planes[i][0:ROWS] * edge + other
    planes[0] = planes[0] * near[0]
    planes[7] = planes[7] * near[1]
    for i in range(8):
        out_ref[i] = planes[i]
    low_ref[...] = planes[0]
    high_ref[...] = planes[7]


def partition_total(own, low_z, high_z, low_y, high_y, near):
    def planes(array):
        total = near[0] * array[0] + near[1] * array[7]
        for i in range(1, 7):
            total = total + array[i]
        return total

    total = planes(own) + 0.5 * (low_z[1] + high_z[0])
    below = planes(low_y) + 0.5 * (low_y[9] + low_y[10])
    above = planes(high_y) + 0.5 * (high_y[9] + high_y[10])
    faces = 0.5 * (below[9:10] + above[0:1])
    return jnp.sum(total * edge_rows(ROWS, near[2], near[3])) + jnp.sum(faces)


def lane_row(entries):
    lane = lax.broadcasted_iota(jnp.int32, (1, LANES), 1)
    row = jnp.zeros((1, LANES), F32)
    for index, value in enumerate(entries):
        row = jnp.where(lane == index, value, row)
    return row


def advect_kernel(
    lev_in, vel_in, src_in, packed_in, b_ref, l_ref, zlo, zhi, lev, vel, src, packed, sems
):
    copies = [
        pltpu.make_async_copy(source, target, sems.at[index])
        for index, (source, target) in enumerate(
            ((vel_in, vel), (lev_in, lev), (packed_in, packed), (src_in, src))
        )
    ]
    for copy in copies:
        copy.start()
    for copy in copies:
        copy.wait()
    level = lev[...]
    v0, v1, v2 = vel[0], vel[1], vel[2]
    gz = stack(along_z([level[i] for i in range(8)], DERIV))
    advect = v0 * gz + v1 * along_y(level, packed, 0) + v2 * along_x(level, packed, 0)
    moved = level - (2.0 * TIME_STEP) * advect
    diverge = stack(along_z([v0[i] for i in range(8)], DERIV))
    diverge = diverge + along_y(v1, packed, 0) + along_x(v2, packed, 0)
    force = src[...] - (2.0 * TIME_STEP) * diverge
    weights = packed[0:ROWS]
    for i in range(8):
        mass = (0.125 * float(WEIGHT[i])) * weights
        term = mass * force[i]
        moved_i = mass * moved[i]
        b_ref[i] = term
        l_ref[i] = moved_i
        if i < 2:
            zlo[i] = term
        if i == 0:
            zlo[2] = moved_i
        if i > 5:
            zhi[i - 6] = term
        if i == 7:
            zhi[2] = moved_i


def rim_kernel(count, *refs):
    own = refs[:count]
    low_z, high_z, low_y, high_y = refs[count:]
    zeros = jnp.zeros((TILE - 10 - (count - 1), LANES), F32)

    def rows(planes, level, at, far):
        pieces = [planes[at, ROWS - 10 : ROWS] if far else planes[at, 0:10]]
        if count == 2:
            if level is None:
                pieces.append(jnp.zeros((1, LANES), F32))
            else:
                array, index = level
                pieces.append(array[index, ROWS - 1 : ROWS] if far else array[index, 0:1])
        return jnp.concatenate(pieces + [zeros], axis=0)

    for far, out in ((False, low_y), (True, high_y)):
        for i in range(8):
            out[i] = rows(own[0], (own[-1], i), i, far)
        for i in range(2):
            out[8 + i] = rows(low_z, (low_z, 2) if i == 1 else None, i, far)
            out[10 + i] = rows(high_z, (high_z, 2) if i == 0 else None, i, far)


def level_kernel(
    near, solid, spread, inv_mass, packed, b, l, zlo, zhi, ylo, yhi, level_ref, flux_ref, stat
):
    row = lax.broadcasted_iota(jnp.int32, (ROWS, LANES), 0)
    planes = []
    for i in range(8):
        plane = l[i]
        first = ylo[i, 10:11]
        last = yhi[i, 10:11]
        if i == 0:
            plane = plane + zlo[2]
            first = first + ylo[9, 10:11]
            last = last + yhi[9, 10:11]
        if i == 7:
            plane = plane + zhi[2]
            first = first + ylo[10, 10:11]
            last = last + yhi[10, 10:11]
        planes.append(plane + jnp.where(row == 0, first, jnp.where(row == ROWS - 1, last, 0.0)))
    own = stack(planes)
    row = lax.broadcasted_iota(jnp.int32, (8, ROWS, LANES), 1)
    lane = lax.broadcasted_iota(jnp.int32, (8, ROWS, LANES), 2)
    before = jnp.where((row % 8 == 0) & (row > 0), pltpu.roll(own, 1, 1), 0.0)
    after = jnp.where((row % 8 == 7) & (row < ROWS - 1), pltpu.roll(own, ROWS - 1, 1), 0.0)
    own = own + before + after
    before = jnp.where((lane % 8 == 0) & (lane > 0), pltpu.roll(own, 1, 2), 0.0)
    after = jnp.where((lane % 8 == 7) & (lane < LANES - 1), pltpu.roll(own, LANES - 1, 2), 0.0)
    own = own + before + after
    inverse = inv_mass[...] * edge_rows(ROWS, near[2], near[3])
    in_solid = dot(solid[...].astype(BF16), spread[...])
    open_part = jnp.concatenate(
        [jnp.broadcast_to(1.0 - (1.0 - SOLID_FACTOR) * in_solid[e : e + 1], (8, LANES)) for e in range(EY)],
        axis=0,
    )
    plane_w = packed[0:ROWS]
    total = jnp.zeros((ROWS, LANES), F32)
    fluxes = []
    for i in range(8):
        scale = 1.0 / float(WEIGHT[i])
        plane = own[i] * (inverse * scale)
        if i == 0:
            plane = plane * near[0]
        if i == 7:
            plane = plane * near[1]
        level_ref[i] = plane
        liquid = jax.nn.sigmoid(plane * (1.0 / LEVEL_WIDTH))
        coef = (GAS_RATIO - (GAS_RATIO - 1.0) * liquid) * open_part
        total = total + coef
        flux = (0.5 * float(WEIGHT[i])) * (coef * plane_w)
        flux_ref[i] = flux
        fluxes.append(flux)
    kbar = jnp.sum(total) * (1.0 / (8 * ROWS * LANES))
    entries = [kbar, partition_total(b, zlo, zhi, ylo, yhi, near)] + [0.0] * 9
    for first, second in ((0, 0), (0, 7), (7, 7)):
        slopes = along_z(fluxes, (DERIV[:, first] * DERIV[:, second])[None, :])[0]
        column = jnp.sum(slopes, axis=1, keepdims=True)
        entries += [jnp.sum(column, axis=0, keepdims=True), column[0:1], column[ROWS - 1 : ROWS]]
    inner = fluxes[0] + fluxes[1]
    for i in range(2, 8):
        inner = inner + fluxes[i]
    for at, start in ((0, 0), (ROWS - 8, 8)):
        square = packed[AT_SQUARE + start : AT_SQUARE + start + 8]
        entries += [jnp.sum(square * plane[at : at + 8]) for plane in (inner, fluxes[0], fluxes[7])]
    stat[...] = lane_row(entries)


def schwarz_kernel(
    near, inv_den, fy, fxhh, fxl, bxh, bxl, by, b, zlo, zhi, ylo, yhi, w_ref, wlo, whi
):
    tables = (fy, fxhh, fxl, bxh, bxl, by)
    schwarz(b, zlo, zhi, ylo, yhi, tables, inv_den, near, w_ref, wlo, whi)


def galerkin_kernel(near, packed, stat_in, flux, w, zlo, zhi, zl_ref, y_ref, stat):
    local = add_planes(w, zlo[...], zhi[...])
    zl_ref[...] = local
    applied = local_operator(local, flux[...], packed)
    y_ref[...] = applied
    inner = near[0] * applied[0] + near[1] * applied[7]
    for i in range(1, 7):
        inner = inner + applied[i]
    edge = edge_rows(ROWS, near[2], near[3])
    entries = [0.0, 0.0]
    for plane in ((1.0 - near[0]) * applied[0], inner, (1.0 - near[1]) * applied[7]):
        entries += [
            (1.0 - near[2]) * jnp.sum(plane[0:1]),
            jnp.sum(edge * plane),
            (1.0 - near[3]) * jnp.sum(plane[ROWS - 1 : ROWS]),
        ]
    stat[...] = jnp.broadcast_to(stat_in[...] + lane_row(entries), stat.shape)


def turn_kernel(gathered, out_ref, wide):
    count = gathered.shape[0]
    wide[...] = jnp.zeros((LANES, LANES), F32)
    wide[0:count] = gathered[...]
    turned = wide[...].T
    tile = turned[0:16] + pltpu.roll(turned[16:32], LANES // 2, 1)
    for i in range(out_ref.shape[0]):
        out_ref[i] = tile


def invert(blocks, sub):
    for k in range(8):
        pivot = 1.0 / blocks[k][k : k + 1]
        scaled = jnp.where(sub == k, pivot, blocks[k] * pivot)
        rows = []
        for r in range(8):
            if r == k:
                rows.append(scaled)
            else:
                rest = jnp.where(sub == k, 0.0, blocks[r])
                rows.append(rest - blocks[r][k : k + 1] * scaled)
        blocks = rows
    return blocks


def multiply(left, right):
    rows = []
    for r in range(8):
        total = left[r][0:1] * right[0]
        for k in range(1, 8):
            total = total + left[r][k : k + 1] * right[k]
        rows.append(total)
    return rows


def matvec(terms, sub):
    result = jnp.zeros_like(terms[0][1])
    for r in range(8):
        product = terms[0][0][r] * terms[0][1]
        for blocks, column in terms[1:]:
            product = product + blocks[r] * column
        result = jnp.where(sub == r, jnp.sum(product, axis=0, keepdims=True), result)
    return result


def coarse_operator(c, sums_z, sums_y, low_z, high_z, low_y, high_y):
    result = [[None] * 3 for _ in range(3)]

    def ends(values, low, high):
        inside = values[1]
        first = (1.0 - low) * inside + low * values[0]
        last = (1.0 - high) * inside + high * values[2]
        return inside, first, last

    def tested(inside, first, last, low, high):
        return (low * first, inside + (1.0 - low) * first + (1.0 - high) * last, high * last)

    by_b = []
    for b in range(3):
        inside, first, last = ends([c[a][b] for a in range(3)], low_z, high_z)
        end = float(WEIGHT[0])
        by_b.append(tested((2.0 - 2.0 * end) * inside, end * first, end * last, low_z, high_z))
    scale = HELM_COEF / 8.0 * float(np.sum(WX))
    for a in range(3):
        inside, first, last = ends([by_b[b][a] for b in range(3)], low_y, high_y)
        end = scale * float(WEIGHT[0])
        middle = scale * (2.0 * EY - 2.0 * float(WEIGHT[0]))
        result[a] = list(tested(middle * inside, end * first, end * last, low_y, high_y))

    slopes = []
    for outer, factor in ((0, low_z), (2, high_z)):
        slopes.append(ends([factor * (c[outer][b] - c[1][b]) for b in range(3)], low_y, high_y))
    for s, (outer, factor) in enumerate(((0, low_z), (2, high_z))):
        parts_y = []
        for place in range(3):
            total = None
            for t in range(2):
                whole, first, last = sums_z[s + t]
                weight = (whole - first - last, first, last)[place]
                term = weight * slopes[t][place]
                total = term if total is None else total + term
            parts_y.append(total)
        for b, value in enumerate(tested(*parts_y, low_y, high_y)):
            result[outer][b] = result[outer][b] + factor * value
            result[1][b] = result[1][b] - factor * value

    for s, (outer, factor) in enumerate(((0, low_y), (2, high_y))):
        slope = ends([factor * (c[a][outer] - c[a][1]) for a in range(3)], low_z, high_z)
        whole, first, last = sums_y[s]
        pieces = ((whole - first - last) * slope[0], first * slope[1], last * slope[2])
        for a, value in enumerate(tested(*pieces, low_z, high_z)):
            result[a][outer] = result[a][outer] + factor * value
            result[a][1] = result[a][1] - factor * value
    return result


def coarse_kernel(count, place, gathered, out_ref):
    lanes = LANES
    sub = lax.broadcasted_iota(jnp.int32, (8, lanes), 0)
    lane = lax.broadcasted_iota(jnp.int32, (8, lanes), 1)

    def value(index):
        row = index % 16
        array = jnp.concatenate([gathered[i, row : row + 1] for i in range(8)], axis=0)
        if index >= 16:
            array = pltpu.roll(array, lanes // 2, 1)
        return jnp.where(lane < count, array, 0.0)

    def move(array, dz, dy):
        if dz:
            array = pltpu.roll(array, (-dz) % 8, 0)
        if dy:
            array = pltpu.roll(array, (-dy) % lanes, 1)
        return array

    kbar = jnp.where(lane < count, value(0), 1.0)
    above = move(kbar, 1, 0)
    link_z = jnp.where(sub < 7, 2.0 * kbar * above / (kbar + above) * (EY * EX / EZ), 0.0)
    link_z = jnp.where(lane < count, link_z, 0.0)
    beside = move(kbar, 0, 1)
    link_y = 2.0 * kbar * beside / (kbar + beside) * (EZ * EX / EY)
    link_y = jnp.where(lane < count - 1, link_y, 0.0)
    back_z = move(link_z, -1, 0)
    back_y = move(link_y, 0, -1)
    diagonal = HELM_COEF * EZ * EY * EX + link_z + back_z + link_y + back_y
    blocks, lower, upper = [], [], []
    for r in range(8):
        row = jnp.where(sub == r, diagonal, 0.0)
        row = jnp.where(sub == r + 1, -back_z, row)
        row = jnp.where(sub == r - 1, -link_z, row)
        blocks.append(row)
        lower.append(jnp.where(sub == r, -back_y, 0.0))
        upper.append(jnp.where(sub == r, -link_y, 0.0))
    levels = []
    step = 1
    while step < count:
        inverse = invert(blocks, sub)
        down = multiply(lower, [move(row, 0, -step) for row in inverse])
        up = multiply(upper, [move(row, 0, step) for row in inverse])
        levels.append((step, down, up))
        before_u = multiply(down, [move(row, 0, -step) for row in upper])
        after_l = multiply(up, [move(row, 0, step) for row in lower])
        if 2 * step < count:
            new_lower = multiply(down, [move(row, 0, -step) for row in lower])
            new_upper = multiply(up, [move(row, 0, step) for row in upper])
            lower = [-row for row in new_lower]
            upper = [-row for row in new_upper]
        blocks = [blocks[r] - before_u[r] - after_l[r] for r in range(8)]
        step *= 2
    inverse = invert(blocks, sub)

    def solve(column):
        for distance, down, up in levels:
            pulled = matvec(
                [(down, move(column, 0, -distance)), (up, move(column, 0, distance))], sub
            )
            column = column - pulled
        return matvec([(inverse, column)], sub)

    offsets = [(a - 1, b - 1) for a in range(3) for b in range(3)]
    first = solve(value(1))
    near_first = [move(first, dz, dy) for dz, dy in offsets]
    low_z = jnp.where(sub > 0, 0.5, 0.0)
    high_z = jnp.where(sub < 7, 0.5, 0.0)
    low_y = jnp.where(lane > 0, 0.5, 0.0)
    high_y = jnp.where(lane < count - 1, 0.5, 0.0)
    sums_z = [[value(11 + 3 * k + j) for j in range(3)] for k in range(3)]
    sums_y = [[value(20 + 3 * k + j) for j in range(3)] for k in range(2)]
    values = [near_first[0:3], near_first[3:6], near_first[6:9]]
    tested = coarse_operator(values, sums_z, sums_y, low_z, high_z, low_y, high_y)
    totals = jnp.zeros((8, lanes), F32)
    for d, (dz, dy) in enumerate(offsets):
        term = jnp.where(lane < count, value(2 + d) + tested[d // 3][d % 3], 0.0)
        totals = totals + move(term, -dz, -dy)
    totals = jnp.where(lane < count, totals, 0.0)
    second = solve(totals)
    near_second = [move(second, dz, dy) for dz, dy in offsets]
    mine = (sub == place[0]) & (lane == place[1])
    for d in range(9):
        out_ref[d : d + 1] = jnp.full((1, lanes), jnp.sum(jnp.where(mine, near_first[d], 0.0)))
        out_ref[16 + d : 17 + d] = jnp.full(
            (1, lanes), jnp.sum(jnp.where(mine, near_second[d], 0.0))
        )


def coarse_columns(near, coarse, start):
    row = lax.broadcasted_iota(jnp.int32, (ROWS, LANES), 0)
    edge = edge_rows(ROWS, near[2], near[3])
    below = jnp.where(row == 0, 1.0 - near[2], 0.0)
    above = jnp.where(row == ROWS - 1, 1.0 - near[3], 0.0)
    columns = []
    for a in range(3):
        at = start + 3 * a
        columns.append(
            below * coarse[at : at + 1] + edge * coarse[at + 1 : at + 2] + above * coarse[at + 2 : at + 3]
        )
    first = (1.0 - near[0]) * (columns[0] - columns[1])
    last = (1.0 - near[1]) * (columns[2] - columns[1])
    return columns[1], first, last


def add_coarse(local, columns):
    inside, first, last = columns
    planes = [local[i] + inside for i in range(8)]
    planes[0] = planes[0] + first
    planes[7] = planes[7] + last
    return stack(planes)


def coarse_applied(columns, flux, packed):
    inside, first, last = columns
    slopes = [
        flux[i] * (float(DERIV[i, 0]) * first + float(DERIV[i, 7]) * last) for i in range(8)
    ]
    fz = along_z(slopes, DERIV.T)
    three = stack([inside + first, inside, inside + last])
    gy = along_y(three, packed, 0)
    fy = along_y(
        stack([flux[i] * gy[0 if i == 0 else 2 if i == 7 else 1] for i in range(8)]), packed, 1
    )
    plane_w = packed[0:ROWS]
    planes = []
    for i in range(8):
        plane = three[0 if i == 0 else 2 if i == 7 else 1]
        planes.append(fz[i] + fy[i] + (HELM_COEF * 0.125 * float(WEIGHT[i])) * (plane_w * plane))
    return stack(planes)


def apply_kernel(near, packed, coarse, flux, b, zl, yl, z_ref, y_ref, ylo, yhi, stat):
    columns = coarse_columns(near, coarse, 0)
    field = add_coarse(zl[...], columns)
    z_ref[...] = field
    applied = yl[...] + coarse_applied(columns, flux[...], packed)
    y_ref[...] = applied
    ylo[...] = applied[0:2]
    yhi[...] = applied[6:8]
    stat[...] = lane_row([jnp.sum(b[...] * field), jnp.sum(field * applied)])


def second_kernel(near, packed, coarse, flux, b, y, w, zlo, zhi, stat_in, q_ref, stat):
    local = add_planes(w, zlo[...], zhi[...])
    field = add_coarse(local, coarse_columns(near, coarse, 16))
    q_ref[...] = field
    applied = local_operator(field, flux[...], packed)
    sums = [0.0, 0.0, jnp.sum(b[...] * field), jnp.sum(y[...] * field), jnp.sum(field * applied)]
    stat[...] = jnp.broadcast_to(stat_in[...] + lane_row(sums), stat.shape)


def combine_kernel(sums, z, q, p_ref):
    total = jnp.sum(sums[...], axis=0, keepdims=True)
    rz, pap, rq, aq, qhq = (total[:, k : k + 1] for k in range(5))
    step = rz / pap
    rz_next = step * (step * aq - rq)
    beta = rz_next / rz
    grown = 1.0 + beta
    curved = grown * grown * pap - 2.0 * step * grown * aq + step * step * qhq
    step_next = rz_next / curved
    on_z = step + step_next * grown
    on_q = step_next * step
    p_ref[...] = on_z.reshape(1, 1, 1) * z[...] - on_q.reshape(1, 1, 1) * q[...]


def run(kernel, outs, smem, args, scratch=(), flops=1000000, place=VMEM, limit=LIMIT):
    nbytes = sum(4 * int(np.prod(out)) for out in outs) * 2
    return pl.pallas_call(
        kernel,
        out_shape=[jax.ShapeDtypeStruct(out, F32) for out in outs],
        in_specs=[pl.BlockSpec(memory_space=SMEM) for _ in smem]
        + [pl.BlockSpec(memory_space=place) for _ in args],
        out_specs=[pl.BlockSpec(memory_space=VMEM) for _ in outs],
        scratch_shapes=list(scratch),
        compiler_params=pltpu.CompilerParams(vmem_limit_bytes=limit),
        cost_estimate=pl.CostEstimate(flops=flops, bytes_accessed=nbytes, transcendentals=0),
    )(*smem, *args)


def shift(axis, low_face, high_face):
    count = lax.axis_size(axis)
    forward = [(i, i + 1) for i in range(count - 1)]
    backward = [(target, source) for source, target in forward]
    return lax.ppermute(high_face, axis, forward), lax.ppermute(low_face, axis, backward)


def body(level_set, velocity, source, wick_solid):
    block = level_set.shape
    count_gx = lax.axis_size("gx")
    count_gy = lax.axis_size("gy")
    index_gx = lax.axis_index("gx")
    index_gy = lax.axis_index("gy")

    def ends(index, count):
        return [jnp.where(index > 0, 0.5, 1.0), jnp.where(index < count - 1, 0.5, 1.0)]

    near = jnp.stack(ends(index_gx, count_gx) + ends(index_gy, count_gy)).astype(F32)
    place = jnp.stack([index_gx, index_gy]).astype(jnp.int32)
    packed = jnp.asarray(PACKED)
    solver = (INV_DEN, FY_W, FX_HH, FX_L, BX_H, BX_L, BY_W)
    solver = tuple(jnp.asarray(table) for table in solver)
    face = (ROWS, LANES)
    rim = (12, TILE, LANES)
    solid = wick_solid.reshape(EY, EX).astype(F32)

    b, l, zlo, zhi = run(
        advect_kernel,
        [block, block, (3, *face), (3, *face)],
        [],
        [
            pltpu.with_memory_space_constraint(array, pltpu.HBM)
            for array in (level_set, velocity, source, packed)
        ],
        [VMEM(block, F32), VMEM((3, *block), F32), VMEM(block, F32), VMEM(PACKED.shape, F32)]
        + [pltpu.SemaphoreType.DMA((4,))],
        place=pltpu.HBM,
    )
    zlo, zhi = shift("gx", zlo, zhi)
    ylo, yhi = run(functools.partial(rim_kernel, 2), [rim, rim], [], [b, l, zlo, zhi])
    ylo, yhi = shift("gy", ylo, yhi)
    w, wlo, whi = run(
        schwarz_kernel, [block, face, face], [near], [*solver, b, zlo, zhi, ylo, yhi]
    )
    wlo, whi = shift("gx", wlo, whi)
    level_new, flux, stat = run(
        level_kernel,
        [block, block, (1, LANES)],
        [near],
        [
            solid, jnp.asarray(SPREAD), jnp.asarray(INV_MASS), packed,
            b, l, zlo, zhi, ylo, yhi,
        ],
        flops=20000000,
    )
    zl, yl, stat = run(
        galerkin_kernel,
        [block, block, (count_gy, LANES)],
        [near],
        [packed, stat, flux, w, wlo, whi],
    )
    gathered = lax.all_to_all(stat, "gy", 0, 0, tiled=True)
    (turned,) = run(
        turn_kernel, [(count_gx, TILE, LANES)], [], [gathered], [VMEM((LANES, LANES), F32)]
    )
    gathered = lax.all_to_all(turned, "gx", 0, 0, tiled=True)
    (coarse,) = run(
        functools.partial(coarse_kernel, count_gy), [(32, LANES)], [place], [gathered]
    )
    z, y, zlo, zhi, sums = run(
        apply_kernel,
        [block, block, (2, *face), (2, *face), (1, LANES)],
        [near],
        [packed, coarse, flux, b, zl, yl],
    )
    zlo, zhi = shift("gx", zlo, zhi)
    ylo, yhi = run(functools.partial(rim_kernel, 1), [rim, rim], [], [y, zlo, zhi])
    ylo, yhi = shift("gy", ylo, yhi)
    w, wlo, whi = run(
        schwarz_kernel, [block, face, face], [near], [*solver, y, zlo, zhi, ylo, yhi]
    )
    zlo, zhi = shift("gx", wlo, whi)
    q, sums = run(
        second_kernel,
        [block, (count_gx, LANES)],
        [near],
        [packed, coarse, flux, b, y, w, zlo, zhi, sums],
    )
    tile = lax.all_to_all(sums, "gx", 0, 0, tiled=True)
    wide = jnp.broadcast_to(jnp.sum(tile, axis=0, keepdims=True), (count_gy, LANES))
    wide = lax.all_to_all(wide, "gy", 0, 0, tiled=True)
    (pressure,) = run(combine_kernel, [block], [], [wide, z, q])
    return (level_new, pressure)


def solution(mesh):
    placed = (
        P("gx", "gy", None),
        P(None, "gx", "gy", None),
        P("gx", "gy", None),
        P("gx", "gy", None),
    )
    return jax.shard_map(
        body,
        mesh=mesh,
        in_specs=placed,
        out_specs=(P("gx", "gy", None), P("gx", "gy", None)),
        check_vma=False,
    )
```

```python
import functools

import jax
import jax.numpy as jnp
import numpy as np
from jax import lax
from jax.experimental import pallas as pl
from jax.experimental.pallas import tpu as pltpu
from jax.sharding import PartitionSpec as P

EZ = 1
EY = 4
EX = 16
ROWS = 8 * EY
LANES = 8 * EX

TIME_STEP = 0.02
HELM_COEF = 0.25
LEVEL_WIDTH = 0.25
GAS_RATIO = 10.0
SOLID_FACTOR = 0.25
SCHWARZ_SCALE = 0.5
SCHWARZ_SHIFT = 0.05

F32 = jnp.float32
BF16 = jnp.bfloat16
VMEM = pltpu.VMEM
SMEM = pltpu.SMEM
LIMIT = 24 * 1024 * 1024


def gll_tables():
    gll_nodes = np.array(
        [
            -1.0,
            -0.8717401485096066,
            -0.5917001814331423,
            -0.2092992179024789,
            0.2092992179024789,
            0.5917001814331423,
            0.8717401485096066,
            1.0,
        ]
    )
    weight_np = np.array(
        [
            1.0 / 28.0,
            0.21070422714350603,
            0.3411226924835044,
            0.4124587946587038,
            0.4124587946587038,
            0.3411226924835044,
            0.21070422714350603,
            1.0 / 28.0,
        ]
    )
    bary_weights = np.array(
        [1.0 / np.prod([gll_nodes[i] - gll_nodes[j] for j in range(8) if j != i]) for i in range(8)]
    )
    derivative = np.zeros((8, 8))
    for i in range(8):
        for j in range(8):
            if i != j:
                derivative[i, j] = bary_weights[j] / bary_weights[i] / (gll_nodes[i] - gll_nodes[j])
        derivative[i, i] = -np.sum(derivative[i])
    return (weight_np, derivative)


def sine_tables():
    indices = np.arange(10) + 1.0
    sine_basis = np.sqrt(2.0 / 11.0) * np.sin(np.pi * np.outer(indices, indices) / 11.0)
    eigen_vals = 2.0 - 2.0 * np.cos(np.pi * indices / 11.0)
    return (sine_basis, eigen_vals)


WEIGHT, DERIV = gll_tables()
SINE, EIGEN = sine_tables()


def split_const(matrix):
    single = matrix.astype(np.float32)
    high = single.astype(jnp.bfloat16)
    low = (single - high.astype(np.float32)).astype(jnp.bfloat16)
    return high, low


def line_maps(count):
    length = 8 * count
    total = length + 4

    def column(position):
        if 0 <= position < length:
            return position
        return {-2: length, -1: length + 1, length: length + 2, length + 1: length + 3}[position]

    assembled = {}
    for position in range(-2, length + 2):
        row = np.zeros(total)
        row[column(position)] = 1.0
        if 0 <= position < length:
            if position % 8 == 0:
                row[column(position - 1)] += 1.0
            if position % 8 == 7:
                row[column(position + 1)] += 1.0
        assembled[position] = row
    forward = np.zeros((10 * count, total))
    for element in range(count):
        places = [8 * element - 2] + list(range(8 * element, 8 * element + 8)) + [8 * element + 9]
        forward[10 * element : 10 * element + 10] = SINE @ np.stack([assembled[p] for p in places])
    backward = np.zeros((length, 10 * count))
    for element in range(count):
        backward[8 * element : 8 * element + 8, 10 * element : 10 * element + 10] = SINE[1:9]
    for element in range(count - 1):
        first, second = 8 * element + 7, 8 * element + 8
        mean = 0.5 * (backward[first] + backward[second])
        backward[first] = mean
        backward[second] = mean
    return forward, backward


def wide_maps():
    count = EY + 2
    forward, backward = line_maps(count)
    length = 8 * count
    columns = np.zeros((10 * count, ROWS + 2 * TILE))
    columns[:, :ROWS] = forward[:, 8 : 8 + ROWS]
    columns[:, ROWS : ROWS + 2] = forward[:, length : length + 2]
    columns[:, ROWS + 2 : ROWS + 10] = forward[:, :8]
    columns[:, ROWS + TILE : ROWS + TILE + 8] = forward[:, length - 8 : length]
    columns[:, ROWS + TILE + 8 : ROWS + TILE + 10] = forward[:, length + 2 : length + 4]
    _, own = line_maps(EY)
    rows = np.zeros((ROWS + 8, 10 * count))
    rows[:ROWS, 10 : 10 + 10 * EY] = own
    rows[ROWS, :10] = SINE[8]
    rows[ROWS + 1, 10 + 10 * EY :] = SINE[1]
    return columns, rows


TILE = 16
FZ, BZ = line_maps(1)
FY, BY = wide_maps()
SPECTRAL_Y = 64
FY = np.pad(FY, ((0, SPECTRAL_Y - FY.shape[0]), (0, 0)))
BY = np.pad(BY, ((0, 0), (0, SPECTRAL_Y - BY.shape[1])))
FX, BX = line_maps(EX)
FX = FX[:, :LANES]


def denominators():
    lam_y = np.tile(EIGEN, EY + 2)
    lam_x = np.tile(EIGEN, EX)
    total = EIGEN[:, None, None] + lam_y[None, :, None] + lam_x[None, None, :]
    inverse = 1.0 / (SCHWARZ_SCALE * total + SCHWARZ_SHIFT)
    inverse = np.pad(inverse, ((0, 0), (0, SPECTRAL_Y - inverse.shape[1]), (0, 0)))
    return inverse.reshape(10 * SPECTRAL_Y, 10 * EX).astype(np.float32)


INV_DEN = denominators()
FX_H, FX_L = split_const(FX.T.copy())
BX_H, BX_L = split_const(BX.T.copy())


def wide_const(table):
    high, low = split_const(table)
    return np.concatenate([high, high, low], axis=1)


FY_W = wide_const(FY)
BY_W = wide_const(BY)
FX_HH = np.concatenate([FX_H, FX_H], axis=0)


def roll_table():
    table = np.zeros((2, 8, 8, LANES))
    for kind, matrix in enumerate((DERIV, DERIV.T)):
        for k in range(8):
            for i in range(8):
                table[kind, k, i, :] = matrix[i, (i + k) % 8]
    return table.reshape(2 * 64, LANES)


WY = np.tile(WEIGHT, EY)
WX = np.tile(WEIGHT, EX)
AT_ROLLS = ROWS
AT_DX = AT_ROLLS + 128
AT_DXT = AT_DX + LANES
AT_SQUARE = AT_DXT + LANES
PACKED = np.concatenate(
    [
        WY[:, None] * WX[None, :],
        roll_table(),
        np.kron(np.eye(EX), DERIV.T),
        np.kron(np.eye(EX), DERIV),
        np.repeat(DERIV[:, :1] ** 2, LANES, axis=1),
        np.repeat(DERIV[:, 7:] ** 2, LANES, axis=1),
    ]
).astype(np.float32)


def inner_count(count):
    mult = np.ones(8 * count)
    position = np.arange(8 * count)
    mult[(position % 8 == 0) & (position > 0)] += 1.0
    mult[(position % 8 == 7) & (position < 8 * count - 1)] += 1.0
    return mult


INV_MASS = (8.0 / (WY * inner_count(EY))[:, None] / (WX * inner_count(EX))[None, :]).astype(
    np.float32
)
SPREAD = np.kron(np.eye(EX), np.ones((1, 8))).astype(jnp.bfloat16)


def parts(values):
    high = values.astype(BF16)
    low = (values - high.astype(F32)).astype(BF16)
    return high, low


def dot(left, right):
    return jnp.dot(left, right, preferred_element_type=F32)


def left_pairs(table, planes):
    results = []
    for i in range(0, len(planes), 2):
        high, low = parts(jnp.concatenate([planes[i], planes[i + 1]], axis=1))
        both = dot(table[...], jnp.concatenate([high, low, high], axis=0))
        results += [both[:, 0:LANES], both[:, LANES : 2 * LANES]]
    return results


def along_z(values, matrix):
    rows = []
    for i in range(matrix.shape[0]):
        total = None
        for j in range(matrix.shape[1]):
            if matrix[i, j] == 0.0:
                continue
            term = float(matrix[i, j]) * values[j]
            total = term if total is None else total + term
        rows.append(total)
    return rows


def along_y(values, packed, kind):
    count = values.shape[0]
    grouped = values.reshape(count * EY, 8, LANES)
    start = AT_ROLLS + 64 * kind
    total = packed[start : start + 8][None] * grouped
    for k in range(1, 8):
        total = total + packed[start + 8 * k : start + 8 * k + 8][None] * pltpu.roll(grouped, 8 - k, 1)
    return total.reshape(count, ROWS, LANES)


def along_x(values, packed, kind):
    start = AT_DXT if kind else AT_DX
    high, low = parts(packed[start : start + LANES])
    first, rest = parts(values.reshape(8 * ROWS, LANES))
    total = dot(
        jnp.concatenate([first, rest], axis=1), jnp.concatenate([high, high], axis=0)
    ) + dot(first, low)
    return total.reshape(8, ROWS, LANES)


def stack(planes):
    return jnp.concatenate([plane[None] for plane in planes], axis=0)


def edge_rows(rows, low, high):
    position = lax.broadcasted_iota(jnp.int32, (rows, LANES), 0)
    return jnp.where(position == 0, low, jnp.where(position == rows - 1, high, 1.0))


def local_operator(values, flux, packed):
    plane_w = packed[0:ROWS]
    gz = along_z([values[i] for i in range(8)], DERIV)
    fz = along_z([flux[i] * gz[i] for i in range(8)], DERIV.T)
    total = along_y(flux * along_y(values, packed, 0), packed, 1)
    total = total + along_x(flux * along_x(values, packed, 0), packed, 1)
    planes = [
        total[i] + fz[i] + (HELM_COEF * 0.125 * float(WEIGHT[i])) * (plane_w * values[i])
        for i in range(8)
    ]
    return stack(planes)


def add_planes(own, low_z, high_z):
    planes = [own[i] for i in range(8)]
    planes[0] = planes[0] + low_z
    planes[7] = planes[7] + high_z
    return stack(planes)


def schwarz(own, low_z, high_z, low_y, high_y, tables, inv_den, near, out_ref, low_ref, high_ref):
    fy, fxhh, fxl, bxh, bxl, by = tables
    middle = along_z([own[i] for i in range(8)] + [low_z[0], low_z[1], high_z[0], high_z[1]], FZ)
    below = along_z([low_y[i] for i in range(12)], FZ)
    above = along_z([high_y[i] for i in range(12)], FZ)
    spectral = left_pairs(
        fy, [jnp.concatenate([middle[i], below[i], above[i]], axis=0) for i in range(10)]
    )
    high, low = parts(jnp.concatenate(spectral, axis=0))
    wide = dot(jnp.concatenate([high, low], axis=1), fxhh[...]) + dot(high, fxl[...])
    high, low = parts(wide * inv_den[...])
    back = dot(high, bxh[...]) + dot(low, bxh[...]) + dot(high, bxl[...])
    step = SPECTRAL_Y
    back = left_pairs(by, [back[step * i : step * (i + 1)] for i in range(10)])
    planes = along_z(back, BZ)
    edge = edge_rows(ROWS, near[2], near[3])
    row = lax.broadcasted_iota(jnp.int32, (ROWS, LANES), 0)
    for i in range(8):
        first = (1.0 - near[2]) * planes[i][ROWS : ROWS + 1]
        last = (1.0 - near[3]) * planes[i][ROWS + 1 : ROWS + 2]
        other = jnp.where(row == 0, first, jnp.where(row == ROWS - 1, last, 0.0))
        planes[i] = planes[i][0:ROWS] * edge + other
    planes[0] = planes[0] * near[0]
    planes[7] = planes[7] * near[1]
    for i in range(8):
        out_ref[i] = planes[i]
    low_ref[...] = planes[0]
    high_ref[...] = planes[7]


def partition_total(own, low_z, high_z, low_y, high_y, near):
    def planes(array):
        total = near[0] * array[0] + near[1] * array[7]
        for i in range(1, 7):
            total = total + array[i]
        return total

    total = planes(own) + 0.5 * (low_z[1] + high_z[0])
    below = planes(low_y) + 0.5 * (low_y[9] + low_y[10])
    above = planes(high_y) + 0.5 * (high_y[9] + high_y[10])
    faces = 0.5 * (below[9:10] + above[0:1])
    return jnp.sum(total * edge_rows(ROWS, near[2], near[3])) + jnp.sum(faces)


def lane_row(entries):
    lane = lax.broadcasted_iota(jnp.int32, (1, LANES), 1)
    row = jnp.zeros((1, LANES), F32)
    for index, value in enumerate(entries):
        row = jnp.where(lane == index, value, row)
    return row


def advect_kernel(
    lev_in, vel_in, src_in, packed_in, b_ref, l_ref, zlo, zhi, lev, vel, src, packed, sems
):
    copies = [
        pltpu.make_async_copy(source, target, sems.at[index])
        for index, (source, target) in enumerate(
            ((vel_in, vel), (lev_in, lev), (packed_in, packed), (src_in, src))
        )
    ]
    for copy in copies:
        copy.start()
    for copy in copies:
        copy.wait()
    level = lev[...]
    v0, v1, v2 = vel[0], vel[1], vel[2]
    gz = stack(along_z([level[i] for i in range(8)], DERIV))
    advect = v0 * gz + v1 * along_y(level, packed, 0) + v2 * along_x(level, packed, 0)
    moved = level - (2.0 * TIME_STEP) * advect
    diverge = stack(along_z([v0[i] for i in range(8)], DERIV))
    diverge = diverge + along_y(v1, packed, 0) + along_x(v2, packed, 0)
    force = src[...] - (2.0 * TIME_STEP) * diverge
    weights = packed[0:ROWS]
    for i in range(8):
        mass = (0.125 * float(WEIGHT[i])) * weights
        term = mass * force[i]
        moved_i = mass * moved[i]
        b_ref[i] = term
        l_ref[i] = moved_i
        if i < 2:
            zlo[i] = term
        if i == 0:
            zlo[2] = moved_i
        if i > 5:
            zhi[i - 6] = term
        if i == 7:
            zhi[2] = moved_i


def rim_kernel(count, *refs):
    own = refs[:count]
    low_z, high_z, low_y, high_y = refs[count:]
    zeros = jnp.zeros((TILE - 10 - (count - 1), LANES), F32)

    def rows(planes, level, at, far):
        pieces = [planes[at, ROWS - 10 : ROWS] if far else planes[at, 0:10]]
        if count == 2:
            if level is None:
                pieces.append(jnp.zeros((1, LANES), F32))
            else:
                array, index = level
                pieces.append(array[index, ROWS - 1 : ROWS] if far else array[index, 0:1])
        return jnp.concatenate(pieces + [zeros], axis=0)

    for far, out in ((False, low_y), (True, high_y)):
        for i in range(8):
            out[i] = rows(own[0], (own[-1], i), i, far)
        for i in range(2):
            out[8 + i] = rows(low_z, (low_z, 2) if i == 1 else None, i, far)
            out[10 + i] = rows(high_z, (high_z, 2) if i == 0 else None, i, far)


def level_kernel(
    near, solid, spread, inv_mass, packed, b, l, zlo, zhi, ylo, yhi, level_ref, flux_ref, stat
):
    row = lax.broadcasted_iota(jnp.int32, (ROWS, LANES), 0)
    planes = []
    for i in range(8):
        plane = l[i]
        first = ylo[i, 10:11]
        last = yhi[i, 10:11]
        if i == 0:
            plane = plane + zlo[2]
            first = first + ylo[9, 10:11]
            last = last + yhi[9, 10:11]
        if i == 7:
            plane = plane + zhi[2]
            first = first + ylo[10, 10:11]
            last = last + yhi[10, 10:11]
        planes.append(plane + jnp.where(row == 0, first, jnp.where(row == ROWS - 1, last, 0.0)))
    own = stack(planes)
    row = lax.broadcasted_iota(jnp.int32, (8, ROWS, LANES), 1)
    lane = lax.broadcasted_iota(jnp.int32, (8, ROWS, LANES), 2)
    before = jnp.where((row % 8 == 0) & (row > 0), pltpu.roll(own, 1, 1), 0.0)
    after = jnp.where((row % 8 == 7) & (row < ROWS - 1), pltpu.roll(own, ROWS - 1, 1), 0.0)
    own = own + before + after
    before = jnp.where((lane % 8 == 0) & (lane > 0), pltpu.roll(own, 1, 2), 0.0)
    after = jnp.where((lane % 8 == 7) & (lane < LANES - 1), pltpu.roll(own, LANES - 1, 2), 0.0)
    own = own + before + after
    inverse = inv_mass[...] * edge_rows(ROWS, near[2], near[3])
    in_solid = dot(solid[...].astype(BF16), spread[...])
    open_part = jnp.concatenate(
        [jnp.broadcast_to(1.0 - (1.0 - SOLID_FACTOR) * in_solid[e : e + 1], (8, LANES)) for e in range(EY)],
        axis=0,
    )
    plane_w = packed[0:ROWS]
    total = jnp.zeros((ROWS, LANES), F32)
    fluxes = []
    for i in range(8):
        scale = 1.0 / float(WEIGHT[i])
        plane = own[i] * (inverse * scale)
        if i == 0:
            plane = plane * near[0]
        if i == 7:
            plane = plane * near[1]
        level_ref[i] = plane
        liquid = jax.nn.sigmoid(plane * (1.0 / LEVEL_WIDTH))
        coef = (GAS_RATIO - (GAS_RATIO - 1.0) * liquid) * open_part
        total = total + coef
        flux = (0.5 * float(WEIGHT[i])) * (coef * plane_w)
        flux_ref[i] = flux
        fluxes.append(flux)
    kbar = jnp.sum(total) * (1.0 / (8 * ROWS * LANES))
    entries = [kbar, partition_total(b, zlo, zhi, ylo, yhi, near)] + [0.0] * 9
    for first, second in ((0, 0), (0, 7), (7, 7)):
        slopes = along_z(fluxes, (DERIV[:, first] * DERIV[:, second])[None, :])[0]
        column = jnp.sum(slopes, axis=1, keepdims=True)
        entries += [jnp.sum(column, axis=0, keepdims=True), column[0:1], column[ROWS - 1 : ROWS]]
    inner = fluxes[0] + fluxes[1]
    for i in range(2, 8):
        inner = inner + fluxes[i]
    for at, start in ((0, 0), (ROWS - 8, 8)):
        square = packed[AT_SQUARE + start : AT_SQUARE + start + 8]
        entries += [jnp.sum(square * plane[at : at + 8]) for plane in (inner, fluxes[0], fluxes[7])]
    stat[...] = lane_row(entries)


def schwarz_kernel(
    near, inv_den, fy, fxhh, fxl, bxh, bxl, by, b, zlo, zhi, ylo, yhi, w_ref, wlo, whi
):
    tables = (fy, fxhh, fxl, bxh, bxl, by)
    schwarz(b, zlo, zhi, ylo, yhi, tables, inv_den, near, w_ref, wlo, whi)


def galerkin_kernel(near, packed, stat_in, flux, w, zlo, zhi, zl_ref, y_ref, stat):
    local = add_planes(w, zlo[...], zhi[...])
    zl_ref[...] = local
    applied = local_operator(local, flux[...], packed)
    y_ref[...] = applied
    inner = near[0] * applied[0] + near[1] * applied[7]
    for i in range(1, 7):
        inner = inner + applied[i]
    edge = edge_rows(ROWS, near[2], near[3])
    entries = [0.0, 0.0]
    for plane in ((1.0 - near[0]) * applied[0], inner, (1.0 - near[1]) * applied[7]):
        entries += [
            (1.0 - near[2]) * jnp.sum(plane[0:1]),
            jnp.sum(edge * plane),
            (1.0 - near[3]) * jnp.sum(plane[ROWS - 1 : ROWS]),
        ]
    stat[...] = jnp.broadcast_to(stat_in[...] + lane_row(entries), stat.shape)


def column_kernel(gathered, out_ref):
    values = gathered[...]
    sub = lax.broadcasted_iota(jnp.int32, (8, LANES), 0)
    lane = lax.broadcasted_iota(jnp.int32, (8, LANES), 1)
    after = jnp.where(sub < 7, pltpu.roll(values, 7, 0), 0.0)
    before = jnp.where(sub > 0, pltpu.roll(values, 1, 0), 0.0)
    first = lax.broadcasted_iota(jnp.int32, (8, 1), 0) == 0
    last = lax.broadcasted_iota(jnp.int32, (8, 1), 0) == 7

    def column(array, index):
        return array[:, index : index + 1]

    def slopes(array, pair):
        whole, low, high = (column(array, 11 + 3 * pair + k) for k in range(3))
        return whole - low - high, low, high

    merged = [column(values, 0), column(values, 1)]
    for b in range(3):
        merged.append(column(values, 5 + b) + column(after, 2 + b) + column(before, 8 + b))
    merged += [own + other for own, other in zip(slopes(values, 0), slopes(before, 2), strict=True)]
    merged += list(slopes(values, 1))
    inside, interface = [], []
    for side in range(2):
        whole, low, high = (column(values, 20 + 3 * side + k) for k in range(3))
        ends = jnp.where(first, low, 0.0) + jnp.where(last, high, 0.0)
        inside.append(whole - low - high + ends)
        interface.append(jnp.where(first, 0.0, low) + column(before, 22 + 3 * side))
    rows = jnp.zeros((8, LANES), F32)
    for index, value in enumerate(merged + inside + interface):
        rows = jnp.where(lane == index, value, rows)
    total = rows[0:1]
    for i in range(1, 8):
        total = total + pltpu.roll(rows[i : i + 1], 16 * i, 1)
    out_ref[...] = jnp.broadcast_to(total, out_ref.shape)


def invert(blocks, sub):
    for k in range(8):
        pivot = 1.0 / blocks[k][k : k + 1]
        scaled = jnp.where(sub == k, pivot, blocks[k] * pivot)
        rows = []
        for r in range(8):
            if r == k:
                rows.append(scaled)
            else:
                rest = jnp.where(sub == k, 0.0, blocks[r])
                rows.append(rest - blocks[r][k : k + 1] * scaled)
        blocks = rows
    return blocks


def multiply(left, right):
    rows = []
    for r in range(8):
        total = left[r][0:1] * right[0]
        for k in range(1, 8):
            total = total + left[r][k : k + 1] * right[k]
        rows.append(total)
    return rows


def matvec(terms, sub):
    result = jnp.zeros_like(terms[0][1])
    for r in range(8):
        product = terms[0][0][r] * terms[0][1]
        for blocks, column in terms[1:]:
            product = product + blocks[r] * column
        result = jnp.where(sub == r, jnp.sum(product, axis=0, keepdims=True), result)
    return result


def coarse_operator(c, count, sums_z, couplings_z, inside_y, interface_y):
    sub = lax.broadcasted_iota(jnp.int32, c.shape, 0)
    lane = lax.broadcasted_iota(jnp.int32, c.shape, 1)
    has_low = lane > 0
    has_high = lane < count - 1

    def after(array):
        return jnp.where(sub < 7, pltpu.roll(array, 7, 0), 0.0)

    def before(array):
        return jnp.where(sub > 0, pltpu.roll(array, 1, 0), 0.0)

    def right(array):
        return jnp.where(has_high, pltpu.roll(array, LANES - 1, 1), 0.0)

    def left(array):
        return jnp.where(has_low, pltpu.roll(array, 1, 1), 0.0)

    on_low = jnp.where(has_low, 0.5 * (c + left(c)), c)
    on_high = jnp.where(has_high, 0.5 * (c + right(c)), c)
    tested = []
    for place, value in enumerate((c, on_low, on_high)):
        slope = jnp.where(sub > 0, 0.5 * (value - before(value)), 0.0)
        coupling = couplings_z[place]
        force = sums_z[place] * slope - coupling * after(slope) - before(coupling * slope)
        force = jnp.where(sub > 0, force, 0.0)
        tested.append(0.5 * (force - after(force)))
    result = tested[0] + jnp.where(has_low, 0.5, 1.0) * tested[1] + jnp.where(has_high, 0.5, 1.0) * tested[2]
    result = result + 0.5 * right(tested[1]) + 0.5 * left(tested[2])

    interface = jnp.where(sub > 0, 0.5 * (c + before(c)), 0.0)
    for side, (move, there) in enumerate(((left, has_low), (right, has_high))):
        force = inside_y[side] * jnp.where(there, 0.5 * (move(c) - c), 0.0)
        face = interface_y[side] * jnp.where(there, 0.5 * (move(interface) - interface), 0.0)
        force = force + 0.5 * (face + after(face))
        back = right if side == 0 else left
        result = result + 0.5 * (back(force) - force)

    end = float(WEIGHT[0])
    mass = (2.0 - 2.0 * end) * c + end * (interface + after(interface))
    mass = mass + jnp.where((sub == 0) | (sub == 7), end * c, 0.0)
    beside = jnp.where(has_low, 0.5 * (mass + left(mass)), 0.0)
    scaled = (2.0 * EY - 2.0 * end) * mass + end * (beside + right(beside))
    scaled = scaled + jnp.where(has_low, 0.0, end * mass) + jnp.where(has_high, 0.0, end * mass)
    return result + HELM_COEF / 8.0 * float(np.sum(WX)) * scaled


def coarse_kernel(count, place, gathered, out_ref, wide, turned):
    lanes = LANES
    sub = lax.broadcasted_iota(jnp.int32, (8, lanes), 0)
    lane = lax.broadcasted_iota(jnp.int32, (8, lanes), 1)
    wide[...] = jnp.zeros((LANES, LANES), F32)
    wide[0:count] = gathered[...]
    turned[...] = wide[...].T

    def value(index):
        return turned[pl.ds(index, 8, stride=16), :]

    def move(array, dz, dy):
        if dz:
            array = pltpu.roll(array, (-dz) % 8, 0)
        if dy:
            array = pltpu.roll(array, (-dy) % lanes, 1)
        return array

    kbar = jnp.where(lane < count, value(0), 1.0)
    above = move(kbar, 1, 0)
    link_z = jnp.where(sub < 7, 2.0 * kbar * above / (kbar + above) * (EY * EX / EZ), 0.0)
    link_z = jnp.where(lane < count, link_z, 0.0)
    beside = move(kbar, 0, 1)
    link_y = 2.0 * kbar * beside / (kbar + beside) * (EZ * EX / EY)
    link_y = jnp.where(lane < count - 1, link_y, 0.0)
    back_z = move(link_z, -1, 0)
    back_y = move(link_y, 0, -1)
    diagonal = HELM_COEF * EZ * EY * EX + link_z + back_z + link_y + back_y
    blocks, lower, upper = [], [], []
    for r in range(8):
        row = jnp.where(sub == r, diagonal, 0.0)
        row = jnp.where(sub == r + 1, -back_z, row)
        row = jnp.where(sub == r - 1, -link_z, row)
        blocks.append(row)
        lower.append(jnp.where(sub == r, -back_y, 0.0))
        upper.append(jnp.where(sub == r, -link_y, 0.0))
    levels = []
    step = 1
    while step < count:
        inverse = invert(blocks, sub)
        down = multiply(lower, [move(row, 0, -step) for row in inverse])
        up = multiply(upper, [move(row, 0, step) for row in inverse])
        levels.append((step, down, up))
        before_u = multiply(down, [move(row, 0, -step) for row in upper])
        after_l = multiply(up, [move(row, 0, step) for row in lower])
        if 2 * step < count:
            new_lower = multiply(down, [move(row, 0, -step) for row in lower])
            new_upper = multiply(up, [move(row, 0, step) for row in upper])
            lower = [-row for row in new_lower]
            upper = [-row for row in new_upper]
        blocks = [blocks[r] - before_u[r] - after_l[r] for r in range(8)]
        step *= 2
    inverse = invert(blocks, sub)

    def solve(column):
        for distance, down, up in levels:
            pulled = matvec(
                [(down, move(column, 0, -distance)), (up, move(column, 0, distance))], sub
            )
            column = column - pulled
        return matvec([(inverse, column)], sub)

    offsets = [(a - 1, b - 1) for a in range(3) for b in range(3)]
    first = solve(value(1))
    near_first = [move(first, dz, dy) for dz, dy in offsets]
    totals = coarse_operator(
        first,
        count,
        [value(5 + k) for k in range(3)],
        [value(8 + k) for k in range(3)],
        [value(11), value(12)],
        [value(13), value(14)],
    )
    totals = totals + value(3)
    totals = totals + jnp.where(lane < count - 1, move(value(2), 0, 1), 0.0)
    totals = totals + jnp.where(lane > 0, move(value(4), 0, -1), 0.0)
    totals = jnp.where(lane < count, totals, 0.0)
    second = solve(totals)
    near_second = [move(second, dz, dy) for dz, dy in offsets]
    mine = (sub == place[0]) & (lane == place[1])
    for d in range(9):
        out_ref[d : d + 1] = jnp.full((1, lanes), jnp.sum(jnp.where(mine, near_first[d], 0.0)))
        out_ref[16 + d : 17 + d] = jnp.full(
            (1, lanes), jnp.sum(jnp.where(mine, near_second[d], 0.0))
        )


def coarse_columns(near, coarse, start):
    row = lax.broadcasted_iota(jnp.int32, (ROWS, LANES), 0)
    edge = edge_rows(ROWS, near[2], near[3])
    below = jnp.where(row == 0, 1.0 - near[2], 0.0)
    above = jnp.where(row == ROWS - 1, 1.0 - near[3], 0.0)
    columns = []
    for a in range(3):
        at = start + 3 * a
        columns.append(
            below * coarse[at : at + 1] + edge * coarse[at + 1 : at + 2] + above * coarse[at + 2 : at + 3]
        )
    first = (1.0 - near[0]) * (columns[0] - columns[1])
    last = (1.0 - near[1]) * (columns[2] - columns[1])
    return columns[1], first, last


def add_coarse(local, columns):
    inside, first, last = columns
    planes = [local[i] + inside for i in range(8)]
    planes[0] = planes[0] + first
    planes[7] = planes[7] + last
    return stack(planes)


def coarse_applied(columns, flux, packed):
    inside, first, last = columns
    slopes = [
        flux[i] * (float(DERIV[i, 0]) * first + float(DERIV[i, 7]) * last) for i in range(8)
    ]
    fz = along_z(slopes, DERIV.T)
    three = stack([inside + first, inside, inside + last])
    gy = along_y(three, packed, 0)
    fy = along_y(
        stack([flux[i] * gy[0 if i == 0 else 2 if i == 7 else 1] for i in range(8)]), packed, 1
    )
    plane_w = packed[0:ROWS]
    planes = []
    for i in range(8):
        plane = three[0 if i == 0 else 2 if i == 7 else 1]
        planes.append(fz[i] + fy[i] + (HELM_COEF * 0.125 * float(WEIGHT[i])) * (plane_w * plane))
    return stack(planes)


def apply_kernel(near, packed, coarse, flux, b, zl, yl, z_ref, y_ref, ylo, yhi, stat):
    columns = coarse_columns(near, coarse, 0)
    field = add_coarse(zl[...], columns)
    z_ref[...] = field
    applied = yl[...] + coarse_applied(columns, flux[...], packed)
    y_ref[...] = applied
    ylo[...] = applied[0:2]
    yhi[...] = applied[6:8]
    stat[...] = lane_row([jnp.sum(b[...] * field), jnp.sum(field * applied)])


def second_kernel(near, packed, coarse, flux, b, y, w, zlo, zhi, stat_in, q_ref, stat):
    local = add_planes(w, zlo[...], zhi[...])
    field = add_coarse(local, coarse_columns(near, coarse, 16))
    q_ref[...] = field
    applied = local_operator(field, flux[...], packed)
    sums = [0.0, 0.0, jnp.sum(b[...] * field), jnp.sum(y[...] * field), jnp.sum(field * applied)]
    stat[...] = jnp.broadcast_to(stat_in[...] + lane_row(sums), stat.shape)


def combine_kernel(sums, z, q, p_ref):
    total = jnp.sum(sums[...], axis=0, keepdims=True)
    rz, pap, rq, aq, qhq = (total[:, k : k + 1] for k in range(5))
    step = rz / pap
    rz_next = step * (step * aq - rq)
    beta = rz_next / rz
    grown = 1.0 + beta
    curved = grown * grown * pap - 2.0 * step * grown * aq + step * step * qhq
    step_next = rz_next / curved
    on_z = step + step_next * grown
    on_q = step_next * step
    p_ref[...] = on_z.reshape(1, 1, 1) * z[...] - on_q.reshape(1, 1, 1) * q[...]


def run(kernel, outs, smem, args, scratch=(), flops=1000000, place=VMEM, limit=LIMIT):
    nbytes = sum(4 * int(np.prod(out)) for out in outs) * 2
    return pl.pallas_call(
        kernel,
        out_shape=[jax.ShapeDtypeStruct(out, F32) for out in outs],
        in_specs=[pl.BlockSpec(memory_space=SMEM) for _ in smem]
        + [pl.BlockSpec(memory_space=place) for _ in args],
        out_specs=[pl.BlockSpec(memory_space=VMEM) for _ in outs],
        scratch_shapes=list(scratch),
        compiler_params=pltpu.CompilerParams(vmem_limit_bytes=limit),
        cost_estimate=pl.CostEstimate(flops=flops, bytes_accessed=nbytes, transcendentals=0),
    )(*smem, *args)


def shift(axis, low_face, high_face):
    count = lax.axis_size(axis)
    forward = [(i, i + 1) for i in range(count - 1)]
    backward = [(target, source) for source, target in forward]
    return lax.ppermute(high_face, axis, forward), lax.ppermute(low_face, axis, backward)


def body(level_set, velocity, source, wick_solid):
    block = level_set.shape
    count_gx = lax.axis_size("gx")
    count_gy = lax.axis_size("gy")
    index_gx = lax.axis_index("gx")
    index_gy = lax.axis_index("gy")

    def ends(index, count):
        return [jnp.where(index > 0, 0.5, 1.0), jnp.where(index < count - 1, 0.5, 1.0)]

    near = jnp.stack(ends(index_gx, count_gx) + ends(index_gy, count_gy)).astype(F32)
    place = jnp.stack([index_gx, index_gy]).astype(jnp.int32)
    packed = jnp.asarray(PACKED)
    solver = (INV_DEN, FY_W, FX_HH, FX_L, BX_H, BX_L, BY_W)
    solver = tuple(jnp.asarray(table) for table in solver)
    face = (ROWS, LANES)
    rim = (12, TILE, LANES)
    solid = wick_solid.reshape(EY, EX).astype(F32)

    b, l, zlo, zhi = run(
        advect_kernel,
        [block, block, (3, *face), (3, *face)],
        [],
        [
            pltpu.with_memory_space_constraint(array, pltpu.HBM)
            for array in (level_set, velocity, source, packed)
        ],
        [VMEM(block, F32), VMEM((3, *block), F32), VMEM(block, F32), VMEM(PACKED.shape, F32)]
        + [pltpu.SemaphoreType.DMA((4,))],
        place=pltpu.HBM,
    )
    zlo, zhi = shift("gx", zlo, zhi)
    ylo, yhi = run(functools.partial(rim_kernel, 2), [rim, rim], [], [b, l, zlo, zhi])
    ylo, yhi = shift("gy", ylo, yhi)
    w, wlo, whi = run(
        schwarz_kernel, [block, face, face], [near], [*solver, b, zlo, zhi, ylo, yhi]
    )
    wlo, whi = shift("gx", wlo, whi)
    level_new, flux, stat = run(
        level_kernel,
        [block, block, (1, LANES)],
        [near],
        [
            solid, jnp.asarray(SPREAD), jnp.asarray(INV_MASS), packed,
            b, l, zlo, zhi, ylo, yhi,
        ],
        flops=20000000,
    )
    zl, yl, stat = run(
        galerkin_kernel,
        [block, block, (count_gx, LANES)],
        [near],
        [packed, stat, flux, w, wlo, whi],
    )
    gathered = lax.all_to_all(stat, "gx", 0, 0, tiled=True)
    (column,) = run(column_kernel, [(count_gy, LANES)], [], [gathered])
    gathered = lax.all_to_all(column, "gy", 0, 0, tiled=True)
    (coarse,) = run(
        functools.partial(coarse_kernel, count_gy),
        [(32, LANES)],
        [place],
        [gathered],
        [VMEM((LANES, LANES), F32), VMEM((LANES, LANES), F32)],
    )
    z, y, zlo, zhi, sums = run(
        apply_kernel,
        [block, block, (2, *face), (2, *face), (1, LANES)],
        [near],
        [packed, coarse, flux, b, zl, yl],
    )
    zlo, zhi = shift("gx", zlo, zhi)
    ylo, yhi = run(functools.partial(rim_kernel, 1), [rim, rim], [], [y, zlo, zhi])
    ylo, yhi = shift("gy", ylo, yhi)
    w, wlo, whi = run(
        schwarz_kernel, [block, face, face], [near], [*solver, y, zlo, zhi, ylo, yhi]
    )
    zlo, zhi = shift("gx", wlo, whi)
    q, sums = run(
        second_kernel,
        [block, (count_gx, LANES)],
        [near],
        [packed, coarse, flux, b, y, w, zlo, zhi, sums],
    )
    tile = lax.all_to_all(sums, "gx", 0, 0, tiled=True)
    wide = jnp.broadcast_to(jnp.sum(tile, axis=0, keepdims=True), (count_gy, LANES))
    wide = lax.all_to_all(wide, "gy", 0, 0, tiled=True)
    (pressure,) = run(combine_kernel, [block], [], [wide, z, q])
    return (level_new, pressure)


def solution(mesh):
    placed = (
        P("gx", "gy", None),
        P(None, "gx", "gy", None),
        P("gx", "gy", None),
        P("gx", "gy", None),
    )
    return jax.shard_map(
        body,
        mesh=mesh,
        in_specs=placed,
        out_specs=(P("gx", "gy", None), P("gx", "gy", None)),
        check_vma=False,
    )
```

```python
import functools

import jax
import jax.numpy as jnp
import numpy as np
from jax import lax
from jax.experimental import pallas as pl
from jax.experimental.pallas import tpu as pltpu
from jax.sharding import PartitionSpec as P

EZ = 1
EY = 4
EX = 16
ROWS = 8 * EY
LANES = 8 * EX

TIME_STEP = 0.02
HELM_COEF = 0.25
LEVEL_WIDTH = 0.25
GAS_RATIO = 10.0
SOLID_FACTOR = 0.25
SCHWARZ_SCALE = 0.5
SCHWARZ_SHIFT = 0.05

F32 = jnp.float32
BF16 = jnp.bfloat16
VMEM = pltpu.VMEM
SMEM = pltpu.SMEM
LIMIT = 24 * 1024 * 1024


def gll_tables():
    gll_nodes = np.array(
        [
            -1.0,
            -0.8717401485096066,
            -0.5917001814331423,
            -0.2092992179024789,
            0.2092992179024789,
            0.5917001814331423,
            0.8717401485096066,
            1.0,
        ]
    )
    weight_np = np.array(
        [
            1.0 / 28.0,
            0.21070422714350603,
            0.3411226924835044,
            0.4124587946587038,
            0.4124587946587038,
            0.3411226924835044,
            0.21070422714350603,
            1.0 / 28.0,
        ]
    )
    bary_weights = np.array(
        [1.0 / np.prod([gll_nodes[i] - gll_nodes[j] for j in range(8) if j != i]) for i in range(8)]
    )
    derivative = np.zeros((8, 8))
    for i in range(8):
        for j in range(8):
            if i != j:
                derivative[i, j] = bary_weights[j] / bary_weights[i] / (gll_nodes[i] - gll_nodes[j])
        derivative[i, i] = -np.sum(derivative[i])
    return (weight_np, derivative)


def sine_tables():
    indices = np.arange(10) + 1.0
    sine_basis = np.sqrt(2.0 / 11.0) * np.sin(np.pi * np.outer(indices, indices) / 11.0)
    eigen_vals = 2.0 - 2.0 * np.cos(np.pi * indices / 11.0)
    return (sine_basis, eigen_vals)


WEIGHT, DERIV = gll_tables()
SINE, EIGEN = sine_tables()


def split_const(matrix):
    single = matrix.astype(np.float32)
    high = single.astype(jnp.bfloat16)
    low = (single - high.astype(np.float32)).astype(jnp.bfloat16)
    return high, low


def line_maps(count):
    length = 8 * count
    total = length + 4

    def column(position):
        if 0 <= position < length:
            return position
        return {-2: length, -1: length + 1, length: length + 2, length + 1: length + 3}[position]

    assembled = {}
    for position in range(-2, length + 2):
        row = np.zeros(total)
        row[column(position)] = 1.0
        if 0 <= position < length:
            if position % 8 == 0:
                row[column(position - 1)] += 1.0
            if position % 8 == 7:
                row[column(position + 1)] += 1.0
        assembled[position] = row
    forward = np.zeros((10 * count, total))
    for element in range(count):
        places = [8 * element - 2] + list(range(8 * element, 8 * element + 8)) + [8 * element + 9]
        forward[10 * element : 10 * element + 10] = SINE @ np.stack([assembled[p] for p in places])
    backward = np.zeros((length, 10 * count))
    for element in range(count):
        backward[8 * element : 8 * element + 8, 10 * element : 10 * element + 10] = SINE[1:9]
    for element in range(count - 1):
        first, second = 8 * element + 7, 8 * element + 8
        mean = 0.5 * (backward[first] + backward[second])
        backward[first] = mean
        backward[second] = mean
    return forward, backward


RING = 16
WIDE = ROWS + 2 * RING
REACH = 26
TILE = 48
TILE_B = 32


def ring_maps(reach, depth, inside):
    count = EY + 2 * depth
    forward, _ = line_maps(count)
    length = 8 * count
    columns = np.zeros((10 * count, len(inside)))
    for at, position in enumerate(inside):
        place = None if position is None else position + 8 * depth
        if place is None or place < -2 or place > length + 1:
            continue
        source = place if 0 <= place < length else {-2: 0, -1: 1}.get(place, place - length + 2) + length
        columns[:, at] = forward[:, source]
    _, backward = line_maps(count)
    own = 8 * depth
    rows = np.concatenate(
        [
            backward[own - reach : own + ROWS + reach],
            np.zeros((8, 10 * count)),
        ]
    )
    rows[ROWS + 2 * reach, 10 * depth : 10 * depth + 10] = SINE[1]
    rows[ROWS + 2 * reach + 1, 10 * (depth + EY - 1) : 10 * (depth + EY)] = SINE[8]
    return columns, rows


FZ, BZ = line_maps(1)
TILES = list(range(-REACH, 0)) + [None] * (TILE_B - REACH) + list(range(ROWS))
TILES += list(range(ROWS, ROWS + REACH)) + [None] * (TILE_B - REACH)
FY_A, BY_A = ring_maps(RING, 3, TILES)
FY_B, BY_B = ring_maps(0, 1, list(range(-RING, ROWS + RING)))
STEP_A = 112
STEP_B = 64


def padded(forward, backward, step):
    forward = np.pad(forward, ((0, step - forward.shape[0]), (0, 0)))
    return forward, np.pad(backward, ((0, 0), (0, step - backward.shape[1])))


FY_A, BY_A = padded(FY_A, BY_A, STEP_A)
FY_B, BY_B = padded(FY_B, BY_B, STEP_B)
FX, BX = line_maps(EX)
FX = FX[:, :LANES]


def denominators(step):
    lam_y = np.tile(EIGEN, step // 10)
    lam_x = np.tile(EIGEN, EX)
    total = EIGEN[:, None, None] + lam_y[None, :, None] + lam_x[None, None, :]
    inverse = 1.0 / (SCHWARZ_SCALE * total + SCHWARZ_SHIFT)
    inverse = np.pad(inverse, ((0, 0), (0, step - inverse.shape[1]), (0, 0)))
    return inverse.reshape(10 * step, 10 * EX).astype(np.float32)


FX_H, FX_L = split_const(FX.T.copy())
BX_H, BX_L = split_const(BX.T.copy())


def wide_const(table):
    high, low = split_const(table)
    return np.concatenate([high, high, low], axis=1)


FX_HH = np.concatenate([FX_H, FX_H], axis=0)
SOLVER_A = (denominators(STEP_A), wide_const(FY_A), FX_HH, FX_L, BX_H, BX_L, wide_const(BY_A))
SOLVER_B = (denominators(STEP_B), wide_const(FY_B), FX_HH, FX_L, BX_H, BX_L, wide_const(BY_B))


def roll_table():
    table = np.zeros((2, 8, 8, LANES))
    for kind, matrix in enumerate((DERIV, DERIV.T)):
        for k in range(8):
            for i in range(8):
                table[kind, k, i, :] = matrix[i, (i + k) % 8]
    return table.reshape(2 * 64, LANES)


WY = np.tile(WEIGHT, WIDE // 8)
WX = np.tile(WEIGHT, EX)
AT_ROLLS = WIDE
AT_DX = AT_ROLLS + 128
AT_DXT = AT_DX + LANES
AT_SQUARE = AT_DXT + LANES
PACKED = np.concatenate(
    [
        WY[:, None] * WX[None, :],
        roll_table(),
        np.kron(np.eye(EX), DERIV.T),
        np.kron(np.eye(EX), DERIV),
        np.repeat(DERIV[:, :1] ** 2, LANES, axis=1),
        np.repeat(DERIV[:, 7:] ** 2, LANES, axis=1),
    ]
).astype(np.float32)


def inner_count(count):
    mult = np.ones(8 * count)
    position = np.arange(8 * count)
    mult[(position % 8 == 0) & (position > 0)] += 1.0
    mult[(position % 8 == 7) & (position < 8 * count - 1)] += 1.0
    return mult


END_MASS = np.where(np.arange(WIDE) % 8 % 7 == 0, 2.0, 1.0)
INV_MASS = (8.0 / (WY * END_MASS)[:, None] / (WX * inner_count(EX))[None, :]).astype(np.float32)
SPREAD = np.kron(np.eye(EX), np.ones((1, 8))).astype(jnp.bfloat16)


def parts(values):
    high = values.astype(BF16)
    low = (values - high.astype(F32)).astype(BF16)
    return high, low


def dot(left, right):
    return jnp.dot(left, right, preferred_element_type=F32)


def left_pairs(table, planes):
    results = []
    for i in range(0, len(planes), 2):
        high, low = parts(jnp.concatenate([planes[i], planes[i + 1]], axis=1))
        both = dot(table[...], jnp.concatenate([high, low, high], axis=0))
        results += [both[:, 0:LANES], both[:, LANES : 2 * LANES]]
    return results


def along_z(values, matrix):
    rows = []
    for i in range(matrix.shape[0]):
        total = None
        for j in range(matrix.shape[1]):
            if matrix[i, j] == 0.0:
                continue
            term = float(matrix[i, j]) * values[j]
            total = term if total is None else total + term
        rows.append(total)
    return rows


def along_y(values, packed, kind):
    count, rows = values.shape[:2]
    grouped = values.reshape(count * rows // 8, 8, LANES)
    start = AT_ROLLS + 64 * kind
    total = packed[start : start + 8][None] * grouped
    for k in range(1, 8):
        total = total + packed[start + 8 * k : start + 8 * k + 8][None] * pltpu.roll(grouped, 8 - k, 1)
    return total.reshape(count, rows, LANES)


def along_x(values, packed, kind):
    start = AT_DXT if kind else AT_DX
    high, low = parts(packed[start : start + LANES])
    first, rest = parts(values.reshape(8 * values.shape[1], LANES))
    total = dot(
        jnp.concatenate([first, rest], axis=1), jnp.concatenate([high, high], axis=0)
    ) + dot(first, low)
    return total.reshape(values.shape)


def stack(planes):
    return jnp.concatenate([plane[None] for plane in planes], axis=0)


def edge_rows(rows, low, high):
    position = lax.broadcasted_iota(jnp.int32, (rows, LANES), 0)
    return jnp.where(position == 0, low, jnp.where(position == rows - 1, high, 1.0))


def local_operator(values, flux, packed):
    plane_w = packed[0 : values.shape[1]]
    gz = along_z([values[i] for i in range(8)], DERIV)
    fz = along_z([flux[i] * gz[i] for i in range(8)], DERIV.T)
    total = along_y(flux * along_y(values, packed, 0), packed, 1)
    total = total + along_x(flux * along_x(values, packed, 0), packed, 1)
    planes = [
        total[i] + fz[i] + (HELM_COEF * 0.125 * float(WEIGHT[i])) * (plane_w * values[i])
        for i in range(8)
    ]
    return stack(planes)


def add_planes(own, low_z, high_z):
    planes = [own[i] for i in range(8)]
    planes[0] = planes[0] + low_z
    planes[7] = planes[7] + high_z
    return stack(planes)


def solve_elements(planes, tables):
    inv_den, fy, fxhh, fxl, bxh, bxl, by = tables
    spectral = left_pairs(fy, along_z(planes, FZ))
    high, low = parts(jnp.concatenate(spectral, axis=0))
    wide = dot(jnp.concatenate([high, low], axis=1), fxhh[...]) + dot(high, fxl[...])
    high, low = parts(wide * inv_den[...])
    back = dot(high, bxh[...]) + dot(low, bxh[...]) + dot(high, bxl[...])
    step = fy.shape[0]
    back = left_pairs(by, [back[step * i : step * (i + 1)] for i in range(10)])
    return along_z(back, BZ)


def store_faces(planes, near, out_ref, low_ref, high_ref):
    planes[0] = planes[0] * near[0]
    planes[7] = planes[7] * near[1]
    for i in range(8):
        out_ref[i] = planes[i]
    low_ref[...] = planes[0]
    high_ref[...] = planes[7]


def ring_rows(near):
    row = lax.broadcasted_iota(jnp.int32, (WIDE, LANES), 0)
    return row, 2.0 - 2.0 * near[2], 2.0 - 2.0 * near[3]


def partition_total(own, low_z, high_z, low_y, high_y, near):
    def planes(array):
        total = near[0] * array[0] + near[1] * array[7]
        for i in range(1, 7):
            total = total + array[i]
        return total

    total = planes(own) + 0.5 * (low_z[1] + high_z[0])
    below = planes(low_y) + 0.5 * (low_y[9] + low_y[10])
    above = planes(high_y) + 0.5 * (high_y[9] + high_y[10])
    faces = 0.5 * (below[REACH - 1 : REACH] + above[0:1])
    return jnp.sum(total * edge_rows(ROWS, near[2], near[3])) + jnp.sum(faces)


def lane_row(entries):
    lane = lax.broadcasted_iota(jnp.int32, (1, LANES), 1)
    row = jnp.zeros((1, LANES), F32)
    for index, value in enumerate(entries):
        row = jnp.where(lane == index, value, row)
    return row


def advect_kernel(
    lev_in, vel_in, src_in, packed_in, b_ref, l_ref, zlo, zhi, lev, vel, src, packed, sems
):
    copies = [
        pltpu.make_async_copy(source, target, sems.at[index])
        for index, (source, target) in enumerate(
            ((vel_in, vel), (lev_in, lev), (packed_in, packed), (src_in, src))
        )
    ]
    for copy in copies:
        copy.start()
    for copy in copies:
        copy.wait()
    level = lev[...]
    v0, v1, v2 = vel[0], vel[1], vel[2]
    gz = stack(along_z([level[i] for i in range(8)], DERIV))
    advect = v0 * gz + v1 * along_y(level, packed, 0) + v2 * along_x(level, packed, 0)
    moved = level - (2.0 * TIME_STEP) * advect
    diverge = stack(along_z([v0[i] for i in range(8)], DERIV))
    diverge = diverge + along_y(v1, packed, 0) + along_x(v2, packed, 0)
    force = src[...] - (2.0 * TIME_STEP) * diverge
    weights = packed[0:ROWS]
    for i in range(8):
        mass = (0.125 * float(WEIGHT[i])) * weights
        term = mass * force[i]
        moved_i = mass * moved[i]
        b_ref[i] = term
        l_ref[i] = moved_i
        if i < 2:
            zlo[i] = term
        if i == 0:
            zlo[2] = moved_i
        if i > 5:
            zhi[i - 6] = term
        if i == 7:
            zhi[2] = moved_i


def rim_kernel(solid, spread, b, l, low_z, high_z, low_y, high_y):
    in_solid = dot(solid[...].astype(BF16), spread[...])
    rest = TILE - REACH - RING - 1

    def rows(planes, at, level, far, extra=None):
        start = ROWS - REACH if far else 0
        pieces = [planes[at, start : start + REACH]]
        if level is None:
            pieces.append(jnp.zeros((RING + 1, LANES), F32))
        else:
            array, index = level
            start = ROWS - RING - 1 if far else 0
            pieces.append(array[index, start : start + RING + 1])
        if extra is None:
            pieces.append(jnp.zeros((rest, LANES), F32))
        else:
            pieces += [extra, jnp.zeros((rest - 2, LANES), F32)]
        return jnp.concatenate(pieces, axis=0)

    for far, out in ((False, low_y), (True, high_y)):
        extra = in_solid[EY - 2 : EY] if far else in_solid[0:2]
        for i in range(8):
            out[i] = rows(b, i, (l, i), far, extra if i == 0 else None)
        for i in range(2):
            out[8 + i] = rows(low_z, i, (low_z, 2) if i == 1 else None, far)
            out[10 + i] = rows(high_z, i, (high_z, 2) if i == 0 else None, far)


def level_kernel(
    near, solid, spread, inv_mass, packed, b, l, zlo, zhi, ylo, yhi, level_ref, flux_ref, stat
):
    row, has_low, has_high = ring_rows(near)
    at = REACH

    def wide_rows(slot, own):
        return jnp.concatenate(
            [ylo[slot, at + 1 : at + 1 + RING], own, yhi[slot, at : at + RING]], axis=0
        )

    planes = []
    for i in range(8):
        plane = wide_rows(i, l[i])
        first = ylo[i, at : at + 1]
        last = yhi[i, at + RING : at + RING + 1]
        if i == 0:
            plane = plane + wide_rows(9, zlo[2])
            first = first + ylo[9, at : at + 1]
            last = last + yhi[9, at + RING : at + RING + 1]
        if i == 7:
            plane = plane + wide_rows(10, zhi[2])
            first = first + ylo[10, at : at + 1]
            last = last + yhi[10, at + RING : at + RING + 1]
        before = jnp.where(row == 0, first, pltpu.roll(plane, 1, 0))
        after = jnp.where(row == WIDE - 1, last, pltpu.roll(plane, WIDE - 1, 0))
        plane = plane + jnp.where(row % 8 == 0, before, jnp.where(row % 8 == 7, after, 0.0))
        planes.append(plane)
    own = stack(planes)
    lane = lax.broadcasted_iota(jnp.int32, (8, WIDE, LANES), 2)
    before = jnp.where((lane % 8 == 0) & (lane > 0), pltpu.roll(own, 1, 2), 0.0)
    after = jnp.where((lane % 8 == 7) & (lane < LANES - 1), pltpu.roll(own, LANES - 1, 2), 0.0)
    own = own + before + after
    ends = jnp.where(row == RING, 2.0 * near[2], jnp.where(row == RING + ROWS - 1, 2.0 * near[3], 1.0))
    inverse = inv_mass[...] * ends
    in_solid = dot(solid[...].astype(BF16), spread[...])
    solids = [ylo[0, at + RING + 1 + k : at + RING + 2 + k] for k in range(2)]
    solids += [in_solid[e : e + 1] for e in range(EY)]
    solids += [yhi[0, at + RING + 1 + k : at + RING + 2 + k] for k in range(2)]
    open_part = jnp.concatenate(
        [jnp.broadcast_to(1.0 - (1.0 - SOLID_FACTOR) * rows, (8, LANES)) for rows in solids], axis=0
    )
    in_grid = jnp.where(row < RING, has_low, jnp.where(row >= RING + ROWS, has_high, 1.0))
    flux_w = packed[0:WIDE] * in_grid
    total = jnp.zeros((ROWS, LANES), F32)
    fluxes = []
    for i in range(8):
        scale = 1.0 / float(WEIGHT[i])
        plane = own[i] * (inverse * scale)
        if i == 0:
            plane = plane * near[0]
        if i == 7:
            plane = plane * near[1]
        level_ref[i] = plane[RING : RING + ROWS]
        liquid = jax.nn.sigmoid(plane * (1.0 / LEVEL_WIDTH))
        coef = (GAS_RATIO - (GAS_RATIO - 1.0) * liquid) * open_part
        total = total + coef[RING : RING + ROWS]
        flux = (0.5 * float(WEIGHT[i])) * (coef * flux_w)
        flux_ref[i] = flux
        fluxes.append(flux[RING : RING + ROWS])
    kbar = jnp.sum(total) * (1.0 / (8 * ROWS * LANES))
    entries = [kbar, partition_total(b, zlo, zhi, ylo, yhi, near)] + [0.0] * 9
    for first, second in ((0, 0), (0, 7), (7, 7)):
        slopes = along_z(fluxes, (DERIV[:, first] * DERIV[:, second])[None, :])[0]
        column = jnp.sum(slopes, axis=1, keepdims=True)
        entries += [jnp.sum(column, axis=0, keepdims=True), column[0:1], column[ROWS - 1 : ROWS]]
    inner = fluxes[0] + fluxes[1]
    for i in range(2, 8):
        inner = inner + fluxes[i]
    for at_row, start in ((0, 0), (ROWS - 8, 8)):
        square = packed[AT_SQUARE + start : AT_SQUARE + start + 8]
        entries += [
            jnp.sum(square * plane[at_row : at_row + 8]) for plane in (inner, fluxes[0], fluxes[7])
        ]
    stat[...] = lane_row(entries)


def first_schwarz_kernel(
    near, inv_den, fy, fxhh, fxl, bxh, bxl, by, b, zlo, zhi, ylo, yhi, w_ref, wlo, whi
):
    own = [b[i] for i in range(8)] + [zlo[0], zlo[1], zhi[0], zhi[1]]
    planes = [
        jnp.concatenate([ylo[i, 0:TILE_B], own[i], yhi[i, 0:TILE_B]], axis=0) for i in range(12)
    ]
    planes = solve_elements(planes, (inv_den, fy, fxhh, fxl, bxh, bxl, by))
    row, has_low, has_high = ring_rows(near)
    in_grid = jnp.where(row < RING, has_low, jnp.where(row >= RING + ROWS, has_high, 1.0))
    in_grid = jnp.where(row == RING, has_low, jnp.where(row == RING + ROWS - 1, has_high, in_grid))
    for i in range(8):
        first = (1.0 - has_low) * planes[i][WIDE : WIDE + 1]
        last = (1.0 - has_high) * planes[i][WIDE + 1 : WIDE + 2]
        alone = jnp.where(row == RING, first, jnp.where(row == RING + ROWS - 1, last, 0.0))
        planes[i] = planes[i][0:WIDE] * in_grid + alone
    store_faces(planes, near, w_ref, wlo, whi)


def second_schwarz_kernel(
    near, inv_den, fy, fxhh, fxl, bxh, bxl, by, y, zlo, zhi, w_ref, wlo, whi
):
    planes = [y[i] for i in range(8)] + [zlo[0], zlo[1], zhi[0], zhi[1]]
    planes = solve_elements(planes, (inv_den, fy, fxhh, fxl, bxh, bxl, by))
    row = lax.broadcasted_iota(jnp.int32, (ROWS, LANES), 0)
    _, has_low, has_high = ring_rows(near)
    in_grid = jnp.where(row == 0, has_low, jnp.where(row == ROWS - 1, has_high, 1.0))
    for i in range(8):
        first = (1.0 - has_low) * planes[i][ROWS : ROWS + 1]
        last = (1.0 - has_high) * planes[i][ROWS + 1 : ROWS + 2]
        alone = jnp.where(row == 0, first, jnp.where(row == ROWS - 1, last, 0.0))
        planes[i] = planes[i][0:ROWS] * in_grid + alone
    store_faces(planes, near, w_ref, wlo, whi)


def galerkin_kernel(near, packed, stat_in, flux, w, zlo, zhi, zl_ref, y_ref, stat):
    local = add_planes(w, zlo[...], zhi[...])
    zl_ref[...] = local
    applied = local_operator(local, flux[...], packed)
    y_ref[...] = applied
    applied = applied[:, RING : RING + ROWS]
    inner = near[0] * applied[0] + near[1] * applied[7]
    for i in range(1, 7):
        inner = inner + applied[i]
    edge = edge_rows(ROWS, near[2], near[3])
    entries = [0.0, 0.0]
    for plane in ((1.0 - near[0]) * applied[0], inner, (1.0 - near[1]) * applied[7]):
        entries += [
            (1.0 - near[2]) * jnp.sum(plane[0:1]),
            jnp.sum(edge * plane),
            (1.0 - near[3]) * jnp.sum(plane[ROWS - 1 : ROWS]),
        ]
    stat[...] = jnp.broadcast_to(stat_in[...] + lane_row(entries), stat.shape)


def column_kernel(gathered, out_ref):
    values = gathered[...]
    sub = lax.broadcasted_iota(jnp.int32, (8, LANES), 0)
    lane = lax.broadcasted_iota(jnp.int32, (8, LANES), 1)
    after = jnp.where(sub < 7, pltpu.roll(values, 7, 0), 0.0)
    before = jnp.where(sub > 0, pltpu.roll(values, 1, 0), 0.0)
    first = lax.broadcasted_iota(jnp.int32, (8, 1), 0) == 0
    last = lax.broadcasted_iota(jnp.int32, (8, 1), 0) == 7

    def column(array, index):
        return array[:, index : index + 1]

    def slopes(array, pair):
        whole, low, high = (column(array, 11 + 3 * pair + k) for k in range(3))
        return whole - low - high, low, high

    merged = [column(values, 0), column(values, 1)]
    for b in range(3):
        merged.append(column(values, 5 + b) + column(after, 2 + b) + column(before, 8 + b))
    merged += [own + other for own, other in zip(slopes(values, 0), slopes(before, 2), strict=True)]
    merged += list(slopes(values, 1))
    inside, interface = [], []
    for side in range(2):
        whole, low, high = (column(values, 20 + 3 * side + k) for k in range(3))
        ends = jnp.where(first, low, 0.0) + jnp.where(last, high, 0.0)
        inside.append(whole - low - high + ends)
        interface.append(jnp.where(first, 0.0, low) + column(before, 22 + 3 * side))
    rows = jnp.zeros((8, LANES), F32)
    for index, value in enumerate(merged + inside + interface):
        rows = jnp.where(lane == index, value, rows)
    total = rows[0:1]
    for i in range(1, 8):
        total = total + pltpu.roll(rows[i : i + 1], 16 * i, 1)
    out_ref[...] = jnp.broadcast_to(total, out_ref.shape)


def invert(blocks, sub):
    for k in range(8):
        pivot = 1.0 / blocks[k][k : k + 1]
        scaled = jnp.where(sub == k, pivot, blocks[k] * pivot)
        rows = []
        for r in range(8):
            if r == k:
                rows.append(scaled)
            else:
                rest = jnp.where(sub == k, 0.0, blocks[r])
                rows.append(rest - blocks[r][k : k + 1] * scaled)
        blocks = rows
    return blocks


def multiply(left, right):
    rows = []
    for r in range(8):
        total = left[r][0:1] * right[0]
        for k in range(1, 8):
            total = total + left[r][k : k + 1] * right[k]
        rows.append(total)
    return rows


def matvec(terms, sub):
    result = jnp.zeros_like(terms[0][1])
    for r in range(8):
        product = terms[0][0][r] * terms[0][1]
        for blocks, column in terms[1:]:
            product = product + blocks[r] * column
        result = jnp.where(sub == r, jnp.sum(product, axis=0, keepdims=True), result)
    return result


def coarse_operator(c, count, sums_z, couplings_z, inside_y, interface_y):
    sub = lax.broadcasted_iota(jnp.int32, c.shape, 0)
    lane = lax.broadcasted_iota(jnp.int32, c.shape, 1)
    has_low = lane > 0
    has_high = lane < count - 1

    def after(array):
        return jnp.where(sub < 7, pltpu.roll(array, 7, 0), 0.0)

    def before(array):
        return jnp.where(sub > 0, pltpu.roll(array, 1, 0), 0.0)

    def right(array):
        return jnp.where(has_high, pltpu.roll(array, LANES - 1, 1), 0.0)

    def left(array):
        return jnp.where(has_low, pltpu.roll(array, 1, 1), 0.0)

    on_low = jnp.where(has_low, 0.5 * (c + left(c)), c)
    on_high = jnp.where(has_high, 0.5 * (c + right(c)), c)
    tested = []
    for place, value in enumerate((c, on_low, on_high)):
        slope = jnp.where(sub > 0, 0.5 * (value - before(value)), 0.0)
        coupling = couplings_z[place]
        force = sums_z[place] * slope - coupling * after(slope) - before(coupling * slope)
        force = jnp.where(sub > 0, force, 0.0)
        tested.append(0.5 * (force - after(force)))
    result = tested[0] + jnp.where(has_low, 0.5, 1.0) * tested[1] + jnp.where(has_high, 0.5, 1.0) * tested[2]
    result = result + 0.5 * right(tested[1]) + 0.5 * left(tested[2])

    interface = jnp.where(sub > 0, 0.5 * (c + before(c)), 0.0)
    for side, (move, there) in enumerate(((left, has_low), (right, has_high))):
        force = inside_y[side] * jnp.where(there, 0.5 * (move(c) - c), 0.0)
        face = interface_y[side] * jnp.where(there, 0.5 * (move(interface) - interface), 0.0)
        force = force + 0.5 * (face + after(face))
        back = right if side == 0 else left
        result = result + 0.5 * (back(force) - force)

    end = float(WEIGHT[0])
    mass = (2.0 - 2.0 * end) * c + end * (interface + after(interface))
    mass = mass + jnp.where((sub == 0) | (sub == 7), end * c, 0.0)
    beside = jnp.where(has_low, 0.5 * (mass + left(mass)), 0.0)
    scaled = (2.0 * EY - 2.0 * end) * mass + end * (beside + right(beside))
    scaled = scaled + jnp.where(has_low, 0.0, end * mass) + jnp.where(has_high, 0.0, end * mass)
    return result + HELM_COEF / 8.0 * float(np.sum(WX)) * scaled


def coarse_kernel(count, place, gathered, out_ref, wide, turned):
    lanes = LANES
    sub = lax.broadcasted_iota(jnp.int32, (8, lanes), 0)
    lane = lax.broadcasted_iota(jnp.int32, (8, lanes), 1)
    wide[...] = jnp.zeros((LANES, LANES), F32)
    wide[0:count] = gathered[...]
    turned[...] = wide[...].T

    def value(index):
        return turned[pl.ds(index, 8, stride=16), :]

    def move(array, dz, dy):
        if dz:
            array = pltpu.roll(array, (-dz) % 8, 0)
        if dy:
            array = pltpu.roll(array, (-dy) % lanes, 1)
        return array

    kbar = jnp.where(lane < count, value(0), 1.0)
    above = move(kbar, 1, 0)
    link_z = jnp.where(sub < 7, 2.0 * kbar * above / (kbar + above) * (EY * EX / EZ), 0.0)
    link_z = jnp.where(lane < count, link_z, 0.0)
    beside = move(kbar, 0, 1)
    link_y = 2.0 * kbar * beside / (kbar + beside) * (EZ * EX / EY)
    link_y = jnp.where(lane < count - 1, link_y, 0.0)
    back_z = move(link_z, -1, 0)
    back_y = move(link_y, 0, -1)
    diagonal = HELM_COEF * EZ * EY * EX + link_z + back_z + link_y + back_y
    blocks, lower, upper = [], [], []
    for r in range(8):
        row = jnp.where(sub == r, diagonal, 0.0)
        row = jnp.where(sub == r + 1, -back_z, row)
        row = jnp.where(sub == r - 1, -link_z, row)
        blocks.append(row)
        lower.append(jnp.where(sub == r, -back_y, 0.0))
        upper.append(jnp.where(sub == r, -link_y, 0.0))
    levels = []
    step = 1
    while step < count:
        inverse = invert(blocks, sub)
        down = multiply(lower, [move(row, 0, -step) for row in inverse])
        up = multiply(upper, [move(row, 0, step) for row in inverse])
        levels.append((step, down, up))
        before_u = multiply(down, [move(row, 0, -step) for row in upper])
        after_l = multiply(up, [move(row, 0, step) for row in lower])
        if 2 * step < count:
            new_lower = multiply(down, [move(row, 0, -step) for row in lower])
            new_upper = multiply(up, [move(row, 0, step) for row in upper])
            lower = [-row for row in new_lower]
            upper = [-row for row in new_upper]
        blocks = [blocks[r] - before_u[r] - after_l[r] for r in range(8)]
        step *= 2
    inverse = invert(blocks, sub)

    def solve(column):
        for distance, down, up in levels:
            pulled = matvec(
                [(down, move(column, 0, -distance)), (up, move(column, 0, distance))], sub
            )
            column = column - pulled
        return matvec([(inverse, column)], sub)

    offsets = [(a - 1, b - 1) for a in range(3) for b in range(3)]
    first = solve(value(1))
    near_first = [move(first, dz, dy) for dz, dy in offsets]
    totals = coarse_operator(
        first,
        count,
        [value(5 + k) for k in range(3)],
        [value(8 + k) for k in range(3)],
        [value(11), value(12)],
        [value(13), value(14)],
    )
    totals = totals + value(3)
    totals = totals + jnp.where(lane < count - 1, move(value(2), 0, 1), 0.0)
    totals = totals + jnp.where(lane > 0, move(value(4), 0, -1), 0.0)
    totals = jnp.where(lane < count, totals, 0.0)
    second = solve(totals)
    near_second = [move(second, dz, dy) for dz, dy in offsets]
    mine = (sub == place[0]) & (lane == place[1])
    for d in range(9):
        out_ref[d : d + 1] = jnp.full((1, lanes), jnp.sum(jnp.where(mine, near_first[d], 0.0)))
        out_ref[16 + d : 17 + d] = jnp.full(
            (1, lanes), jnp.sum(jnp.where(mine, near_second[d], 0.0))
        )


def coarse_columns(near, coarse, start):
    row, has_low, has_high = ring_rows(near)
    below = jnp.where(row < RING - 1, 1.0, jnp.where(row <= RING, 0.5, 0.0)) * has_low
    above = jnp.where(row > RING + ROWS, 1.0, jnp.where(row >= RING + ROWS - 1, 0.5, 0.0)) * has_high
    edge = jnp.where((row > RING) & (row < RING + ROWS - 1), 1.0, 0.0)
    edge = jnp.where(row == RING, near[2], jnp.where(row == RING + ROWS - 1, near[3], edge))
    edge = jnp.where(row == RING - 1, 0.5 * has_low, edge)
    edge = jnp.where(row == RING + ROWS, 0.5 * has_high, edge)
    columns = []
    for a in range(3):
        at = start + 3 * a
        columns.append(
            below * coarse[at : at + 1] + edge * coarse[at + 1 : at + 2] + above * coarse[at + 2 : at + 3]
        )
    first = (1.0 - near[0]) * (columns[0] - columns[1])
    last = (1.0 - near[1]) * (columns[2] - columns[1])
    return columns[1], first, last


def add_coarse(local, columns):
    inside, first, last = columns
    planes = [local[i] + inside for i in range(8)]
    planes[0] = planes[0] + first
    planes[7] = planes[7] + last
    return stack(planes)


def coarse_applied(columns, flux, packed):
    inside, first, last = columns
    slopes = [
        flux[i] * (float(DERIV[i, 0]) * first + float(DERIV[i, 7]) * last) for i in range(8)
    ]
    fz = along_z(slopes, DERIV.T)
    three = stack([inside + first, inside, inside + last])
    gy = along_y(three, packed, 0)
    fy = along_y(
        stack([flux[i] * gy[0 if i == 0 else 2 if i == 7 else 1] for i in range(8)]), packed, 1
    )
    plane_w = packed[0:WIDE]
    planes = []
    for i in range(8):
        plane = three[0 if i == 0 else 2 if i == 7 else 1]
        planes.append(fz[i] + fy[i] + (HELM_COEF * 0.125 * float(WEIGHT[i])) * (plane_w * plane))
    return stack(planes)


def apply_kernel(near, packed, coarse, flux, b, zl, yl, z_ref, y_ref, ylo, yhi, stat):
    columns = coarse_columns(near, coarse, 0)
    field = add_coarse(zl[...], columns)[:, RING : RING + ROWS]
    z_ref[...] = field
    applied = yl[...] + coarse_applied(columns, flux[...], packed)
    y_ref[...] = applied
    ylo[...] = applied[0:2]
    yhi[...] = applied[6:8]
    own = applied[:, RING : RING + ROWS]
    stat[...] = lane_row([jnp.sum(b[...] * field), jnp.sum(field * own)])


def second_kernel(near, packed, coarse, flux, b, y, w, zlo, zhi, stat_in, q_ref, stat):
    local = add_planes(w, zlo[...], zhi[...])
    columns = [column[RING : RING + ROWS] for column in coarse_columns(near, coarse, 16)]
    field = add_coarse(local, columns)
    q_ref[...] = field
    applied = local_operator(field, flux[:, RING : RING + ROWS], packed)
    own = y[:, RING : RING + ROWS]
    sums = [0.0, 0.0, jnp.sum(b[...] * field), jnp.sum(own * field), jnp.sum(field * applied)]
    stat[...] = jnp.broadcast_to(stat_in[...] + lane_row(sums), stat.shape)


def combine_kernel(sums, z, q, p_ref):
    total = jnp.sum(sums[...], axis=0, keepdims=True)
    rz, pap, rq, aq, qhq = (total[:, k : k + 1] for k in range(5))
    step = rz / pap
    rz_next = step * (step * aq - rq)
    beta = rz_next / rz
    grown = 1.0 + beta
    curved = grown * grown * pap - 2.0 * step * grown * aq + step * step * qhq
    step_next = rz_next / curved
    on_z = step + step_next * grown
    on_q = step_next * step
    p_ref[...] = on_z.reshape(1, 1, 1) * z[...] - on_q.reshape(1, 1, 1) * q[...]


def run(kernel, outs, smem, args, scratch=(), flops=1000000, place=VMEM, limit=LIMIT):
    nbytes = sum(4 * int(np.prod(out)) for out in outs) * 2
    return pl.pallas_call(
        kernel,
        out_shape=[jax.ShapeDtypeStruct(out, F32) for out in outs],
        in_specs=[pl.BlockSpec(memory_space=SMEM) for _ in smem]
        + [pl.BlockSpec(memory_space=place) for _ in args],
        out_specs=[pl.BlockSpec(memory_space=VMEM) for _ in outs],
        scratch_shapes=list(scratch),
        compiler_params=pltpu.CompilerParams(vmem_limit_bytes=limit),
        cost_estimate=pl.CostEstimate(flops=flops, bytes_accessed=nbytes, transcendentals=0),
    )(*smem, *args)


def shift(axis, low_face, high_face):
    count = lax.axis_size(axis)
    forward = [(i, i + 1) for i in range(count - 1)]
    backward = [(target, source) for source, target in forward]
    return lax.ppermute(high_face, axis, forward), lax.ppermute(low_face, axis, backward)


def body(level_set, velocity, source, wick_solid):
    block = level_set.shape
    count_gx = lax.axis_size("gx")
    count_gy = lax.axis_size("gy")
    index_gx = lax.axis_index("gx")
    index_gy = lax.axis_index("gy")

    def ends(index, count):
        return [jnp.where(index > 0, 0.5, 1.0), jnp.where(index < count - 1, 0.5, 1.0)]

    near = jnp.stack(ends(index_gx, count_gx) + ends(index_gy, count_gy)).astype(F32)
    place = jnp.stack([index_gx, index_gy]).astype(jnp.int32)
    packed = jnp.asarray(PACKED)
    solver_a = tuple(jnp.asarray(table) for table in SOLVER_A)
    solver_b = tuple(jnp.asarray(table) for table in SOLVER_B)
    spread = jnp.asarray(SPREAD)
    face = (ROWS, LANES)
    wide_block = (8, WIDE, LANES)
    wide_face = (WIDE, LANES)
    rim = (12, TILE, LANES)
    solid = wick_solid.reshape(EY, EX).astype(F32)

    b, l, zlo, zhi = run(
        advect_kernel,
        [block, block, (3, *face), (3, *face)],
        [],
        [
            pltpu.with_memory_space_constraint(array, pltpu.HBM)
            for array in (level_set, velocity, source, packed)
        ],
        [VMEM(block, F32), VMEM((3, *block), F32), VMEM(block, F32), VMEM(PACKED.shape, F32)]
        + [pltpu.SemaphoreType.DMA((4,))],
        place=pltpu.HBM,
    )
    zlo, zhi = shift("gx", zlo, zhi)
    ylo, yhi = run(rim_kernel, [rim, rim], [], [solid, spread, b, l, zlo, zhi])
    ylo, yhi = shift("gy", ylo, yhi)
    w, wlo, whi = run(
        first_schwarz_kernel,
        [wide_block, wide_face, wide_face],
        [near],
        [*solver_a, b, zlo, zhi, ylo, yhi],
    )
    wlo, whi = shift("gx", wlo, whi)
    level_new, flux, stat = run(
        level_kernel,
        [block, wide_block, (1, LANES)],
        [near],
        [solid, spread, jnp.asarray(INV_MASS), packed, b, l, zlo, zhi, ylo, yhi],
        flops=20000000,
    )
    zl, yl, stat = run(
        galerkin_kernel,
        [wide_block, wide_block, (count_gx, LANES)],
        [near],
        [packed, stat, flux, w, wlo, whi],
    )
    gathered = lax.all_to_all(stat, "gx", 0, 0, tiled=True)
    (column,) = run(column_kernel, [(count_gy, LANES)], [], [gathered])
    gathered = lax.all_to_all(column, "gy", 0, 0, tiled=True)
    (coarse,) = run(
        functools.partial(coarse_kernel, count_gy),
        [(32, LANES)],
        [place],
        [gathered],
        [VMEM((LANES, LANES), F32), VMEM((LANES, LANES), F32)],
    )
    z, y, zlo, zhi, sums = run(
        apply_kernel,
        [block, wide_block, (2, *wide_face), (2, *wide_face), (1, LANES)],
        [near],
        [packed, coarse, flux, b, zl, yl],
    )
    zlo, zhi = shift("gx", zlo, zhi)
    w, wlo, whi = run(
        second_schwarz_kernel, [block, face, face], [near], [*solver_b, y, zlo, zhi]
    )
    zlo, zhi = shift("gx", wlo, whi)
    q, sums = run(
        second_kernel,
        [block, (count_gx, LANES)],
        [near],
        [packed, coarse, flux, b, y, w, zlo, zhi, sums],
    )
    tile = lax.all_to_all(sums, "gx", 0, 0, tiled=True)
    wide = jnp.broadcast_to(jnp.sum(tile, axis=0, keepdims=True), (count_gy, LANES))
    wide = lax.all_to_all(wide, "gy", 0, 0, tiled=True)
    (pressure,) = run(combine_kernel, [block], [], [wide, z, q])
    return (level_new, pressure)


def solution(mesh):
    placed = (
        P("gx", "gy", None),
        P(None, "gx", "gy", None),
        P("gx", "gy", None),
        P("gx", "gy", None),
    )
    return jax.shard_map(
        body,
        mesh=mesh,
        in_specs=placed,
        out_specs=(P("gx", "gy", None), P("gx", "gy", None)),
        check_vma=False,
    )
```

```python
import functools

import jax
import jax.numpy as jnp
import numpy as np
from jax import lax
from jax.experimental import pallas as pl
from jax.experimental.pallas import tpu as pltpu
from jax.sharding import PartitionSpec as P

EZ = 1
EY = 4
EX = 16
ROWS = 8 * EY
LANES = 8 * EX

TIME_STEP = 0.02
HELM_COEF = 0.25
LEVEL_WIDTH = 0.25
GAS_RATIO = 10.0
SOLID_FACTOR = 0.25
SCHWARZ_SCALE = 0.5
SCHWARZ_SHIFT = 0.05

F32 = jnp.float32
BF16 = jnp.bfloat16
VMEM = pltpu.VMEM
SMEM = pltpu.SMEM
LIMIT = 24 * 1024 * 1024


def gll_tables():
    gll_nodes = np.array(
        [
            -1.0,
            -0.8717401485096066,
            -0.5917001814331423,
            -0.2092992179024789,
            0.2092992179024789,
            0.5917001814331423,
            0.8717401485096066,
            1.0,
        ]
    )
    weight_np = np.array(
        [
            1.0 / 28.0,
            0.21070422714350603,
            0.3411226924835044,
            0.4124587946587038,
            0.4124587946587038,
            0.3411226924835044,
            0.21070422714350603,
            1.0 / 28.0,
        ]
    )
    bary_weights = np.array(
        [1.0 / np.prod([gll_nodes[i] - gll_nodes[j] for j in range(8) if j != i]) for i in range(8)]
    )
    derivative = np.zeros((8, 8))
    for i in range(8):
        for j in range(8):
            if i != j:
                derivative[i, j] = bary_weights[j] / bary_weights[i] / (gll_nodes[i] - gll_nodes[j])
        derivative[i, i] = -np.sum(derivative[i])
    return (weight_np, derivative)


def sine_tables():
    indices = np.arange(10) + 1.0
    sine_basis = np.sqrt(2.0 / 11.0) * np.sin(np.pi * np.outer(indices, indices) / 11.0)
    eigen_vals = 2.0 - 2.0 * np.cos(np.pi * indices / 11.0)
    return (sine_basis, eigen_vals)


WEIGHT, DERIV = gll_tables()
SINE, EIGEN = sine_tables()


def split_const(matrix):
    single = matrix.astype(np.float32)
    high = single.astype(jnp.bfloat16)
    low = (single - high.astype(np.float32)).astype(jnp.bfloat16)
    return high, low


def line_maps(count):
    length = 8 * count
    total = length + 4

    def column(position):
        if 0 <= position < length:
            return position
        return {-2: length, -1: length + 1, length: length + 2, length + 1: length + 3}[position]

    assembled = {}
    for position in range(-2, length + 2):
        row = np.zeros(total)
        row[column(position)] = 1.0
        if 0 <= position < length:
            if position % 8 == 0:
                row[column(position - 1)] += 1.0
            if position % 8 == 7:
                row[column(position + 1)] += 1.0
        assembled[position] = row
    forward = np.zeros((10 * count, total))
    for element in range(count):
        places = [8 * element - 2] + list(range(8 * element, 8 * element + 8)) + [8 * element + 9]
        forward[10 * element : 10 * element + 10] = SINE @ np.stack([assembled[p] for p in places])
    backward = np.zeros((length, 10 * count))
    for element in range(count):
        backward[8 * element : 8 * element + 8, 10 * element : 10 * element + 10] = SINE[1:9]
    for element in range(count - 1):
        first, second = 8 * element + 7, 8 * element + 8
        mean = 0.5 * (backward[first] + backward[second])
        backward[first] = mean
        backward[second] = mean
    return forward, backward


RING = 16
WIDE = ROWS + 2 * RING
REACH = 26
TILE = 48
TILE_B = 32


def ring_maps(reach, depth, inside):
    count = EY + 2 * depth
    forward, _ = line_maps(count)
    length = 8 * count
    columns = np.zeros((10 * count, len(inside)))
    for at, position in enumerate(inside):
        place = None if position is None else position + 8 * depth
        if place is None or place < -2 or place > length + 1:
            continue
        source = place if 0 <= place < length else {-2: 0, -1: 1}.get(place, place - length + 2) + length
        columns[:, at] = forward[:, source]
    _, backward = line_maps(count)
    own = 8 * depth
    rows = np.concatenate(
        [
            backward[own - reach : own + ROWS + reach],
            np.zeros((8, 10 * count)),
        ]
    )
    rows[ROWS + 2 * reach, 10 * depth : 10 * depth + 10] = SINE[1]
    rows[ROWS + 2 * reach + 1, 10 * (depth + EY - 1) : 10 * (depth + EY)] = SINE[8]
    return columns, rows


FZ, BZ = line_maps(1)
TILES = list(range(-REACH, 0)) + [None] * (TILE_B - REACH) + list(range(ROWS))
TILES += list(range(ROWS, ROWS + REACH)) + [None] * (TILE_B - REACH)
FY_A, BY_A = ring_maps(RING, 3, TILES)
FY_B, BY_B = ring_maps(0, 1, list(range(-RING, ROWS + RING)))
STEP_A = 112
STEP_B = 64


def padded(forward, backward, step):
    forward = np.pad(forward, ((0, step - forward.shape[0]), (0, 0)))
    return forward, np.pad(backward, ((0, 0), (0, step - backward.shape[1])))


FY_A, BY_A = padded(FY_A, BY_A, STEP_A)
FY_B, BY_B = padded(FY_B, BY_B, STEP_B)
FX, BX = line_maps(EX)
FX = FX[:, :LANES]


def denominators(step):
    lam_y = np.tile(EIGEN, step // 10)
    lam_x = np.tile(EIGEN, EX)
    total = EIGEN[:, None, None] + lam_y[None, :, None] + lam_x[None, None, :]
    inverse = 1.0 / (SCHWARZ_SCALE * total + SCHWARZ_SHIFT)
    inverse = np.pad(inverse, ((0, 0), (0, step - inverse.shape[1]), (0, 0)))
    return inverse.reshape(10 * step, 10 * EX).astype(np.float32)


FX_H, FX_L = split_const(FX.T.copy())
BX_H, BX_L = split_const(BX.T.copy())


def wide_const(table):
    high, low = split_const(table)
    return np.concatenate([high, high, low], axis=1)


def pack_tables(tables):
    places, pieces, at = [], [], 0
    for table in tables:
        rows = -(-table.shape[0] // 16) * 16
        extra = ((0, rows - table.shape[0]), (0, 384 - table.shape[1]))
        pieces.append(np.pad(table.astype(np.float32), extra))
        places.append((at, rows, table.shape[1]))
        at += rows
    return np.concatenate(pieces).astype(jnp.bfloat16), places


TABLES, PLACES = pack_tables(
    [
        np.concatenate([FX_H, FX_H], axis=0),
        FX_L,
        BX_H,
        BX_L,
        wide_const(FY_A),
        wide_const(BY_A),
        wide_const(FY_B),
        wide_const(BY_B),
    ]
)
DEN_A = denominators(STEP_A)
DEN_B = denominators(STEP_B)


def roll_table():
    table = np.zeros((2, 8, 8, LANES))
    for kind, matrix in enumerate((DERIV, DERIV.T)):
        for k in range(8):
            for i in range(8):
                table[kind, k, i, :] = matrix[i, (i + k) % 8]
    return table.reshape(2 * 64, LANES)


WY = np.tile(WEIGHT, WIDE // 8)
WX = np.tile(WEIGHT, EX)


def inner_count(count):
    mult = np.ones(8 * count)
    position = np.arange(8 * count)
    mult[(position % 8 == 0) & (position > 0)] += 1.0
    mult[(position % 8 == 7) & (position < 8 * count - 1)] += 1.0
    return mult


END_MASS = np.where(np.arange(WIDE) % 8 % 7 == 0, 2.0, 1.0)
INV_MASS = (8.0 / (WY * END_MASS)[:, None] / (WX * inner_count(EX))[None, :]).astype(np.float32)

AT_ROLLS = WIDE
AT_DX = AT_ROLLS + 128
AT_DXT = AT_DX + LANES
AT_SQUARE = AT_DXT + LANES
AT_MASS = AT_SQUARE + 16
AT_SPREAD = AT_MASS + WIDE
PACKED = np.concatenate(
    [
        WY[:, None] * WX[None, :],
        roll_table(),
        np.kron(np.eye(EX), DERIV.T),
        np.kron(np.eye(EX), DERIV),
        np.repeat(DERIV[:, :1] ** 2, LANES, axis=1),
        np.repeat(DERIV[:, 7:] ** 2, LANES, axis=1),
        INV_MASS,
        np.kron(np.eye(EX), np.ones((1, 8))),
    ]
).astype(np.float32)


def parts(values):
    high = values.astype(BF16)
    low = (values - high.astype(F32)).astype(BF16)
    return high, low


def dot(left, right):
    return jnp.dot(left, right, preferred_element_type=F32)


def left_pairs(table, planes):
    results = []
    for i in range(0, len(planes), 2):
        high, low = parts(jnp.concatenate([planes[i], planes[i + 1]], axis=1))
        both = dot(table, jnp.concatenate([high, low, high], axis=0))
        results += [both[:, 0:LANES], both[:, LANES : 2 * LANES]]
    return results


def along_z(values, matrix):
    rows = []
    for i in range(matrix.shape[0]):
        total = None
        for j in range(matrix.shape[1]):
            if matrix[i, j] == 0.0:
                continue
            term = float(matrix[i, j]) * values[j]
            total = term if total is None else total + term
        rows.append(total)
    return rows


def along_y(values, packed, kind):
    count, rows = values.shape[:2]
    grouped = values.reshape(count * rows // 8, 8, LANES)
    start = AT_ROLLS + 64 * kind
    total = packed[start : start + 8][None] * grouped
    for k in range(1, 8):
        total = total + packed[start + 8 * k : start + 8 * k + 8][None] * pltpu.roll(grouped, 8 - k, 1)
    return total.reshape(count, rows, LANES)


def along_x(values, packed, kind):
    start = AT_DXT if kind else AT_DX
    high, low = parts(packed[start : start + LANES])
    first, rest = parts(values.reshape(8 * values.shape[1], LANES))
    total = dot(
        jnp.concatenate([first, rest], axis=1), jnp.concatenate([high, high], axis=0)
    ) + dot(first, low)
    return total.reshape(values.shape)


def stack(planes):
    return jnp.concatenate([plane[None] for plane in planes], axis=0)


def edge_rows(rows, low, high):
    position = lax.broadcasted_iota(jnp.int32, (rows, LANES), 0)
    return jnp.where(position == 0, low, jnp.where(position == rows - 1, high, 1.0))


def local_operator(values, flux, packed):
    plane_w = packed[0 : values.shape[1]]
    gz = along_z([values[i] for i in range(8)], DERIV)
    fz = along_z([flux[i] * gz[i] for i in range(8)], DERIV.T)
    total = along_y(flux * along_y(values, packed, 0), packed, 1)
    total = total + along_x(flux * along_x(values, packed, 0), packed, 1)
    planes = [
        total[i] + fz[i] + (HELM_COEF * 0.125 * float(WEIGHT[i])) * (plane_w * values[i])
        for i in range(8)
    ]
    return stack(planes)


def add_planes(own, low_z, high_z):
    planes = [own[i] for i in range(8)]
    planes[0] = planes[0] + low_z
    planes[7] = planes[7] + high_z
    return stack(planes)


def solve_elements(planes, inv_den, tables, kind):
    def table(index):
        at, rows, width = PLACES[index]
        return tables[at : at + rows, 0:width]

    fxhh, fxl, bxh, bxl = (table(index) for index in range(4))
    spectral = left_pairs(table(4 + 2 * kind), along_z(planes, FZ))
    high, low = parts(jnp.concatenate(spectral, axis=0))
    wide = dot(jnp.concatenate([high, low], axis=1), fxhh) + dot(high, fxl)
    high, low = parts(wide * inv_den[...])
    back = dot(high, bxh) + dot(low, bxh) + dot(high, bxl)
    step = PLACES[4 + 2 * kind][1]
    back = left_pairs(table(5 + 2 * kind), [back[step * i : step * (i + 1)] for i in range(10)])
    return along_z(back, BZ)


def store_faces(planes, near, out_ref, low_ref, high_ref):
    planes[0] = planes[0] * near[0]
    planes[7] = planes[7] * near[1]
    for i in range(8):
        out_ref[i] = planes[i]
    low_ref[...] = planes[0]
    high_ref[...] = planes[7]


def ring_rows(near):
    row = lax.broadcasted_iota(jnp.int32, (WIDE, LANES), 0)
    return row, 2.0 - 2.0 * near[2], 2.0 - 2.0 * near[3]


def partition_total(own, low_z, high_z, low_y, high_y, near):
    def planes(array):
        total = near[0] * array[0] + near[1] * array[7]
        for i in range(1, 7):
            total = total + array[i]
        return total

    total = planes(own) + 0.5 * (low_z[1] + high_z[0])
    below = planes(low_y) + 0.5 * (low_y[9] + low_y[10])
    above = planes(high_y) + 0.5 * (high_y[9] + high_y[10])
    faces = 0.5 * (below[REACH - 1 : REACH] + above[0:1])
    return jnp.sum(total * edge_rows(ROWS, near[2], near[3])) + jnp.sum(faces)


def lane_row(entries):
    lane = lax.broadcasted_iota(jnp.int32, (1, LANES), 1)
    row = jnp.zeros((1, LANES), F32)
    for index, value in enumerate(entries):
        row = jnp.where(lane == index, value, row)
    return row


def advect_kernel(
    lev_in, vel_in, src_in, packed_in, solid_in, b_ref, l_ref, zlo, zhi, solid_ref,
    lev, vel, src, packed, solid, sems,
):
    copies = [
        pltpu.make_async_copy(source, target, sems.at[index])
        for index, (source, target) in enumerate(
            (
                (vel_in, vel), (lev_in, lev), (packed_in, packed), (src_in, src), (solid_in, solid),
            )
        )
    ]
    for copy in copies:
        copy.start()
    for copy in copies:
        copy.wait()
    spread = packed[AT_SPREAD : AT_SPREAD + EX].astype(BF16)
    in_solid = dot(solid[...].astype(F32).astype(BF16), spread)
    solid_ref[...] = jnp.concatenate([in_solid, jnp.zeros((8 - EY, LANES), F32)], axis=0)
    level = lev[...]
    v0, v1, v2 = vel[0], vel[1], vel[2]
    gz = stack(along_z([level[i] for i in range(8)], DERIV))
    advect = v0 * gz + v1 * along_y(level, packed, 0) + v2 * along_x(level, packed, 0)
    moved = level - (2.0 * TIME_STEP) * advect
    diverge = stack(along_z([v0[i] for i in range(8)], DERIV))
    diverge = diverge + along_y(v1, packed, 0) + along_x(v2, packed, 0)
    force = src[...] - (2.0 * TIME_STEP) * diverge
    weights = packed[0:ROWS]
    for i in range(8):
        mass = (0.125 * float(WEIGHT[i])) * weights
        term = mass * force[i]
        moved_i = mass * moved[i]
        b_ref[i] = term
        l_ref[i] = moved_i
        if i < 2:
            zlo[i] = term
        if i == 0:
            zlo[2] = moved_i
        if i > 5:
            zhi[i - 6] = term
        if i == 7:
            zhi[2] = moved_i


def rim_kernel(solid, b, l, low_z, high_z, low_y, high_y):
    in_solid = solid[...]
    rest = TILE - REACH - RING - 1

    def rows(planes, at, level, far, extra=None):
        start = ROWS - REACH if far else 0
        pieces = [planes[at, start : start + REACH]]
        if level is None:
            pieces.append(jnp.zeros((RING + 1, LANES), F32))
        else:
            array, index = level
            start = ROWS - RING - 1 if far else 0
            pieces.append(array[index, start : start + RING + 1])
        if extra is None:
            pieces.append(jnp.zeros((rest, LANES), F32))
        else:
            pieces += [extra, jnp.zeros((rest - 2, LANES), F32)]
        return jnp.concatenate(pieces, axis=0)

    for far, out in ((False, low_y), (True, high_y)):
        extra = in_solid[EY - 2 : EY] if far else in_solid[0:2]
        for i in range(8):
            out[i] = rows(b, i, (l, i), far, extra if i == 0 else None)
        for i in range(2):
            out[8 + i] = rows(low_z, i, (low_z, 2) if i == 1 else None, far)
            out[10 + i] = rows(high_z, i, (high_z, 2) if i == 0 else None, far)


def level_kernel(
    near, solid, packed, b, l, zlo, zhi, ylo, yhi, level_ref, flux_ref, stat
):
    row, has_low, has_high = ring_rows(near)
    at = REACH

    def wide_rows(slot, own):
        return jnp.concatenate(
            [ylo[slot, at + 1 : at + 1 + RING], own, yhi[slot, at : at + RING]], axis=0
        )

    planes = []
    for i in range(8):
        plane = wide_rows(i, l[i])
        first = ylo[i, at : at + 1]
        last = yhi[i, at + RING : at + RING + 1]
        if i == 0:
            plane = plane + wide_rows(9, zlo[2])
            first = first + ylo[9, at : at + 1]
            last = last + yhi[9, at + RING : at + RING + 1]
        if i == 7:
            plane = plane + wide_rows(10, zhi[2])
            first = first + ylo[10, at : at + 1]
            last = last + yhi[10, at + RING : at + RING + 1]
        before = jnp.where(row == 0, first, pltpu.roll(plane, 1, 0))
        after = jnp.where(row == WIDE - 1, last, pltpu.roll(plane, WIDE - 1, 0))
        plane = plane + jnp.where(row % 8 == 0, before, jnp.where(row % 8 == 7, after, 0.0))
        planes.append(plane)
    own = stack(planes)
    lane = lax.broadcasted_iota(jnp.int32, (8, WIDE, LANES), 2)
    before = jnp.where((lane % 8 == 0) & (lane > 0), pltpu.roll(own, 1, 2), 0.0)
    after = jnp.where((lane % 8 == 7) & (lane < LANES - 1), pltpu.roll(own, LANES - 1, 2), 0.0)
    own = own + before + after
    ends = jnp.where(row == RING, 2.0 * near[2], jnp.where(row == RING + ROWS - 1, 2.0 * near[3], 1.0))
    inverse = packed[AT_MASS : AT_MASS + WIDE] * ends
    in_solid = solid[...]
    solids = [ylo[0, at + RING + 1 + k : at + RING + 2 + k] for k in range(2)]
    solids += [in_solid[e : e + 1] for e in range(EY)]
    solids += [yhi[0, at + RING + 1 + k : at + RING + 2 + k] for k in range(2)]
    open_part = jnp.concatenate(
        [jnp.broadcast_to(1.0 - (1.0 - SOLID_FACTOR) * rows, (8, LANES)) for rows in solids], axis=0
    )
    in_grid = jnp.where(row < RING, has_low, jnp.where(row >= RING + ROWS, has_high, 1.0))
    flux_w = packed[0:WIDE] * in_grid
    total = jnp.zeros((ROWS, LANES), F32)
    fluxes = []
    for i in range(8):
        scale = 1.0 / float(WEIGHT[i])
        plane = own[i] * (inverse * scale)
        if i == 0:
            plane = plane * near[0]
        if i == 7:
            plane = plane * near[1]
        level_ref[i] = plane[RING : RING + ROWS]
        liquid = jax.nn.sigmoid(plane * (1.0 / LEVEL_WIDTH))
        coef = (GAS_RATIO - (GAS_RATIO - 1.0) * liquid) * open_part
        total = total + coef[RING : RING + ROWS]
        flux = (0.5 * float(WEIGHT[i])) * (coef * flux_w)
        flux_ref[i] = flux
        fluxes.append(flux[RING : RING + ROWS])
    kbar = jnp.sum(total) * (1.0 / (8 * ROWS * LANES))
    entries = [kbar, partition_total(b, zlo, zhi, ylo, yhi, near)] + [0.0] * 9
    for first, second in ((0, 0), (0, 7), (7, 7)):
        slopes = along_z(fluxes, (DERIV[:, first] * DERIV[:, second])[None, :])[0]
        column = jnp.sum(slopes, axis=1, keepdims=True)
        entries += [jnp.sum(column, axis=0, keepdims=True), column[0:1], column[ROWS - 1 : ROWS]]
    inner = fluxes[0] + fluxes[1]
    for i in range(2, 8):
        inner = inner + fluxes[i]
    for at_row, start in ((0, 0), (ROWS - 8, 8)):
        square = packed[AT_SQUARE + start : AT_SQUARE + start + 8]
        entries += [
            jnp.sum(square * plane[at_row : at_row + 8]) for plane in (inner, fluxes[0], fluxes[7])
        ]
    stat[...] = lane_row(entries)


def first_schwarz_kernel(
    near, inv_den, tables, b, zlo, zhi, ylo, yhi, w_ref, wlo, whi
):
    own = [b[i] for i in range(8)] + [zlo[0], zlo[1], zhi[0], zhi[1]]
    planes = [
        jnp.concatenate([ylo[i, 0:TILE_B], own[i], yhi[i, 0:TILE_B]], axis=0) for i in range(12)
    ]
    planes = solve_elements(planes, inv_den, tables, 0)
    row, has_low, has_high = ring_rows(near)
    in_grid = jnp.where(row < RING, has_low, jnp.where(row >= RING + ROWS, has_high, 1.0))
    in_grid = jnp.where(row == RING, has_low, jnp.where(row == RING + ROWS - 1, has_high, in_grid))
    for i in range(8):
        first = (1.0 - has_low) * planes[i][WIDE : WIDE + 1]
        last = (1.0 - has_high) * planes[i][WIDE + 1 : WIDE + 2]
        alone = jnp.where(row == RING, first, jnp.where(row == RING + ROWS - 1, last, 0.0))
        planes[i] = planes[i][0:WIDE] * in_grid + alone
    store_faces(planes, near, w_ref, wlo, whi)


def second_schwarz_kernel(near, inv_den, tables, y, zlo, zhi, w_ref, wlo, whi):
    planes = [y[i] for i in range(8)] + [zlo[0], zlo[1], zhi[0], zhi[1]]
    planes = solve_elements(planes, inv_den, tables, 1)
    row = lax.broadcasted_iota(jnp.int32, (ROWS, LANES), 0)
    _, has_low, has_high = ring_rows(near)
    in_grid = jnp.where(row == 0, has_low, jnp.where(row == ROWS - 1, has_high, 1.0))
    for i in range(8):
        first = (1.0 - has_low) * planes[i][ROWS : ROWS + 1]
        last = (1.0 - has_high) * planes[i][ROWS + 1 : ROWS + 2]
        alone = jnp.where(row == 0, first, jnp.where(row == ROWS - 1, last, 0.0))
        planes[i] = planes[i][0:ROWS] * in_grid + alone
    store_faces(planes, near, w_ref, wlo, whi)


def galerkin_kernel(near, packed, stat_in, flux, w, zlo, zhi, zl_ref, y_ref, stat):
    local = add_planes(w, zlo[...], zhi[...])
    zl_ref[...] = local
    applied = local_operator(local, flux[...], packed)
    y_ref[...] = applied
    applied = applied[:, RING : RING + ROWS]
    inner = near[0] * applied[0] + near[1] * applied[7]
    for i in range(1, 7):
        inner = inner + applied[i]
    edge = edge_rows(ROWS, near[2], near[3])
    entries = [0.0, 0.0]
    for plane in ((1.0 - near[0]) * applied[0], inner, (1.0 - near[1]) * applied[7]):
        entries += [
            (1.0 - near[2]) * jnp.sum(plane[0:1]),
            jnp.sum(edge * plane),
            (1.0 - near[3]) * jnp.sum(plane[ROWS - 1 : ROWS]),
        ]
    stat[...] = jnp.broadcast_to(stat_in[...] + lane_row(entries), stat.shape)


def column_kernel(gathered, out_ref):
    values = gathered[...]
    sub = lax.broadcasted_iota(jnp.int32, (8, LANES), 0)
    lane = lax.broadcasted_iota(jnp.int32, (8, LANES), 1)
    after = jnp.where(sub < 7, pltpu.roll(values, 7, 0), 0.0)
    before = jnp.where(sub > 0, pltpu.roll(values, 1, 0), 0.0)
    first = lax.broadcasted_iota(jnp.int32, (8, 1), 0) == 0
    last = lax.broadcasted_iota(jnp.int32, (8, 1), 0) == 7

    def column(array, index):
        return array[:, index : index + 1]

    def slopes(array, pair):
        whole, low, high = (column(array, 11 + 3 * pair + k) for k in range(3))
        return whole - low - high, low, high

    merged = [column(values, 0), column(values, 1)]
    for b in range(3):
        merged.append(column(values, 5 + b) + column(after, 2 + b) + column(before, 8 + b))
    merged += [own + other for own, other in zip(slopes(values, 0), slopes(before, 2), strict=True)]
    merged += list(slopes(values, 1))
    inside, interface = [], []
    for side in range(2):
        whole, low, high = (column(values, 20 + 3 * side + k) for k in range(3))
        ends = jnp.where(first, low, 0.0) + jnp.where(last, high, 0.0)
        inside.append(whole - low - high + ends)
        interface.append(jnp.where(first, 0.0, low) + column(before, 22 + 3 * side))
    rows = jnp.zeros((8, LANES), F32)
    for index, value in enumerate(merged + inside + interface):
        rows = jnp.where(lane == index, value, rows)
    total = rows[0:1]
    for i in range(1, 8):
        total = total + pltpu.roll(rows[i : i + 1], 16 * i, 1)
    out_ref[...] = jnp.broadcast_to(total, out_ref.shape)


def invert(blocks, sub):
    for k in range(8):
        pivot = 1.0 / blocks[k][k : k + 1]
        scaled = jnp.where(sub == k, pivot, blocks[k] * pivot)
        rows = []
        for r in range(8):
            if r == k:
                rows.append(scaled)
            else:
                rest = jnp.where(sub == k, 0.0, blocks[r])
                rows.append(rest - blocks[r][k : k + 1] * scaled)
        blocks = rows
    return blocks


def multiply(left, right):
    rows = []
    for r in range(8):
        total = left[r][0:1] * right[0]
        for k in range(1, 8):
            total = total + left[r][k : k + 1] * right[k]
        rows.append(total)
    return rows


def matvec(terms, sub):
    result = jnp.zeros_like(terms[0][1])
    for r in range(8):
        product = terms[0][0][r] * terms[0][1]
        for blocks, column in terms[1:]:
            product = product + blocks[r] * column
        result = jnp.where(sub == r, jnp.sum(product, axis=0, keepdims=True), result)
    return result


def coarse_operator(c, count, sums_z, couplings_z, inside_y, interface_y):
    sub = lax.broadcasted_iota(jnp.int32, c.shape, 0)
    lane = lax.broadcasted_iota(jnp.int32, c.shape, 1)
    has_low = lane > 0
    has_high = lane < count - 1

    def after(array):
        return jnp.where(sub < 7, pltpu.roll(array, 7, 0), 0.0)

    def before(array):
        return jnp.where(sub > 0, pltpu.roll(array, 1, 0), 0.0)

    def right(array):
        return jnp.where(has_high, pltpu.roll(array, LANES - 1, 1), 0.0)

    def left(array):
        return jnp.where(has_low, pltpu.roll(array, 1, 1), 0.0)

    on_low = jnp.where(has_low, 0.5 * (c + left(c)), c)
    on_high = jnp.where(has_high, 0.5 * (c + right(c)), c)
    tested = []
    for place, value in enumerate((c, on_low, on_high)):
        slope = jnp.where(sub > 0, 0.5 * (value - before(value)), 0.0)
        coupling = couplings_z[place]
        force = sums_z[place] * slope - coupling * after(slope) - before(coupling * slope)
        force = jnp.where(sub > 0, force, 0.0)
        tested.append(0.5 * (force - after(force)))
    result = tested[0] + jnp.where(has_low, 0.5, 1.0) * tested[1] + jnp.where(has_high, 0.5, 1.0) * tested[2]
    result = result + 0.5 * right(tested[1]) + 0.5 * left(tested[2])

    interface = jnp.where(sub > 0, 0.5 * (c + before(c)), 0.0)
    for side, (move, there) in enumerate(((left, has_low), (right, has_high))):
        force = inside_y[side] * jnp.where(there, 0.5 * (move(c) - c), 0.0)
        face = interface_y[side] * jnp.where(there, 0.5 * (move(interface) - interface), 0.0)
        force = force + 0.5 * (face + after(face))
        back = right if side == 0 else left
        result = result + 0.5 * (back(force) - force)

    end = float(WEIGHT[0])
    mass = (2.0 - 2.0 * end) * c + end * (interface + after(interface))
    mass = mass + jnp.where((sub == 0) | (sub == 7), end * c, 0.0)
    beside = jnp.where(has_low, 0.5 * (mass + left(mass)), 0.0)
    scaled = (2.0 * EY - 2.0 * end) * mass + end * (beside + right(beside))
    scaled = scaled + jnp.where(has_low, 0.0, end * mass) + jnp.where(has_high, 0.0, end * mass)
    return result + HELM_COEF / 8.0 * float(np.sum(WX)) * scaled


def coarse_kernel(count, near, gathered, out_ref, wide, turned):
    lanes = LANES
    sub = lax.broadcasted_iota(jnp.int32, (8, lanes), 0)
    lane = lax.broadcasted_iota(jnp.int32, (8, lanes), 1)
    wide[...] = jnp.zeros((LANES, LANES), F32)
    wide[0:count] = gathered[...]
    turned[...] = wide[...].T

    def value(index):
        return turned[pl.ds(index, 8, stride=16), :]

    def move(array, dz, dy):
        if dz:
            array = pltpu.roll(array, (-dz) % 8, 0)
        if dy:
            array = pltpu.roll(array, (-dy) % lanes, 1)
        return array

    kbar = jnp.where(lane < count, value(0), 1.0)
    above = move(kbar, 1, 0)
    link_z = jnp.where(sub < 7, 2.0 * kbar * above / (kbar + above) * (EY * EX / EZ), 0.0)
    link_z = jnp.where(lane < count, link_z, 0.0)
    beside = move(kbar, 0, 1)
    link_y = 2.0 * kbar * beside / (kbar + beside) * (EZ * EX / EY)
    link_y = jnp.where(lane < count - 1, link_y, 0.0)
    back_z = move(link_z, -1, 0)
    back_y = move(link_y, 0, -1)
    diagonal = HELM_COEF * EZ * EY * EX + link_z + back_z + link_y + back_y
    half = lanes // 2
    low_half = lane < half

    def twice(array):
        return jnp.where(low_half, array, pltpu.roll(array, half, 1))

    def swap(array):
        return pltpu.roll(array, half, 1)

    def beside_rows(rows, distance):
        return [
            jnp.where(low_half, pltpu.roll(row, distance, 1), pltpu.roll(row, lanes - distance, 1))
            for row in rows
        ]

    diagonal, link_z, back_z = twice(diagonal), twice(link_z), twice(back_z)
    link = jnp.where(low_half, back_y, swap(link_y))
    blocks, sides = [], []
    for r in range(8):
        row = jnp.where(sub == r, diagonal, 0.0)
        row = jnp.where(sub == r + 1, -back_z, row)
        row = jnp.where(sub == r - 1, -link_z, row)
        blocks.append(row)
        sides.append(jnp.where(sub == r, -link, 0.0))
    levels = []
    step = 1
    while step < count:
        factors = multiply(sides, beside_rows(invert(blocks, sub), step))
        levels.append((step, factors))
        terms = multiply(factors, beside_rows([swap(row) for row in sides], step))
        blocks = [blocks[r] - terms[r] - swap(terms[r]) for r in range(8)]
        if 2 * step < count:
            sides = [-row for row in multiply(factors, beside_rows(sides, step))]
        step *= 2
    inverse = invert(blocks, sub)

    def solve(column):
        column = twice(column)
        for distance, factors in levels:
            pulled = matvec([(factors, beside_rows([column], distance)[0])], sub)
            column = column - pulled - swap(pulled)
        solved = matvec([(inverse, column)], sub)
        return jnp.where(lane < count, solved, 0.0)

    offsets = [(a - 1, b - 1) for a in range(3) for b in range(3)]
    first = solve(value(1))
    near_first = [move(first, dz, dy) for dz, dy in offsets]
    totals = coarse_operator(
        first,
        count,
        [value(5 + k) for k in range(3)],
        [value(8 + k) for k in range(3)],
        [value(11), value(12)],
        [value(13), value(14)],
    )
    totals = totals + value(3)
    totals = totals + jnp.where(lane < count - 1, move(value(2), 0, 1), 0.0)
    totals = totals + jnp.where(lane > 0, move(value(4), 0, -1), 0.0)
    totals = jnp.where(lane < count, totals, 0.0)
    second = solve(totals)
    near_second = [move(second, dz, dy) for dz, dy in offsets]
    mine = (sub.astype(F32) == near[4]) & (lane.astype(F32) == near[5])
    for d in range(9):
        out_ref[d : d + 1] = jnp.full((1, lanes), jnp.sum(jnp.where(mine, near_first[d], 0.0)))
        out_ref[16 + d : 17 + d] = jnp.full(
            (1, lanes), jnp.sum(jnp.where(mine, near_second[d], 0.0))
        )


def coarse_columns(near, coarse, start):
    row, has_low, has_high = ring_rows(near)
    below = jnp.where(row < RING - 1, 1.0, jnp.where(row <= RING, 0.5, 0.0)) * has_low
    above = jnp.where(row > RING + ROWS, 1.0, jnp.where(row >= RING + ROWS - 1, 0.5, 0.0)) * has_high
    edge = jnp.where((row > RING) & (row < RING + ROWS - 1), 1.0, 0.0)
    edge = jnp.where(row == RING, near[2], jnp.where(row == RING + ROWS - 1, near[3], edge))
    edge = jnp.where(row == RING - 1, 0.5 * has_low, edge)
    edge = jnp.where(row == RING + ROWS, 0.5 * has_high, edge)
    columns = []
    for a in range(3):
        at = start + 3 * a
        columns.append(
            below * coarse[at : at + 1] + edge * coarse[at + 1 : at + 2] + above * coarse[at + 2 : at + 3]
        )
    first = (1.0 - near[0]) * (columns[0] - columns[1])
    last = (1.0 - near[1]) * (columns[2] - columns[1])
    return columns[1], first, last


def add_coarse(local, columns):
    inside, first, last = columns
    planes = [local[i] + inside for i in range(8)]
    planes[0] = planes[0] + first
    planes[7] = planes[7] + last
    return stack(planes)


def coarse_applied(columns, flux, packed):
    inside, first, last = columns
    slopes = [
        flux[i] * (float(DERIV[i, 0]) * first + float(DERIV[i, 7]) * last) for i in range(8)
    ]
    fz = along_z(slopes, DERIV.T)
    three = stack([inside + first, inside, inside + last])
    gy = along_y(three, packed, 0)
    fy = along_y(
        stack([flux[i] * gy[0 if i == 0 else 2 if i == 7 else 1] for i in range(8)]), packed, 1
    )
    plane_w = packed[0:WIDE]
    planes = []
    for i in range(8):
        plane = three[0 if i == 0 else 2 if i == 7 else 1]
        planes.append(fz[i] + fy[i] + (HELM_COEF * 0.125 * float(WEIGHT[i])) * (plane_w * plane))
    return stack(planes)


def apply_kernel(near, packed, coarse, flux, b, zl, yl, z_ref, y_ref, ylo, yhi, stat):
    columns = coarse_columns(near, coarse, 0)
    field = add_coarse(zl[...], columns)[:, RING : RING + ROWS]
    z_ref[...] = field
    applied = yl[...] + coarse_applied(columns, flux[...], packed)
    y_ref[...] = applied
    ylo[...] = applied[0:2]
    yhi[...] = applied[6:8]
    own = applied[:, RING : RING + ROWS]
    stat[...] = lane_row([jnp.sum(b[...] * field), jnp.sum(field * own)])


def second_kernel(near, packed, coarse, flux, b, y, w, zlo, zhi, stat_in, q_ref, stat):
    local = add_planes(w, zlo[...], zhi[...])
    columns = [column[RING : RING + ROWS] for column in coarse_columns(near, coarse, 16)]
    field = add_coarse(local, columns)
    q_ref[...] = field
    applied = local_operator(field, flux[:, RING : RING + ROWS], packed)
    own = y[:, RING : RING + ROWS]
    sums = [0.0, 0.0, jnp.sum(b[...] * field), jnp.sum(own * field), jnp.sum(field * applied)]
    stat[...] = jnp.broadcast_to(stat_in[...] + lane_row(sums), stat.shape)


def combine_kernel(sums, z, q, p_ref):
    total = jnp.sum(sums[...], axis=0, keepdims=True)
    rz, pap, rq, aq, qhq = (total[:, k : k + 1] for k in range(5))
    step = rz / pap
    rz_next = step * (step * aq - rq)
    beta = rz_next / rz
    grown = 1.0 + beta
    curved = grown * grown * pap - 2.0 * step * grown * aq + step * step * qhq
    step_next = rz_next / curved
    on_z = step + step_next * grown
    on_q = step_next * step
    p_ref[...] = on_z.reshape(1, 1, 1) * z[...] - on_q.reshape(1, 1, 1) * q[...]


def run(kernel, outs, smem, args, scratch=(), flops=1000000, place=VMEM, limit=LIMIT):
    nbytes = sum(4 * int(np.prod(out)) for out in outs) * 2
    return pl.pallas_call(
        kernel,
        out_shape=[jax.ShapeDtypeStruct(out, F32) for out in outs],
        in_specs=[pl.BlockSpec(memory_space=SMEM) for _ in smem]
        + [pl.BlockSpec(memory_space=place) for _ in args],
        out_specs=[pl.BlockSpec(memory_space=VMEM) for _ in outs],
        scratch_shapes=list(scratch),
        compiler_params=pltpu.CompilerParams(vmem_limit_bytes=limit),
        cost_estimate=pl.CostEstimate(flops=flops, bytes_accessed=nbytes, transcendentals=0),
    )(*smem, *args)


def shift(axis, low_face, high_face):
    count = lax.axis_size(axis)
    forward = [(i, i + 1) for i in range(count - 1)]
    backward = [(target, source) for source, target in forward]
    return lax.ppermute(high_face, axis, forward), lax.ppermute(low_face, axis, backward)


def body(level_set, velocity, source, wick_solid):
    block = level_set.shape
    count_gx = lax.axis_size("gx")
    count_gy = lax.axis_size("gy")
    index_gx = lax.axis_index("gx")
    index_gy = lax.axis_index("gy")

    def ends(index, count):
        return [jnp.where(index > 0, 0.5, 1.0), jnp.where(index < count - 1, 0.5, 1.0)]

    place = [index_gx.astype(F32), index_gy.astype(F32)]
    near = jnp.stack(ends(index_gx, count_gx) + ends(index_gy, count_gy) + place).astype(F32)
    packed = jnp.asarray(PACKED)
    tables = jnp.asarray(TABLES)
    face = (ROWS, LANES)
    wide_block = (8, WIDE, LANES)
    wide_face = (WIDE, LANES)
    rim = (12, TILE, LANES)

    b, l, zlo, zhi, solid = run(
        advect_kernel,
        [block, block, (3, *face), (3, *face), (8, LANES)],
        [],
        [
            pltpu.with_memory_space_constraint(array, pltpu.HBM)
            for array in (level_set, velocity, source, packed, wick_solid.reshape(EY, EX))
        ],
        [VMEM(block, F32), VMEM((3, *block), F32), VMEM(block, F32), VMEM(PACKED.shape, F32)]
        + [VMEM((EY, EX), jnp.int32), pltpu.SemaphoreType.DMA((5,))],
        place=pltpu.HBM,
    )
    zlo, zhi = shift("gx", zlo, zhi)
    ylo, yhi = run(rim_kernel, [rim, rim], [], [solid, b, l, zlo, zhi])
    ylo, yhi = shift("gy", ylo, yhi)
    w, wlo, whi = run(
        first_schwarz_kernel,
        [wide_block, wide_face, wide_face],
        [near],
        [jnp.asarray(DEN_A), tables, b, zlo, zhi, ylo, yhi],
    )
    wlo, whi = shift("gx", wlo, whi)
    level_new, flux, stat = run(
        level_kernel,
        [block, wide_block, (1, LANES)],
        [near],
        [solid, packed, b, l, zlo, zhi, ylo, yhi],
        flops=20000000,
    )
    zl, yl, stat = run(
        galerkin_kernel,
        [wide_block, wide_block, (count_gx, LANES)],
        [near],
        [packed, stat, flux, w, wlo, whi],
    )
    gathered = lax.all_to_all(stat, "gx", 0, 0, tiled=True)
    (column,) = run(column_kernel, [(count_gy, LANES)], [], [gathered])
    gathered = lax.all_to_all(column, "gy", 0, 0, tiled=True)
    (coarse,) = run(
        functools.partial(coarse_kernel, count_gy),
        [(32, LANES)],
        [near],
        [gathered],
        [VMEM((LANES, LANES), F32), VMEM((LANES, LANES), F32)],
    )
    z, y, zlo, zhi, sums = run(
        apply_kernel,
        [block, wide_block, (2, *wide_face), (2, *wide_face), (1, LANES)],
        [near],
        [packed, coarse, flux, b, zl, yl],
    )
    zlo, zhi = shift("gx", zlo, zhi)
    w, wlo, whi = run(
        second_schwarz_kernel, [block, face, face], [near], [jnp.asarray(DEN_B), tables, y, zlo, zhi]
    )
    zlo, zhi = shift("gx", wlo, whi)
    q, sums = run(
        second_kernel,
        [block, (count_gx, LANES)],
        [near],
        [packed, coarse, flux, b, y, w, zlo, zhi, sums],
    )
    tile = lax.all_to_all(sums, "gx", 0, 0, tiled=True)
    wide = jnp.broadcast_to(jnp.sum(tile, axis=0, keepdims=True), (count_gy, LANES))
    wide = lax.all_to_all(wide, "gy", 0, 0, tiled=True)
    (pressure,) = run(combine_kernel, [block], [], [wide, z, q])
    return (level_new, pressure)


def solution(mesh):
    placed = (
        P("gx", "gy", None),
        P(None, "gx", "gy", None),
        P("gx", "gy", None),
        P("gx", "gy", None),
    )
    return jax.shard_map(
        body,
        mesh=mesh,
        in_specs=placed,
        out_specs=(P("gx", "gy", None), P("gx", "gy", None)),
        check_vma=False,
    )
```

```python
import functools

import jax
import jax.numpy as jnp
import numpy as np
from jax import lax
from jax.experimental import pallas as pl
from jax.experimental.pallas import tpu as pltpu
from jax.sharding import PartitionSpec as P

EZ = 1
EY = 4
EX = 16
ROWS = 8 * EY
LANES = 8 * EX

TIME_STEP = 0.02
HELM_COEF = 0.25
LEVEL_WIDTH = 0.25
GAS_RATIO = 10.0
SOLID_FACTOR = 0.25
SCHWARZ_SCALE = 0.5
SCHWARZ_SHIFT = 0.05

F32 = jnp.float32
BF16 = jnp.bfloat16
VMEM = pltpu.VMEM
SMEM = pltpu.SMEM
LIMIT = 24 * 1024 * 1024


def gll_tables():
    gll_nodes = np.array(
        [
            -1.0,
            -0.8717401485096066,
            -0.5917001814331423,
            -0.2092992179024789,
            0.2092992179024789,
            0.5917001814331423,
            0.8717401485096066,
            1.0,
        ]
    )
    weight_np = np.array(
        [
            1.0 / 28.0,
            0.21070422714350603,
            0.3411226924835044,
            0.4124587946587038,
            0.4124587946587038,
            0.3411226924835044,
            0.21070422714350603,
            1.0 / 28.0,
        ]
    )
    bary_weights = np.array(
        [1.0 / np.prod([gll_nodes[i] - gll_nodes[j] for j in range(8) if j != i]) for i in range(8)]
    )
    derivative = np.zeros((8, 8))
    for i in range(8):
        for j in range(8):
            if i != j:
                derivative[i, j] = bary_weights[j] / bary_weights[i] / (gll_nodes[i] - gll_nodes[j])
        derivative[i, i] = -np.sum(derivative[i])
    return (weight_np, derivative)


def sine_tables():
    indices = np.arange(10) + 1.0
    sine_basis = np.sqrt(2.0 / 11.0) * np.sin(np.pi * np.outer(indices, indices) / 11.0)
    eigen_vals = 2.0 - 2.0 * np.cos(np.pi * indices / 11.0)
    return (sine_basis, eigen_vals)


WEIGHT, DERIV = gll_tables()
SINE, EIGEN = sine_tables()


def split_const(matrix):
    single = matrix.astype(np.float32)
    high = single.astype(jnp.bfloat16)
    low = (single - high.astype(np.float32)).astype(jnp.bfloat16)
    return high, low


def line_maps(count):
    length = 8 * count
    total = length + 4

    def column(position):
        if 0 <= position < length:
            return position
        return {-2: length, -1: length + 1, length: length + 2, length + 1: length + 3}[position]

    assembled = {}
    for position in range(-2, length + 2):
        row = np.zeros(total)
        row[column(position)] = 1.0
        if 0 <= position < length:
            if position % 8 == 0:
                row[column(position - 1)] += 1.0
            if position % 8 == 7:
                row[column(position + 1)] += 1.0
        assembled[position] = row
    forward = np.zeros((10 * count, total))
    for element in range(count):
        places = [8 * element - 2] + list(range(8 * element, 8 * element + 8)) + [8 * element + 9]
        forward[10 * element : 10 * element + 10] = SINE @ np.stack([assembled[p] for p in places])
    backward = np.zeros((length, 10 * count))
    for element in range(count):
        backward[8 * element : 8 * element + 8, 10 * element : 10 * element + 10] = SINE[1:9]
    for element in range(count - 1):
        first, second = 8 * element + 7, 8 * element + 8
        mean = 0.5 * (backward[first] + backward[second])
        backward[first] = mean
        backward[second] = mean
    return forward, backward


RING = 16
WIDE = ROWS + 2 * RING
REACH = 26
TILE = 48
TILE_B = 32


def ring_maps(reach, depth, inside):
    count = EY + 2 * depth
    forward, _ = line_maps(count)
    length = 8 * count
    columns = np.zeros((10 * count, len(inside)))
    for at, position in enumerate(inside):
        place = None if position is None else position + 8 * depth
        if place is None or place < -2 or place > length + 1:
            continue
        source = place if 0 <= place < length else {-2: 0, -1: 1}.get(place, place - length + 2) + length
        columns[:, at] = forward[:, source]
    _, backward = line_maps(count)
    own = 8 * depth
    rows = np.concatenate(
        [
            backward[own - reach : own + ROWS + reach],
            np.zeros((8, 10 * count)),
        ]
    )
    rows[ROWS + 2 * reach, 10 * depth : 10 * depth + 10] = SINE[1]
    rows[ROWS + 2 * reach + 1, 10 * (depth + EY - 1) : 10 * (depth + EY)] = SINE[8]
    return columns, rows


FZ, BZ = line_maps(1)
TILES = list(range(-REACH, 0)) + [None] * (TILE_B - REACH) + list(range(ROWS))
TILES += list(range(ROWS, ROWS + REACH)) + [None] * (TILE_B - REACH)
FY_A, BY_A = ring_maps(RING, 3, TILES)
FY_B, BY_B = ring_maps(0, 1, list(range(-RING, ROWS + RING)))
STEP_A = 112
STEP_B = 64


def padded(forward, backward, step):
    forward = np.pad(forward, ((0, step - forward.shape[0]), (0, 0)))
    return forward, np.pad(backward, ((0, 0), (0, step - backward.shape[1])))


FY_A, BY_A = padded(FY_A, BY_A, STEP_A)
FY_B, BY_B = padded(FY_B, BY_B, STEP_B)
FX, BX = line_maps(EX)
FX = FX[:, :LANES]


FX_H, FX_L = split_const(FX.T.copy())
BX_H, BX_L = split_const(BX.T.copy())


def wide_const(table):
    high, low = split_const(table)
    return np.concatenate([high, high, low], axis=1)


def pack_tables(tables):
    places, pieces, at = [], [], 0
    for table in tables:
        rows = -(-table.shape[0] // 16) * 16
        extra = ((0, rows - table.shape[0]), (0, 384 - table.shape[1]))
        pieces.append(np.pad(table.astype(np.float32), extra))
        places.append((at, rows, table.shape[1]))
        at += rows
    return np.concatenate(pieces).astype(jnp.bfloat16), places


TABLES, PLACES = pack_tables(
    [
        np.concatenate([FX_H, FX_H], axis=0),
        FX_L,
        BX_H,
        BX_L,
        wide_const(FY_A),
        wide_const(BY_A),
        wide_const(FY_B),
        wide_const(BY_B),
    ]
)


def roll_table():
    table = np.zeros((2, 8, 8, LANES))
    for kind, matrix in enumerate((DERIV, DERIV.T)):
        for k in range(8):
            for i in range(8):
                table[kind, k, i, :] = matrix[i, (i + k) % 8]
    return table.reshape(2 * 64, LANES)


WY = np.tile(WEIGHT, WIDE // 8)
WX = np.tile(WEIGHT, EX)


def inner_count(count):
    mult = np.ones(8 * count)
    position = np.arange(8 * count)
    mult[(position % 8 == 0) & (position > 0)] += 1.0
    mult[(position % 8 == 7) & (position < 8 * count - 1)] += 1.0
    return mult


END_MASS = np.where(np.arange(WIDE) % 8 % 7 == 0, 2.0, 1.0)
INV_MASS = (8.0 / (WY * END_MASS)[:, None] / (WX * inner_count(EX))[None, :]).astype(np.float32)

AT_ROLLS = WIDE
AT_DX = AT_ROLLS + 128
AT_DXT = AT_DX + LANES
AT_SQUARE = AT_DXT + LANES
AT_MASS = AT_SQUARE + 16
AT_SPREAD = AT_MASS + WIDE
AT_EIGEN_Y = AT_SPREAD + EX
AT_EIGEN_X = AT_EIGEN_Y + STEP_A
LAM_Y = np.resize(EIGEN, STEP_A)
LAM_X = np.resize(EIGEN, 8 * LANES).reshape(8, LANES)
PACKED = np.concatenate(
    [
        WY[:, None] * WX[None, :],
        roll_table(),
        np.kron(np.eye(EX), DERIV.T),
        np.kron(np.eye(EX), DERIV),
        np.repeat(DERIV[:, :1] ** 2, LANES, axis=1),
        np.repeat(DERIV[:, 7:] ** 2, LANES, axis=1),
        INV_MASS,
        np.kron(np.eye(EX), np.ones((1, 8))),
        np.repeat(LAM_Y[:, None], LANES, axis=1),
        LAM_X,
    ]
).astype(np.float32)


def parts(values):
    high = values.astype(BF16)
    low = (values - high.astype(F32)).astype(BF16)
    return high, low


def dot(left, right):
    return jnp.dot(left, right, preferred_element_type=F32)


def left_pairs(table, planes):
    results = []
    for i in range(0, len(planes), 2):
        high, low = parts(jnp.concatenate([planes[i], planes[i + 1]], axis=1))
        both = dot(table, jnp.concatenate([high, low, high], axis=0))
        results += [both[:, 0:LANES], both[:, LANES : 2 * LANES]]
    return results


def along_z(values, matrix):
    rows = []
    for i in range(matrix.shape[0]):
        total = None
        for j in range(matrix.shape[1]):
            if matrix[i, j] == 0.0:
                continue
            term = float(matrix[i, j]) * values[j]
            total = term if total is None else total + term
        rows.append(total)
    return rows


def along_y(values, packed, kind):
    count, rows = values.shape[:2]
    grouped = values.reshape(count * rows // 8, 8, LANES)
    start = AT_ROLLS + 64 * kind
    total = packed[start : start + 8][None] * grouped
    for k in range(1, 8):
        total = total + packed[start + 8 * k : start + 8 * k + 8][None] * pltpu.roll(grouped, 8 - k, 1)
    return total.reshape(count, rows, LANES)


def along_x(values, packed, kind):
    start = AT_DXT if kind else AT_DX
    high, low = parts(packed[start : start + LANES])
    first, rest = parts(values.reshape(8 * values.shape[1], LANES))
    total = dot(
        jnp.concatenate([first, rest], axis=1), jnp.concatenate([high, high], axis=0)
    ) + dot(first, low)
    return total.reshape(values.shape)


def stack(planes):
    return jnp.concatenate([plane[None] for plane in planes], axis=0)


def edge_rows(rows, low, high):
    position = lax.broadcasted_iota(jnp.int32, (rows, LANES), 0)
    return jnp.where(position == 0, low, jnp.where(position == rows - 1, high, 1.0))


def local_operator(values, flux, packed):
    plane_w = packed[0 : values.shape[1]]
    gz = along_z([values[i] for i in range(8)], DERIV)
    fz = along_z([flux[i] * gz[i] for i in range(8)], DERIV.T)
    total = along_y(flux * along_y(values, packed, 0), packed, 1)
    total = total + along_x(flux * along_x(values, packed, 0), packed, 1)
    planes = [
        total[i] + fz[i] + (HELM_COEF * 0.125 * float(WEIGHT[i])) * (plane_w * values[i])
        for i in range(8)
    ]
    return stack(planes)


def add_planes(own, low_z, high_z):
    planes = [own[i] for i in range(8)]
    planes[0] = planes[0] + low_z
    planes[7] = planes[7] + high_z
    return stack(planes)


def solve_elements(planes, packed, tables, kind):
    def table(index):
        at, rows, width = PLACES[index]
        return tables[at : at + rows, 0:width]

    fxhh, fxl, bxh, bxl = (table(index) for index in range(4))
    spectral = left_pairs(table(4 + 2 * kind), along_z(planes, FZ))
    high, low = parts(jnp.concatenate(spectral, axis=0))
    wide = dot(jnp.concatenate([high, low], axis=1), fxhh) + dot(high, fxl)
    step = PLACES[4 + 2 * kind][1]
    column = packed[AT_EIGEN_Y : AT_EIGEN_Y + step]
    rest = 10 * EX - LANES
    lam = jnp.concatenate(
        [
            column + packed[AT_EIGEN_X : AT_EIGEN_X + 1],
            column[:, 0:rest] + packed[AT_EIGEN_X + 1 : AT_EIGEN_X + 2, 0:rest],
        ],
        axis=1,
    )
    scaled = [
        wide[step * i : step * (i + 1)]
        / (SCHWARZ_SCALE * lam + float(SCHWARZ_SCALE * EIGEN[i] + SCHWARZ_SHIFT))
        for i in range(10)
    ]
    high, low = parts(jnp.concatenate(scaled, axis=0))
    back = dot(high, bxh) + dot(low, bxh) + dot(high, bxl)
    back = left_pairs(table(5 + 2 * kind), [back[step * i : step * (i + 1)] for i in range(10)])
    return along_z(back, BZ)


def store_faces(planes, near, out_ref, low_ref, high_ref):
    planes[0] = planes[0] * near[0]
    planes[7] = planes[7] * near[1]
    for i in range(8):
        out_ref[i] = planes[i]
    low_ref[...] = planes[0]
    high_ref[...] = planes[7]


def ring_rows(near):
    row = lax.broadcasted_iota(jnp.int32, (WIDE, LANES), 0)
    return row, 2.0 - 2.0 * near[2], 2.0 - 2.0 * near[3]


def partition_total(own, low_z, high_z, low_y, high_y, near):
    def planes(array):
        total = near[0] * array[0] + near[1] * array[7]
        for i in range(1, 7):
            total = total + array[i]
        return total

    total = planes(own) + 0.5 * (low_z[1] + high_z[0])
    below = planes(low_y) + 0.5 * (low_y[9] + low_y[10])
    above = planes(high_y) + 0.5 * (high_y[9] + high_y[10])
    faces = 0.5 * (below[REACH - 1 : REACH] + above[0:1])
    return jnp.sum(total * edge_rows(ROWS, near[2], near[3])) + jnp.sum(faces)


def lane_row(entries):
    lane = lax.broadcasted_iota(jnp.int32, (1, LANES), 1)
    row = jnp.zeros((1, LANES), F32)
    for index, value in enumerate(entries):
        row = jnp.where(lane == index, value, row)
    return row


def advect_kernel(
    lev_in, vel_in, src_in, packed_in, solid_in, b_ref, l_ref, zlo, zhi, solid_ref,
    lev, vel, src, packed, solid, sems,
):
    copies = [
        pltpu.make_async_copy(source, target, sems.at[index])
        for index, (source, target) in enumerate(
            (
                (vel_in, vel), (lev_in, lev), (packed_in, packed), (src_in, src), (solid_in, solid),
            )
        )
    ]
    for copy in copies:
        copy.start()
    for copy in copies:
        copy.wait()
    spread = packed[AT_SPREAD : AT_SPREAD + EX].astype(BF16)
    in_solid = dot(solid[...].astype(F32).astype(BF16), spread)
    solid_ref[...] = jnp.concatenate([in_solid, jnp.zeros((8 - EY, LANES), F32)], axis=0)
    level = lev[...]
    v0, v1, v2 = vel[0], vel[1], vel[2]
    gz = stack(along_z([level[i] for i in range(8)], DERIV))
    advect = v0 * gz + v1 * along_y(level, packed, 0) + v2 * along_x(level, packed, 0)
    moved = level - (2.0 * TIME_STEP) * advect
    diverge = stack(along_z([v0[i] for i in range(8)], DERIV))
    diverge = diverge + along_y(v1, packed, 0) + along_x(v2, packed, 0)
    force = src[...] - (2.0 * TIME_STEP) * diverge
    weights = packed[0:ROWS]
    for i in range(8):
        mass = (0.125 * float(WEIGHT[i])) * weights
        term = mass * force[i]
        moved_i = mass * moved[i]
        b_ref[i] = term
        l_ref[i] = moved_i
        if i < 2:
            zlo[i] = term
        if i == 0:
            zlo[2] = moved_i
        if i > 5:
            zhi[i - 6] = term
        if i == 7:
            zhi[2] = moved_i


def rim_kernel(solid, b, l, low_z, high_z, low_y, high_y):
    in_solid = solid[...]
    rest = TILE - REACH - RING - 1

    def rows(planes, at, level, far, extra=None):
        start = ROWS - REACH if far else 0
        pieces = [planes[at, start : start + REACH]]
        if level is None:
            pieces.append(jnp.zeros((RING + 1, LANES), F32))
        else:
            array, index = level
            start = ROWS - RING - 1 if far else 0
            pieces.append(array[index, start : start + RING + 1])
        if extra is None:
            pieces.append(jnp.zeros((rest, LANES), F32))
        else:
            pieces += [extra, jnp.zeros((rest - 2, LANES), F32)]
        return jnp.concatenate(pieces, axis=0)

    for far, out in ((False, low_y), (True, high_y)):
        extra = in_solid[EY - 2 : EY] if far else in_solid[0:2]
        for i in range(8):
            out[i] = rows(b, i, (l, i), far, extra if i == 0 else None)
        for i in range(2):
            out[8 + i] = rows(low_z, i, (low_z, 2) if i == 1 else None, far)
            out[10 + i] = rows(high_z, i, (high_z, 2) if i == 0 else None, far)


def level_kernel(
    near, solid, packed, b, l, zlo, zhi, ylo, yhi, level_ref, flux_ref, stat
):
    row, has_low, has_high = ring_rows(near)
    at = REACH

    def wide_rows(slot, own):
        return jnp.concatenate(
            [ylo[slot, at + 1 : at + 1 + RING], own, yhi[slot, at : at + RING]], axis=0
        )

    planes = []
    for i in range(8):
        plane = wide_rows(i, l[i])
        first = ylo[i, at : at + 1]
        last = yhi[i, at + RING : at + RING + 1]
        if i == 0:
            plane = plane + wide_rows(9, zlo[2])
            first = first + ylo[9, at : at + 1]
            last = last + yhi[9, at + RING : at + RING + 1]
        if i == 7:
            plane = plane + wide_rows(10, zhi[2])
            first = first + ylo[10, at : at + 1]
            last = last + yhi[10, at + RING : at + RING + 1]
        before = jnp.where(row == 0, first, pltpu.roll(plane, 1, 0))
        after = jnp.where(row == WIDE - 1, last, pltpu.roll(plane, WIDE - 1, 0))
        plane = plane + jnp.where(row % 8 == 0, before, jnp.where(row % 8 == 7, after, 0.0))
        planes.append(plane)
    own = stack(planes)
    lane = lax.broadcasted_iota(jnp.int32, (8, WIDE, LANES), 2)
    before = jnp.where((lane % 8 == 0) & (lane > 0), pltpu.roll(own, 1, 2), 0.0)
    after = jnp.where((lane % 8 == 7) & (lane < LANES - 1), pltpu.roll(own, LANES - 1, 2), 0.0)
    own = own + before + after
    ends = jnp.where(row == RING, 2.0 * near[2], jnp.where(row == RING + ROWS - 1, 2.0 * near[3], 1.0))
    inverse = packed[AT_MASS : AT_MASS + WIDE] * ends
    in_solid = solid[...]
    solids = [ylo[0, at + RING + 1 + k : at + RING + 2 + k] for k in range(2)]
    solids += [in_solid[e : e + 1] for e in range(EY)]
    solids += [yhi[0, at + RING + 1 + k : at + RING + 2 + k] for k in range(2)]
    open_part = jnp.concatenate(
        [jnp.broadcast_to(1.0 - (1.0 - SOLID_FACTOR) * rows, (8, LANES)) for rows in solids], axis=0
    )
    in_grid = jnp.where(row < RING, has_low, jnp.where(row >= RING + ROWS, has_high, 1.0))
    flux_w = packed[0:WIDE] * in_grid
    total = jnp.zeros((ROWS, LANES), F32)
    fluxes = []
    for i in range(8):
        scale = 1.0 / float(WEIGHT[i])
        plane = own[i] * (inverse * scale)
        if i == 0:
            plane = plane * near[0]
        if i == 7:
            plane = plane * near[1]
        level_ref[i] = plane[RING : RING + ROWS]
        liquid = jax.nn.sigmoid(plane * (1.0 / LEVEL_WIDTH))
        coef = (GAS_RATIO - (GAS_RATIO - 1.0) * liquid) * open_part
        total = total + coef[RING : RING + ROWS]
        flux = (0.5 * float(WEIGHT[i])) * (coef * flux_w)
        flux_ref[i] = flux
        fluxes.append(flux[RING : RING + ROWS])
    kbar = jnp.sum(total) * (1.0 / (8 * ROWS * LANES))
    entries = [kbar, partition_total(b, zlo, zhi, ylo, yhi, near)] + [0.0] * 9
    for first, second in ((0, 0), (0, 7), (7, 7)):
        slopes = along_z(fluxes, (DERIV[:, first] * DERIV[:, second])[None, :])[0]
        column = jnp.sum(slopes, axis=1, keepdims=True)
        entries += [jnp.sum(column, axis=0, keepdims=True), column[0:1], column[ROWS - 1 : ROWS]]
    inner = fluxes[0] + fluxes[1]
    for i in range(2, 8):
        inner = inner + fluxes[i]
    for at_row, start in ((0, 0), (ROWS - 8, 8)):
        square = packed[AT_SQUARE + start : AT_SQUARE + start + 8]
        entries += [
            jnp.sum(square * plane[at_row : at_row + 8]) for plane in (inner, fluxes[0], fluxes[7])
        ]
    stat[...] = lane_row(entries)


def first_schwarz_kernel(
    near, packed, tables, b, zlo, zhi, ylo, yhi, w_ref, wlo, whi
):
    own = [b[i] for i in range(8)] + [zlo[0], zlo[1], zhi[0], zhi[1]]
    planes = [
        jnp.concatenate([ylo[i, 0:TILE_B], own[i], yhi[i, 0:TILE_B]], axis=0) for i in range(12)
    ]
    planes = solve_elements(planes, packed, tables, 0)
    row, has_low, has_high = ring_rows(near)
    in_grid = jnp.where(row < RING, has_low, jnp.where(row >= RING + ROWS, has_high, 1.0))
    in_grid = jnp.where(row == RING, has_low, jnp.where(row == RING + ROWS - 1, has_high, in_grid))
    for i in range(8):
        first = (1.0 - has_low) * planes[i][WIDE : WIDE + 1]
        last = (1.0 - has_high) * planes[i][WIDE + 1 : WIDE + 2]
        alone = jnp.where(row == RING, first, jnp.where(row == RING + ROWS - 1, last, 0.0))
        planes[i] = planes[i][0:WIDE] * in_grid + alone
    store_faces(planes, near, w_ref, wlo, whi)


def second_schwarz_kernel(near, packed, tables, y, zlo, zhi, w_ref, wlo, whi):
    planes = [y[i] for i in range(8)] + [zlo[0], zlo[1], zhi[0], zhi[1]]
    planes = solve_elements(planes, packed, tables, 1)
    row = lax.broadcasted_iota(jnp.int32, (ROWS, LANES), 0)
    _, has_low, has_high = ring_rows(near)
    in_grid = jnp.where(row == 0, has_low, jnp.where(row == ROWS - 1, has_high, 1.0))
    for i in range(8):
        first = (1.0 - has_low) * planes[i][ROWS : ROWS + 1]
        last = (1.0 - has_high) * planes[i][ROWS + 1 : ROWS + 2]
        alone = jnp.where(row == 0, first, jnp.where(row == ROWS - 1, last, 0.0))
        planes[i] = planes[i][0:ROWS] * in_grid + alone
    store_faces(planes, near, w_ref, wlo, whi)


def galerkin_kernel(near, packed, stat_in, flux, w, zlo, zhi, zl_ref, y_ref, stat):
    local = add_planes(w, zlo[...], zhi[...])
    zl_ref[...] = local
    applied = local_operator(local, flux[...], packed)
    y_ref[...] = applied
    applied = applied[:, RING : RING + ROWS]
    inner = near[0] * applied[0] + near[1] * applied[7]
    for i in range(1, 7):
        inner = inner + applied[i]
    edge = edge_rows(ROWS, near[2], near[3])
    entries = [0.0, 0.0]
    for plane in ((1.0 - near[0]) * applied[0], inner, (1.0 - near[1]) * applied[7]):
        entries += [
            (1.0 - near[2]) * jnp.sum(plane[0:1]),
            jnp.sum(edge * plane),
            (1.0 - near[3]) * jnp.sum(plane[ROWS - 1 : ROWS]),
        ]
    stat[...] = jnp.broadcast_to(stat_in[...] + lane_row(entries), stat.shape)


def column_kernel(gathered, out_ref):
    values = gathered[...]
    sub = lax.broadcasted_iota(jnp.int32, (8, LANES), 0)
    lane = lax.broadcasted_iota(jnp.int32, (8, LANES), 1)
    after = jnp.where(sub < 7, pltpu.roll(values, 7, 0), 0.0)
    before = jnp.where(sub > 0, pltpu.roll(values, 1, 0), 0.0)
    first = lax.broadcasted_iota(jnp.int32, (8, 1), 0) == 0
    last = lax.broadcasted_iota(jnp.int32, (8, 1), 0) == 7

    def column(array, index):
        return array[:, index : index + 1]

    def slopes(array, pair):
        whole, low, high = (column(array, 11 + 3 * pair + k) for k in range(3))
        return whole - low - high, low, high

    merged = [column(values, 0), column(values, 1)]
    for b in range(3):
        merged.append(column(values, 5 + b) + column(after, 2 + b) + column(before, 8 + b))
    merged += [own + other for own, other in zip(slopes(values, 0), slopes(before, 2), strict=True)]
    merged += list(slopes(values, 1))
    inside, interface = [], []
    for side in range(2):
        whole, low, high = (column(values, 20 + 3 * side + k) for k in range(3))
        ends = jnp.where(first, low, 0.0) + jnp.where(last, high, 0.0)
        inside.append(whole - low - high + ends)
        interface.append(jnp.where(first, 0.0, low) + column(before, 22 + 3 * side))
    rows = jnp.zeros((8, LANES), F32)
    for index, value in enumerate(merged + inside + interface):
        rows = jnp.where(lane == index, value, rows)
    total = rows[0:1]
    for i in range(1, 8):
        total = total + pltpu.roll(rows[i : i + 1], 16 * i, 1)
    out_ref[...] = jnp.broadcast_to(total, out_ref.shape)


def invert(blocks, sub):
    for k in range(8):
        pivot = 1.0 / blocks[k][k : k + 1]
        scaled = jnp.where(sub == k, pivot, blocks[k] * pivot)
        rows = []
        for r in range(8):
            if r == k:
                rows.append(scaled)
            else:
                rest = jnp.where(sub == k, 0.0, blocks[r])
                rows.append(rest - blocks[r][k : k + 1] * scaled)
        blocks = rows
    return blocks


def multiply(left, right):
    rows = []
    for r in range(8):
        total = left[r][0:1] * right[0]
        for k in range(1, 8):
            total = total + left[r][k : k + 1] * right[k]
        rows.append(total)
    return rows


def matvec(terms, sub):
    result = jnp.zeros_like(terms[0][1])
    for r in range(8):
        product = terms[0][0][r] * terms[0][1]
        for blocks, column in terms[1:]:
            product = product + blocks[r] * column
        result = jnp.where(sub == r, jnp.sum(product, axis=0, keepdims=True), result)
    return result


def coarse_operator(c, count, sums_z, couplings_z, inside_y, interface_y):
    sub = lax.broadcasted_iota(jnp.int32, c.shape, 0)
    lane = lax.broadcasted_iota(jnp.int32, c.shape, 1)
    has_low = lane > 0
    has_high = lane < count - 1

    def after(array):
        return jnp.where(sub < 7, pltpu.roll(array, 7, 0), 0.0)

    def before(array):
        return jnp.where(sub > 0, pltpu.roll(array, 1, 0), 0.0)

    def right(array):
        return jnp.where(has_high, pltpu.roll(array, LANES - 1, 1), 0.0)

    def left(array):
        return jnp.where(has_low, pltpu.roll(array, 1, 1), 0.0)

    on_low = jnp.where(has_low, 0.5 * (c + left(c)), c)
    on_high = jnp.where(has_high, 0.5 * (c + right(c)), c)
    tested = []
    for place, value in enumerate((c, on_low, on_high)):
        slope = jnp.where(sub > 0, 0.5 * (value - before(value)), 0.0)
        coupling = couplings_z[place]
        force = sums_z[place] * slope - coupling * after(slope) - before(coupling * slope)
        force = jnp.where(sub > 0, force, 0.0)
        tested.append(0.5 * (force - after(force)))
    result = tested[0] + jnp.where(has_low, 0.5, 1.0) * tested[1] + jnp.where(has_high, 0.5, 1.0) * tested[2]
    result = result + 0.5 * right(tested[1]) + 0.5 * left(tested[2])

    interface = jnp.where(sub > 0, 0.5 * (c + before(c)), 0.0)
    for side, (move, there) in enumerate(((left, has_low), (right, has_high))):
        force = inside_y[side] * jnp.where(there, 0.5 * (move(c) - c), 0.0)
        face = interface_y[side] * jnp.where(there, 0.5 * (move(interface) - interface), 0.0)
        force = force + 0.5 * (face + after(face))
        back = right if side == 0 else left
        result = result + 0.5 * (back(force) - force)

    end = float(WEIGHT[0])
    mass = (2.0 - 2.0 * end) * c + end * (interface + after(interface))
    mass = mass + jnp.where((sub == 0) | (sub == 7), end * c, 0.0)
    beside = jnp.where(has_low, 0.5 * (mass + left(mass)), 0.0)
    scaled = (2.0 * EY - 2.0 * end) * mass + end * (beside + right(beside))
    scaled = scaled + jnp.where(has_low, 0.0, end * mass) + jnp.where(has_high, 0.0, end * mass)
    return result + HELM_COEF / 8.0 * float(np.sum(WX)) * scaled


def coarse_kernel(count, near, gathered, out_ref, wide, turned):
    lanes = LANES
    sub = lax.broadcasted_iota(jnp.int32, (8, lanes), 0)
    lane = lax.broadcasted_iota(jnp.int32, (8, lanes), 1)
    wide[...] = jnp.zeros((LANES, LANES), F32)
    wide[0:count] = gathered[...]
    turned[...] = wide[...].T

    def value(index):
        return turned[pl.ds(index, 8, stride=16), :]

    def move(array, dz, dy):
        if dz:
            array = pltpu.roll(array, (-dz) % 8, 0)
        if dy:
            array = pltpu.roll(array, (-dy) % lanes, 1)
        return array

    kbar = jnp.where(lane < count, value(0), 1.0)
    above = move(kbar, 1, 0)
    link_z = jnp.where(sub < 7, 2.0 * kbar * above / (kbar + above) * (EY * EX / EZ), 0.0)
    link_z = jnp.where(lane < count, link_z, 0.0)
    beside = move(kbar, 0, 1)
    link_y = 2.0 * kbar * beside / (kbar + beside) * (EZ * EX / EY)
    link_y = jnp.where(lane < count - 1, link_y, 0.0)
    back_z = move(link_z, -1, 0)
    back_y = move(link_y, 0, -1)
    diagonal = HELM_COEF * EZ * EY * EX + link_z + back_z + link_y + back_y
    blocks, lower, upper = [], [], []
    for r in range(8):
        row = jnp.where(sub == r, diagonal, 0.0)
        row = jnp.where(sub == r + 1, -back_z, row)
        row = jnp.where(sub == r - 1, -link_z, row)
        blocks.append(row)
        lower.append(jnp.where(sub == r, -back_y, 0.0))
        upper.append(jnp.where(sub == r, -link_y, 0.0))
    levels = []
    step = 1
    while step < count:
        inverse = invert(blocks, sub)
        down = multiply(lower, [move(row, 0, -step) for row in inverse])
        up = multiply(upper, [move(row, 0, step) for row in inverse])
        levels.append((step, down, up))
        before_u = multiply(down, [move(row, 0, -step) for row in upper])
        after_l = multiply(up, [move(row, 0, step) for row in lower])
        if 2 * step < count:
            new_lower = multiply(down, [move(row, 0, -step) for row in lower])
            new_upper = multiply(up, [move(row, 0, step) for row in upper])
            lower = [-row for row in new_lower]
            upper = [-row for row in new_upper]
        blocks = [blocks[r] - before_u[r] - after_l[r] for r in range(8)]
        step *= 2
    inverse = invert(blocks, sub)

    def solve(column):
        for distance, down, up in levels:
            pulled = matvec(
                [(down, move(column, 0, -distance)), (up, move(column, 0, distance))], sub
            )
            column = column - pulled
        return matvec([(inverse, column)], sub)

    offsets = [(a - 1, b - 1) for a in range(3) for b in range(3)]
    first = solve(value(1))
    near_first = [move(first, dz, dy) for dz, dy in offsets]
    totals = coarse_operator(
        first,
        count,
        [value(5 + k) for k in range(3)],
        [value(8 + k) for k in range(3)],
        [value(11), value(12)],
        [value(13), value(14)],
    )
    totals = totals + value(3)
    totals = totals + jnp.where(lane < count - 1, move(value(2), 0, 1), 0.0)
    totals = totals + jnp.where(lane > 0, move(value(4), 0, -1), 0.0)
    totals = jnp.where(lane < count, totals, 0.0)
    second = solve(totals)
    near_second = [move(second, dz, dy) for dz, dy in offsets]
    mine = (sub.astype(F32) == near[4]) & (lane.astype(F32) == near[5])
    for d in range(9):
        out_ref[d : d + 1] = jnp.full((1, lanes), jnp.sum(jnp.where(mine, near_first[d], 0.0)))
        out_ref[16 + d : 17 + d] = jnp.full(
            (1, lanes), jnp.sum(jnp.where(mine, near_second[d], 0.0))
        )


def coarse_columns(near, coarse, start):
    row, has_low, has_high = ring_rows(near)
    below = jnp.where(row < RING - 1, 1.0, jnp.where(row <= RING, 0.5, 0.0)) * has_low
    above = jnp.where(row > RING + ROWS, 1.0, jnp.where(row >= RING + ROWS - 1, 0.5, 0.0)) * has_high
    edge = jnp.where((row > RING) & (row < RING + ROWS - 1), 1.0, 0.0)
    edge = jnp.where(row == RING, near[2], jnp.where(row == RING + ROWS - 1, near[3], edge))
    edge = jnp.where(row == RING - 1, 0.5 * has_low, edge)
    edge = jnp.where(row == RING + ROWS, 0.5 * has_high, edge)
    columns = []
    for a in range(3):
        at = start + 3 * a
        columns.append(
            below * coarse[at : at + 1] + edge * coarse[at + 1 : at + 2] + above * coarse[at + 2 : at + 3]
        )
    first = (1.0 - near[0]) * (columns[0] - columns[1])
    last = (1.0 - near[1]) * (columns[2] - columns[1])
    return columns[1], first, last


def add_coarse(local, columns):
    inside, first, last = columns
    planes = [local[i] + inside for i in range(8)]
    planes[0] = planes[0] + first
    planes[7] = planes[7] + last
    return stack(planes)


def coarse_applied(columns, flux, packed):
    inside, first, last = columns
    slopes = [
        flux[i] * (float(DERIV[i, 0]) * first + float(DERIV[i, 7]) * last) for i in range(8)
    ]
    fz = along_z(slopes, DERIV.T)
    three = stack([inside + first, inside, inside + last])
    gy = along_y(three, packed, 0)
    fy = along_y(
        stack([flux[i] * gy[0 if i == 0 else 2 if i == 7 else 1] for i in range(8)]), packed, 1
    )
    plane_w = packed[0:WIDE]
    planes = []
    for i in range(8):
        plane = three[0 if i == 0 else 2 if i == 7 else 1]
        planes.append(fz[i] + fy[i] + (HELM_COEF * 0.125 * float(WEIGHT[i])) * (plane_w * plane))
    return stack(planes)


def apply_kernel(near, packed, coarse, flux, b, zl, yl, z_ref, y_ref, ylo, yhi, stat):
    columns = coarse_columns(near, coarse, 0)
    field = add_coarse(zl[...], columns)[:, RING : RING + ROWS]
    z_ref[...] = field
    applied = yl[...] + coarse_applied(columns, flux[...], packed)
    y_ref[...] = applied
    ylo[...] = applied[0:2]
    yhi[...] = applied[6:8]
    own = applied[:, RING : RING + ROWS]
    stat[...] = lane_row([jnp.sum(b[...] * field), jnp.sum(field * own)])


def second_kernel(near, packed, coarse, flux, b, y, w, zlo, zhi, stat_in, q_ref, stat):
    local = add_planes(w, zlo[...], zhi[...])
    columns = [column[RING : RING + ROWS] for column in coarse_columns(near, coarse, 16)]
    field = add_coarse(local, columns)
    q_ref[...] = field
    applied = local_operator(field, flux[:, RING : RING + ROWS], packed)
    own = y[:, RING : RING + ROWS]
    sums = [0.0, 0.0, jnp.sum(b[...] * field), jnp.sum(own * field), jnp.sum(field * applied)]
    stat[...] = jnp.broadcast_to(stat_in[...] + lane_row(sums), stat.shape)


def combine_kernel(sums, z, q, p_ref):
    total = jnp.sum(sums[...], axis=0, keepdims=True)
    rz, pap, rq, aq, qhq = (total[:, k : k + 1] for k in range(5))
    step = rz / pap
    rz_next = step * (step * aq - rq)
    beta = rz_next / rz
    grown = 1.0 + beta
    curved = grown * grown * pap - 2.0 * step * grown * aq + step * step * qhq
    step_next = rz_next / curved
    on_z = step + step_next * grown
    on_q = step_next * step
    p_ref[...] = on_z.reshape(1, 1, 1) * z[...] - on_q.reshape(1, 1, 1) * q[...]


def run(kernel, outs, smem, args, scratch=(), flops=1000000, place=VMEM, limit=LIMIT):
    nbytes = sum(4 * int(np.prod(out)) for out in outs) * 2
    return pl.pallas_call(
        kernel,
        out_shape=[jax.ShapeDtypeStruct(out, F32) for out in outs],
        in_specs=[pl.BlockSpec(memory_space=SMEM) for _ in smem]
        + [pl.BlockSpec(memory_space=place) for _ in args],
        out_specs=[pl.BlockSpec(memory_space=VMEM) for _ in outs],
        scratch_shapes=list(scratch),
        compiler_params=pltpu.CompilerParams(vmem_limit_bytes=limit),
        cost_estimate=pl.CostEstimate(flops=flops, bytes_accessed=nbytes, transcendentals=0),
    )(*smem, *args)


def shift(axis, low_face, high_face):
    count = lax.axis_size(axis)
    forward = [(i, i + 1) for i in range(count - 1)]
    backward = [(target, source) for source, target in forward]
    return lax.ppermute(high_face, axis, forward), lax.ppermute(low_face, axis, backward)


def body(level_set, velocity, source, wick_solid):
    block = level_set.shape
    count_gx = lax.axis_size("gx")
    count_gy = lax.axis_size("gy")
    index_gx = lax.axis_index("gx")
    index_gy = lax.axis_index("gy")

    def ends(index, count):
        return [jnp.where(index > 0, 0.5, 1.0), jnp.where(index < count - 1, 0.5, 1.0)]

    place = [index_gx.astype(F32), index_gy.astype(F32)]
    near = jnp.stack(ends(index_gx, count_gx) + ends(index_gy, count_gy) + place).astype(F32)
    packed = jnp.asarray(PACKED)
    tables = jnp.asarray(TABLES)
    face = (ROWS, LANES)
    wide_block = (8, WIDE, LANES)
    wide_face = (WIDE, LANES)
    rim = (12, TILE, LANES)

    b, l, zlo, zhi, solid = run(
        advect_kernel,
        [block, block, (3, *face), (3, *face), (8, LANES)],
        [],
        [
            pltpu.with_memory_space_constraint(array, pltpu.HBM)
            for array in (level_set, velocity, source, packed, wick_solid.reshape(EY, EX))
        ],
        [VMEM(block, F32), VMEM((3, *block), F32), VMEM(block, F32), VMEM(PACKED.shape, F32)]
        + [VMEM((EY, EX), jnp.int32), pltpu.SemaphoreType.DMA((5,))],
        place=pltpu.HBM,
    )
    zlo, zhi = shift("gx", zlo, zhi)
    ylo, yhi = run(rim_kernel, [rim, rim], [], [solid, b, l, zlo, zhi])
    ylo, yhi = shift("gy", ylo, yhi)
    w, wlo, whi = run(
        first_schwarz_kernel,
        [wide_block, wide_face, wide_face],
        [near],
        [packed, tables, b, zlo, zhi, ylo, yhi],
    )
    wlo, whi = shift("gx", wlo, whi)
    level_new, flux, stat = run(
        level_kernel,
        [block, wide_block, (1, LANES)],
        [near],
        [solid, packed, b, l, zlo, zhi, ylo, yhi],
        flops=20000000,
    )
    zl, yl, stat = run(
        galerkin_kernel,
        [wide_block, wide_block, (count_gx, LANES)],
        [near],
        [packed, stat, flux, w, wlo, whi],
    )
    gathered = lax.all_to_all(stat, "gx", 0, 0, tiled=True)
    (column,) = run(column_kernel, [(count_gy, LANES)], [], [gathered])
    gathered = lax.all_to_all(column, "gy", 0, 0, tiled=True)
    (coarse,) = run(
        functools.partial(coarse_kernel, count_gy),
        [(32, LANES)],
        [near],
        [gathered],
        [VMEM((LANES, LANES), F32), VMEM((LANES, LANES), F32)],
    )
    z, y, zlo, zhi, sums = run(
        apply_kernel,
        [block, wide_block, (2, *wide_face), (2, *wide_face), (1, LANES)],
        [near],
        [packed, coarse, flux, b, zl, yl],
    )
    zlo, zhi = shift("gx", zlo, zhi)
    w, wlo, whi = run(
        second_schwarz_kernel, [block, face, face], [near], [packed, tables, y, zlo, zhi]
    )
    zlo, zhi = shift("gx", wlo, whi)
    q, sums = run(
        second_kernel,
        [block, (count_gx, LANES)],
        [near],
        [packed, coarse, flux, b, y, w, zlo, zhi, sums],
    )
    tile = lax.all_to_all(sums, "gx", 0, 0, tiled=True)
    wide = jnp.broadcast_to(jnp.sum(tile, axis=0, keepdims=True), (count_gy, LANES))
    wide = lax.all_to_all(wide, "gy", 0, 0, tiled=True)
    (pressure,) = run(combine_kernel, [block], [], [wide, z, q])
    return (level_new, pressure)


def solution(mesh):
    placed = (
        P("gx", "gy", None),
        P(None, "gx", "gy", None),
        P("gx", "gy", None),
        P("gx", "gy", None),
    )
    return jax.shard_map(
        body,
        mesh=mesh,
        in_specs=placed,
        out_specs=(P("gx", "gy", None), P("gx", "gy", None)),
        check_vma=False,
    )
```

```python
import functools

import jax
import jax.numpy as jnp
import numpy as np
from jax import lax
from jax.experimental import pallas as pl
from jax.experimental.pallas import tpu as pltpu
from jax.sharding import PartitionSpec as P

EZ = 1
EY = 4
EX = 16
ROWS = 8 * EY
LANES = 8 * EX

TIME_STEP = 0.02
HELM_COEF = 0.25
LEVEL_WIDTH = 0.25
GAS_RATIO = 10.0
SOLID_FACTOR = 0.25
SCHWARZ_SCALE = 0.5
SCHWARZ_SHIFT = 0.05

F32 = jnp.float32
BF16 = jnp.bfloat16
VMEM = pltpu.VMEM
SMEM = pltpu.SMEM
LIMIT = 24 * 1024 * 1024


def gll_tables():
    gll_nodes = np.array(
        [
            -1.0,
            -0.8717401485096066,
            -0.5917001814331423,
            -0.2092992179024789,
            0.2092992179024789,
            0.5917001814331423,
            0.8717401485096066,
            1.0,
        ]
    )
    weight_np = np.array(
        [
            1.0 / 28.0,
            0.21070422714350603,
            0.3411226924835044,
            0.4124587946587038,
            0.4124587946587038,
            0.3411226924835044,
            0.21070422714350603,
            1.0 / 28.0,
        ]
    )
    bary_weights = np.array(
        [1.0 / np.prod([gll_nodes[i] - gll_nodes[j] for j in range(8) if j != i]) for i in range(8)]
    )
    derivative = np.zeros((8, 8))
    for i in range(8):
        for j in range(8):
            if i != j:
                derivative[i, j] = bary_weights[j] / bary_weights[i] / (gll_nodes[i] - gll_nodes[j])
        derivative[i, i] = -np.sum(derivative[i])
    return (weight_np, derivative)


def sine_tables():
    indices = np.arange(10) + 1.0
    sine_basis = np.sqrt(2.0 / 11.0) * np.sin(np.pi * np.outer(indices, indices) / 11.0)
    eigen_vals = 2.0 - 2.0 * np.cos(np.pi * indices / 11.0)
    return (sine_basis, eigen_vals)


WEIGHT, DERIV = gll_tables()
SINE, EIGEN = sine_tables()


def split_const(matrix):
    single = matrix.astype(np.float32)
    high = single.astype(jnp.bfloat16)
    low = (single - high.astype(np.float32)).astype(jnp.bfloat16)
    return high, low


def line_maps(count):
    length = 8 * count
    total = length + 4

    def column(position):
        if 0 <= position < length:
            return position
        return {-2: length, -1: length + 1, length: length + 2, length + 1: length + 3}[position]

    assembled = {}
    for position in range(-2, length + 2):
        row = np.zeros(total)
        row[column(position)] = 1.0
        if 0 <= position < length:
            if position % 8 == 0:
                row[column(position - 1)] += 1.0
            if position % 8 == 7:
                row[column(position + 1)] += 1.0
        assembled[position] = row
    forward = np.zeros((10 * count, total))
    for element in range(count):
        places = [8 * element - 2] + list(range(8 * element, 8 * element + 8)) + [8 * element + 9]
        forward[10 * element : 10 * element + 10] = SINE @ np.stack([assembled[p] for p in places])
    backward = np.zeros((length, 10 * count))
    for element in range(count):
        backward[8 * element : 8 * element + 8, 10 * element : 10 * element + 10] = SINE[1:9]
    for element in range(count - 1):
        first, second = 8 * element + 7, 8 * element + 8
        mean = 0.5 * (backward[first] + backward[second])
        backward[first] = mean
        backward[second] = mean
    return forward, backward


RING = 16
WIDE = ROWS + 2 * RING
REACH = 26
TILE = 48
TILE_B = 32


def ring_maps(reach, depth, inside):
    count = EY + 2 * depth
    forward, _ = line_maps(count)
    length = 8 * count
    columns = np.zeros((10 * count, len(inside)))
    for at, position in enumerate(inside):
        place = None if position is None else position + 8 * depth
        if place is None or place < -2 or place > length + 1:
            continue
        source = place if 0 <= place < length else {-2: 0, -1: 1}.get(place, place - length + 2) + length
        columns[:, at] = forward[:, source]
    _, backward = line_maps(count)
    own = 8 * depth
    rows = np.concatenate(
        [
            backward[own - reach : own + ROWS + reach],
            np.zeros((8, 10 * count)),
        ]
    )
    rows[ROWS + 2 * reach, 10 * depth : 10 * depth + 10] = SINE[1]
    rows[ROWS + 2 * reach + 1, 10 * (depth + EY - 1) : 10 * (depth + EY)] = SINE[8]
    return columns, rows


FZ, BZ = line_maps(1)
TILES = list(range(-REACH, 0)) + [None] * (TILE_B - REACH) + list(range(ROWS))
TILES += list(range(ROWS, ROWS + REACH)) + [None] * (TILE_B - REACH)
FY_A, BY_A = ring_maps(RING, 3, TILES)
FY_B, BY_B = ring_maps(0, 1, list(range(-RING, ROWS + RING)))
STEP_A = 112
STEP_B = 64


def padded(forward, backward, step):
    forward = np.pad(forward, ((0, step - forward.shape[0]), (0, 0)))
    return forward, np.pad(backward, ((0, 0), (0, step - backward.shape[1])))


FY_A, BY_A = padded(FY_A, BY_A, STEP_A)
FY_B, BY_B = padded(FY_B, BY_B, STEP_B)
FX, BX = line_maps(EX)
FX = FX[:, :LANES]


FX_H, FX_L = split_const(FX.T.copy())
BX_H, BX_L = split_const(BX.T.copy())


def wide_const(table):
    high, low = split_const(table)
    return np.concatenate([high, high, low], axis=1)


def pack_tables(tables):
    places, pieces, at = [], [], 0
    for table in tables:
        rows = -(-table.shape[0] // 16) * 16
        extra = ((0, rows - table.shape[0]), (0, 384 - table.shape[1]))
        pieces.append(np.pad(table.astype(np.float32), extra))
        places.append((at, rows, table.shape[1]))
        at += rows
    return np.concatenate(pieces).astype(jnp.bfloat16), places


TABLES, PLACES = pack_tables(
    [
        np.concatenate([FX_H, FX_H], axis=0),
        FX_L,
        BX_H,
        BX_L,
        wide_const(FY_A),
        wide_const(BY_A),
        wide_const(FY_B),
        wide_const(BY_B),
    ]
)


def roll_table():
    table = np.zeros((2, 8, 8, LANES))
    for kind, matrix in enumerate((DERIV, DERIV.T)):
        for k in range(8):
            for i in range(8):
                table[kind, k, i, :] = matrix[i, (i + k) % 8]
    return table.reshape(2 * 64, LANES)


WY = np.tile(WEIGHT, WIDE // 8)
WX = np.tile(WEIGHT, EX)


def inner_count(count):
    mult = np.ones(8 * count)
    position = np.arange(8 * count)
    mult[(position % 8 == 0) & (position > 0)] += 1.0
    mult[(position % 8 == 7) & (position < 8 * count - 1)] += 1.0
    return mult


END_MASS = np.where(np.arange(WIDE) % 8 % 7 == 0, 2.0, 1.0)
INV_MASS = (8.0 / (WY * END_MASS)[:, None] / (WX * inner_count(EX))[None, :]).astype(np.float32)

AT_ROLLS = WIDE
AT_DX = AT_ROLLS + 128
AT_DXT = AT_DX + LANES
AT_SQUARE = AT_DXT + LANES
AT_MASS = AT_SQUARE + 16
AT_SPREAD = AT_MASS + WIDE
AT_EIGEN_Y = AT_SPREAD + EX
AT_EIGEN_X = AT_EIGEN_Y + STEP_A
LAM_Y = np.resize(EIGEN, STEP_A)
LAM_X = np.resize(EIGEN, 8 * LANES).reshape(8, LANES)
PACKED = np.concatenate(
    [
        WY[:, None] * WX[None, :],
        roll_table(),
        np.kron(np.eye(EX), DERIV.T),
        np.kron(np.eye(EX), DERIV),
        np.repeat(DERIV[:, :1] ** 2, LANES, axis=1),
        np.repeat(DERIV[:, 7:] ** 2, LANES, axis=1),
        INV_MASS,
        np.kron(np.eye(EX), np.ones((1, 8))),
        np.repeat(LAM_Y[:, None], LANES, axis=1),
        LAM_X,
    ]
).astype(np.float32)


def parts(values):
    high = values.astype(BF16)
    low = (values - high.astype(F32)).astype(BF16)
    return high, low


def dot(left, right):
    return jnp.dot(left, right, preferred_element_type=F32)


def left_pairs(table, planes):
    results = []
    for i in range(0, len(planes), 2):
        high, low = parts(jnp.concatenate([planes[i], planes[i + 1]], axis=1))
        both = dot(table, jnp.concatenate([high, low, high], axis=0))
        results += [both[:, 0:LANES], both[:, LANES : 2 * LANES]]
    return results


def along_z(values, matrix):
    rows = []
    for i in range(matrix.shape[0]):
        total = None
        for j in range(matrix.shape[1]):
            if matrix[i, j] == 0.0:
                continue
            term = float(matrix[i, j]) * values[j]
            total = term if total is None else total + term
        rows.append(total)
    return rows


def along_y(values, packed, kind):
    count, rows = values.shape[:2]
    grouped = values.reshape(count * rows // 8, 8, LANES)
    start = AT_ROLLS + 64 * kind
    total = packed[start : start + 8][None] * grouped
    for k in range(1, 8):
        total = total + packed[start + 8 * k : start + 8 * k + 8][None] * pltpu.roll(grouped, 8 - k, 1)
    return total.reshape(count, rows, LANES)


def along_x(values, packed, kind):
    start = AT_DXT if kind else AT_DX
    high, low = parts(packed[start : start + LANES])
    first, rest = parts(values.reshape(8 * values.shape[1], LANES))
    total = dot(
        jnp.concatenate([first, rest], axis=1), jnp.concatenate([high, high], axis=0)
    ) + dot(first, low)
    return total.reshape(values.shape)


def stack(planes):
    return jnp.concatenate([plane[None] for plane in planes], axis=0)


def edge_rows(rows, low, high):
    position = lax.broadcasted_iota(jnp.int32, (rows, LANES), 0)
    return jnp.where(position == 0, low, jnp.where(position == rows - 1, high, 1.0))


def local_operator(values, flux, packed):
    plane_w = packed[0 : values.shape[1]]
    gz = along_z([values[i] for i in range(8)], DERIV)
    fz = along_z([flux[i] * gz[i] for i in range(8)], DERIV.T)
    total = along_y(flux * along_y(values, packed, 0), packed, 1)
    total = total + along_x(flux * along_x(values, packed, 0), packed, 1)
    planes = [
        total[i] + fz[i] + (HELM_COEF * 0.125 * float(WEIGHT[i])) * (plane_w * values[i])
        for i in range(8)
    ]
    return stack(planes)


def add_planes(own, low_z, high_z):
    planes = [own[i] for i in range(8)]
    planes[0] = planes[0] + low_z
    planes[7] = planes[7] + high_z
    return stack(planes)


def solve_elements(planes, packed, tables, kind):
    def table(index):
        at, rows, width = PLACES[index]
        return tables[at : at + rows, 0:width]

    fxhh, fxl, bxh, bxl = (table(index) for index in range(4))
    spectral = left_pairs(table(4 + 2 * kind), along_z(planes, FZ))
    high, low = parts(jnp.concatenate(spectral, axis=0))
    wide = dot(jnp.concatenate([high, low], axis=1), fxhh) + dot(high, fxl)
    step = PLACES[4 + 2 * kind][1]
    column = packed[AT_EIGEN_Y : AT_EIGEN_Y + step]
    rest = 10 * EX - LANES
    lam = jnp.concatenate(
        [
            column + packed[AT_EIGEN_X : AT_EIGEN_X + 1],
            column[:, 0:rest] + packed[AT_EIGEN_X + 1 : AT_EIGEN_X + 2, 0:rest],
        ],
        axis=1,
    )
    scaled = [
        wide[step * i : step * (i + 1)]
        / (SCHWARZ_SCALE * lam + float(SCHWARZ_SCALE * EIGEN[i] + SCHWARZ_SHIFT))
        for i in range(10)
    ]
    high, low = parts(jnp.concatenate(scaled, axis=0))
    back = dot(high, bxh) + dot(low, bxh) + dot(high, bxl)
    back = left_pairs(table(5 + 2 * kind), [back[step * i : step * (i + 1)] for i in range(10)])
    return along_z(back, BZ)


def store_faces(planes, near, out_ref, low_ref, high_ref):
    planes[0] = planes[0] * near[0]
    planes[7] = planes[7] * near[1]
    for i in range(8):
        out_ref[i] = planes[i]
    low_ref[...] = planes[0]
    high_ref[...] = planes[7]


def ring_rows(near):
    row = lax.broadcasted_iota(jnp.int32, (WIDE, LANES), 0)
    return row, 2.0 - 2.0 * near[2], 2.0 - 2.0 * near[3]


def partition_total(own, low_z, high_z, low_y, high_y, near):
    def planes(array):
        total = near[0] * array[0] + near[1] * array[7]
        for i in range(1, 7):
            total = total + array[i]
        return total

    total = planes(own) + 0.5 * (low_z[1] + high_z[0])
    below = planes(low_y) + 0.5 * (low_y[9] + low_y[10])
    above = planes(high_y) + 0.5 * (high_y[9] + high_y[10])
    faces = 0.5 * (below[REACH - 1 : REACH] + above[0:1])
    return jnp.sum(total * edge_rows(ROWS, near[2], near[3])) + jnp.sum(faces)


def lane_row(entries):
    lane = lax.broadcasted_iota(jnp.int32, (1, LANES), 1)
    row = jnp.zeros((1, LANES), F32)
    for index, value in enumerate(entries):
        row = jnp.where(lane == index, value, row)
    return row


def advect_kernel(
    lev_in, vel_in, src_in, packed_in, solid_in, b_ref, l_ref, zlo, zhi, solid_ref,
    lev, vel, src, packed, solid, sems,
):
    copies = [
        pltpu.make_async_copy(source, target, sems.at[index])
        for index, (source, target) in enumerate(
            (
                (vel_in, vel), (lev_in, lev), (packed_in, packed), (src_in, src), (solid_in, solid),
            )
        )
    ]
    for copy in copies:
        copy.start()
    for copy in copies:
        copy.wait()
    spread = packed[AT_SPREAD : AT_SPREAD + EX].astype(BF16)
    in_solid = dot(solid[...].astype(F32).astype(BF16), spread)
    solid_ref[...] = jnp.concatenate([in_solid, jnp.zeros((8 - EY, LANES), F32)], axis=0)
    level = lev[...]
    v0, v1, v2 = vel[0], vel[1], vel[2]
    gz = stack(along_z([level[i] for i in range(8)], DERIV))
    advect = v0 * gz + v1 * along_y(level, packed, 0) + v2 * along_x(level, packed, 0)
    moved = level - (2.0 * TIME_STEP) * advect
    diverge = stack(along_z([v0[i] for i in range(8)], DERIV))
    diverge = diverge + along_y(v1, packed, 0) + along_x(v2, packed, 0)
    force = src[...] - (2.0 * TIME_STEP) * diverge
    weights = packed[0:ROWS]
    for i in range(8):
        mass = (0.125 * float(WEIGHT[i])) * weights
        term = mass * force[i]
        moved_i = mass * moved[i]
        b_ref[i] = term
        l_ref[i] = moved_i
        if i < 2:
            zlo[i] = term
        if i == 0:
            zlo[2] = moved_i
        if i > 5:
            zhi[i - 6] = term
        if i == 7:
            zhi[2] = moved_i


def rim_kernel(solid, b, l, low_z, high_z, low_y, high_y):
    in_solid = solid[...]
    rest = TILE - REACH - RING - 1

    def rows(planes, at, level, far, extra=None):
        start = ROWS - REACH if far else 0
        pieces = [planes[at, start : start + REACH]]
        if level is None:
            pieces.append(jnp.zeros((RING + 1, LANES), F32))
        else:
            array, index = level
            start = ROWS - RING - 1 if far else 0
            pieces.append(array[index, start : start + RING + 1])
        if extra is None:
            pieces.append(jnp.zeros((rest, LANES), F32))
        else:
            pieces += [extra, jnp.zeros((rest - 2, LANES), F32)]
        return jnp.concatenate(pieces, axis=0)

    for far, out in ((False, low_y), (True, high_y)):
        extra = in_solid[EY - 2 : EY] if far else in_solid[0:2]
        for i in range(8):
            out[i] = rows(b, i, (l, i), far, extra if i == 0 else None)
        for i in range(2):
            out[8 + i] = rows(low_z, i, (low_z, 2) if i == 1 else None, far)
            out[10 + i] = rows(high_z, i, (high_z, 2) if i == 0 else None, far)


def level_kernel(
    near, solid, packed, b, l, zlo, zhi, ylo, yhi, level_ref, flux_ref, stat
):
    row, has_low, has_high = ring_rows(near)
    at = REACH

    def wide_rows(slot, own):
        return jnp.concatenate(
            [ylo[slot, at + 1 : at + 1 + RING], own, yhi[slot, at : at + RING]], axis=0
        )

    planes = []
    for i in range(8):
        plane = wide_rows(i, l[i])
        first = ylo[i, at : at + 1]
        last = yhi[i, at + RING : at + RING + 1]
        if i == 0:
            plane = plane + wide_rows(9, zlo[2])
            first = first + ylo[9, at : at + 1]
            last = last + yhi[9, at + RING : at + RING + 1]
        if i == 7:
            plane = plane + wide_rows(10, zhi[2])
            first = first + ylo[10, at : at + 1]
            last = last + yhi[10, at + RING : at + RING + 1]
        before = jnp.where(row == 0, first, pltpu.roll(plane, 1, 0))
        after = jnp.where(row == WIDE - 1, last, pltpu.roll(plane, WIDE - 1, 0))
        plane = plane + jnp.where(row % 8 == 0, before, jnp.where(row % 8 == 7, after, 0.0))
        planes.append(plane)
    own = stack(planes)
    lane = lax.broadcasted_iota(jnp.int32, (8, WIDE, LANES), 2)
    before = jnp.where((lane % 8 == 0) & (lane > 0), pltpu.roll(own, 1, 2), 0.0)
    after = jnp.where((lane % 8 == 7) & (lane < LANES - 1), pltpu.roll(own, LANES - 1, 2), 0.0)
    own = own + before + after
    ends = jnp.where(row == RING, 2.0 * near[2], jnp.where(row == RING + ROWS - 1, 2.0 * near[3], 1.0))
    inverse = packed[AT_MASS : AT_MASS + WIDE] * ends
    in_solid = solid[...]
    solids = [ylo[0, at + RING + 1 + k : at + RING + 2 + k] for k in range(2)]
    solids += [in_solid[e : e + 1] for e in range(EY)]
    solids += [yhi[0, at + RING + 1 + k : at + RING + 2 + k] for k in range(2)]
    open_part = jnp.concatenate(
        [jnp.broadcast_to(1.0 - (1.0 - SOLID_FACTOR) * rows, (8, LANES)) for rows in solids], axis=0
    )
    in_grid = jnp.where(row < RING, has_low, jnp.where(row >= RING + ROWS, has_high, 1.0))
    flux_w = packed[0:WIDE] * in_grid
    total = jnp.zeros((ROWS, LANES), F32)
    fluxes = []
    for i in range(8):
        scale = 1.0 / float(WEIGHT[i])
        plane = own[i] * (inverse * scale)
        if i == 0:
            plane = plane * near[0]
        if i == 7:
            plane = plane * near[1]
        level_ref[i] = plane[RING : RING + ROWS]
        liquid = jax.nn.sigmoid(plane * (1.0 / LEVEL_WIDTH))
        coef = (GAS_RATIO - (GAS_RATIO - 1.0) * liquid) * open_part
        total = total + coef[RING : RING + ROWS]
        flux = (0.5 * float(WEIGHT[i])) * (coef * flux_w)
        flux_ref[i] = flux
        fluxes.append(flux[RING : RING + ROWS])
    kbar = jnp.sum(total) * (1.0 / (8 * ROWS * LANES))
    entries = [kbar, partition_total(b, zlo, zhi, ylo, yhi, near)] + [0.0] * 9
    for first, second in ((0, 0), (0, 7), (7, 7)):
        slopes = along_z(fluxes, (DERIV[:, first] * DERIV[:, second])[None, :])[0]
        column = jnp.sum(slopes, axis=1, keepdims=True)
        entries += [jnp.sum(column, axis=0, keepdims=True), column[0:1], column[ROWS - 1 : ROWS]]
    inner = fluxes[0] + fluxes[1]
    for i in range(2, 8):
        inner = inner + fluxes[i]
    for at_row, start in ((0, 0), (ROWS - 8, 8)):
        square = packed[AT_SQUARE + start : AT_SQUARE + start + 8]
        entries += [
            jnp.sum(square * plane[at_row : at_row + 8]) for plane in (inner, fluxes[0], fluxes[7])
        ]
    stat[...] = lane_row(entries)


def first_schwarz_kernel(
    near, packed, tables, b, zlo, zhi, ylo, yhi, w_ref, wlo, whi
):
    own = [b[i] for i in range(8)] + [zlo[0], zlo[1], zhi[0], zhi[1]]
    planes = [
        jnp.concatenate([ylo[i, 0:TILE_B], own[i], yhi[i, 0:TILE_B]], axis=0) for i in range(12)
    ]
    planes = solve_elements(planes, packed, tables, 0)
    row, has_low, has_high = ring_rows(near)
    in_grid = jnp.where(row < RING, has_low, jnp.where(row >= RING + ROWS, has_high, 1.0))
    in_grid = jnp.where(row == RING, has_low, jnp.where(row == RING + ROWS - 1, has_high, in_grid))
    for i in range(8):
        first = (1.0 - has_low) * planes[i][WIDE : WIDE + 1]
        last = (1.0 - has_high) * planes[i][WIDE + 1 : WIDE + 2]
        alone = jnp.where(row == RING, first, jnp.where(row == RING + ROWS - 1, last, 0.0))
        planes[i] = planes[i][0:WIDE] * in_grid + alone
    store_faces(planes, near, w_ref, wlo, whi)


def galerkin_kernel(near, packed, stat_in, flux, w, zlo, zhi, zl_ref, y_ref, ylo, yhi, stat):
    local = add_planes(w, zlo[...], zhi[...])
    zl_ref[...] = local
    applied = local_operator(local, flux[...], packed)
    y_ref[...] = applied
    fluxes = [flux[i] for i in range(8)]
    for out, rows in ((ylo, (0, 1)), (yhi, (6, 7))):
        for k, i in enumerate(rows):
            out[k] = applied[i]
            for t, end in enumerate((0, 7)):
                out[2 + 2 * t + k] = along_z(fluxes, (DERIV[:, i] * DERIV[:, end])[None, :])[0]
            out[6 + k] = fluxes[i]
    applied = applied[:, RING : RING + ROWS]
    inner = near[0] * applied[0] + near[1] * applied[7]
    for i in range(1, 7):
        inner = inner + applied[i]
    edge = edge_rows(ROWS, near[2], near[3])
    entries = [0.0, 0.0]
    for plane in ((1.0 - near[0]) * applied[0], inner, (1.0 - near[1]) * applied[7]):
        entries += [
            (1.0 - near[2]) * jnp.sum(plane[0:1]),
            jnp.sum(edge * plane),
            (1.0 - near[3]) * jnp.sum(plane[ROWS - 1 : ROWS]),
        ]
    stat[...] = jnp.broadcast_to(stat_in[...] + lane_row(entries), stat.shape)


def column_kernel(gathered, out_ref):
    values = gathered[...]
    sub = lax.broadcasted_iota(jnp.int32, (8, LANES), 0)
    lane = lax.broadcasted_iota(jnp.int32, (8, LANES), 1)
    after = jnp.where(sub < 7, pltpu.roll(values, 7, 0), 0.0)
    before = jnp.where(sub > 0, pltpu.roll(values, 1, 0), 0.0)
    first = lax.broadcasted_iota(jnp.int32, (8, 1), 0) == 0
    last = lax.broadcasted_iota(jnp.int32, (8, 1), 0) == 7

    def column(array, index):
        return array[:, index : index + 1]

    def slopes(array, pair):
        whole, low, high = (column(array, 11 + 3 * pair + k) for k in range(3))
        return whole - low - high, low, high

    merged = [column(values, 0), column(values, 1)]
    for b in range(3):
        merged.append(column(values, 5 + b) + column(after, 2 + b) + column(before, 8 + b))
    merged += [own + other for own, other in zip(slopes(values, 0), slopes(before, 2), strict=True)]
    merged += list(slopes(values, 1))
    inside, interface = [], []
    for side in range(2):
        whole, low, high = (column(values, 20 + 3 * side + k) for k in range(3))
        ends = jnp.where(first, low, 0.0) + jnp.where(last, high, 0.0)
        inside.append(whole - low - high + ends)
        interface.append(jnp.where(first, 0.0, low) + column(before, 22 + 3 * side))
    rows = jnp.zeros((8, LANES), F32)
    for index, value in enumerate(merged + inside + interface):
        rows = jnp.where(lane == index, value, rows)
    total = rows[0:1]
    for i in range(1, 8):
        total = total + pltpu.roll(rows[i : i + 1], 16 * i, 1)
    out_ref[...] = jnp.broadcast_to(total, out_ref.shape)


def invert(blocks, sub):
    for k in range(8):
        pivot = 1.0 / blocks[k][k : k + 1]
        scaled = jnp.where(sub == k, pivot, blocks[k] * pivot)
        rows = []
        for r in range(8):
            if r == k:
                rows.append(scaled)
            else:
                rest = jnp.where(sub == k, 0.0, blocks[r])
                rows.append(rest - blocks[r][k : k + 1] * scaled)
        blocks = rows
    return blocks


def multiply(left, right):
    rows = []
    for r in range(8):
        total = left[r][0:1] * right[0]
        for k in range(1, 8):
            total = total + left[r][k : k + 1] * right[k]
        rows.append(total)
    return rows


def matvec(terms, sub):
    result = jnp.zeros_like(terms[0][1])
    for r in range(8):
        product = terms[0][0][r] * terms[0][1]
        for blocks, column in terms[1:]:
            product = product + blocks[r] * column
        result = jnp.where(sub == r, jnp.sum(product, axis=0, keepdims=True), result)
    return result


def coarse_operator(c, count, sums_z, couplings_z, inside_y, interface_y):
    sub = lax.broadcasted_iota(jnp.int32, c.shape, 0)
    lane = lax.broadcasted_iota(jnp.int32, c.shape, 1)
    has_low = lane > 0
    has_high = lane < count - 1

    def after(array):
        return jnp.where(sub < 7, pltpu.roll(array, 7, 0), 0.0)

    def before(array):
        return jnp.where(sub > 0, pltpu.roll(array, 1, 0), 0.0)

    def right(array):
        return jnp.where(has_high, pltpu.roll(array, LANES - 1, 1), 0.0)

    def left(array):
        return jnp.where(has_low, pltpu.roll(array, 1, 1), 0.0)

    on_low = jnp.where(has_low, 0.5 * (c + left(c)), c)
    on_high = jnp.where(has_high, 0.5 * (c + right(c)), c)
    tested = []
    for place, value in enumerate((c, on_low, on_high)):
        slope = jnp.where(sub > 0, 0.5 * (value - before(value)), 0.0)
        coupling = couplings_z[place]
        force = sums_z[place] * slope - coupling * after(slope) - before(coupling * slope)
        force = jnp.where(sub > 0, force, 0.0)
        tested.append(0.5 * (force - after(force)))
    result = tested[0] + jnp.where(has_low, 0.5, 1.0) * tested[1] + jnp.where(has_high, 0.5, 1.0) * tested[2]
    result = result + 0.5 * right(tested[1]) + 0.5 * left(tested[2])

    interface = jnp.where(sub > 0, 0.5 * (c + before(c)), 0.0)
    for side, (move, there) in enumerate(((left, has_low), (right, has_high))):
        force = inside_y[side] * jnp.where(there, 0.5 * (move(c) - c), 0.0)
        face = interface_y[side] * jnp.where(there, 0.5 * (move(interface) - interface), 0.0)
        force = force + 0.5 * (face + after(face))
        back = right if side == 0 else left
        result = result + 0.5 * (back(force) - force)

    end = float(WEIGHT[0])
    mass = (2.0 - 2.0 * end) * c + end * (interface + after(interface))
    mass = mass + jnp.where((sub == 0) | (sub == 7), end * c, 0.0)
    beside = jnp.where(has_low, 0.5 * (mass + left(mass)), 0.0)
    scaled = (2.0 * EY - 2.0 * end) * mass + end * (beside + right(beside))
    scaled = scaled + jnp.where(has_low, 0.0, end * mass) + jnp.where(has_high, 0.0, end * mass)
    return result + HELM_COEF / 8.0 * float(np.sum(WX)) * scaled


def coarse_kernel(count, near, gathered, out_ref, wide, turned):
    lanes = LANES
    sub = lax.broadcasted_iota(jnp.int32, (8, lanes), 0)
    lane = lax.broadcasted_iota(jnp.int32, (8, lanes), 1)
    wide[...] = jnp.zeros((LANES, LANES), F32)
    wide[0:count] = gathered[...]
    turned[...] = wide[...].T

    def value(index):
        return turned[pl.ds(index, 8, stride=16), :]

    def move(array, dz, dy):
        if dz:
            array = pltpu.roll(array, (-dz) % 8, 0)
        if dy:
            array = pltpu.roll(array, (-dy) % lanes, 1)
        return array

    kbar = jnp.where(lane < count, value(0), 1.0)
    above = move(kbar, 1, 0)
    link_z = jnp.where(sub < 7, 2.0 * kbar * above / (kbar + above) * (EY * EX / EZ), 0.0)
    link_z = jnp.where(lane < count, link_z, 0.0)
    beside = move(kbar, 0, 1)
    link_y = 2.0 * kbar * beside / (kbar + beside) * (EZ * EX / EY)
    link_y = jnp.where(lane < count - 1, link_y, 0.0)
    back_z = move(link_z, -1, 0)
    back_y = move(link_y, 0, -1)
    diagonal = HELM_COEF * EZ * EY * EX + link_z + back_z + link_y + back_y
    blocks, lower, upper = [], [], []
    for r in range(8):
        row = jnp.where(sub == r, diagonal, 0.0)
        row = jnp.where(sub == r + 1, -back_z, row)
        row = jnp.where(sub == r - 1, -link_z, row)
        blocks.append(row)
        lower.append(jnp.where(sub == r, -back_y, 0.0))
        upper.append(jnp.where(sub == r, -link_y, 0.0))
    levels = []
    step = 1
    while step < count:
        inverse = invert(blocks, sub)
        down = multiply(lower, [move(row, 0, -step) for row in inverse])
        up = multiply(upper, [move(row, 0, step) for row in inverse])
        levels.append((step, down, up))
        before_u = multiply(down, [move(row, 0, -step) for row in upper])
        after_l = multiply(up, [move(row, 0, step) for row in lower])
        if 2 * step < count:
            new_lower = multiply(down, [move(row, 0, -step) for row in lower])
            new_upper = multiply(up, [move(row, 0, step) for row in upper])
            lower = [-row for row in new_lower]
            upper = [-row for row in new_upper]
        blocks = [blocks[r] - before_u[r] - after_l[r] for r in range(8)]
        step *= 2
    inverse = invert(blocks, sub)

    def solve(column):
        for distance, down, up in levels:
            pulled = matvec(
                [(down, move(column, 0, -distance)), (up, move(column, 0, distance))], sub
            )
            column = column - pulled
        return matvec([(inverse, column)], sub)

    first = solve(value(1))
    totals = coarse_operator(
        first,
        count,
        [value(5 + k) for k in range(3)],
        [value(8 + k) for k in range(3)],
        [value(11), value(12)],
        [value(13), value(14)],
    )
    totals = totals + value(3)
    totals = totals + jnp.where(lane < count - 1, move(value(2), 0, 1), 0.0)
    totals = totals + jnp.where(lane > 0, move(value(4), 0, -1), 0.0)
    totals = jnp.where(lane < count, totals, 0.0)
    second = solve(totals)
    mine = (sub.astype(F32) == near[4]) & (lane.astype(F32) == near[5])

    def store(at, solved, reach):
        for a in range(-reach, reach + 1):
            for b in range(-1, 2):
                picked = jnp.sum(jnp.where(mine, move(solved, a, b), 0.0))
                row = at + 3 * (a + reach) + b + 1
                out_ref[row : row + 1] = jnp.full((1, lanes), picked)

    store(0, first, 2)
    store(16, second, 1)


def coarse_columns(near, coarse, start, count):
    row, has_low, has_high = ring_rows(near)
    below = jnp.where(row < RING - 1, 1.0, jnp.where(row <= RING, 0.5, 0.0)) * has_low
    above = jnp.where(row > RING + ROWS, 1.0, jnp.where(row >= RING + ROWS - 1, 0.5, 0.0)) * has_high
    edge = jnp.where((row > RING) & (row < RING + ROWS - 1), 1.0, 0.0)
    edge = jnp.where(row == RING, near[2], jnp.where(row == RING + ROWS - 1, near[3], edge))
    edge = jnp.where(row == RING - 1, 0.5 * has_low, edge)
    edge = jnp.where(row == RING + ROWS, 0.5 * has_high, edge)
    columns = []
    for a in range(count):
        at = start + 3 * a
        columns.append(
            below * coarse[at : at + 1] + edge * coarse[at + 1 : at + 2] + above * coarse[at + 2 : at + 3]
        )
    return columns


def coarse_planes(columns, low, high):
    before, inside, after = columns
    return inside, low * (before - inside), high * (after - inside)


def add_coarse(local, columns):
    inside, first, last = columns
    planes = [local[i] + inside for i in range(8)]
    planes[0] = planes[0] + first
    planes[7] = planes[7] + last
    return stack(planes)


def coarse_applied(columns, flux, packed):
    inside, first, last = columns
    slopes = [
        flux[i] * (float(DERIV[i, 0]) * first + float(DERIV[i, 7]) * last) for i in range(8)
    ]
    fz = along_z(slopes, DERIV.T)
    three = stack([inside + first, inside, inside + last])
    gy = along_y(three, packed, 0)
    fy = along_y(
        stack([flux[i] * gy[0 if i == 0 else 2 if i == 7 else 1] for i in range(8)]), packed, 1
    )
    plane_w = packed[0:WIDE]
    planes = []
    for i in range(8):
        plane = three[0 if i == 0 else 2 if i == 7 else 1]
        planes.append(fz[i] + fy[i] + (HELM_COEF * 0.125 * float(WEIGHT[i])) * (plane_w * plane))
    return stack(planes)


def face_applied(planes, payload, packed, rows, in_grid):
    inside, first, last = planes
    fields = [inside + (first if i == 0 else last if i == 7 else 0.0) for i in rows]
    gy = along_y(stack(fields), packed, 0)
    fy = along_y(stack([payload[6 + k] * gy[k] for k in range(2)]), packed, 1)
    plane_w = packed[0:WIDE]
    result = []
    for k, i in enumerate(rows):
        slopes = payload[2 + k] * first + payload[4 + k] * last
        mass = (HELM_COEF * 0.125 * float(WEIGHT[i])) * in_grid * (plane_w * fields[k])
        result.append(payload[k] + slopes + fy[k] + mass)
    return result


def apply_kernel(
    near, packed, tables, coarse, flux, b, zl, yl, ylo, yhi,
    z_ref, y_ref, w_ref, wlo, whi, stat,
):
    columns = coarse_columns(near, coarse, 0, 5)
    own = coarse_planes(columns[1:4], 1.0 - near[0], 1.0 - near[1])
    field = add_coarse(zl[...], own)[:, RING : RING + ROWS]
    z_ref[...] = field
    applied = yl[...] + coarse_applied(own, flux[...], packed)
    kept = applied[:, RING : RING + ROWS]
    y_ref[...] = kept
    stat[...] = lane_row([jnp.sum(b[...] * field), jnp.sum(field * kept)])
    lower = coarse_planes(columns[0:3], 1.0 - near[7], 0.5)
    upper = coarse_planes(columns[2:5], 0.5, 1.0 - near[6])
    planes = [applied[i] for i in range(8)]
    planes += face_applied(lower, ylo, packed, (6, 7), 2.0 - 2.0 * near[0])
    planes += face_applied(upper, yhi, packed, (0, 1), 2.0 - 2.0 * near[1])
    planes = solve_elements(planes, packed, tables, 1)
    row = lax.broadcasted_iota(jnp.int32, (ROWS, LANES), 0)
    _, has_low, has_high = ring_rows(near)
    in_grid = jnp.where(row == 0, has_low, jnp.where(row == ROWS - 1, has_high, 1.0))
    for i in range(8):
        first = (1.0 - has_low) * planes[i][ROWS : ROWS + 1]
        last = (1.0 - has_high) * planes[i][ROWS + 1 : ROWS + 2]
        alone = jnp.where(row == 0, first, jnp.where(row == ROWS - 1, last, 0.0))
        planes[i] = planes[i][0:ROWS] * in_grid + alone
    store_faces(planes, near, w_ref, wlo, whi)


def second_kernel(near, packed, coarse, flux, b, y, w, zlo, zhi, stat_in, q_ref, stat):
    local = add_planes(w, zlo[...], zhi[...])
    columns = [column[RING : RING + ROWS] for column in coarse_columns(near, coarse, 16, 3)]
    field = add_coarse(local, coarse_planes(columns, 1.0 - near[0], 1.0 - near[1]))
    q_ref[...] = field
    applied = local_operator(field, flux[:, RING : RING + ROWS], packed)
    sums = [0.0, 0.0, jnp.sum(b[...] * field), jnp.sum(y[...] * field), jnp.sum(field * applied)]
    stat[...] = jnp.broadcast_to(stat_in[...] + lane_row(sums), stat.shape)


def combine_kernel(sums, z, q, p_ref):
    total = jnp.sum(sums[...], axis=0, keepdims=True)
    rz, pap, rq, aq, qhq = (total[:, k : k + 1] for k in range(5))
    step = rz / pap
    rz_next = step * (step * aq - rq)
    beta = rz_next / rz
    grown = 1.0 + beta
    curved = grown * grown * pap - 2.0 * step * grown * aq + step * step * qhq
    step_next = rz_next / curved
    on_z = step + step_next * grown
    on_q = step_next * step
    p_ref[...] = on_z.reshape(1, 1, 1) * z[...] - on_q.reshape(1, 1, 1) * q[...]


def run(kernel, outs, smem, args, scratch=(), flops=1000000, place=VMEM, limit=LIMIT):
    nbytes = sum(4 * int(np.prod(out)) for out in outs) * 2
    return pl.pallas_call(
        kernel,
        out_shape=[jax.ShapeDtypeStruct(out, F32) for out in outs],
        in_specs=[pl.BlockSpec(memory_space=SMEM) for _ in smem]
        + [pl.BlockSpec(memory_space=place) for _ in args],
        out_specs=[pl.BlockSpec(memory_space=VMEM) for _ in outs],
        scratch_shapes=list(scratch),
        compiler_params=pltpu.CompilerParams(vmem_limit_bytes=limit),
        cost_estimate=pl.CostEstimate(flops=flops, bytes_accessed=nbytes, transcendentals=0),
    )(*smem, *args)


def shift(axis, low_face, high_face):
    count = lax.axis_size(axis)
    forward = [(i, i + 1) for i in range(count - 1)]
    backward = [(target, source) for source, target in forward]
    return lax.ppermute(high_face, axis, forward), lax.ppermute(low_face, axis, backward)


def body(level_set, velocity, source, wick_solid):
    block = level_set.shape
    count_gx = lax.axis_size("gx")
    count_gy = lax.axis_size("gy")
    index_gx = lax.axis_index("gx")
    index_gy = lax.axis_index("gy")

    def ends(index, count):
        return [jnp.where(index > 0, 0.5, 1.0), jnp.where(index < count - 1, 0.5, 1.0)]

    place = [index_gx.astype(F32), index_gy.astype(F32)]
    beyond = [
        jnp.where(index_gx < count_gx - 2, 0.5, 1.0),
        jnp.where(index_gx > 1, 0.5, 1.0),
    ]
    near = jnp.stack(ends(index_gx, count_gx) + ends(index_gy, count_gy) + place + beyond)
    near = near.astype(F32)
    packed = jnp.asarray(PACKED)
    tables = jnp.asarray(TABLES)
    face = (ROWS, LANES)
    wide_block = (8, WIDE, LANES)
    wide_face = (WIDE, LANES)
    rim = (12, TILE, LANES)

    b, l, zlo, zhi, solid = run(
        advect_kernel,
        [block, block, (3, *face), (3, *face), (8, LANES)],
        [],
        [
            pltpu.with_memory_space_constraint(array, pltpu.HBM)
            for array in (level_set, velocity, source, packed, wick_solid.reshape(EY, EX))
        ],
        [VMEM(block, F32), VMEM((3, *block), F32), VMEM(block, F32), VMEM(PACKED.shape, F32)]
        + [VMEM((EY, EX), jnp.int32), pltpu.SemaphoreType.DMA((5,))],
        place=pltpu.HBM,
    )
    zlo, zhi = shift("gx", zlo, zhi)
    ylo, yhi = run(rim_kernel, [rim, rim], [], [solid, b, l, zlo, zhi])
    ylo, yhi = shift("gy", ylo, yhi)
    w, wlo, whi = run(
        first_schwarz_kernel,
        [wide_block, wide_face, wide_face],
        [near],
        [packed, tables, b, zlo, zhi, ylo, yhi],
    )
    wlo, whi = shift("gx", wlo, whi)
    level_new, flux, stat = run(
        level_kernel,
        [block, wide_block, (1, LANES)],
        [near],
        [solid, packed, b, l, zlo, zhi, ylo, yhi],
        flops=20000000,
    )
    zl, yl, zlo, zhi, stat = run(
        galerkin_kernel,
        [wide_block, wide_block, wide_block, wide_block, (count_gx, LANES)],
        [near],
        [packed, stat, flux, w, wlo, whi],
    )
    zlo, zhi = shift("gx", zlo, zhi)
    gathered = lax.all_to_all(stat, "gx", 0, 0, tiled=True)
    (column,) = run(column_kernel, [(count_gy, LANES)], [], [gathered])
    gathered = lax.all_to_all(column, "gy", 0, 0, tiled=True)
    (coarse,) = run(
        functools.partial(coarse_kernel, count_gy),
        [(32, LANES)],
        [near],
        [gathered],
        [VMEM((LANES, LANES), F32), VMEM((LANES, LANES), F32)],
    )
    z, y, w, wlo, whi, sums = run(
        apply_kernel,
        [block, block, block, face, face, (1, LANES)],
        [near],
        [packed, tables, coarse, flux, b, zl, yl, zlo, zhi],
    )
    zlo, zhi = shift("gx", wlo, whi)
    q, sums = run(
        second_kernel,
        [block, (count_gx, LANES)],
        [near],
        [packed, coarse, flux, b, y, w, zlo, zhi, sums],
    )
    tile = lax.all_to_all(sums, "gx", 0, 0, tiled=True)
    wide = jnp.broadcast_to(jnp.sum(tile, axis=0, keepdims=True), (count_gy, LANES))
    wide = lax.all_to_all(wide, "gy", 0, 0, tiled=True)
    (pressure,) = run(combine_kernel, [block], [], [wide, z, q])
    return (level_new, pressure)


def solution(mesh):
    placed = (
        P("gx", "gy", None),
        P(None, "gx", "gy", None),
        P("gx", "gy", None),
        P("gx", "gy", None),
    )
    return jax.shard_map(
        body,
        mesh=mesh,
        in_specs=placed,
        out_specs=(P("gx", "gy", None), P("gx", "gy", None)),
        check_vma=False,
    )
```

```python
import functools

import jax
import jax.numpy as jnp
import numpy as np
from jax import lax
from jax.experimental import pallas as pl
from jax.experimental.pallas import tpu as pltpu
from jax.sharding import PartitionSpec as P

EZ = 1
EY = 4
EX = 16
ROWS = 8 * EY
LANES = 8 * EX

TIME_STEP = 0.02
HELM_COEF = 0.25
LEVEL_WIDTH = 0.25
GAS_RATIO = 10.0
SOLID_FACTOR = 0.25
SCHWARZ_SCALE = 0.5
SCHWARZ_SHIFT = 0.05

F32 = jnp.float32
BF16 = jnp.bfloat16
VMEM = pltpu.VMEM
SMEM = pltpu.SMEM
LIMIT = 24 * 1024 * 1024


def gll_tables():
    gll_nodes = np.array(
        [
            -1.0,
            -0.8717401485096066,
            -0.5917001814331423,
            -0.2092992179024789,
            0.2092992179024789,
            0.5917001814331423,
            0.8717401485096066,
            1.0,
        ]
    )
    weight_np = np.array(
        [
            1.0 / 28.0,
            0.21070422714350603,
            0.3411226924835044,
            0.4124587946587038,
            0.4124587946587038,
            0.3411226924835044,
            0.21070422714350603,
            1.0 / 28.0,
        ]
    )
    bary_weights = np.array(
        [1.0 / np.prod([gll_nodes[i] - gll_nodes[j] for j in range(8) if j != i]) for i in range(8)]
    )
    derivative = np.zeros((8, 8))
    for i in range(8):
        for j in range(8):
            if i != j:
                derivative[i, j] = bary_weights[j] / bary_weights[i] / (gll_nodes[i] - gll_nodes[j])
        derivative[i, i] = -np.sum(derivative[i])
    return (weight_np, derivative)


def sine_tables():
    indices = np.arange(10) + 1.0
    sine_basis = np.sqrt(2.0 / 11.0) * np.sin(np.pi * np.outer(indices, indices) / 11.0)
    eigen_vals = 2.0 - 2.0 * np.cos(np.pi * indices / 11.0)
    return (sine_basis, eigen_vals)


WEIGHT, DERIV = gll_tables()
SINE, EIGEN = sine_tables()


def split_const(matrix):
    single = matrix.astype(np.float32)
    high = single.astype(jnp.bfloat16)
    low = (single - high.astype(np.float32)).astype(jnp.bfloat16)
    return high, low


def line_maps(count):
    length = 8 * count
    total = length + 4

    def column(position):
        if 0 <= position < length:
            return position
        return {-2: length, -1: length + 1, length: length + 2, length + 1: length + 3}[position]

    assembled = {}
    for position in range(-2, length + 2):
        row = np.zeros(total)
        row[column(position)] = 1.0
        if 0 <= position < length:
            if position % 8 == 0:
                row[column(position - 1)] += 1.0
            if position % 8 == 7:
                row[column(position + 1)] += 1.0
        assembled[position] = row
    forward = np.zeros((10 * count, total))
    for element in range(count):
        places = [8 * element - 2] + list(range(8 * element, 8 * element + 8)) + [8 * element + 9]
        forward[10 * element : 10 * element + 10] = SINE @ np.stack([assembled[p] for p in places])
    backward = np.zeros((length, 10 * count))
    for element in range(count):
        backward[8 * element : 8 * element + 8, 10 * element : 10 * element + 10] = SINE[1:9]
    for element in range(count - 1):
        first, second = 8 * element + 7, 8 * element + 8
        mean = 0.5 * (backward[first] + backward[second])
        backward[first] = mean
        backward[second] = mean
    return forward, backward


RING = 16
WIDE = ROWS + 2 * RING
REACH = 26
TILE = 48
TILE_B = 32


def ring_maps(reach, depth, inside):
    count = EY + 2 * depth
    forward, _ = line_maps(count)
    length = 8 * count
    columns = np.zeros((10 * count, len(inside)))
    for at, position in enumerate(inside):
        place = None if position is None else position + 8 * depth
        if place is None or place < -2 or place > length + 1:
            continue
        source = place if 0 <= place < length else {-2: 0, -1: 1}.get(place, place - length + 2) + length
        columns[:, at] = forward[:, source]
    _, backward = line_maps(count)
    own = 8 * depth
    rows = np.concatenate(
        [
            backward[own - reach : own + ROWS + reach],
            np.zeros((8, 10 * count)),
        ]
    )
    rows[ROWS + 2 * reach, 10 * depth : 10 * depth + 10] = SINE[1]
    rows[ROWS + 2 * reach + 1, 10 * (depth + EY - 1) : 10 * (depth + EY)] = SINE[8]
    return columns, rows


FZ, BZ = line_maps(1)
TILES = list(range(-REACH, 0)) + [None] * (TILE_B - REACH) + list(range(ROWS))
TILES += list(range(ROWS, ROWS + REACH)) + [None] * (TILE_B - REACH)
FY_A, BY_A = ring_maps(RING, 3, TILES)
FY_B, BY_B = ring_maps(0, 1, list(range(-RING, ROWS + RING)))
STEP_A = 112
STEP_B = 64


def padded(forward, backward, step):
    forward = np.pad(forward, ((0, step - forward.shape[0]), (0, 0)))
    return forward, np.pad(backward, ((0, 0), (0, step - backward.shape[1])))


FY_A, BY_A = padded(FY_A, BY_A, STEP_A)
FY_B, BY_B = padded(FY_B, BY_B, STEP_B)
FX, BX = line_maps(EX)
FX = FX[:, :LANES]


FX_H, FX_L = split_const(FX.T.copy())
BX_H, BX_L = split_const(BX.T.copy())


def wide_const(table):
    high, low = split_const(table)
    return np.concatenate([high, high, low], axis=1)


def pack_tables(tables):
    places, pieces, at = [], [], 0
    for table in tables:
        rows = -(-table.shape[0] // 16) * 16
        extra = ((0, rows - table.shape[0]), (0, 384 - table.shape[1]))
        pieces.append(np.pad(table.astype(np.float32), extra))
        places.append((at, rows, table.shape[1]))
        at += rows
    return np.concatenate(pieces).astype(jnp.bfloat16), places


TABLES, PLACES = pack_tables(
    [
        np.concatenate([FX_H, FX_H], axis=0),
        FX_L,
        BX_H,
        BX_L,
        wide_const(FY_A),
        wide_const(BY_A),
        wide_const(FY_B),
        wide_const(BY_B),
    ]
)


def roll_table():
    table = np.zeros((2, 8, 8, LANES))
    for kind, matrix in enumerate((DERIV, DERIV.T)):
        for k in range(8):
            for i in range(8):
                table[kind, k, i, :] = matrix[i, (i + k) % 8]
    return table.reshape(2 * 64, LANES)


WY = np.tile(WEIGHT, WIDE // 8)
WX = np.tile(WEIGHT, EX)


def inner_count(count):
    mult = np.ones(8 * count)
    position = np.arange(8 * count)
    mult[(position % 8 == 0) & (position > 0)] += 1.0
    mult[(position % 8 == 7) & (position < 8 * count - 1)] += 1.0
    return mult


END_MASS = np.where(np.arange(WIDE) % 8 % 7 == 0, 2.0, 1.0)
INV_MASS = (8.0 / (WY * END_MASS)[:, None] / (WX * inner_count(EX))[None, :]).astype(np.float32)

AT_ROLLS = WIDE
AT_DX = AT_ROLLS + 128
AT_DXT = AT_DX + LANES
AT_SQUARE = AT_DXT + LANES
AT_MASS = AT_SQUARE + 16
AT_SPREAD = AT_MASS + WIDE
AT_EIGEN_Y = AT_SPREAD + EX
AT_EIGEN_X = AT_EIGEN_Y + STEP_A
LAM_Y = np.resize(EIGEN, STEP_A)
LAM_X = np.resize(EIGEN, 8 * LANES).reshape(8, LANES)
PACKED = np.concatenate(
    [
        WY[:, None] * WX[None, :],
        roll_table(),
        np.kron(np.eye(EX), DERIV.T),
        np.kron(np.eye(EX), DERIV),
        np.repeat(DERIV[:, :1] ** 2, LANES, axis=1),
        np.repeat(DERIV[:, 7:] ** 2, LANES, axis=1),
        INV_MASS,
        np.kron(np.eye(EX), np.ones((1, 8))),
        np.repeat(LAM_Y[:, None], LANES, axis=1),
        LAM_X,
    ]
).astype(np.float32)


def parts(values):
    high = values.astype(BF16)
    low = (values - high.astype(F32)).astype(BF16)
    return high, low


def dot(left, right):
    return jnp.dot(left, right, preferred_element_type=F32)


def left_pairs(table, planes):
    results = []
    for i in range(0, len(planes), 2):
        high, low = parts(jnp.concatenate([planes[i], planes[i + 1]], axis=1))
        both = dot(table, jnp.concatenate([high, low, high], axis=0))
        results += [both[:, 0:LANES], both[:, LANES : 2 * LANES]]
    return results


def along_z(values, matrix):
    rows = []
    for i in range(matrix.shape[0]):
        total = None
        for j in range(matrix.shape[1]):
            if matrix[i, j] == 0.0:
                continue
            term = float(matrix[i, j]) * values[j]
            total = term if total is None else total + term
        rows.append(total)
    return rows


def along_y(values, packed, kind):
    count, rows = values.shape[:2]
    grouped = values.reshape(count * rows // 8, 8, LANES)
    start = AT_ROLLS + 64 * kind
    total = packed[start : start + 8][None] * grouped
    for k in range(1, 8):
        total = total + packed[start + 8 * k : start + 8 * k + 8][None] * pltpu.roll(grouped, 8 - k, 1)
    return total.reshape(count, rows, LANES)


def along_x(values, packed, kind):
    start = AT_DXT if kind else AT_DX
    high, low = parts(packed[start : start + LANES])
    first, rest = parts(values.reshape(values.shape[0] * values.shape[1], LANES))
    total = dot(
        jnp.concatenate([first, rest], axis=1), jnp.concatenate([high, high], axis=0)
    ) + dot(first, low)
    return total.reshape(values.shape)


def stack(planes):
    return jnp.concatenate([plane[None] for plane in planes], axis=0)


def edge_rows(rows, low, high):
    position = lax.broadcasted_iota(jnp.int32, (rows, LANES), 0)
    return jnp.where(position == 0, low, jnp.where(position == rows - 1, high, 1.0))


def local_operator(values, flux, packed):
    plane_w = packed[0 : values.shape[1]]
    gz = along_z([values[i] for i in range(8)], DERIV)
    fz = along_z([flux[i] * gz[i] for i in range(8)], DERIV.T)
    total = along_y(flux * along_y(values, packed, 0), packed, 1)
    total = total + along_x(flux * along_x(values, packed, 0), packed, 1)
    planes = [
        total[i] + fz[i] + (HELM_COEF * 0.125 * float(WEIGHT[i])) * (plane_w * values[i])
        for i in range(8)
    ]
    return stack(planes)


def add_planes(own, low_z, high_z):
    planes = [own[i] for i in range(8)]
    planes[0] = planes[0] + low_z
    planes[7] = planes[7] + high_z
    return stack(planes)


def solve_elements(planes, packed, tables, kind):
    def table(index):
        at, rows, width = PLACES[index]
        return tables[at : at + rows, 0:width]

    fxhh, fxl, bxh, bxl = (table(index) for index in range(4))
    spectral = left_pairs(table(4 + 2 * kind), along_z(planes, FZ))
    high, low = parts(jnp.concatenate(spectral, axis=0))
    wide = dot(jnp.concatenate([high, low], axis=1), fxhh) + dot(high, fxl)
    step = PLACES[4 + 2 * kind][1]
    column = packed[AT_EIGEN_Y : AT_EIGEN_Y + step]
    rest = 10 * EX - LANES
    lam = jnp.concatenate(
        [
            column + packed[AT_EIGEN_X : AT_EIGEN_X + 1],
            column[:, 0:rest] + packed[AT_EIGEN_X + 1 : AT_EIGEN_X + 2, 0:rest],
        ],
        axis=1,
    )
    scaled = [
        wide[step * i : step * (i + 1)]
        / (SCHWARZ_SCALE * lam + float(SCHWARZ_SCALE * EIGEN[i] + SCHWARZ_SHIFT))
        for i in range(10)
    ]
    high, low = parts(jnp.concatenate(scaled, axis=0))
    back = dot(high, bxh) + dot(low, bxh) + dot(high, bxl)
    back = left_pairs(table(5 + 2 * kind), [back[step * i : step * (i + 1)] for i in range(10)])
    return along_z(back, BZ)


def store_faces(planes, near, out_ref, low_ref, high_ref):
    planes[0] = planes[0] * near[0]
    planes[7] = planes[7] * near[1]
    for i in range(8):
        out_ref[i] = planes[i]
    low_ref[...] = planes[0]
    high_ref[...] = planes[7]


def ring_rows(near):
    row = lax.broadcasted_iota(jnp.int32, (WIDE, LANES), 0)
    return row, 2.0 - 2.0 * near[2], 2.0 - 2.0 * near[3]


def partition_total(own, low_z, high_z, low_y, high_y, near):
    def planes(array):
        total = near[0] * array[0] + near[1] * array[7]
        for i in range(1, 7):
            total = total + array[i]
        return total

    total = planes(own) + 0.5 * (low_z[1] + high_z[0])
    below = planes(low_y) + 0.5 * (low_y[9] + low_y[10])
    above = planes(high_y) + 0.5 * (high_y[9] + high_y[10])
    faces = 0.5 * (below[REACH - 1 : REACH] + above[0:1])
    return jnp.sum(total * edge_rows(ROWS, near[2], near[3])) + jnp.sum(faces)


def lane_row(entries):
    lane = lax.broadcasted_iota(jnp.int32, (1, LANES), 1)
    row = jnp.zeros((1, LANES), F32)
    for index, value in enumerate(entries):
        row = jnp.where(lane == index, value, row)
    return row


def advect_kernel(
    lev_in, vel_in, src_in, packed_in, solid_in, b_ref, l_ref, zlo, zhi, solid_ref,
    lev, vel, src, packed, solid, sems,
):
    copies = [
        pltpu.make_async_copy(source, target, sems.at[index])
        for index, (source, target) in enumerate(
            (
                (vel_in, vel), (lev_in, lev), (packed_in, packed), (src_in, src), (solid_in, solid),
            )
        )
    ]
    for copy in copies:
        copy.start()
    for copy in copies:
        copy.wait()
    spread = packed[AT_SPREAD : AT_SPREAD + EX].astype(BF16)
    in_solid = dot(solid[...].astype(F32).astype(BF16), spread)
    solid_ref[...] = jnp.concatenate([in_solid, jnp.zeros((8 - EY, LANES), F32)], axis=0)
    level = lev[...]
    v0, v1, v2 = vel[0], vel[1], vel[2]
    gz = stack(along_z([level[i] for i in range(8)], DERIV))
    advect = v0 * gz + v1 * along_y(level, packed, 0) + v2 * along_x(level, packed, 0)
    moved = level - (2.0 * TIME_STEP) * advect
    diverge = stack(along_z([v0[i] for i in range(8)], DERIV))
    diverge = diverge + along_y(v1, packed, 0) + along_x(v2, packed, 0)
    force = src[...] - (2.0 * TIME_STEP) * diverge
    weights = packed[0:ROWS]
    for i in range(8):
        mass = (0.125 * float(WEIGHT[i])) * weights
        term = mass * force[i]
        moved_i = mass * moved[i]
        b_ref[i] = term
        l_ref[i] = moved_i
        if i < 2:
            zlo[i] = term
        if i == 0:
            zlo[2] = moved_i
        if i > 5:
            zhi[i - 6] = term
        if i == 7:
            zhi[2] = moved_i


def rim_kernel(solid, b, l, low_z, high_z, low_y, high_y):
    in_solid = solid[...]
    rest = TILE - REACH - RING - 1

    def rows(planes, at, level, far, extra=None):
        start = ROWS - REACH if far else 0
        pieces = [planes[at, start : start + REACH]]
        if level is None:
            pieces.append(jnp.zeros((RING + 1, LANES), F32))
        else:
            array, index = level
            start = ROWS - RING - 1 if far else 0
            pieces.append(array[index, start : start + RING + 1])
        if extra is None:
            pieces.append(jnp.zeros((rest, LANES), F32))
        else:
            pieces += [extra, jnp.zeros((rest - 2, LANES), F32)]
        return jnp.concatenate(pieces, axis=0)

    for far, out in ((False, low_y), (True, high_y)):
        extra = in_solid[EY - 2 : EY] if far else in_solid[0:2]
        for i in range(8):
            out[i] = rows(b, i, (l, i), far, extra if i == 0 else None)
        for i in range(2):
            out[8 + i] = rows(low_z, i, (low_z, 2) if i == 1 else None, far)
            out[10 + i] = rows(high_z, i, (high_z, 2) if i == 0 else None, far)


def level_kernel(
    near, solid, packed, b, l, zlo, zhi, ylo, yhi, level_ref, flux_ref, stat
):
    row, has_low, has_high = ring_rows(near)
    at = REACH

    def wide_rows(slot, own):
        return jnp.concatenate(
            [ylo[slot, at + 1 : at + 1 + RING], own, yhi[slot, at : at + RING]], axis=0
        )

    planes = []
    for i in range(8):
        plane = wide_rows(i, l[i])
        first = ylo[i, at : at + 1]
        last = yhi[i, at + RING : at + RING + 1]
        if i == 0:
            plane = plane + wide_rows(9, zlo[2])
            first = first + ylo[9, at : at + 1]
            last = last + yhi[9, at + RING : at + RING + 1]
        if i == 7:
            plane = plane + wide_rows(10, zhi[2])
            first = first + ylo[10, at : at + 1]
            last = last + yhi[10, at + RING : at + RING + 1]
        before = jnp.where(row == 0, first, pltpu.roll(plane, 1, 0))
        after = jnp.where(row == WIDE - 1, last, pltpu.roll(plane, WIDE - 1, 0))
        plane = plane + jnp.where(row % 8 == 0, before, jnp.where(row % 8 == 7, after, 0.0))
        planes.append(plane)
    own = stack(planes)
    lane = lax.broadcasted_iota(jnp.int32, (8, WIDE, LANES), 2)
    before = jnp.where((lane % 8 == 0) & (lane > 0), pltpu.roll(own, 1, 2), 0.0)
    after = jnp.where((lane % 8 == 7) & (lane < LANES - 1), pltpu.roll(own, LANES - 1, 2), 0.0)
    own = own + before + after
    ends = jnp.where(row == RING, 2.0 * near[2], jnp.where(row == RING + ROWS - 1, 2.0 * near[3], 1.0))
    inverse = packed[AT_MASS : AT_MASS + WIDE] * ends
    in_solid = solid[...]
    solids = [ylo[0, at + RING + 1 + k : at + RING + 2 + k] for k in range(2)]
    solids += [in_solid[e : e + 1] for e in range(EY)]
    solids += [yhi[0, at + RING + 1 + k : at + RING + 2 + k] for k in range(2)]
    open_part = jnp.concatenate(
        [jnp.broadcast_to(1.0 - (1.0 - SOLID_FACTOR) * rows, (8, LANES)) for rows in solids], axis=0
    )
    in_grid = jnp.where(row < RING, has_low, jnp.where(row >= RING + ROWS, has_high, 1.0))
    flux_w = packed[0:WIDE] * in_grid
    total = jnp.zeros((ROWS, LANES), F32)
    fluxes = []
    for i in range(8):
        scale = 1.0 / float(WEIGHT[i])
        plane = own[i] * (inverse * scale)
        if i == 0:
            plane = plane * near[0]
        if i == 7:
            plane = plane * near[1]
        level_ref[i] = plane[RING : RING + ROWS]
        liquid = jax.nn.sigmoid(plane * (1.0 / LEVEL_WIDTH))
        coef = (GAS_RATIO - (GAS_RATIO - 1.0) * liquid) * open_part
        total = total + coef[RING : RING + ROWS]
        flux = (0.5 * float(WEIGHT[i])) * (coef * flux_w)
        flux_ref[i] = flux
        fluxes.append(flux[RING : RING + ROWS])
    kbar = jnp.sum(total) * (1.0 / (8 * ROWS * LANES))
    entries = [kbar, partition_total(b, zlo, zhi, ylo, yhi, near)] + [0.0] * 9
    for first, second in ((0, 0), (0, 7), (7, 7)):
        slopes = along_z(fluxes, (DERIV[:, first] * DERIV[:, second])[None, :])[0]
        column = jnp.sum(slopes, axis=1, keepdims=True)
        entries += [jnp.sum(column, axis=0, keepdims=True), column[0:1], column[ROWS - 1 : ROWS]]
    inner = fluxes[0] + fluxes[1]
    for i in range(2, 8):
        inner = inner + fluxes[i]
    for at_row, start in ((0, 0), (ROWS - 8, 8)):
        square = packed[AT_SQUARE + start : AT_SQUARE + start + 8]
        entries += [
            jnp.sum(square * plane[at_row : at_row + 8]) for plane in (inner, fluxes[0], fluxes[7])
        ]
    stat[...] = lane_row(entries)


def first_schwarz_kernel(
    near, packed, tables, b, zlo, zhi, ylo, yhi, w_ref, wlo, whi
):
    own = [b[i] for i in range(8)] + [zlo[0], zlo[1], zhi[0], zhi[1]]
    planes = [
        jnp.concatenate([ylo[i, 0:TILE_B], own[i], yhi[i, 0:TILE_B]], axis=0) for i in range(12)
    ]
    planes = solve_elements(planes, packed, tables, 0)
    row, has_low, has_high = ring_rows(near)
    in_grid = jnp.where(row < RING, has_low, jnp.where(row >= RING + ROWS, has_high, 1.0))
    in_grid = jnp.where(row == RING, has_low, jnp.where(row == RING + ROWS - 1, has_high, in_grid))
    for i in range(8):
        first = (1.0 - has_low) * planes[i][WIDE : WIDE + 1]
        last = (1.0 - has_high) * planes[i][WIDE + 1 : WIDE + 2]
        alone = jnp.where(row == RING, first, jnp.where(row == RING + ROWS - 1, last, 0.0))
        planes[i] = planes[i][0:WIDE] * in_grid + alone
    store_faces(planes, near, w_ref, wlo, whi)


def galerkin_kernel(near, packed, stat_in, flux, w, zlo, zhi, zl_ref, y_ref, ylo, yhi, stat):
    local = add_planes(w, zlo[...], zhi[...])
    zl_ref[...] = local
    applied = local_operator(local, flux[...], packed)
    y_ref[...] = applied
    fluxes = [flux[i] for i in range(8)]
    for out, rows in ((ylo, (0, 1)), (yhi, (6, 7))):
        for k, i in enumerate(rows):
            out[k] = applied[i]
            for t, end in enumerate((0, 7)):
                out[2 + 2 * t + k] = along_z(fluxes, (DERIV[:, i] * DERIV[:, end])[None, :])[0]
            out[6 + k] = fluxes[i]
    applied = applied[:, RING : RING + ROWS]
    inner = near[0] * applied[0] + near[1] * applied[7]
    for i in range(1, 7):
        inner = inner + applied[i]
    edge = edge_rows(ROWS, near[2], near[3])
    entries = [0.0, 0.0]
    for plane in ((1.0 - near[0]) * applied[0], inner, (1.0 - near[1]) * applied[7]):
        entries += [
            (1.0 - near[2]) * jnp.sum(plane[0:1]),
            jnp.sum(edge * plane),
            (1.0 - near[3]) * jnp.sum(plane[ROWS - 1 : ROWS]),
        ]
    stat[...] = jnp.broadcast_to(stat_in[...] + lane_row(entries), stat.shape)


def column_kernel(gathered, out_ref):
    values = gathered[...]
    sub = lax.broadcasted_iota(jnp.int32, (8, LANES), 0)
    lane = lax.broadcasted_iota(jnp.int32, (8, LANES), 1)
    after = jnp.where(sub < 7, pltpu.roll(values, 7, 0), 0.0)
    before = jnp.where(sub > 0, pltpu.roll(values, 1, 0), 0.0)
    first = lax.broadcasted_iota(jnp.int32, (8, 1), 0) == 0
    last = lax.broadcasted_iota(jnp.int32, (8, 1), 0) == 7

    def column(array, index):
        return array[:, index : index + 1]

    def slopes(array, pair):
        whole, low, high = (column(array, 11 + 3 * pair + k) for k in range(3))
        return whole - low - high, low, high

    merged = [column(values, 0), column(values, 1)]
    for b in range(3):
        merged.append(column(values, 5 + b) + column(after, 2 + b) + column(before, 8 + b))
    merged += [own + other for own, other in zip(slopes(values, 0), slopes(before, 2), strict=True)]
    merged += list(slopes(values, 1))
    inside, interface = [], []
    for side in range(2):
        whole, low, high = (column(values, 20 + 3 * side + k) for k in range(3))
        ends = jnp.where(first, low, 0.0) + jnp.where(last, high, 0.0)
        inside.append(whole - low - high + ends)
        interface.append(jnp.where(first, 0.0, low) + column(before, 22 + 3 * side))
    rows = jnp.zeros((8, LANES), F32)
    for index, value in enumerate(merged + inside + interface):
        rows = jnp.where(lane == index, value, rows)
    total = rows[0:1]
    for i in range(1, 8):
        total = total + pltpu.roll(rows[i : i + 1], 16 * i, 1)
    out_ref[...] = jnp.broadcast_to(total, out_ref.shape)


def invert(blocks, sub):
    for k in range(8):
        pivot = 1.0 / blocks[k][k : k + 1]
        scaled = jnp.where(sub == k, pivot, blocks[k] * pivot)
        rows = []
        for r in range(8):
            if r == k:
                rows.append(scaled)
            else:
                rest = jnp.where(sub == k, 0.0, blocks[r])
                rows.append(rest - blocks[r][k : k + 1] * scaled)
        blocks = rows
    return blocks


def multiply(left, right):
    rows = []
    for r in range(8):
        total = left[r][0:1] * right[0]
        for k in range(1, 8):
            total = total + left[r][k : k + 1] * right[k]
        rows.append(total)
    return rows


def matvec(terms, sub):
    result = jnp.zeros_like(terms[0][1])
    for r in range(8):
        product = terms[0][0][r] * terms[0][1]
        for blocks, column in terms[1:]:
            product = product + blocks[r] * column
        result = jnp.where(sub == r, jnp.sum(product, axis=0, keepdims=True), result)
    return result


def coarse_operator(c, count, sums_z, couplings_z, inside_y, interface_y):
    sub = lax.broadcasted_iota(jnp.int32, c.shape, 0)
    lane = lax.broadcasted_iota(jnp.int32, c.shape, 1)
    has_low = lane > 0
    has_high = lane < count - 1

    def after(array):
        return jnp.where(sub < 7, pltpu.roll(array, 7, 0), 0.0)

    def before(array):
        return jnp.where(sub > 0, pltpu.roll(array, 1, 0), 0.0)

    def right(array):
        return jnp.where(has_high, pltpu.roll(array, LANES - 1, 1), 0.0)

    def left(array):
        return jnp.where(has_low, pltpu.roll(array, 1, 1), 0.0)

    on_low = jnp.where(has_low, 0.5 * (c + left(c)), c)
    on_high = jnp.where(has_high, 0.5 * (c + right(c)), c)
    tested = []
    for place, value in enumerate((c, on_low, on_high)):
        slope = jnp.where(sub > 0, 0.5 * (value - before(value)), 0.0)
        coupling = couplings_z[place]
        force = sums_z[place] * slope - coupling * after(slope) - before(coupling * slope)
        force = jnp.where(sub > 0, force, 0.0)
        tested.append(0.5 * (force - after(force)))
    result = tested[0] + jnp.where(has_low, 0.5, 1.0) * tested[1] + jnp.where(has_high, 0.5, 1.0) * tested[2]
    result = result + 0.5 * right(tested[1]) + 0.5 * left(tested[2])

    interface = jnp.where(sub > 0, 0.5 * (c + before(c)), 0.0)
    for side, (move, there) in enumerate(((left, has_low), (right, has_high))):
        force = inside_y[side] * jnp.where(there, 0.5 * (move(c) - c), 0.0)
        face = interface_y[side] * jnp.where(there, 0.5 * (move(interface) - interface), 0.0)
        force = force + 0.5 * (face + after(face))
        back = right if side == 0 else left
        result = result + 0.5 * (back(force) - force)

    end = float(WEIGHT[0])
    mass = (2.0 - 2.0 * end) * c + end * (interface + after(interface))
    mass = mass + jnp.where((sub == 0) | (sub == 7), end * c, 0.0)
    beside = jnp.where(has_low, 0.5 * (mass + left(mass)), 0.0)
    scaled = (2.0 * EY - 2.0 * end) * mass + end * (beside + right(beside))
    scaled = scaled + jnp.where(has_low, 0.0, end * mass) + jnp.where(has_high, 0.0, end * mass)
    return result + HELM_COEF / 8.0 * float(np.sum(WX)) * scaled


def coarse_kernel(count, near, gathered, out_ref, wide, turned):
    lanes = LANES
    sub = lax.broadcasted_iota(jnp.int32, (8, lanes), 0)
    lane = lax.broadcasted_iota(jnp.int32, (8, lanes), 1)
    wide[...] = jnp.zeros((LANES, LANES), F32)
    wide[0:count] = gathered[...]
    turned[...] = wide[...].T

    def value(index):
        return turned[pl.ds(index, 8, stride=16), :]

    def move(array, dz, dy):
        if dz:
            array = pltpu.roll(array, (-dz) % 8, 0)
        if dy:
            array = pltpu.roll(array, (-dy) % lanes, 1)
        return array

    kbar = jnp.where(lane < count, value(0), 1.0)
    above = move(kbar, 1, 0)
    link_z = jnp.where(sub < 7, 2.0 * kbar * above / (kbar + above) * (EY * EX / EZ), 0.0)
    link_z = jnp.where(lane < count, link_z, 0.0)
    beside = move(kbar, 0, 1)
    link_y = 2.0 * kbar * beside / (kbar + beside) * (EZ * EX / EY)
    link_y = jnp.where(lane < count - 1, link_y, 0.0)
    back_z = move(link_z, -1, 0)
    back_y = move(link_y, 0, -1)
    diagonal = HELM_COEF * EZ * EY * EX + link_z + back_z + link_y + back_y
    blocks = []
    for r in range(8):
        row = jnp.where(sub == r, diagonal, 0.0)
        row = jnp.where(sub == r + 1, -back_z, row)
        row = jnp.where(sub == r - 1, -link_z, row)
        blocks.append(row)
    inverse = invert(blocks, sub)
    down = [-back_y[r : r + 1] * move(inverse[r], 0, -1) for r in range(8)]
    up = [-link_y[r : r + 1] * move(inverse[r], 0, 1) for r in range(8)]
    levels = [(1, down, up)]
    link_before, link_after = move(link_y, 0, -1), move(back_y, 0, 1)
    blocks = [blocks[r] + down[r] * link_before + up[r] * link_after for r in range(8)]
    lower = [row * move(back_y, 0, -1) for row in down]
    upper = [row * move(link_y, 0, 1) for row in up]
    step = 2
    while step < count:
        inverse = invert(blocks, sub)
        down = multiply(lower, [move(row, 0, -step) for row in inverse])
        up = multiply(upper, [move(row, 0, step) for row in inverse])
        levels.append((step, down, up))
        before_u = multiply(down, [move(row, 0, -step) for row in upper])
        after_l = multiply(up, [move(row, 0, step) for row in lower])
        if 2 * step < count:
            new_lower = multiply(down, [move(row, 0, -step) for row in lower])
            new_upper = multiply(up, [move(row, 0, step) for row in upper])
            lower = [-row for row in new_lower]
            upper = [-row for row in new_upper]
        blocks = [blocks[r] - before_u[r] - after_l[r] for r in range(8)]
        step *= 2
    inverse = invert(blocks, sub)

    def solve(column):
        for distance, down, up in levels:
            pulled = matvec(
                [(down, move(column, 0, -distance)), (up, move(column, 0, distance))], sub
            )
            column = column - pulled
        return matvec([(inverse, column)], sub)

    first = solve(value(1))
    totals = coarse_operator(
        first,
        count,
        [value(5 + k) for k in range(3)],
        [value(8 + k) for k in range(3)],
        [value(11), value(12)],
        [value(13), value(14)],
    )
    totals = totals + value(3)
    totals = totals + jnp.where(lane < count - 1, move(value(2), 0, 1), 0.0)
    totals = totals + jnp.where(lane > 0, move(value(4), 0, -1), 0.0)
    totals = jnp.where(lane < count, totals, 0.0)
    second = solve(totals)
    mine = (sub.astype(F32) == near[4]) & (lane.astype(F32) == near[5])

    def store(at, solved, reach):
        for a in range(-reach, reach + 1):
            for b in range(-1, 2):
                picked = jnp.sum(jnp.where(mine, move(solved, a, b), 0.0))
                row = at + 3 * (a + reach) + b + 1
                out_ref[row : row + 1] = jnp.full((1, lanes), picked)

    store(0, first, 2)
    store(16, second, 1)


def coarse_columns(near, coarse, start, count):
    row, has_low, has_high = ring_rows(near)
    below = jnp.where(row < RING - 1, 1.0, jnp.where(row <= RING, 0.5, 0.0)) * has_low
    above = jnp.where(row > RING + ROWS, 1.0, jnp.where(row >= RING + ROWS - 1, 0.5, 0.0)) * has_high
    edge = jnp.where((row > RING) & (row < RING + ROWS - 1), 1.0, 0.0)
    edge = jnp.where(row == RING, near[2], jnp.where(row == RING + ROWS - 1, near[3], edge))
    edge = jnp.where(row == RING - 1, 0.5 * has_low, edge)
    edge = jnp.where(row == RING + ROWS, 0.5 * has_high, edge)
    columns = []
    for a in range(count):
        at = start + 3 * a
        columns.append(
            below * coarse[at : at + 1] + edge * coarse[at + 1 : at + 2] + above * coarse[at + 2 : at + 3]
        )
    return columns


def coarse_planes(columns, low, high):
    before, inside, after = columns
    return inside, low * (before - inside), high * (after - inside)


def add_coarse(local, columns):
    inside, first, last = columns
    planes = [local[i] + inside for i in range(8)]
    planes[0] = planes[0] + first
    planes[7] = planes[7] + last
    return stack(planes)


def coarse_applied(columns, flux, packed):
    inside, first, last = columns
    slopes = [
        flux[i] * (float(DERIV[i, 0]) * first + float(DERIV[i, 7]) * last) for i in range(8)
    ]
    fz = along_z(slopes, DERIV.T)
    three = stack([inside + first, inside, inside + last])
    gy = along_y(three, packed, 0)
    fy = along_y(
        stack([flux[i] * gy[0 if i == 0 else 2 if i == 7 else 1] for i in range(8)]), packed, 1
    )
    plane_w = packed[0:WIDE]
    planes = []
    for i in range(8):
        plane = three[0 if i == 0 else 2 if i == 7 else 1]
        planes.append(fz[i] + fy[i] + (HELM_COEF * 0.125 * float(WEIGHT[i])) * (plane_w * plane))
    return stack(planes)


def face_applied(planes, payload, packed, rows, in_grid):
    inside, first, last = planes
    fields = [inside + (first if i == 0 else last if i == 7 else 0.0) for i in rows]
    gy = along_y(stack(fields), packed, 0)
    fy = along_y(stack([payload[6 + k] * gy[k] for k in range(2)]), packed, 1)
    plane_w = packed[0:WIDE]
    result = []
    for k, i in enumerate(rows):
        slopes = payload[2 + k] * first + payload[4 + k] * last
        mass = (HELM_COEF * 0.125 * float(WEIGHT[i])) * in_grid * (plane_w * fields[k])
        result.append(payload[k] + slopes + fy[k] + mass)
    return result


def apply_kernel(
    near, packed, tables, coarse, flux, zl, yl, ylo, yhi,
    z_ref, y_ref, w_ref, wlo, whi,
):
    columns = coarse_columns(near, coarse, 0, 5)
    own = coarse_planes(columns[1:4], 1.0 - near[0], 1.0 - near[1])
    field = add_coarse(zl[...], own)[:, RING : RING + ROWS]
    z_ref[...] = field
    applied = yl[...] + coarse_applied(own, flux[...], packed)
    y_ref[...] = applied[:, RING : RING + ROWS]
    lower = coarse_planes(columns[0:3], 1.0 - near[7], 0.5)
    upper = coarse_planes(columns[2:5], 0.5, 1.0 - near[6])
    planes = [applied[i] for i in range(8)]
    planes += face_applied(lower, ylo, packed, (6, 7), 2.0 - 2.0 * near[0])
    planes += face_applied(upper, yhi, packed, (0, 1), 2.0 - 2.0 * near[1])
    planes = solve_elements(planes, packed, tables, 1)
    row = lax.broadcasted_iota(jnp.int32, (ROWS, LANES), 0)
    _, has_low, has_high = ring_rows(near)
    in_grid = jnp.where(row == 0, has_low, jnp.where(row == ROWS - 1, has_high, 1.0))
    for i in range(8):
        first = (1.0 - has_low) * planes[i][ROWS : ROWS + 1]
        last = (1.0 - has_high) * planes[i][ROWS + 1 : ROWS + 2]
        alone = jnp.where(row == 0, first, jnp.where(row == ROWS - 1, last, 0.0))
        planes[i] = planes[i][0:ROWS] * in_grid + alone
    store_faces(planes, near, w_ref, wlo, whi)


def second_kernel(near, packed, coarse, flux, b, y, z, w, x_ref, kx_ref, stat):
    columns = [column[RING : RING + ROWS] for column in coarse_columns(near, coarse, 16, 3)]
    field = add_coarse(w[...], coarse_planes(columns, 1.0 - near[0], 1.0 - near[1]))
    x_ref[...] = field
    fluxes = flux[:, RING : RING + ROWS]
    gz = along_z([field[i] for i in range(8)], DERIV)
    gy = along_y(field, packed, 0)
    gx = along_x(field, packed, 0)
    slopes = [fluxes[i] * gz[i] for i in range(8)]
    ends = (0, 7)
    back = along_z(slopes, DERIV.T[[0, 7]])
    back_y = along_y(stack([fluxes[i] * gy[i] for i in ends]), packed, 1)
    back_x = along_x(stack([fluxes[i] * gx[i] for i in ends]), packed, 1)
    plane_w = packed[0:ROWS]
    mass = HELM_COEF * 0.125
    for k, i in enumerate(ends):
        weighted = (mass * float(WEIGHT[i])) * (plane_w * field[i])
        kx_ref[k] = back[k] + back_y[k] + back_x[k] + weighted
    energy = None
    for i in range(8):
        term = slopes[i] * gz[i] + fluxes[i] * (gy[i] * gy[i] + gx[i] * gx[i])
        term = term + (mass * float(WEIGHT[i])) * (plane_w * field[i] * field[i])
        energy = term if energy is None else energy + term
    first, right = z[...], b[...]
    sums = [right * first, y[...] * first, right * field, y[...] * field]
    stat[...] = lane_row([jnp.sum(term) for term in sums] + [jnp.sum(energy)])


def face_kernel(packed, flux, b, y, kx, zlo, zhi, stat_in, stat):
    faces = stack([zlo[...], zhi[...]])
    fluxes = flux[:, RING : RING + ROWS]
    gy = along_y(faces, packed, 0)
    gx = along_x(faces, packed, 0)
    plane_w = packed[0:ROWS]
    energy = 2.0 * (kx[0] * faces[0] + kx[1] * faces[1])
    for k, i in enumerate((0, 7)):
        mass = (HELM_COEF * 0.125 * float(WEIGHT[i])) * (plane_w * faces[k] * faces[k])
        energy = energy + mass + fluxes[i] * (gy[k] * gy[k] + gx[k] * gx[k])
    for i in range(8):
        slope = float(DERIV[i, 0]) * faces[0] + float(DERIV[i, 7]) * faces[1]
        energy = energy + fluxes[i] * slope * slope
    sums = [
        0.0,
        0.0,
        jnp.sum(b[0] * faces[0] + b[7] * faces[1]),
        jnp.sum(y[0] * faces[0] + y[7] * faces[1]),
        jnp.sum(energy),
    ]
    stat[...] = jnp.broadcast_to(stat_in[...] + lane_row(sums), stat.shape)


def combine_kernel(sums, z, x, zlo, zhi, p_ref):
    total = jnp.sum(sums[...], axis=0, keepdims=True)
    rz, pap, rq, aq, qhq = (total[:, k : k + 1] for k in range(5))
    step = rz / pap
    rz_next = step * (step * aq - rq)
    beta = rz_next / rz
    grown = 1.0 + beta
    curved = grown * grown * pap - 2.0 * step * grown * aq + step * step * qhq
    step_next = rz_next / curved
    on_z = step + step_next * grown
    on_q = step_next * step
    for i in range(8):
        plane = x[i]
        if i == 0:
            plane = plane + zlo[...]
        if i == 7:
            plane = plane + zhi[...]
        p_ref[i] = on_z * z[i] - on_q * plane


def run(kernel, outs, smem, args, scratch=(), flops=1000000, place=VMEM, limit=LIMIT):
    nbytes = sum(4 * int(np.prod(out)) for out in outs) * 2
    return pl.pallas_call(
        kernel,
        out_shape=[jax.ShapeDtypeStruct(out, F32) for out in outs],
        in_specs=[pl.BlockSpec(memory_space=SMEM) for _ in smem]
        + [pl.BlockSpec(memory_space=place) for _ in args],
        out_specs=[pl.BlockSpec(memory_space=VMEM) for _ in outs],
        scratch_shapes=list(scratch),
        compiler_params=pltpu.CompilerParams(vmem_limit_bytes=limit),
        cost_estimate=pl.CostEstimate(flops=flops, bytes_accessed=nbytes, transcendentals=0),
    )(*smem, *args)


def shift(axis, low_face, high_face):
    count = lax.axis_size(axis)
    forward = [(i, i + 1) for i in range(count - 1)]
    backward = [(target, source) for source, target in forward]
    return lax.ppermute(high_face, axis, forward), lax.ppermute(low_face, axis, backward)


def body(level_set, velocity, source, wick_solid):
    block = level_set.shape
    count_gx = lax.axis_size("gx")
    count_gy = lax.axis_size("gy")
    index_gx = lax.axis_index("gx")
    index_gy = lax.axis_index("gy")

    def ends(index, count):
        return [jnp.where(index > 0, 0.5, 1.0), jnp.where(index < count - 1, 0.5, 1.0)]

    place = [index_gx.astype(F32), index_gy.astype(F32)]
    beyond = [
        jnp.where(index_gx < count_gx - 2, 0.5, 1.0),
        jnp.where(index_gx > 1, 0.5, 1.0),
    ]
    near = jnp.stack(ends(index_gx, count_gx) + ends(index_gy, count_gy) + place + beyond)
    near = near.astype(F32)
    packed = jnp.asarray(PACKED)
    tables = jnp.asarray(TABLES)
    face = (ROWS, LANES)
    wide_block = (8, WIDE, LANES)
    wide_face = (WIDE, LANES)
    rim = (12, TILE, LANES)

    b, l, zlo, zhi, solid = run(
        advect_kernel,
        [block, block, (3, *face), (3, *face), (8, LANES)],
        [],
        [
            pltpu.with_memory_space_constraint(array, pltpu.HBM)
            for array in (level_set, velocity, source, packed, wick_solid.reshape(EY, EX))
        ],
        [VMEM(block, F32), VMEM((3, *block), F32), VMEM(block, F32), VMEM(PACKED.shape, F32)]
        + [VMEM((EY, EX), jnp.int32), pltpu.SemaphoreType.DMA((5,))],
        place=pltpu.HBM,
    )
    zlo, zhi = shift("gx", zlo, zhi)
    ylo, yhi = run(rim_kernel, [rim, rim], [], [solid, b, l, zlo, zhi])
    ylo, yhi = shift("gy", ylo, yhi)
    w, wlo, whi = run(
        first_schwarz_kernel,
        [wide_block, wide_face, wide_face],
        [near],
        [packed, tables, b, zlo, zhi, ylo, yhi],
    )
    wlo, whi = shift("gx", wlo, whi)
    level_new, flux, stat = run(
        level_kernel,
        [block, wide_block, (1, LANES)],
        [near],
        [solid, packed, b, l, zlo, zhi, ylo, yhi],
        flops=20000000,
    )
    zl, yl, zlo, zhi, stat = run(
        galerkin_kernel,
        [wide_block, wide_block, wide_block, wide_block, (count_gx, LANES)],
        [near],
        [packed, stat, flux, w, wlo, whi],
    )
    zlo, zhi = shift("gx", zlo, zhi)
    gathered = lax.all_to_all(stat, "gx", 0, 0, tiled=True)
    (column,) = run(column_kernel, [(count_gy, LANES)], [], [gathered])
    gathered = lax.all_to_all(column, "gy", 0, 0, tiled=True)
    (coarse,) = run(
        functools.partial(coarse_kernel, count_gy),
        [(32, LANES)],
        [near],
        [gathered],
        [VMEM((LANES, LANES), F32), VMEM((LANES, LANES), F32)],
    )
    z, y, w, wlo, whi = run(
        apply_kernel,
        [block, block, block, face, face],
        [near],
        [packed, tables, coarse, flux, zl, yl, zlo, zhi],
    )
    zlo, zhi = shift("gx", wlo, whi)
    x, kx, sums = run(
        second_kernel,
        [block, (2, *face), (1, LANES)],
        [near],
        [packed, coarse, flux, b, y, z, w],
        flops=20000000,
    )
    (sums,) = run(
        face_kernel, [(count_gx, LANES)], [], [packed, flux, b, y, kx, zlo, zhi, sums]
    )
    tile = lax.all_to_all(sums, "gx", 0, 0, tiled=True)
    wide = jnp.broadcast_to(jnp.sum(tile, axis=0, keepdims=True), (count_gy, LANES))
    wide = lax.all_to_all(wide, "gy", 0, 0, tiled=True)
    (pressure,) = run(combine_kernel, [block], [], [wide, z, x, zlo, zhi])
    return (level_new, pressure)


def solution(mesh):
    placed = (
        P("gx", "gy", None),
        P(None, "gx", "gy", None),
        P("gx", "gy", None),
        P("gx", "gy", None),
    )
    return jax.shard_map(
        body,
        mesh=mesh,
        in_specs=placed,
        out_specs=(P("gx", "gy", None), P("gx", "gy", None)),
        check_vma=False,
    )
```

```python
import functools

import jax
import jax.numpy as jnp
import numpy as np
from jax import lax
from jax.experimental import pallas as pl
from jax.experimental.pallas import tpu as pltpu
from jax.sharding import PartitionSpec as P

EZ = 1
EY = 4
EX = 16
ROWS = 8 * EY
LANES = 8 * EX

TIME_STEP = 0.02
HELM_COEF = 0.25
LEVEL_WIDTH = 0.25
GAS_RATIO = 10.0
SOLID_FACTOR = 0.25
SCHWARZ_SCALE = 0.5
SCHWARZ_SHIFT = 0.05

F32 = jnp.float32
BF16 = jnp.bfloat16
VMEM = pltpu.VMEM
SMEM = pltpu.SMEM
LIMIT = 24 * 1024 * 1024


def gll_tables():
    gll_nodes = np.array(
        [
            -1.0,
            -0.8717401485096066,
            -0.5917001814331423,
            -0.2092992179024789,
            0.2092992179024789,
            0.5917001814331423,
            0.8717401485096066,
            1.0,
        ]
    )
    weight_np = np.array(
        [
            1.0 / 28.0,
            0.21070422714350603,
            0.3411226924835044,
            0.4124587946587038,
            0.4124587946587038,
            0.3411226924835044,
            0.21070422714350603,
            1.0 / 28.0,
        ]
    )
    bary_weights = np.array(
        [1.0 / np.prod([gll_nodes[i] - gll_nodes[j] for j in range(8) if j != i]) for i in range(8)]
    )
    derivative = np.zeros((8, 8))
    for i in range(8):
        for j in range(8):
            if i != j:
                derivative[i, j] = bary_weights[j] / bary_weights[i] / (gll_nodes[i] - gll_nodes[j])
        derivative[i, i] = -np.sum(derivative[i])
    return (weight_np, derivative)


def sine_tables():
    indices = np.arange(10) + 1.0
    sine_basis = np.sqrt(2.0 / 11.0) * np.sin(np.pi * np.outer(indices, indices) / 11.0)
    eigen_vals = 2.0 - 2.0 * np.cos(np.pi * indices / 11.0)
    return (sine_basis, eigen_vals)


WEIGHT, DERIV = gll_tables()
SINE, EIGEN = sine_tables()


def split_const(matrix):
    single = matrix.astype(np.float32)
    high = single.astype(jnp.bfloat16)
    low = (single - high.astype(np.float32)).astype(jnp.bfloat16)
    return high, low


def line_maps(count):
    length = 8 * count
    total = length + 4

    def column(position):
        if 0 <= position < length:
            return position
        return {-2: length, -1: length + 1, length: length + 2, length + 1: length + 3}[position]

    assembled = {}
    for position in range(-2, length + 2):
        row = np.zeros(total)
        row[column(position)] = 1.0
        if 0 <= position < length:
            if position % 8 == 0:
                row[column(position - 1)] += 1.0
            if position % 8 == 7:
                row[column(position + 1)] += 1.0
        assembled[position] = row
    forward = np.zeros((10 * count, total))
    for element in range(count):
        places = [8 * element - 2] + list(range(8 * element, 8 * element + 8)) + [8 * element + 9]
        forward[10 * element : 10 * element + 10] = SINE @ np.stack([assembled[p] for p in places])
    backward = np.zeros((length, 10 * count))
    for element in range(count):
        backward[8 * element : 8 * element + 8, 10 * element : 10 * element + 10] = SINE[1:9]
    for element in range(count - 1):
        first, second = 8 * element + 7, 8 * element + 8
        mean = 0.5 * (backward[first] + backward[second])
        backward[first] = mean
        backward[second] = mean
    return forward, backward


RING = 16
WIDE = ROWS + 2 * RING
REACH = 26
TILE = 48
TILE_B = 32


def ring_maps(reach, depth, inside):
    count = EY + 2 * depth
    forward, _ = line_maps(count)
    length = 8 * count
    columns = np.zeros((10 * count, len(inside)))
    for at, position in enumerate(inside):
        place = None if position is None else position + 8 * depth
        if place is None or place < -2 or place > length + 1:
            continue
        source = place if 0 <= place < length else {-2: 0, -1: 1}.get(place, place - length + 2) + length
        columns[:, at] = forward[:, source]
    _, backward = line_maps(count)
    own = 8 * depth
    rows = np.concatenate(
        [
            backward[own - reach : own + ROWS + reach],
            np.zeros((8, 10 * count)),
        ]
    )
    rows[ROWS + 2 * reach, 10 * depth : 10 * depth + 10] = SINE[1]
    rows[ROWS + 2 * reach + 1, 10 * (depth + EY - 1) : 10 * (depth + EY)] = SINE[8]
    return columns, rows


FZ, BZ = line_maps(1)
TILES = list(range(-REACH, 0)) + [None] * (TILE_B - REACH) + list(range(ROWS))
TILES += list(range(ROWS, ROWS + REACH)) + [None] * (TILE_B - REACH)
FY_A, BY_A = ring_maps(RING, 3, TILES)
FY_B, BY_B = ring_maps(0, 1, list(range(-RING, ROWS + RING)))
STEP_A = 112
STEP_B = 64


def padded(forward, backward, step):
    forward = np.pad(forward, ((0, step - forward.shape[0]), (0, 0)))
    return forward, np.pad(backward, ((0, 0), (0, step - backward.shape[1])))


FY_A, BY_A = padded(FY_A, BY_A, STEP_A)
FY_B, BY_B = padded(FY_B, BY_B, STEP_B)
FX, BX = line_maps(EX)
FX = FX[:, :LANES]


FX_H, FX_L = split_const(FX.T.copy())
BX_H, BX_L = split_const(BX.T.copy())


def wide_const(table):
    high, low = split_const(table)
    return np.concatenate([high, high, low], axis=1)


def pack_tables(tables):
    places, pieces, at = [], [], 0
    for table in tables:
        rows = -(-table.shape[0] // 16) * 16
        extra = ((0, rows - table.shape[0]), (0, 384 - table.shape[1]))
        pieces.append(np.pad(table.astype(np.float32), extra))
        places.append((at, rows, table.shape[1]))
        at += rows
    return np.concatenate(pieces).astype(jnp.bfloat16), places


TABLES, PLACES = pack_tables(
    [
        np.concatenate([FX_H, FX_H], axis=0),
        FX_L,
        BX_H,
        BX_L,
        wide_const(FY_A),
        wide_const(BY_A),
        wide_const(FY_B),
        wide_const(BY_B),
    ]
)


def roll_table():
    table = np.zeros((2, 8, 8, LANES))
    for kind, matrix in enumerate((DERIV, DERIV.T)):
        for k in range(8):
            for i in range(8):
                table[kind, k, i, :] = matrix[i, (i + k) % 8]
    return table.reshape(2 * 64, LANES)


WY = np.tile(WEIGHT, WIDE // 8)
WX = np.tile(WEIGHT, EX)


def inner_count(count):
    mult = np.ones(8 * count)
    position = np.arange(8 * count)
    mult[(position % 8 == 0) & (position > 0)] += 1.0
    mult[(position % 8 == 7) & (position < 8 * count - 1)] += 1.0
    return mult


END_MASS = np.where(np.arange(WIDE) % 8 % 7 == 0, 2.0, 1.0)
INV_MASS = (8.0 / (WY * END_MASS)[:, None] / (WX * inner_count(EX))[None, :]).astype(np.float32)

AT_ROLLS = WIDE
AT_DX = AT_ROLLS + 128
AT_DXT = AT_DX + LANES
AT_SQUARE = AT_DXT + LANES
AT_MASS = AT_SQUARE + 16
AT_SPREAD = AT_MASS + WIDE
AT_EIGEN_Y = AT_SPREAD + EX
AT_EIGEN_X = AT_EIGEN_Y + STEP_A
LAM_Y = np.resize(EIGEN, STEP_A)
LAM_X = np.resize(EIGEN, 8 * LANES).reshape(8, LANES)
PACKED = np.concatenate(
    [
        WY[:, None] * WX[None, :],
        roll_table(),
        np.kron(np.eye(EX), DERIV.T),
        np.kron(np.eye(EX), DERIV),
        np.repeat(DERIV[:, :1] ** 2, LANES, axis=1),
        np.repeat(DERIV[:, 7:] ** 2, LANES, axis=1),
        INV_MASS,
        np.kron(np.eye(EX), np.ones((1, 8))),
        np.repeat(LAM_Y[:, None], LANES, axis=1),
        LAM_X,
    ]
).astype(np.float32)


def parts(values):
    high = values.astype(BF16)
    low = (values - high.astype(F32)).astype(BF16)
    return high, low


def dot(left, right):
    return jnp.dot(left, right, preferred_element_type=F32)


def left_pairs(table, planes):
    results = []
    for i in range(0, len(planes), 2):
        high, low = parts(jnp.concatenate([planes[i], planes[i + 1]], axis=1))
        both = dot(table, jnp.concatenate([high, low, high], axis=0))
        results += [both[:, 0:LANES], both[:, LANES : 2 * LANES]]
    return results


def along_z(values, matrix):
    rows = []
    for i in range(matrix.shape[0]):
        total = None
        for j in range(matrix.shape[1]):
            if matrix[i, j] == 0.0:
                continue
            term = float(matrix[i, j]) * values[j]
            total = term if total is None else total + term
        rows.append(total)
    return rows


def along_y(values, packed, kind):
    count, rows = values.shape[:2]
    grouped = values.reshape(count * rows // 8, 8, LANES)
    start = AT_ROLLS + 64 * kind
    total = packed[start : start + 8][None] * grouped
    for k in range(1, 8):
        total = total + packed[start + 8 * k : start + 8 * k + 8][None] * pltpu.roll(grouped, 8 - k, 1)
    return total.reshape(count, rows, LANES)


def along_x(values, packed, kind):
    start = AT_DXT if kind else AT_DX
    high, low = parts(packed[start : start + LANES])
    first, rest = parts(values.reshape(values.shape[0] * values.shape[1], LANES))
    total = dot(
        jnp.concatenate([first, rest], axis=1), jnp.concatenate([high, high], axis=0)
    ) + dot(first, low)
    return total.reshape(values.shape)


def stack(planes):
    return jnp.concatenate([plane[None] for plane in planes], axis=0)


def edge_rows(rows, low, high):
    position = lax.broadcasted_iota(jnp.int32, (rows, LANES), 0)
    return jnp.where(position == 0, low, jnp.where(position == rows - 1, high, 1.0))


def local_operator(values, flux, packed):
    plane_w = packed[0 : values.shape[1]]
    gz = along_z([values[i] for i in range(8)], DERIV)
    fz = along_z([flux[i] * gz[i] for i in range(8)], DERIV.T)
    total = along_y(flux * along_y(values, packed, 0), packed, 1)
    total = total + along_x(flux * along_x(values, packed, 0), packed, 1)
    planes = [
        total[i] + fz[i] + (HELM_COEF * 0.125 * float(WEIGHT[i])) * (plane_w * values[i])
        for i in range(8)
    ]
    return stack(planes)


def add_planes(own, low_z, high_z):
    planes = [own[i] for i in range(8)]
    planes[0] = planes[0] + low_z
    planes[7] = planes[7] + high_z
    return stack(planes)


def solve_elements(planes, packed, tables, kind):
    def table(index):
        at, rows, width = PLACES[index]
        return tables[at : at + rows, 0:width]

    fxhh, fxl, bxh, bxl = (table(index) for index in range(4))
    spectral = left_pairs(table(4 + 2 * kind), along_z(planes, FZ))
    high, low = parts(jnp.concatenate(spectral, axis=0))
    wide = dot(jnp.concatenate([high, low], axis=1), fxhh) + dot(high, fxl)
    step = PLACES[4 + 2 * kind][1]
    column = packed[AT_EIGEN_Y : AT_EIGEN_Y + step]
    rest = 10 * EX - LANES
    lam = jnp.concatenate(
        [
            column + packed[AT_EIGEN_X : AT_EIGEN_X + 1],
            column[:, 0:rest] + packed[AT_EIGEN_X + 1 : AT_EIGEN_X + 2, 0:rest],
        ],
        axis=1,
    )
    scaled = [
        wide[step * i : step * (i + 1)]
        / (SCHWARZ_SCALE * lam + float(SCHWARZ_SCALE * EIGEN[i] + SCHWARZ_SHIFT))
        for i in range(10)
    ]
    high, low = parts(jnp.concatenate(scaled, axis=0))
    back = dot(high, bxh) + dot(low, bxh) + dot(high, bxl)
    back = left_pairs(table(5 + 2 * kind), [back[step * i : step * (i + 1)] for i in range(10)])
    return along_z(back, BZ)


def store_faces(planes, near, out_ref, low_ref, high_ref):
    planes[0] = planes[0] * near[0]
    planes[7] = planes[7] * near[1]
    for i in range(8):
        out_ref[i] = planes[i]
    low_ref[...] = planes[0]
    high_ref[...] = planes[7]


def ring_rows(near):
    row = lax.broadcasted_iota(jnp.int32, (WIDE, LANES), 0)
    return row, 2.0 - 2.0 * near[2], 2.0 - 2.0 * near[3]


def partition_total(own, low_z, high_z, low_y, high_y, near):
    def planes(array):
        total = near[0] * array[0] + near[1] * array[7]
        for i in range(1, 7):
            total = total + array[i]
        return total

    total = planes(own) + 0.5 * (low_z[1] + high_z[0])
    below = planes(low_y) + 0.5 * (low_y[9] + low_y[10])
    above = planes(high_y) + 0.5 * (high_y[9] + high_y[10])
    faces = 0.5 * (below[REACH - 1 : REACH] + above[0:1])
    return jnp.sum(total * edge_rows(ROWS, near[2], near[3])) + jnp.sum(faces)


def lane_row(entries):
    lane = lax.broadcasted_iota(jnp.int32, (1, LANES), 1)
    row = jnp.zeros((1, LANES), F32)
    for index, value in enumerate(entries):
        row = jnp.where(lane == index, value, row)
    return row


def advect_kernel(
    lev_in, vel_in, src_in, packed_in, solid_in, b_ref, l_ref, zlo, zhi, solid_ref,
    lev, vel, src, packed, solid, sems,
):
    copies = [
        pltpu.make_async_copy(source, target, sems.at[index])
        for index, (source, target) in enumerate(
            (
                (vel_in, vel), (lev_in, lev), (packed_in, packed), (src_in, src), (solid_in, solid),
            )
        )
    ]
    for copy in copies:
        copy.start()
    for copy in copies:
        copy.wait()
    spread = packed[AT_SPREAD : AT_SPREAD + EX].astype(BF16)
    in_solid = dot(solid[...].astype(F32).astype(BF16), spread)
    solid_ref[...] = jnp.concatenate([in_solid, jnp.zeros((8 - EY, LANES), F32)], axis=0)
    level = lev[...]
    v0, v1, v2 = vel[0], vel[1], vel[2]
    gz = stack(along_z([level[i] for i in range(8)], DERIV))
    advect = v0 * gz + v1 * along_y(level, packed, 0) + v2 * along_x(level, packed, 0)
    moved = level - (2.0 * TIME_STEP) * advect
    diverge = stack(along_z([v0[i] for i in range(8)], DERIV))
    diverge = diverge + along_y(v1, packed, 0) + along_x(v2, packed, 0)
    force = src[...] - (2.0 * TIME_STEP) * diverge
    weights = packed[0:ROWS]
    for i in range(8):
        mass = (0.125 * float(WEIGHT[i])) * weights
        term = mass * force[i]
        moved_i = mass * moved[i]
        b_ref[i] = term
        l_ref[i] = moved_i
        if i < 2:
            zlo[i] = term
        if i == 0:
            zlo[2] = moved_i
        if i > 5:
            zhi[i - 6] = term
        if i == 7:
            zhi[2] = moved_i


def rim_kernel(solid, b, l, low_z, high_z, low_y, high_y):
    in_solid = solid[...]
    rest = TILE - REACH - RING - 1

    def rows(planes, at, level, far, extra=None):
        start = ROWS - REACH if far else 0
        pieces = [planes[at, start : start + REACH]]
        if level is None:
            pieces.append(jnp.zeros((RING + 1, LANES), F32))
        else:
            array, index = level
            start = ROWS - RING - 1 if far else 0
            pieces.append(array[index, start : start + RING + 1])
        if extra is None:
            pieces.append(jnp.zeros((rest, LANES), F32))
        else:
            pieces += [extra, jnp.zeros((rest - 2, LANES), F32)]
        return jnp.concatenate(pieces, axis=0)

    for far, out in ((False, low_y), (True, high_y)):
        extra = in_solid[EY - 2 : EY] if far else in_solid[0:2]
        for i in range(8):
            out[i] = rows(b, i, (l, i), far, extra if i == 0 else None)
        for i in range(2):
            out[8 + i] = rows(low_z, i, (low_z, 2) if i == 1 else None, far)
            out[10 + i] = rows(high_z, i, (high_z, 2) if i == 0 else None, far)


def level_kernel(
    near, solid, packed, b, l, zlo, zhi, ylo, yhi, level_ref, flux_ref, stat
):
    row, has_low, has_high = ring_rows(near)
    at = REACH

    def wide_rows(slot, own):
        return jnp.concatenate(
            [ylo[slot, at + 1 : at + 1 + RING], own, yhi[slot, at : at + RING]], axis=0
        )

    planes = []
    for i in range(8):
        plane = wide_rows(i, l[i])
        first = ylo[i, at : at + 1]
        last = yhi[i, at + RING : at + RING + 1]
        if i == 0:
            plane = plane + wide_rows(9, zlo[2])
            first = first + ylo[9, at : at + 1]
            last = last + yhi[9, at + RING : at + RING + 1]
        if i == 7:
            plane = plane + wide_rows(10, zhi[2])
            first = first + ylo[10, at : at + 1]
            last = last + yhi[10, at + RING : at + RING + 1]
        before = jnp.where(row == 0, first, pltpu.roll(plane, 1, 0))
        after = jnp.where(row == WIDE - 1, last, pltpu.roll(plane, WIDE - 1, 0))
        plane = plane + jnp.where(row % 8 == 0, before, jnp.where(row % 8 == 7, after, 0.0))
        planes.append(plane)
    own = stack(planes)
    lane = lax.broadcasted_iota(jnp.int32, (8, WIDE, LANES), 2)
    before = jnp.where((lane % 8 == 0) & (lane > 0), pltpu.roll(own, 1, 2), 0.0)
    after = jnp.where((lane % 8 == 7) & (lane < LANES - 1), pltpu.roll(own, LANES - 1, 2), 0.0)
    own = own + before + after
    ends = jnp.where(row == RING, 2.0 * near[2], jnp.where(row == RING + ROWS - 1, 2.0 * near[3], 1.0))
    inverse = packed[AT_MASS : AT_MASS + WIDE] * ends
    in_solid = solid[...]
    solids = [ylo[0, at + RING + 1 + k : at + RING + 2 + k] for k in range(2)]
    solids += [in_solid[e : e + 1] for e in range(EY)]
    solids += [yhi[0, at + RING + 1 + k : at + RING + 2 + k] for k in range(2)]
    open_part = jnp.concatenate(
        [jnp.broadcast_to(1.0 - (1.0 - SOLID_FACTOR) * rows, (8, LANES)) for rows in solids], axis=0
    )
    in_grid = jnp.where(row < RING, has_low, jnp.where(row >= RING + ROWS, has_high, 1.0))
    flux_w = packed[0:WIDE] * in_grid
    total = jnp.zeros((ROWS, LANES), F32)
    fluxes = []
    for i in range(8):
        scale = 1.0 / float(WEIGHT[i])
        plane = own[i] * (inverse * scale)
        if i == 0:
            plane = plane * near[0]
        if i == 7:
            plane = plane * near[1]
        level_ref[i] = plane[RING : RING + ROWS]
        liquid = jax.nn.sigmoid(plane * (1.0 / LEVEL_WIDTH))
        coef = (GAS_RATIO - (GAS_RATIO - 1.0) * liquid) * open_part
        total = total + coef[RING : RING + ROWS]
        flux = (0.5 * float(WEIGHT[i])) * (coef * flux_w)
        flux_ref[i] = flux
        fluxes.append(flux[RING : RING + ROWS])
    kbar = jnp.sum(total) * (1.0 / (8 * ROWS * LANES))
    entries = [kbar, partition_total(b, zlo, zhi, ylo, yhi, near)] + [0.0] * 9
    for first, second in ((0, 0), (0, 7), (7, 7)):
        slopes = along_z(fluxes, (DERIV[:, first] * DERIV[:, second])[None, :])[0]
        column = jnp.sum(slopes, axis=1, keepdims=True)
        entries += [jnp.sum(column, axis=0, keepdims=True), column[0:1], column[ROWS - 1 : ROWS]]
    inner = fluxes[0] + fluxes[1]
    for i in range(2, 8):
        inner = inner + fluxes[i]
    for at_row, start in ((0, 0), (ROWS - 8, 8)):
        square = packed[AT_SQUARE + start : AT_SQUARE + start + 8]
        entries += [
            jnp.sum(square * plane[at_row : at_row + 8]) for plane in (inner, fluxes[0], fluxes[7])
        ]
    stat[...] = lane_row(entries)


def first_schwarz_kernel(
    near, packed, tables, b, zlo, zhi, ylo, yhi, w_ref, wlo, whi
):
    own = [b[i] for i in range(8)] + [zlo[0], zlo[1], zhi[0], zhi[1]]
    planes = [
        jnp.concatenate([ylo[i, 0:TILE_B], own[i], yhi[i, 0:TILE_B]], axis=0) for i in range(12)
    ]
    planes = solve_elements(planes, packed, tables, 0)
    row, has_low, has_high = ring_rows(near)
    in_grid = jnp.where(row < RING, has_low, jnp.where(row >= RING + ROWS, has_high, 1.0))
    in_grid = jnp.where(row == RING, has_low, jnp.where(row == RING + ROWS - 1, has_high, in_grid))
    for i in range(8):
        first = (1.0 - has_low) * planes[i][WIDE : WIDE + 1]
        last = (1.0 - has_high) * planes[i][WIDE + 1 : WIDE + 2]
        alone = jnp.where(row == RING, first, jnp.where(row == RING + ROWS - 1, last, 0.0))
        planes[i] = planes[i][0:WIDE] * in_grid + alone
    store_faces(planes, near, w_ref, wlo, whi)


def galerkin_kernel(near, packed, stat_in, flux, w, zlo, zhi, zl_ref, y_ref, ylo, yhi, stat):
    local = add_planes(w, zlo[...], zhi[...])
    zl_ref[...] = local
    applied = local_operator(local, flux[...], packed)
    y_ref[...] = applied
    fluxes = [flux[i] for i in range(8)]
    for out, rows in ((ylo, (0, 1)), (yhi, (6, 7))):
        for k, i in enumerate(rows):
            out[k] = applied[i]
            for t, end in enumerate((0, 7)):
                out[2 + 2 * t + k] = along_z(fluxes, (DERIV[:, i] * DERIV[:, end])[None, :])[0]
            out[6 + k] = fluxes[i]
    applied = applied[:, RING : RING + ROWS]
    inner = near[0] * applied[0] + near[1] * applied[7]
    for i in range(1, 7):
        inner = inner + applied[i]
    edge = edge_rows(ROWS, near[2], near[3])
    entries = [0.0, 0.0]
    for plane in ((1.0 - near[0]) * applied[0], inner, (1.0 - near[1]) * applied[7]):
        entries += [
            (1.0 - near[2]) * jnp.sum(plane[0:1]),
            jnp.sum(edge * plane),
            (1.0 - near[3]) * jnp.sum(plane[ROWS - 1 : ROWS]),
        ]
    stat[...] = jnp.broadcast_to(stat_in[...] + lane_row(entries), stat.shape)


def column_kernel(gathered, out_ref):
    values = gathered[...]
    sub = lax.broadcasted_iota(jnp.int32, (8, LANES), 0)
    lane = lax.broadcasted_iota(jnp.int32, (8, LANES), 1)
    after = jnp.where(sub < 7, pltpu.roll(values, 7, 0), 0.0)
    before = jnp.where(sub > 0, pltpu.roll(values, 1, 0), 0.0)
    first = lax.broadcasted_iota(jnp.int32, (8, 1), 0) == 0
    last = lax.broadcasted_iota(jnp.int32, (8, 1), 0) == 7

    def column(array, index):
        return array[:, index : index + 1]

    def slopes(array, pair):
        whole, low, high = (column(array, 11 + 3 * pair + k) for k in range(3))
        return whole - low - high, low, high

    merged = [column(values, 0), column(values, 1)]
    for b in range(3):
        merged.append(column(values, 5 + b) + column(after, 2 + b) + column(before, 8 + b))
    merged += [own + other for own, other in zip(slopes(values, 0), slopes(before, 2), strict=True)]
    merged += list(slopes(values, 1))
    inside, interface = [], []
    for side in range(2):
        whole, low, high = (column(values, 20 + 3 * side + k) for k in range(3))
        ends = jnp.where(first, low, 0.0) + jnp.where(last, high, 0.0)
        inside.append(whole - low - high + ends)
        interface.append(jnp.where(first, 0.0, low) + column(before, 22 + 3 * side))
    rows = jnp.zeros((8, LANES), F32)
    for index, value in enumerate(merged + inside + interface):
        rows = jnp.where(lane == index, value, rows)
    total = rows[0:1]
    for i in range(1, 8):
        total = total + pltpu.roll(rows[i : i + 1], 16 * i, 1)
    out_ref[...] = jnp.broadcast_to(total, out_ref.shape)


def invert(blocks, sub):
    for k in range(0, 8, 2):
        first, second = blocks[k], blocks[k + 1]
        a, b = first[k : k + 1], first[k + 1 : k + 2]
        c, d = second[k : k + 1], second[k + 1 : k + 2]
        scale = 1.0 / (a * d - b * c)
        first = jnp.where(sub == k, 1.0, jnp.where(sub == k + 1, 0.0, first))
        second = jnp.where(sub == k + 1, 1.0, jnp.where(sub == k, 0.0, second))
        low = (d * scale) * first - (b * scale) * second
        high = (a * scale) * second - (c * scale) * first
        pivots = (sub == k) | (sub == k + 1)
        rows = []
        for r in range(8):
            if r == k:
                rows.append(low)
            elif r == k + 1:
                rows.append(high)
            else:
                rest = jnp.where(pivots, 0.0, blocks[r])
                rows.append(rest - blocks[r][k : k + 1] * low - blocks[r][k + 1 : k + 2] * high)
        blocks = rows
    return blocks


def multiply(left, right):
    rows = []
    for r in range(8):
        total = left[r][0:1] * right[0]
        for k in range(1, 8):
            total = total + left[r][k : k + 1] * right[k]
        rows.append(total)
    return rows


def matvec(terms, sub):
    result = jnp.zeros_like(terms[0][1])
    for r in range(8):
        product = terms[0][0][r] * terms[0][1]
        for blocks, column in terms[1:]:
            product = product + blocks[r] * column
        result = jnp.where(sub == r, jnp.sum(product, axis=0, keepdims=True), result)
    return result


def coarse_operator(c, count, sums_z, couplings_z, inside_y, interface_y):
    sub = lax.broadcasted_iota(jnp.int32, c.shape, 0)
    lane = lax.broadcasted_iota(jnp.int32, c.shape, 1)
    has_low = lane > 0
    has_high = lane < count - 1

    def after(array):
        return jnp.where(sub < 7, pltpu.roll(array, 7, 0), 0.0)

    def before(array):
        return jnp.where(sub > 0, pltpu.roll(array, 1, 0), 0.0)

    def right(array):
        return jnp.where(has_high, pltpu.roll(array, LANES - 1, 1), 0.0)

    def left(array):
        return jnp.where(has_low, pltpu.roll(array, 1, 1), 0.0)

    on_low = jnp.where(has_low, 0.5 * (c + left(c)), c)
    on_high = jnp.where(has_high, 0.5 * (c + right(c)), c)
    tested = []
    for place, value in enumerate((c, on_low, on_high)):
        slope = jnp.where(sub > 0, 0.5 * (value - before(value)), 0.0)
        coupling = couplings_z[place]
        force = sums_z[place] * slope - coupling * after(slope) - before(coupling * slope)
        force = jnp.where(sub > 0, force, 0.0)
        tested.append(0.5 * (force - after(force)))
    result = tested[0] + jnp.where(has_low, 0.5, 1.0) * tested[1] + jnp.where(has_high, 0.5, 1.0) * tested[2]
    result = result + 0.5 * right(tested[1]) + 0.5 * left(tested[2])

    interface = jnp.where(sub > 0, 0.5 * (c + before(c)), 0.0)
    for side, (move, there) in enumerate(((left, has_low), (right, has_high))):
        force = inside_y[side] * jnp.where(there, 0.5 * (move(c) - c), 0.0)
        face = interface_y[side] * jnp.where(there, 0.5 * (move(interface) - interface), 0.0)
        force = force + 0.5 * (face + after(face))
        back = right if side == 0 else left
        result = result + 0.5 * (back(force) - force)

    end = float(WEIGHT[0])
    mass = (2.0 - 2.0 * end) * c + end * (interface + after(interface))
    mass = mass + jnp.where((sub == 0) | (sub == 7), end * c, 0.0)
    beside = jnp.where(has_low, 0.5 * (mass + left(mass)), 0.0)
    scaled = (2.0 * EY - 2.0 * end) * mass + end * (beside + right(beside))
    scaled = scaled + jnp.where(has_low, 0.0, end * mass) + jnp.where(has_high, 0.0, end * mass)
    return result + HELM_COEF / 8.0 * float(np.sum(WX)) * scaled


def coarse_kernel(count, near, gathered, out_ref, wide, turned):
    lanes = LANES
    sub = lax.broadcasted_iota(jnp.int32, (8, lanes), 0)
    lane = lax.broadcasted_iota(jnp.int32, (8, lanes), 1)
    wide[...] = jnp.zeros((LANES, LANES), F32)
    wide[0:count] = gathered[...]
    turned[...] = wide[...].T

    def value(index):
        return turned[pl.ds(index, 8, stride=16), :]

    def move(array, dz, dy):
        if dz:
            array = pltpu.roll(array, (-dz) % 8, 0)
        if dy:
            array = pltpu.roll(array, (-dy) % lanes, 1)
        return array

    kbar = jnp.where(lane < count, value(0), 1.0)
    above = move(kbar, 1, 0)
    link_z = jnp.where(sub < 7, 2.0 * kbar * above / (kbar + above) * (EY * EX / EZ), 0.0)
    link_z = jnp.where(lane < count, link_z, 0.0)
    beside = move(kbar, 0, 1)
    link_y = 2.0 * kbar * beside / (kbar + beside) * (EZ * EX / EY)
    link_y = jnp.where(lane < count - 1, link_y, 0.0)
    back_z = move(link_z, -1, 0)
    back_y = move(link_y, 0, -1)
    diagonal = HELM_COEF * EZ * EY * EX + link_z + back_z + link_y + back_y
    blocks = []
    for r in range(8):
        row = jnp.where(sub == r, diagonal, 0.0)
        row = jnp.where(sub == r + 1, -back_z, row)
        row = jnp.where(sub == r - 1, -link_z, row)
        blocks.append(row)
    inverse = invert(blocks, sub)
    down = [-back_y[r : r + 1] * move(inverse[r], 0, -1) for r in range(8)]
    up = [-link_y[r : r + 1] * move(inverse[r], 0, 1) for r in range(8)]
    levels = [(1, down, up)]
    link_before, link_after = move(link_y, 0, -1), move(back_y, 0, 1)
    blocks = [blocks[r] + down[r] * link_before + up[r] * link_after for r in range(8)]
    lower = [row * move(back_y, 0, -1) for row in down]
    upper = [row * move(link_y, 0, 1) for row in up]
    step = 2
    while step < count:
        inverse = invert(blocks, sub)
        down = multiply(lower, [move(row, 0, -step) for row in inverse])
        up = multiply(upper, [move(row, 0, step) for row in inverse])
        levels.append((step, down, up))
        before_u = multiply(down, [move(row, 0, -step) for row in upper])
        after_l = multiply(up, [move(row, 0, step) for row in lower])
        if 2 * step < count:
            new_lower = multiply(down, [move(row, 0, -step) for row in lower])
            new_upper = multiply(up, [move(row, 0, step) for row in upper])
            lower = [-row for row in new_lower]
            upper = [-row for row in new_upper]
        blocks = [blocks[r] - before_u[r] - after_l[r] for r in range(8)]
        step *= 2
    inverse = invert(blocks, sub)

    def solve(column):
        for distance, down, up in levels:
            pulled = matvec(
                [(down, move(column, 0, -distance)), (up, move(column, 0, distance))], sub
            )
            column = column - pulled
        return matvec([(inverse, column)], sub)

    first = solve(value(1))
    totals = coarse_operator(
        first,
        count,
        [value(5 + k) for k in range(3)],
        [value(8 + k) for k in range(3)],
        [value(11), value(12)],
        [value(13), value(14)],
    )
    totals = totals + value(3)
    totals = totals + jnp.where(lane < count - 1, move(value(2), 0, 1), 0.0)
    totals = totals + jnp.where(lane > 0, move(value(4), 0, -1), 0.0)
    totals = jnp.where(lane < count, totals, 0.0)
    second = solve(totals)
    mine = (sub.astype(F32) == near[4]) & (lane.astype(F32) == near[5])

    def store(at, solved, reach):
        for a in range(-reach, reach + 1):
            for b in range(-1, 2):
                picked = jnp.sum(jnp.where(mine, move(solved, a, b), 0.0))
                row = at + 3 * (a + reach) + b + 1
                out_ref[row : row + 1] = jnp.full((1, lanes), picked)

    store(0, first, 2)
    store(16, second, 1)


def coarse_columns(near, coarse, start, count):
    row, has_low, has_high = ring_rows(near)
    below = jnp.where(row < RING - 1, 1.0, jnp.where(row <= RING, 0.5, 0.0)) * has_low
    above = jnp.where(row > RING + ROWS, 1.0, jnp.where(row >= RING + ROWS - 1, 0.5, 0.0)) * has_high
    edge = jnp.where((row > RING) & (row < RING + ROWS - 1), 1.0, 0.0)
    edge = jnp.where(row == RING, near[2], jnp.where(row == RING + ROWS - 1, near[3], edge))
    edge = jnp.where(row == RING - 1, 0.5 * has_low, edge)
    edge = jnp.where(row == RING + ROWS, 0.5 * has_high, edge)
    columns = []
    for a in range(count):
        at = start + 3 * a
        columns.append(
            below * coarse[at : at + 1] + edge * coarse[at + 1 : at + 2] + above * coarse[at + 2 : at + 3]
        )
    return columns


def coarse_planes(columns, low, high):
    before, inside, after = columns
    return inside, low * (before - inside), high * (after - inside)


def add_coarse(local, columns):
    inside, first, last = columns
    planes = [local[i] + inside for i in range(8)]
    planes[0] = planes[0] + first
    planes[7] = planes[7] + last
    return stack(planes)


def coarse_applied(columns, flux, packed):
    inside, first, last = columns
    slopes = [
        flux[i] * (float(DERIV[i, 0]) * first + float(DERIV[i, 7]) * last) for i in range(8)
    ]
    fz = along_z(slopes, DERIV.T)
    three = stack([inside + first, inside, inside + last])
    gy = along_y(three, packed, 0)
    fy = along_y(
        stack([flux[i] * gy[0 if i == 0 else 2 if i == 7 else 1] for i in range(8)]), packed, 1
    )
    plane_w = packed[0:WIDE]
    planes = []
    for i in range(8):
        plane = three[0 if i == 0 else 2 if i == 7 else 1]
        planes.append(fz[i] + fy[i] + (HELM_COEF * 0.125 * float(WEIGHT[i])) * (plane_w * plane))
    return stack(planes)


def face_applied(planes, payload, packed, rows, in_grid):
    inside, first, last = planes
    fields = [inside + (first if i == 0 else last if i == 7 else 0.0) for i in rows]
    gy = along_y(stack(fields), packed, 0)
    fy = along_y(stack([payload[6 + k] * gy[k] for k in range(2)]), packed, 1)
    plane_w = packed[0:WIDE]
    result = []
    for k, i in enumerate(rows):
        slopes = payload[2 + k] * first + payload[4 + k] * last
        mass = (HELM_COEF * 0.125 * float(WEIGHT[i])) * in_grid * (plane_w * fields[k])
        result.append(payload[k] + slopes + fy[k] + mass)
    return result


def apply_kernel(
    near, packed, tables, coarse, flux, zl, yl, ylo, yhi,
    z_ref, y_ref, w_ref, wlo, whi,
):
    columns = coarse_columns(near, coarse, 0, 5)
    own = coarse_planes(columns[1:4], 1.0 - near[0], 1.0 - near[1])
    field = add_coarse(zl[...], own)[:, RING : RING + ROWS]
    z_ref[...] = field
    applied = yl[...] + coarse_applied(own, flux[...], packed)
    y_ref[...] = applied[:, RING : RING + ROWS]
    lower = coarse_planes(columns[0:3], 1.0 - near[7], 0.5)
    upper = coarse_planes(columns[2:5], 0.5, 1.0 - near[6])
    planes = [applied[i] for i in range(8)]
    planes += face_applied(lower, ylo, packed, (6, 7), 2.0 - 2.0 * near[0])
    planes += face_applied(upper, yhi, packed, (0, 1), 2.0 - 2.0 * near[1])
    planes = solve_elements(planes, packed, tables, 1)
    row = lax.broadcasted_iota(jnp.int32, (ROWS, LANES), 0)
    _, has_low, has_high = ring_rows(near)
    in_grid = jnp.where(row == 0, has_low, jnp.where(row == ROWS - 1, has_high, 1.0))
    for i in range(8):
        first = (1.0 - has_low) * planes[i][ROWS : ROWS + 1]
        last = (1.0 - has_high) * planes[i][ROWS + 1 : ROWS + 2]
        alone = jnp.where(row == 0, first, jnp.where(row == ROWS - 1, last, 0.0))
        planes[i] = planes[i][0:ROWS] * in_grid + alone
    store_faces(planes, near, w_ref, wlo, whi)


def second_kernel(near, packed, coarse, flux, b, y, z, w, x_ref, kx_ref, stat):
    columns = [column[RING : RING + ROWS] for column in coarse_columns(near, coarse, 16, 3)]
    field = add_coarse(w[...], coarse_planes(columns, 1.0 - near[0], 1.0 - near[1]))
    x_ref[...] = field
    fluxes = flux[:, RING : RING + ROWS]
    gz = along_z([field[i] for i in range(8)], DERIV)
    gy = along_y(field, packed, 0)
    gx = along_x(field, packed, 0)
    slopes = [fluxes[i] * gz[i] for i in range(8)]
    ends = (0, 7)
    back = along_z(slopes, DERIV.T[[0, 7]])
    back_y = along_y(stack([fluxes[i] * gy[i] for i in ends]), packed, 1)
    back_x = along_x(stack([fluxes[i] * gx[i] for i in ends]), packed, 1)
    plane_w = packed[0:ROWS]
    mass = HELM_COEF * 0.125
    for k, i in enumerate(ends):
        weighted = (mass * float(WEIGHT[i])) * (plane_w * field[i])
        kx_ref[k] = back[k] + back_y[k] + back_x[k] + weighted
    energy = None
    for i in range(8):
        term = slopes[i] * gz[i] + fluxes[i] * (gy[i] * gy[i] + gx[i] * gx[i])
        term = term + (mass * float(WEIGHT[i])) * (plane_w * field[i] * field[i])
        energy = term if energy is None else energy + term
    first, right = z[...], b[...]
    sums = [right * first, y[...] * first, right * field, y[...] * field]
    stat[...] = lane_row([jnp.sum(term) for term in sums] + [jnp.sum(energy)])


def face_kernel(packed, flux, b, y, kx, zlo, zhi, stat_in, stat):
    faces = stack([zlo[...], zhi[...]])
    fluxes = flux[:, RING : RING + ROWS]
    gy = along_y(faces, packed, 0)
    gx = along_x(faces, packed, 0)
    plane_w = packed[0:ROWS]
    energy = 2.0 * (kx[0] * faces[0] + kx[1] * faces[1])
    for k, i in enumerate((0, 7)):
        mass = (HELM_COEF * 0.125 * float(WEIGHT[i])) * (plane_w * faces[k] * faces[k])
        energy = energy + mass + fluxes[i] * (gy[k] * gy[k] + gx[k] * gx[k])
    for i in range(8):
        slope = float(DERIV[i, 0]) * faces[0] + float(DERIV[i, 7]) * faces[1]
        energy = energy + fluxes[i] * slope * slope
    sums = [
        0.0,
        0.0,
        jnp.sum(b[0] * faces[0] + b[7] * faces[1]),
        jnp.sum(y[0] * faces[0] + y[7] * faces[1]),
        jnp.sum(energy),
    ]
    stat[...] = jnp.broadcast_to(stat_in[...] + lane_row(sums), stat.shape)


def combine_kernel(sums, z, x, zlo, zhi, p_ref):
    total = jnp.sum(sums[...], axis=0, keepdims=True)
    rz, pap, rq, aq, qhq = (total[:, k : k + 1] for k in range(5))
    step = rz / pap
    rz_next = step * (step * aq - rq)
    beta = rz_next / rz
    grown = 1.0 + beta
    curved = grown * grown * pap - 2.0 * step * grown * aq + step * step * qhq
    step_next = rz_next / curved
    on_z = step + step_next * grown
    on_q = step_next * step
    for i in range(8):
        plane = x[i]
        if i == 0:
            plane = plane + zlo[...]
        if i == 7:
            plane = plane + zhi[...]
        p_ref[i] = on_z * z[i] - on_q * plane


def run(kernel, outs, smem, args, scratch=(), flops=1000000, place=VMEM, limit=LIMIT):
    nbytes = sum(4 * int(np.prod(out)) for out in outs) * 2
    return pl.pallas_call(
        kernel,
        out_shape=[jax.ShapeDtypeStruct(out, F32) for out in outs],
        in_specs=[pl.BlockSpec(memory_space=SMEM) for _ in smem]
        + [pl.BlockSpec(memory_space=place) for _ in args],
        out_specs=[pl.BlockSpec(memory_space=VMEM) for _ in outs],
        scratch_shapes=list(scratch),
        compiler_params=pltpu.CompilerParams(vmem_limit_bytes=limit),
        cost_estimate=pl.CostEstimate(flops=flops, bytes_accessed=nbytes, transcendentals=0),
    )(*smem, *args)


def shift(axis, low_face, high_face):
    count = lax.axis_size(axis)
    forward = [(i, i + 1) for i in range(count - 1)]
    backward = [(target, source) for source, target in forward]
    return lax.ppermute(high_face, axis, forward), lax.ppermute(low_face, axis, backward)


def body(level_set, velocity, source, wick_solid):
    block = level_set.shape
    count_gx = lax.axis_size("gx")
    count_gy = lax.axis_size("gy")
    index_gx = lax.axis_index("gx")
    index_gy = lax.axis_index("gy")

    def ends(index, count):
        return [jnp.where(index > 0, 0.5, 1.0), jnp.where(index < count - 1, 0.5, 1.0)]

    place = [index_gx.astype(F32), index_gy.astype(F32)]
    beyond = [
        jnp.where(index_gx < count_gx - 2, 0.5, 1.0),
        jnp.where(index_gx > 1, 0.5, 1.0),
    ]
    near = jnp.stack(ends(index_gx, count_gx) + ends(index_gy, count_gy) + place + beyond)
    near = near.astype(F32)
    packed = jnp.asarray(PACKED)
    tables = jnp.asarray(TABLES)
    face = (ROWS, LANES)
    wide_block = (8, WIDE, LANES)
    wide_face = (WIDE, LANES)
    rim = (12, TILE, LANES)

    b, l, zlo, zhi, solid = run(
        advect_kernel,
        [block, block, (3, *face), (3, *face), (8, LANES)],
        [],
        [
            pltpu.with_memory_space_constraint(array, pltpu.HBM)
            for array in (level_set, velocity, source, packed, wick_solid.reshape(EY, EX))
        ],
        [VMEM(block, F32), VMEM((3, *block), F32), VMEM(block, F32), VMEM(PACKED.shape, F32)]
        + [VMEM((EY, EX), jnp.int32), pltpu.SemaphoreType.DMA((5,))],
        place=pltpu.HBM,
    )
    zlo, zhi = shift("gx", zlo, zhi)
    ylo, yhi = run(rim_kernel, [rim, rim], [], [solid, b, l, zlo, zhi])
    ylo, yhi = shift("gy", ylo, yhi)
    w, wlo, whi = run(
        first_schwarz_kernel,
        [wide_block, wide_face, wide_face],
        [near],
        [packed, tables, b, zlo, zhi, ylo, yhi],
    )
    wlo, whi = shift("gx", wlo, whi)
    level_new, flux, stat = run(
        level_kernel,
        [block, wide_block, (1, LANES)],
        [near],
        [solid, packed, b, l, zlo, zhi, ylo, yhi],
        flops=20000000,
    )
    zl, yl, zlo, zhi, stat = run(
        galerkin_kernel,
        [wide_block, wide_block, wide_block, wide_block, (count_gx, LANES)],
        [near],
        [packed, stat, flux, w, wlo, whi],
    )
    gathered = lax.all_to_all(stat, "gx", 0, 0, tiled=True)
    gathered, zlo, zhi = lax.optimization_barrier((gathered, zlo, zhi))
    zlo, zhi = shift("gx", zlo, zhi)
    (column,) = run(column_kernel, [(count_gy, LANES)], [], [gathered])
    gathered = lax.all_to_all(column, "gy", 0, 0, tiled=True)
    (coarse,) = run(
        functools.partial(coarse_kernel, count_gy),
        [(32, LANES)],
        [near],
        [gathered],
        [VMEM((LANES, LANES), F32), VMEM((LANES, LANES), F32)],
    )
    z, y, w, wlo, whi = run(
        apply_kernel,
        [block, block, block, face, face],
        [near],
        [packed, tables, coarse, flux, zl, yl, zlo, zhi],
    )
    zlo, zhi = shift("gx", wlo, whi)
    x, kx, sums = run(
        second_kernel,
        [block, (2, *face), (1, LANES)],
        [near],
        [packed, coarse, flux, b, y, z, w],
        flops=20000000,
    )
    (sums,) = run(
        face_kernel, [(count_gx, LANES)], [], [packed, flux, b, y, kx, zlo, zhi, sums]
    )
    tile = lax.all_to_all(sums, "gx", 0, 0, tiled=True)
    wide = jnp.broadcast_to(jnp.sum(tile, axis=0, keepdims=True), (count_gy, LANES))
    wide = lax.all_to_all(wide, "gy", 0, 0, tiled=True)
    (pressure,) = run(combine_kernel, [block], [], [wide, z, x, zlo, zhi])
    return (level_new, pressure)


def solution(mesh):
    placed = (
        P("gx", "gy", None),
        P(None, "gx", "gy", None),
        P("gx", "gy", None),
        P("gx", "gy", None),
    )
    return jax.shard_map(
        body,
        mesh=mesh,
        in_specs=placed,
        out_specs=(P("gx", "gy", None), P("gx", "gy", None)),
        check_vma=False,
    )
```

```python
import functools

import jax
import jax.numpy as jnp
import numpy as np
from jax import lax
from jax.experimental import pallas as pl
from jax.experimental.pallas import tpu as pltpu
from jax.sharding import PartitionSpec as P

EZ = 1
EY = 4
EX = 16
ROWS = 8 * EY
LANES = 8 * EX

TIME_STEP = 0.02
HELM_COEF = 0.25
LEVEL_WIDTH = 0.25
GAS_RATIO = 10.0
SOLID_FACTOR = 0.25
SCHWARZ_SCALE = 0.5
SCHWARZ_SHIFT = 0.05

F32 = jnp.float32
BF16 = jnp.bfloat16
VMEM = pltpu.VMEM
SMEM = pltpu.SMEM
LIMIT = 24 * 1024 * 1024


def gll_tables():
    gll_nodes = np.array(
        [
            -1.0,
            -0.8717401485096066,
            -0.5917001814331423,
            -0.2092992179024789,
            0.2092992179024789,
            0.5917001814331423,
            0.8717401485096066,
            1.0,
        ]
    )
    weight_np = np.array(
        [
            1.0 / 28.0,
            0.21070422714350603,
            0.3411226924835044,
            0.4124587946587038,
            0.4124587946587038,
            0.3411226924835044,
            0.21070422714350603,
            1.0 / 28.0,
        ]
    )
    bary_weights = np.array(
        [1.0 / np.prod([gll_nodes[i] - gll_nodes[j] for j in range(8) if j != i]) for i in range(8)]
    )
    derivative = np.zeros((8, 8))
    for i in range(8):
        for j in range(8):
            if i != j:
                derivative[i, j] = bary_weights[j] / bary_weights[i] / (gll_nodes[i] - gll_nodes[j])
        derivative[i, i] = -np.sum(derivative[i])
    return (weight_np, derivative)


def sine_tables():
    indices = np.arange(10) + 1.0
    sine_basis = np.sqrt(2.0 / 11.0) * np.sin(np.pi * np.outer(indices, indices) / 11.0)
    eigen_vals = 2.0 - 2.0 * np.cos(np.pi * indices / 11.0)
    return (sine_basis, eigen_vals)


WEIGHT, DERIV = gll_tables()
SINE, EIGEN = sine_tables()


def split_const(matrix):
    single = matrix.astype(np.float32)
    high = single.astype(jnp.bfloat16)
    low = (single - high.astype(np.float32)).astype(jnp.bfloat16)
    return high, low


def line_maps(count):
    length = 8 * count
    total = length + 4

    def column(position):
        if 0 <= position < length:
            return position
        return {-2: length, -1: length + 1, length: length + 2, length + 1: length + 3}[position]

    assembled = {}
    for position in range(-2, length + 2):
        row = np.zeros(total)
        row[column(position)] = 1.0
        if 0 <= position < length:
            if position % 8 == 0:
                row[column(position - 1)] += 1.0
            if position % 8 == 7:
                row[column(position + 1)] += 1.0
        assembled[position] = row
    forward = np.zeros((10 * count, total))
    for element in range(count):
        places = [8 * element - 2] + list(range(8 * element, 8 * element + 8)) + [8 * element + 9]
        forward[10 * element : 10 * element + 10] = SINE @ np.stack([assembled[p] for p in places])
    backward = np.zeros((length, 10 * count))
    for element in range(count):
        backward[8 * element : 8 * element + 8, 10 * element : 10 * element + 10] = SINE[1:9]
    for element in range(count - 1):
        first, second = 8 * element + 7, 8 * element + 8
        mean = 0.5 * (backward[first] + backward[second])
        backward[first] = mean
        backward[second] = mean
    return forward, backward


RING = 16
WIDE = ROWS + 2 * RING
REACH = 26
TILE = 48
TILE_B = 32


def ring_maps(reach, depth, inside):
    count = EY + 2 * depth
    forward, _ = line_maps(count)
    length = 8 * count
    columns = np.zeros((10 * count, len(inside)))
    for at, position in enumerate(inside):
        place = None if position is None else position + 8 * depth
        if place is None or place < -2 or place > length + 1:
            continue
        source = place if 0 <= place < length else {-2: 0, -1: 1}.get(place, place - length + 2) + length
        columns[:, at] = forward[:, source]
    _, backward = line_maps(count)
    own = 8 * depth
    rows = np.concatenate(
        [
            backward[own - reach : own + ROWS + reach],
            np.zeros((8, 10 * count)),
        ]
    )
    rows[ROWS + 2 * reach, 10 * depth : 10 * depth + 10] = SINE[1]
    rows[ROWS + 2 * reach + 1, 10 * (depth + EY - 1) : 10 * (depth + EY)] = SINE[8]
    return columns, rows


FZ, BZ = line_maps(1)
TILES = list(range(-REACH, 0)) + [None] * (TILE_B - REACH) + list(range(ROWS))
TILES += list(range(ROWS, ROWS + REACH)) + [None] * (TILE_B - REACH)
FY_A, BY_A = ring_maps(RING, 3, TILES)
FY_B, BY_B = ring_maps(0, 1, list(range(-RING, ROWS + RING)))
STEP_A = 112
STEP_B = 64


def padded(forward, backward, step):
    forward = np.pad(forward, ((0, step - forward.shape[0]), (0, 0)))
    return forward, np.pad(backward, ((0, 0), (0, step - backward.shape[1])))


FY_A, BY_A = padded(FY_A, BY_A, STEP_A)
FY_B, BY_B = padded(FY_B, BY_B, STEP_B)
FX, BX = line_maps(EX)
FX = FX[:, :LANES]


FX_H, FX_L = split_const(FX.T.copy())
BX_H, BX_L = split_const(BX.T.copy())


def wide_const(table):
    high, low = split_const(table)
    return np.concatenate([high, high, low], axis=1)


def pack_tables(tables):
    places, pieces, at = [], [], 0
    for table in tables:
        rows = -(-table.shape[0] // 16) * 16
        extra = ((0, rows - table.shape[0]), (0, 384 - table.shape[1]))
        pieces.append(np.pad(table.astype(np.float32), extra))
        places.append((at, rows, table.shape[1]))
        at += rows
    return np.concatenate(pieces).astype(jnp.bfloat16), places


TABLES, PLACES = pack_tables(
    [
        np.concatenate([FX_H, FX_H], axis=0),
        FX_L,
        BX_H,
        BX_L,
        wide_const(FY_A),
        wide_const(BY_A),
        wide_const(FY_B),
        wide_const(BY_B),
    ]
)


def roll_table():
    table = np.zeros((2, 8, 8, LANES))
    for kind, matrix in enumerate((DERIV, DERIV.T)):
        for k in range(8):
            for i in range(8):
                table[kind, k, i, :] = matrix[i, (i + k) % 8]
    return table.reshape(2 * 64, LANES)


WY = np.tile(WEIGHT, WIDE // 8)
WX = np.tile(WEIGHT, EX)


def inner_count(count):
    mult = np.ones(8 * count)
    position = np.arange(8 * count)
    mult[(position % 8 == 0) & (position > 0)] += 1.0
    mult[(position % 8 == 7) & (position < 8 * count - 1)] += 1.0
    return mult


END_MASS = np.where(np.arange(WIDE) % 8 % 7 == 0, 2.0, 1.0)
INV_MASS = (8.0 / (WY * END_MASS)[:, None] / (WX * inner_count(EX))[None, :]).astype(np.float32)

AT_ROLLS = WIDE
AT_DX = AT_ROLLS + 128
AT_DXT = AT_DX + LANES
AT_SQUARE = AT_DXT + LANES
AT_MASS = AT_SQUARE + 16
AT_SPREAD = AT_MASS + WIDE
AT_EIGEN_Y = AT_SPREAD + EX
AT_EIGEN_X = AT_EIGEN_Y + STEP_A
LAM_Y = np.resize(EIGEN, STEP_A)
LAM_X = np.resize(EIGEN, 8 * LANES).reshape(8, LANES)
PACKED = np.concatenate(
    [
        WY[:, None] * WX[None, :],
        roll_table(),
        np.kron(np.eye(EX), DERIV.T),
        np.kron(np.eye(EX), DERIV),
        np.repeat(DERIV[:, :1] ** 2, LANES, axis=1),
        np.repeat(DERIV[:, 7:] ** 2, LANES, axis=1),
        INV_MASS,
        np.kron(np.eye(EX), np.ones((1, 8))),
        np.repeat(LAM_Y[:, None], LANES, axis=1),
        LAM_X,
    ]
).astype(np.float32)


def parts(values):
    high = values.astype(BF16)
    low = (values - high.astype(F32)).astype(BF16)
    return high, low


def dot(left, right):
    return jnp.dot(left, right, preferred_element_type=F32)


def left_pairs(table, planes):
    results = []
    for i in range(0, len(planes), 2):
        high, low = parts(jnp.concatenate([planes[i], planes[i + 1]], axis=1))
        both = dot(table, jnp.concatenate([high, low, high], axis=0))
        results += [both[:, 0:LANES], both[:, LANES : 2 * LANES]]
    return results


def along_z(values, matrix):
    rows = []
    for i in range(matrix.shape[0]):
        total = None
        for j in range(matrix.shape[1]):
            if matrix[i, j] == 0.0:
                continue
            term = float(matrix[i, j]) * values[j]
            total = term if total is None else total + term
        rows.append(total)
    return rows


def along_y(values, packed, kind):
    count, rows = values.shape[:2]
    grouped = values.reshape(count * rows // 8, 8, LANES)
    start = AT_ROLLS + 64 * kind
    total = packed[start : start + 8][None] * grouped
    for k in range(1, 8):
        total = total + packed[start + 8 * k : start + 8 * k + 8][None] * pltpu.roll(grouped, 8 - k, 1)
    return total.reshape(count, rows, LANES)


def along_x(values, packed, kind):
    start = AT_DXT if kind else AT_DX
    high, low = parts(packed[start : start + LANES])
    first, rest = parts(values.reshape(values.shape[0] * values.shape[1], LANES))
    total = dot(
        jnp.concatenate([first, rest], axis=1), jnp.concatenate([high, high], axis=0)
    ) + dot(first, low)
    return total.reshape(values.shape)


def stack(planes):
    return jnp.concatenate([plane[None] for plane in planes], axis=0)


def edge_rows(rows, low, high):
    position = lax.broadcasted_iota(jnp.int32, (rows, LANES), 0)
    return jnp.where(position == 0, low, jnp.where(position == rows - 1, high, 1.0))


def local_operator(values, flux, packed):
    plane_w = packed[0 : values.shape[1]]
    gz = along_z([values[i] for i in range(8)], DERIV)
    fz = along_z([flux[i] * gz[i] for i in range(8)], DERIV.T)
    total = along_y(flux * along_y(values, packed, 0), packed, 1)
    total = total + along_x(flux * along_x(values, packed, 0), packed, 1)
    planes = [
        total[i] + fz[i] + (HELM_COEF * 0.125 * float(WEIGHT[i])) * (plane_w * values[i])
        for i in range(8)
    ]
    return stack(planes)


def add_planes(own, low_z, high_z):
    planes = [own[i] for i in range(8)]
    planes[0] = planes[0] + low_z
    planes[7] = planes[7] + high_z
    return stack(planes)


def solve_elements(planes, packed, tables, kind):
    def table(index):
        at, rows, width = PLACES[index]
        return tables[at : at + rows, 0:width]

    fxhh, fxl, bxh, bxl = (table(index) for index in range(4))
    spectral = left_pairs(table(4 + 2 * kind), along_z(planes, FZ))
    high, low = parts(jnp.concatenate(spectral, axis=0))
    wide = dot(jnp.concatenate([high, low], axis=1), fxhh) + dot(high, fxl)
    step = PLACES[4 + 2 * kind][1]
    column = packed[AT_EIGEN_Y : AT_EIGEN_Y + step]
    rest = 10 * EX - LANES
    lam = jnp.concatenate(
        [
            column + packed[AT_EIGEN_X : AT_EIGEN_X + 1],
            column[:, 0:rest] + packed[AT_EIGEN_X + 1 : AT_EIGEN_X + 2, 0:rest],
        ],
        axis=1,
    )
    scaled = [
        wide[step * i : step * (i + 1)]
        / (SCHWARZ_SCALE * lam + float(SCHWARZ_SCALE * EIGEN[i] + SCHWARZ_SHIFT))
        for i in range(10)
    ]
    high, low = parts(jnp.concatenate(scaled, axis=0))
    back = dot(high, bxh) + dot(low, bxh) + dot(high, bxl)
    back = left_pairs(table(5 + 2 * kind), [back[step * i : step * (i + 1)] for i in range(10)])
    return along_z(back, BZ)


def store_faces(planes, near, out_ref, low_ref, high_ref):
    planes[0] = planes[0] * near[0]
    planes[7] = planes[7] * near[1]
    for i in range(8):
        out_ref[i] = planes[i]
    low_ref[...] = planes[0]
    high_ref[...] = planes[7]


def ring_rows(near):
    row = lax.broadcasted_iota(jnp.int32, (WIDE, LANES), 0)
    return row, 2.0 - 2.0 * near[2], 2.0 - 2.0 * near[3]


def partition_total(own, low_z, high_z, low_y, high_y, near):
    def planes(array):
        total = near[0] * array[0] + near[1] * array[7]
        for i in range(1, 7):
            total = total + array[i]
        return total

    total = planes(own) + 0.5 * (low_z[1] + high_z[0])
    below = planes(low_y) + 0.5 * (low_y[9] + low_y[10])
    above = planes(high_y) + 0.5 * (high_y[9] + high_y[10])
    faces = 0.5 * (below[REACH - 1 : REACH] + above[0:1])
    return jnp.sum(total * edge_rows(ROWS, near[2], near[3])) + jnp.sum(faces)


def lane_row(entries):
    lane = lax.broadcasted_iota(jnp.int32, (1, LANES), 1)
    row = jnp.zeros((1, LANES), F32)
    for index, value in enumerate(entries):
        row = jnp.where(lane == index, value, row)
    return row


def advect_kernel(
    lev_in, vel_in, src_in, packed_in, solid_in, b_ref, l_ref, zlo, zhi, solid_ref,
    lev, vel, src, packed, solid, sems,
):
    copies = [
        pltpu.make_async_copy(source, target, sems.at[index])
        for index, (source, target) in enumerate(
            (
                (vel_in, vel), (lev_in, lev), (packed_in, packed), (src_in, src), (solid_in, solid),
            )
        )
    ]
    for copy in copies:
        copy.start()
    for copy in copies:
        copy.wait()
    spread = packed[AT_SPREAD : AT_SPREAD + EX].astype(BF16)
    in_solid = dot(solid[...].astype(F32).astype(BF16), spread)
    solid_ref[...] = jnp.concatenate([in_solid, jnp.zeros((8 - EY, LANES), F32)], axis=0)
    level = lev[...]
    v0, v1, v2 = vel[0], vel[1], vel[2]
    gz = stack(along_z([level[i] for i in range(8)], DERIV))
    advect = v0 * gz + v1 * along_y(level, packed, 0) + v2 * along_x(level, packed, 0)
    moved = level - (2.0 * TIME_STEP) * advect
    diverge = stack(along_z([v0[i] for i in range(8)], DERIV))
    diverge = diverge + along_y(v1, packed, 0) + along_x(v2, packed, 0)
    force = src[...] - (2.0 * TIME_STEP) * diverge
    weights = packed[0:ROWS]
    for i in range(8):
        mass = (0.125 * float(WEIGHT[i])) * weights
        term = mass * force[i]
        moved_i = mass * moved[i]
        b_ref[i] = term
        l_ref[i] = moved_i
        if i < 2:
            zlo[i] = term
        if i == 0:
            zlo[2] = moved_i
        if i > 5:
            zhi[i - 6] = term
        if i == 7:
            zhi[2] = moved_i


def rim_kernel(solid, b, l, low_z, high_z, low_y, high_y):
    in_solid = solid[...]
    rest = TILE - REACH - RING - 1

    def rows(planes, at, level, far, extra=None):
        start = ROWS - REACH if far else 0
        pieces = [planes[at, start : start + REACH]]
        if level is None:
            pieces.append(jnp.zeros((RING + 1, LANES), F32))
        else:
            array, index = level
            start = ROWS - RING - 1 if far else 0
            pieces.append(array[index, start : start + RING + 1])
        if extra is None:
            pieces.append(jnp.zeros((rest, LANES), F32))
        else:
            pieces += [extra, jnp.zeros((rest - 2, LANES), F32)]
        return jnp.concatenate(pieces, axis=0)

    for far, out in ((False, low_y), (True, high_y)):
        extra = in_solid[EY - 2 : EY] if far else in_solid[0:2]
        for i in range(8):
            out[i] = rows(b, i, (l, i), far, extra if i == 0 else None)
        for i in range(2):
            out[8 + i] = rows(low_z, i, (low_z, 2) if i == 1 else None, far)
            out[10 + i] = rows(high_z, i, (high_z, 2) if i == 0 else None, far)


def level_kernel(
    near, solid, packed, b, l, zlo, zhi, ylo, yhi, level_ref, flux_ref, stat
):
    row, has_low, has_high = ring_rows(near)
    at = REACH

    def wide_rows(slot, own):
        return jnp.concatenate(
            [ylo[slot, at + 1 : at + 1 + RING], own, yhi[slot, at : at + RING]], axis=0
        )

    planes = []
    for i in range(8):
        plane = wide_rows(i, l[i])
        first = ylo[i, at : at + 1]
        last = yhi[i, at + RING : at + RING + 1]
        if i == 0:
            plane = plane + wide_rows(9, zlo[2])
            first = first + ylo[9, at : at + 1]
            last = last + yhi[9, at + RING : at + RING + 1]
        if i == 7:
            plane = plane + wide_rows(10, zhi[2])
            first = first + ylo[10, at : at + 1]
            last = last + yhi[10, at + RING : at + RING + 1]
        before = jnp.where(row == 0, first, pltpu.roll(plane, 1, 0))
        after = jnp.where(row == WIDE - 1, last, pltpu.roll(plane, WIDE - 1, 0))
        plane = plane + jnp.where(row % 8 == 0, before, jnp.where(row % 8 == 7, after, 0.0))
        planes.append(plane)
    own = stack(planes)
    lane = lax.broadcasted_iota(jnp.int32, (8, WIDE, LANES), 2)
    before = jnp.where((lane % 8 == 0) & (lane > 0), pltpu.roll(own, 1, 2), 0.0)
    after = jnp.where((lane % 8 == 7) & (lane < LANES - 1), pltpu.roll(own, LANES - 1, 2), 0.0)
    own = own + before + after
    ends = jnp.where(row == RING, 2.0 * near[2], jnp.where(row == RING + ROWS - 1, 2.0 * near[3], 1.0))
    inverse = packed[AT_MASS : AT_MASS + WIDE] * ends
    in_solid = solid[...]
    solids = [ylo[0, at + RING + 1 + k : at + RING + 2 + k] for k in range(2)]
    solids += [in_solid[e : e + 1] for e in range(EY)]
    solids += [yhi[0, at + RING + 1 + k : at + RING + 2 + k] for k in range(2)]
    open_part = jnp.concatenate(
        [jnp.broadcast_to(1.0 - (1.0 - SOLID_FACTOR) * rows, (8, LANES)) for rows in solids], axis=0
    )
    in_grid = jnp.where(row < RING, has_low, jnp.where(row >= RING + ROWS, has_high, 1.0))
    flux_w = packed[0:WIDE] * in_grid
    total = jnp.zeros((ROWS, LANES), F32)
    fluxes = []
    for i in range(8):
        scale = 1.0 / float(WEIGHT[i])
        plane = own[i] * (inverse * scale)
        if i == 0:
            plane = plane * near[0]
        if i == 7:
            plane = plane * near[1]
        level_ref[i] = plane[RING : RING + ROWS]
        liquid = jax.nn.sigmoid(plane * (1.0 / LEVEL_WIDTH))
        coef = (GAS_RATIO - (GAS_RATIO - 1.0) * liquid) * open_part
        total = total + coef[RING : RING + ROWS]
        flux = (0.5 * float(WEIGHT[i])) * (coef * flux_w)
        flux_ref[i] = flux
        fluxes.append(flux[RING : RING + ROWS])
    kbar = jnp.sum(total) * (1.0 / (8 * ROWS * LANES))
    entries = [kbar, partition_total(b, zlo, zhi, ylo, yhi, near)] + [0.0] * 9
    for first, second in ((0, 0), (0, 7), (7, 7)):
        slopes = along_z(fluxes, (DERIV[:, first] * DERIV[:, second])[None, :])[0]
        column = jnp.sum(slopes, axis=1, keepdims=True)
        entries += [jnp.sum(column, axis=0, keepdims=True), column[0:1], column[ROWS - 1 : ROWS]]
    inner = fluxes[0] + fluxes[1]
    for i in range(2, 8):
        inner = inner + fluxes[i]
    for at_row, start in ((0, 0), (ROWS - 8, 8)):
        square = packed[AT_SQUARE + start : AT_SQUARE + start + 8]
        entries += [
            jnp.sum(square * plane[at_row : at_row + 8]) for plane in (inner, fluxes[0], fluxes[7])
        ]
    stat[...] = lane_row(entries)


def first_schwarz_kernel(
    near, packed, tables, b, zlo, zhi, ylo, yhi, w_ref, wlo, whi
):
    own = [b[i] for i in range(8)] + [zlo[0], zlo[1], zhi[0], zhi[1]]
    planes = [
        jnp.concatenate([ylo[i, 0:TILE_B], own[i], yhi[i, 0:TILE_B]], axis=0) for i in range(12)
    ]
    planes = solve_elements(planes, packed, tables, 0)
    row, has_low, has_high = ring_rows(near)
    in_grid = jnp.where(row < RING, has_low, jnp.where(row >= RING + ROWS, has_high, 1.0))
    in_grid = jnp.where(row == RING, has_low, jnp.where(row == RING + ROWS - 1, has_high, in_grid))
    for i in range(8):
        first = (1.0 - has_low) * planes[i][WIDE : WIDE + 1]
        last = (1.0 - has_high) * planes[i][WIDE + 1 : WIDE + 2]
        alone = jnp.where(row == RING, first, jnp.where(row == RING + ROWS - 1, last, 0.0))
        planes[i] = planes[i][0:WIDE] * in_grid + alone
    store_faces(planes, near, w_ref, wlo, whi)


def galerkin_kernel(near, packed, stat_in, flux, w, zlo, zhi, zl_ref, y_ref, ylo, yhi, stat):
    local = add_planes(w, zlo[...], zhi[...])
    zl_ref[...] = local
    applied = local_operator(local, flux[...], packed)
    y_ref[...] = applied
    fluxes = [flux[i] for i in range(8)]
    for out, rows in ((ylo, (0, 1)), (yhi, (6, 7))):
        for k, i in enumerate(rows):
            out[k] = applied[i]
            for t, end in enumerate((0, 7)):
                out[2 + 2 * t + k] = along_z(fluxes, (DERIV[:, i] * DERIV[:, end])[None, :])[0]
            out[6 + k] = fluxes[i]
    applied = applied[:, RING : RING + ROWS]
    inner = near[0] * applied[0] + near[1] * applied[7]
    for i in range(1, 7):
        inner = inner + applied[i]
    edge = edge_rows(ROWS, near[2], near[3])
    entries = [0.0, 0.0]
    for plane in ((1.0 - near[0]) * applied[0], inner, (1.0 - near[1]) * applied[7]):
        entries += [
            (1.0 - near[2]) * jnp.sum(plane[0:1]),
            jnp.sum(edge * plane),
            (1.0 - near[3]) * jnp.sum(plane[ROWS - 1 : ROWS]),
        ]
    stat[...] = jnp.broadcast_to(stat_in[...] + lane_row(entries), stat.shape)


def column_kernel(gathered, out_ref):
    values = gathered[...]
    sub = lax.broadcasted_iota(jnp.int32, (8, LANES), 0)
    lane = lax.broadcasted_iota(jnp.int32, (8, LANES), 1)
    after = jnp.where(sub < 7, pltpu.roll(values, 7, 0), 0.0)
    before = jnp.where(sub > 0, pltpu.roll(values, 1, 0), 0.0)
    first = lax.broadcasted_iota(jnp.int32, (8, 1), 0) == 0
    last = lax.broadcasted_iota(jnp.int32, (8, 1), 0) == 7

    def column(array, index):
        return array[:, index : index + 1]

    def slopes(array, pair):
        whole, low, high = (column(array, 11 + 3 * pair + k) for k in range(3))
        return whole - low - high, low, high

    merged = [column(values, 0), column(values, 1)]
    for b in range(3):
        merged.append(column(values, 5 + b) + column(after, 2 + b) + column(before, 8 + b))
    merged += [own + other for own, other in zip(slopes(values, 0), slopes(before, 2), strict=True)]
    merged += list(slopes(values, 1))
    inside, interface = [], []
    for side in range(2):
        whole, low, high = (column(values, 20 + 3 * side + k) for k in range(3))
        ends = jnp.where(first, low, 0.0) + jnp.where(last, high, 0.0)
        inside.append(whole - low - high + ends)
        interface.append(jnp.where(first, 0.0, low) + column(before, 22 + 3 * side))
    rows = jnp.zeros((8, LANES), F32)
    for index, value in enumerate(merged + inside + interface):
        rows = jnp.where(lane == index, value, rows)
    total = rows[0:1]
    for i in range(1, 8):
        total = total + pltpu.roll(rows[i : i + 1], 16 * i, 1)
    out_ref[...] = jnp.broadcast_to(total, out_ref.shape)


def invert(blocks, sub):
    for k in range(0, 8, 2):
        first, second = blocks[k], blocks[k + 1]
        a, b = first[k : k + 1], first[k + 1 : k + 2]
        c, d = second[k : k + 1], second[k + 1 : k + 2]
        scale = 1.0 / (a * d - b * c)
        first = jnp.where(sub == k, 1.0, jnp.where(sub == k + 1, 0.0, first))
        second = jnp.where(sub == k + 1, 1.0, jnp.where(sub == k, 0.0, second))
        low = (d * scale) * first - (b * scale) * second
        high = (a * scale) * second - (c * scale) * first
        pivots = (sub == k) | (sub == k + 1)
        rows = []
        for r in range(8):
            if r == k:
                rows.append(low)
            elif r == k + 1:
                rows.append(high)
            else:
                rest = jnp.where(pivots, 0.0, blocks[r])
                rows.append(rest - blocks[r][k : k + 1] * low - blocks[r][k + 1 : k + 2] * high)
        blocks = rows
    return blocks


def multiply(left, right):
    rows = []
    for r in range(8):
        total = left[r][0:1] * right[0]
        for k in range(1, 8):
            total = total + left[r][k : k + 1] * right[k]
        rows.append(total)
    return rows


def multiply_turned(left, right):
    rows = []
    for r in range(8):
        total = left[0][r : r + 1] * right[0]
        for k in range(1, 8):
            total = total + left[k][r : r + 1] * right[k]
        rows.append(total)
    return rows


def apply_turned(blocks, column):
    total = blocks[0] * column[0:1]
    for k in range(1, 8):
        total = total + blocks[k] * column[k : k + 1]
    return total


def coarse_operator(c, count, sums_z, couplings_z, inside_y, interface_y):
    sub = lax.broadcasted_iota(jnp.int32, c.shape, 0)
    lane = lax.broadcasted_iota(jnp.int32, c.shape, 1)
    has_low = lane > 0
    has_high = lane < count - 1

    def after(array):
        return jnp.where(sub < 7, pltpu.roll(array, 7, 0), 0.0)

    def before(array):
        return jnp.where(sub > 0, pltpu.roll(array, 1, 0), 0.0)

    def right(array):
        return jnp.where(has_high, pltpu.roll(array, LANES - 1, 1), 0.0)

    def left(array):
        return jnp.where(has_low, pltpu.roll(array, 1, 1), 0.0)

    on_low = jnp.where(has_low, 0.5 * (c + left(c)), c)
    on_high = jnp.where(has_high, 0.5 * (c + right(c)), c)
    tested = []
    for place, value in enumerate((c, on_low, on_high)):
        slope = jnp.where(sub > 0, 0.5 * (value - before(value)), 0.0)
        coupling = couplings_z[place]
        force = sums_z[place] * slope - coupling * after(slope) - before(coupling * slope)
        force = jnp.where(sub > 0, force, 0.0)
        tested.append(0.5 * (force - after(force)))
    result = tested[0] + jnp.where(has_low, 0.5, 1.0) * tested[1] + jnp.where(has_high, 0.5, 1.0) * tested[2]
    result = result + 0.5 * right(tested[1]) + 0.5 * left(tested[2])

    interface = jnp.where(sub > 0, 0.5 * (c + before(c)), 0.0)
    for side, (move, there) in enumerate(((left, has_low), (right, has_high))):
        force = inside_y[side] * jnp.where(there, 0.5 * (move(c) - c), 0.0)
        face = interface_y[side] * jnp.where(there, 0.5 * (move(interface) - interface), 0.0)
        force = force + 0.5 * (face + after(face))
        back = right if side == 0 else left
        result = result + 0.5 * (back(force) - force)

    end = float(WEIGHT[0])
    mass = (2.0 - 2.0 * end) * c + end * (interface + after(interface))
    mass = mass + jnp.where((sub == 0) | (sub == 7), end * c, 0.0)
    beside = jnp.where(has_low, 0.5 * (mass + left(mass)), 0.0)
    scaled = (2.0 * EY - 2.0 * end) * mass + end * (beside + right(beside))
    scaled = scaled + jnp.where(has_low, 0.0, end * mass) + jnp.where(has_high, 0.0, end * mass)
    return result + HELM_COEF / 8.0 * float(np.sum(WX)) * scaled


def coarse_kernel(count, near, gathered, out_ref, wide, turned):
    lanes = LANES
    sub = lax.broadcasted_iota(jnp.int32, (8, lanes), 0)
    lane = lax.broadcasted_iota(jnp.int32, (8, lanes), 1)
    wide[...] = jnp.zeros((LANES, LANES), F32)
    wide[0:count] = gathered[...]
    turned[...] = wide[...].T

    def value(index):
        return turned[pl.ds(index, 8, stride=16), :]

    def move(array, dz, dy):
        if dz:
            array = pltpu.roll(array, (-dz) % 8, 0)
        if dy:
            array = pltpu.roll(array, (-dy) % lanes, 1)
        return array

    kbar = jnp.where(lane < count, value(0), 1.0)
    above = move(kbar, 1, 0)
    link_z = jnp.where(sub < 7, 2.0 * kbar * above / (kbar + above) * (EY * EX / EZ), 0.0)
    link_z = jnp.where(lane < count, link_z, 0.0)
    beside = move(kbar, 0, 1)
    link_y = 2.0 * kbar * beside / (kbar + beside) * (EZ * EX / EY)
    link_y = jnp.where(lane < count - 1, link_y, 0.0)
    back_z = move(link_z, -1, 0)
    back_y = move(link_y, 0, -1)
    diagonal = HELM_COEF * EZ * EY * EX + link_z + back_z + link_y + back_y
    blocks = []
    for r in range(8):
        row = jnp.where(sub == r, diagonal, 0.0)
        row = jnp.where(sub == r + 1, -back_z, row)
        row = jnp.where(sub == r - 1, -link_z, row)
        blocks.append(row)

    levels = []
    step = 1
    while step < count:
        inverse = invert(blocks, sub)
        if step == 1:
            up, low = -link_y, -back_y
            solved_up = [row * up for row in inverse]
            solved_low = [row * low for row in inverse]
            pull_up = [up[r : r + 1] * solved_up[r] for r in range(8)]
            pull_low = [low[r : r + 1] * solved_low[r] for r in range(8)]
            new_low = [up[r : r + 1] * solved_low[r] for r in range(8)]
            new_up = [low[r : r + 1] * solved_up[r] for r in range(8)]
        else:
            solved_up, solved_low = multiply(inverse, upper), multiply(inverse, lower)
            pull_up = multiply_turned(solved_up, upper)
            pull_low = multiply_turned(solved_low, lower)
            if 2 * step < count:
                new_low = multiply_turned(solved_up, lower)
                new_up = multiply_turned(solved_low, upper)
        levels.append((step, solved_up, solved_low))
        blocks = [
            blocks[r] - move(pull_up[r], 0, -step) - move(pull_low[r], 0, step) for r in range(8)
        ]
        if 2 * step < count:
            lower = [-move(row, 0, -step) for row in new_low]
            upper = [-move(row, 0, step) for row in new_up]
        step *= 2
    inverse = invert(blocks, sub)

    def solve(column):
        for distance, solved_up, solved_low in levels:
            before = move(apply_turned(solved_up, column), 0, -distance)
            after = move(apply_turned(solved_low, column), 0, distance)
            column = column - before - after
        return apply_turned(inverse, column)

    first = solve(value(1))
    totals = coarse_operator(
        first,
        count,
        [value(5 + k) for k in range(3)],
        [value(8 + k) for k in range(3)],
        [value(11), value(12)],
        [value(13), value(14)],
    )
    totals = totals + value(3)
    totals = totals + jnp.where(lane < count - 1, move(value(2), 0, 1), 0.0)
    totals = totals + jnp.where(lane > 0, move(value(4), 0, -1), 0.0)
    totals = jnp.where(lane < count, totals, 0.0)
    second = solve(totals)
    gx = near[4].astype(jnp.int32)
    gy = near[5].astype(jnp.int32)
    for at, solved in ((0, first), (8, second)):
        turned_z = pltpu.roll(solved, (10 - gx) % 8, 0)
        out_ref[at : at + 8] = pltpu.roll(turned_z, (lanes + 1 - gy) % lanes, 1)


def coarse_columns(near, coarse, start, count):
    row, has_low, has_high = ring_rows(near)
    below = jnp.where(row < RING - 1, 1.0, jnp.where(row <= RING, 0.5, 0.0)) * has_low
    above = jnp.where(row > RING + ROWS, 1.0, jnp.where(row >= RING + ROWS - 1, 0.5, 0.0)) * has_high
    edge = jnp.where((row > RING) & (row < RING + ROWS - 1), 1.0, 0.0)
    edge = jnp.where(row == RING, near[2], jnp.where(row == RING + ROWS - 1, near[3], edge))
    edge = jnp.where(row == RING - 1, 0.5 * has_low, edge)
    edge = jnp.where(row == RING + ROWS, 0.5 * has_high, edge)
    columns = []
    for a in range(start, start + count):
        low, own, high = (coarse[a : a + 1, b : b + 1] for b in range(3))
        columns.append(below * low + edge * own + above * high)
    return columns


def coarse_planes(columns, low, high):
    before, inside, after = columns
    return inside, low * (before - inside), high * (after - inside)


def add_coarse(local, columns):
    inside, first, last = columns
    planes = [local[i] + inside for i in range(8)]
    planes[0] = planes[0] + first
    planes[7] = planes[7] + last
    return stack(planes)


def coarse_applied(columns, flux, packed):
    inside, first, last = columns
    slopes = [
        flux[i] * (float(DERIV[i, 0]) * first + float(DERIV[i, 7]) * last) for i in range(8)
    ]
    fz = along_z(slopes, DERIV.T)
    three = stack([inside + first, inside, inside + last])
    gy = along_y(three, packed, 0)
    fy = along_y(
        stack([flux[i] * gy[0 if i == 0 else 2 if i == 7 else 1] for i in range(8)]), packed, 1
    )
    plane_w = packed[0:WIDE]
    planes = []
    for i in range(8):
        plane = three[0 if i == 0 else 2 if i == 7 else 1]
        planes.append(fz[i] + fy[i] + (HELM_COEF * 0.125 * float(WEIGHT[i])) * (plane_w * plane))
    return stack(planes)


def face_applied(planes, payload, packed, rows, in_grid):
    inside, first, last = planes
    fields = [inside + (first if i == 0 else last if i == 7 else 0.0) for i in rows]
    gy = along_y(stack(fields), packed, 0)
    fy = along_y(stack([payload[6 + k] * gy[k] for k in range(2)]), packed, 1)
    plane_w = packed[0:WIDE]
    result = []
    for k, i in enumerate(rows):
        slopes = payload[2 + k] * first + payload[4 + k] * last
        mass = (HELM_COEF * 0.125 * float(WEIGHT[i])) * in_grid * (plane_w * fields[k])
        result.append(payload[k] + slopes + fy[k] + mass)
    return result


def apply_kernel(
    near, packed, tables, coarse, flux, zl, yl, ylo, yhi,
    z_ref, y_ref, w_ref, wlo, whi,
):
    columns = coarse_columns(near, coarse, 0, 5)
    own = coarse_planes(columns[1:4], 1.0 - near[0], 1.0 - near[1])
    field = add_coarse(zl[...], own)[:, RING : RING + ROWS]
    z_ref[...] = field
    applied = yl[...] + coarse_applied(own, flux[...], packed)
    y_ref[...] = applied[:, RING : RING + ROWS]
    lower = coarse_planes(columns[0:3], 1.0 - near[7], 0.5)
    upper = coarse_planes(columns[2:5], 0.5, 1.0 - near[6])
    planes = [applied[i] for i in range(8)]
    planes += face_applied(lower, ylo, packed, (6, 7), 2.0 - 2.0 * near[0])
    planes += face_applied(upper, yhi, packed, (0, 1), 2.0 - 2.0 * near[1])
    planes = solve_elements(planes, packed, tables, 1)
    row = lax.broadcasted_iota(jnp.int32, (ROWS, LANES), 0)
    _, has_low, has_high = ring_rows(near)
    in_grid = jnp.where(row == 0, has_low, jnp.where(row == ROWS - 1, has_high, 1.0))
    for i in range(8):
        first = (1.0 - has_low) * planes[i][ROWS : ROWS + 1]
        last = (1.0 - has_high) * planes[i][ROWS + 1 : ROWS + 2]
        alone = jnp.where(row == 0, first, jnp.where(row == ROWS - 1, last, 0.0))
        planes[i] = planes[i][0:ROWS] * in_grid + alone
    store_faces(planes, near, w_ref, wlo, whi)


def second_kernel(near, packed, coarse, flux, b, y, z, w, x_ref, kx_ref, stat):
    columns = [column[RING : RING + ROWS] for column in coarse_columns(near, coarse, 9, 3)]
    field = add_coarse(w[...], coarse_planes(columns, 1.0 - near[0], 1.0 - near[1]))
    x_ref[...] = field
    fluxes = flux[:, RING : RING + ROWS]
    gz = along_z([field[i] for i in range(8)], DERIV)
    gy = along_y(field, packed, 0)
    gx = along_x(field, packed, 0)
    slopes = [fluxes[i] * gz[i] for i in range(8)]
    ends = (0, 7)
    back = along_z(slopes, DERIV.T[[0, 7]])
    back_y = along_y(stack([fluxes[i] * gy[i] for i in ends]), packed, 1)
    back_x = along_x(stack([fluxes[i] * gx[i] for i in ends]), packed, 1)
    plane_w = packed[0:ROWS]
    mass = HELM_COEF * 0.125
    for k, i in enumerate(ends):
        weighted = (mass * float(WEIGHT[i])) * (plane_w * field[i])
        kx_ref[k] = back[k] + back_y[k] + back_x[k] + weighted
    energy = None
    for i in range(8):
        term = slopes[i] * gz[i] + fluxes[i] * (gy[i] * gy[i] + gx[i] * gx[i])
        term = term + (mass * float(WEIGHT[i])) * (plane_w * field[i] * field[i])
        energy = term if energy is None else energy + term
    first, right = z[...], b[...]
    sums = [right * first, y[...] * first, right * field, y[...] * field]
    stat[...] = lane_row([jnp.sum(term) for term in sums] + [jnp.sum(energy)])


def face_kernel(packed, flux, b, y, kx, zlo, zhi, stat_in, stat):
    faces = stack([zlo[...], zhi[...]])
    fluxes = flux[:, RING : RING + ROWS]
    gy = along_y(faces, packed, 0)
    gx = along_x(faces, packed, 0)
    plane_w = packed[0:ROWS]
    energy = 2.0 * (kx[0] * faces[0] + kx[1] * faces[1])
    for k, i in enumerate((0, 7)):
        mass = (HELM_COEF * 0.125 * float(WEIGHT[i])) * (plane_w * faces[k] * faces[k])
        energy = energy + mass + fluxes[i] * (gy[k] * gy[k] + gx[k] * gx[k])
    for i in range(8):
        slope = float(DERIV[i, 0]) * faces[0] + float(DERIV[i, 7]) * faces[1]
        energy = energy + fluxes[i] * slope * slope
    sums = [
        0.0,
        0.0,
        jnp.sum(b[0] * faces[0] + b[7] * faces[1]),
        jnp.sum(y[0] * faces[0] + y[7] * faces[1]),
        jnp.sum(energy),
    ]
    stat[...] = jnp.broadcast_to(stat_in[...] + lane_row(sums), stat.shape)


def combine_kernel(sums, z, x, zlo, zhi, p_ref):
    total = jnp.sum(sums[...], axis=0, keepdims=True)
    rz, pap, rq, aq, qhq = (total[:, k : k + 1] for k in range(5))
    step = rz / pap
    rz_next = step * (step * aq - rq)
    beta = rz_next / rz
    grown = 1.0 + beta
    curved = grown * grown * pap - 2.0 * step * grown * aq + step * step * qhq
    step_next = rz_next / curved
    on_z = step + step_next * grown
    on_q = step_next * step
    for i in range(8):
        plane = x[i]
        if i == 0:
            plane = plane + zlo[...]
        if i == 7:
            plane = plane + zhi[...]
        p_ref[i] = on_z * z[i] - on_q * plane


def run(kernel, outs, smem, args, scratch=(), flops=1000000, place=VMEM, limit=LIMIT):
    nbytes = sum(4 * int(np.prod(out)) for out in outs) * 2
    return pl.pallas_call(
        kernel,
        out_shape=[jax.ShapeDtypeStruct(out, F32) for out in outs],
        in_specs=[pl.BlockSpec(memory_space=SMEM) for _ in smem]
        + [pl.BlockSpec(memory_space=place) for _ in args],
        out_specs=[pl.BlockSpec(memory_space=VMEM) for _ in outs],
        scratch_shapes=list(scratch),
        compiler_params=pltpu.CompilerParams(vmem_limit_bytes=limit),
        cost_estimate=pl.CostEstimate(flops=flops, bytes_accessed=nbytes, transcendentals=0),
    )(*smem, *args)


def shift(axis, low_face, high_face):
    count = lax.axis_size(axis)
    forward = [(i, i + 1) for i in range(count - 1)]
    backward = [(target, source) for source, target in forward]
    return lax.ppermute(high_face, axis, forward), lax.ppermute(low_face, axis, backward)


def body(level_set, velocity, source, wick_solid):
    block = level_set.shape
    count_gx = lax.axis_size("gx")
    count_gy = lax.axis_size("gy")
    index_gx = lax.axis_index("gx")
    index_gy = lax.axis_index("gy")

    def ends(index, count):
        return [jnp.where(index > 0, 0.5, 1.0), jnp.where(index < count - 1, 0.5, 1.0)]

    place = [index_gx.astype(F32), index_gy.astype(F32)]
    beyond = [
        jnp.where(index_gx < count_gx - 2, 0.5, 1.0),
        jnp.where(index_gx > 1, 0.5, 1.0),
    ]
    near = jnp.stack(ends(index_gx, count_gx) + ends(index_gy, count_gy) + place + beyond)
    near = near.astype(F32)
    packed = jnp.asarray(PACKED)
    tables = jnp.asarray(TABLES)
    face = (ROWS, LANES)
    wide_block = (8, WIDE, LANES)
    wide_face = (WIDE, LANES)
    rim = (12, TILE, LANES)

    b, l, zlo, zhi, solid = run(
        advect_kernel,
        [block, block, (3, *face), (3, *face), (8, LANES)],
        [],
        [
            pltpu.with_memory_space_constraint(array, pltpu.HBM)
            for array in (level_set, velocity, source, packed, wick_solid.reshape(EY, EX))
        ],
        [VMEM(block, F32), VMEM((3, *block), F32), VMEM(block, F32), VMEM(PACKED.shape, F32)]
        + [VMEM((EY, EX), jnp.int32), pltpu.SemaphoreType.DMA((5,))],
        place=pltpu.HBM,
    )
    zlo, zhi = shift("gx", zlo, zhi)
    ylo, yhi = run(rim_kernel, [rim, rim], [], [solid, b, l, zlo, zhi])
    ylo, yhi = shift("gy", ylo, yhi)
    w, wlo, whi = run(
        first_schwarz_kernel,
        [wide_block, wide_face, wide_face],
        [near],
        [packed, tables, b, zlo, zhi, ylo, yhi],
    )
    wlo, whi = shift("gx", wlo, whi)
    level_new, flux, stat = run(
        level_kernel,
        [block, wide_block, (1, LANES)],
        [near],
        [solid, packed, b, l, zlo, zhi, ylo, yhi],
        flops=20000000,
    )
    zl, yl, zlo, zhi, stat = run(
        galerkin_kernel,
        [wide_block, wide_block, wide_block, wide_block, (count_gx, LANES)],
        [near],
        [packed, stat, flux, w, wlo, whi],
    )
    zlo, zhi = shift("gx", zlo, zhi)
    gathered = lax.all_to_all(stat, "gx", 0, 0, tiled=True)
    (column,) = run(column_kernel, [(count_gy, LANES)], [], [gathered])
    gathered = lax.all_to_all(column, "gy", 0, 0, tiled=True)
    (coarse,) = run(
        functools.partial(coarse_kernel, count_gy),
        [(16, LANES)],
        [near],
        [gathered],
        [VMEM((LANES, LANES), F32), VMEM((LANES, LANES), F32)],
    )
    z, y, w, wlo, whi = run(
        apply_kernel,
        [block, block, block, face, face],
        [near],
        [packed, tables, coarse, flux, zl, yl, zlo, zhi],
    )
    zlo, zhi = shift("gx", wlo, whi)
    x, kx, sums = run(
        second_kernel,
        [block, (2, *face), (1, LANES)],
        [near],
        [packed, coarse, flux, b, y, z, w],
        flops=20000000,
    )
    (sums,) = run(
        face_kernel, [(count_gx, LANES)], [], [packed, flux, b, y, kx, zlo, zhi, sums]
    )
    tile = lax.all_to_all(sums, "gx", 0, 0, tiled=True)
    wide = jnp.broadcast_to(jnp.sum(tile, axis=0, keepdims=True), (count_gy, LANES))
    wide = lax.all_to_all(wide, "gy", 0, 0, tiled=True)
    (pressure,) = run(combine_kernel, [block], [], [wide, z, x, zlo, zhi])
    return (level_new, pressure)


def solution(mesh):
    placed = (
        P("gx", "gy", None),
        P(None, "gx", "gy", None),
        P("gx", "gy", None),
        P("gx", "gy", None),
    )
    return jax.shard_map(
        body,
        mesh=mesh,
        in_specs=placed,
        out_specs=(P("gx", "gy", None), P("gx", "gy", None)),
        check_vma=False,
    )
```

```python
import functools

import jax
import jax.numpy as jnp
import numpy as np
from jax import lax
from jax.experimental import pallas as pl
from jax.experimental.pallas import tpu as pltpu
from jax.sharding import PartitionSpec as P

EZ = 1
EY = 4
EX = 16
ROWS = 8 * EY
LANES = 8 * EX

TIME_STEP = 0.02
HELM_COEF = 0.25
LEVEL_WIDTH = 0.25
GAS_RATIO = 10.0
SOLID_FACTOR = 0.25
SCHWARZ_SCALE = 0.5
SCHWARZ_SHIFT = 0.05

F32 = jnp.float32
BF16 = jnp.bfloat16
VMEM = pltpu.VMEM
SMEM = pltpu.SMEM
LIMIT = 24 * 1024 * 1024


def gll_tables():
    gll_nodes = np.array(
        [
            -1.0,
            -0.8717401485096066,
            -0.5917001814331423,
            -0.2092992179024789,
            0.2092992179024789,
            0.5917001814331423,
            0.8717401485096066,
            1.0,
        ]
    )
    weight_np = np.array(
        [
            1.0 / 28.0,
            0.21070422714350603,
            0.3411226924835044,
            0.4124587946587038,
            0.4124587946587038,
            0.3411226924835044,
            0.21070422714350603,
            1.0 / 28.0,
        ]
    )
    bary_weights = np.array(
        [1.0 / np.prod([gll_nodes[i] - gll_nodes[j] for j in range(8) if j != i]) for i in range(8)]
    )
    derivative = np.zeros((8, 8))
    for i in range(8):
        for j in range(8):
            if i != j:
                derivative[i, j] = bary_weights[j] / bary_weights[i] / (gll_nodes[i] - gll_nodes[j])
        derivative[i, i] = -np.sum(derivative[i])
    return (weight_np, derivative)


def sine_tables():
    indices = np.arange(10) + 1.0
    sine_basis = np.sqrt(2.0 / 11.0) * np.sin(np.pi * np.outer(indices, indices) / 11.0)
    eigen_vals = 2.0 - 2.0 * np.cos(np.pi * indices / 11.0)
    return (sine_basis, eigen_vals)


WEIGHT, DERIV = gll_tables()
SINE, EIGEN = sine_tables()


def split_const(matrix):
    single = matrix.astype(np.float32)
    high = single.astype(jnp.bfloat16)
    low = (single - high.astype(np.float32)).astype(jnp.bfloat16)
    return high, low


def line_maps(count):
    length = 8 * count
    total = length + 4

    def column(position):
        if 0 <= position < length:
            return position
        return {-2: length, -1: length + 1, length: length + 2, length + 1: length + 3}[position]

    assembled = {}
    for position in range(-2, length + 2):
        row = np.zeros(total)
        row[column(position)] = 1.0
        if 0 <= position < length:
            if position % 8 == 0:
                row[column(position - 1)] += 1.0
            if position % 8 == 7:
                row[column(position + 1)] += 1.0
        assembled[position] = row
    forward = np.zeros((10 * count, total))
    for element in range(count):
        places = [8 * element - 2] + list(range(8 * element, 8 * element + 8)) + [8 * element + 9]
        forward[10 * element : 10 * element + 10] = SINE @ np.stack([assembled[p] for p in places])
    backward = np.zeros((length, 10 * count))
    for element in range(count):
        backward[8 * element : 8 * element + 8, 10 * element : 10 * element + 10] = SINE[1:9]
    for element in range(count - 1):
        first, second = 8 * element + 7, 8 * element + 8
        mean = 0.5 * (backward[first] + backward[second])
        backward[first] = mean
        backward[second] = mean
    return forward, backward


RING = 16
WIDE = ROWS + 2 * RING
REACH = 26
TILE = 48
TILE_B = 32


def ring_maps(reach, depth, inside):
    count = EY + 2 * depth
    forward, _ = line_maps(count)
    length = 8 * count
    columns = np.zeros((10 * count, len(inside)))
    for at, position in enumerate(inside):
        place = None if position is None else position + 8 * depth
        if place is None or place < -2 or place > length + 1:
            continue
        source = place if 0 <= place < length else {-2: 0, -1: 1}.get(place, place - length + 2) + length
        columns[:, at] = forward[:, source]
    _, backward = line_maps(count)
    own = 8 * depth
    rows = np.concatenate(
        [
            backward[own - reach : own + ROWS + reach],
            np.zeros((8, 10 * count)),
        ]
    )
    rows[ROWS + 2 * reach, 10 * depth : 10 * depth + 10] = SINE[1]
    rows[ROWS + 2 * reach + 1, 10 * (depth + EY - 1) : 10 * (depth + EY)] = SINE[8]
    return columns, rows


FZ, BZ = line_maps(1)
TILES = list(range(-REACH, 0)) + [None] * (TILE_B - REACH) + list(range(ROWS))
TILES += list(range(ROWS, ROWS + REACH)) + [None] * (TILE_B - REACH)
FY_A, BY_A = ring_maps(RING, 3, TILES)
FY_B, BY_B = ring_maps(0, 1, list(range(-RING, ROWS + RING)))
INNER = np.arange(40, 60)
OUTER = np.concatenate([np.arange(0, 40), np.arange(60, 100)])
FY_I, BY_I = FY_A[INNER, TILE_B : TILE_B + ROWS], BY_A[RING : RING + ROWS, INNER]
FY_A, BY_A = FY_A[OUTER], BY_A[:, OUTER]
STEP_A = 80
STEP_B = 64
STEP_I = 32


def padded(forward, backward, step):
    forward = np.pad(forward, ((0, step - forward.shape[0]), (0, 0)))
    return forward, np.pad(backward, ((0, 0), (0, step - backward.shape[1])))


FY_A, BY_A = padded(FY_A, BY_A, STEP_A)
FY_B, BY_B = padded(FY_B, BY_B, STEP_B)
FY_I, BY_I = padded(FY_I, BY_I, STEP_I)
FX, BX = line_maps(EX)
FX = FX[:, :LANES]


FX_H, FX_L = split_const(FX.T.copy())
BX_H, BX_L = split_const(BX.T.copy())


def wide_const(table):
    high, low = split_const(table)
    return np.concatenate([high, high, low], axis=1)


def pack_tables(tables):
    places, pieces, at = [], [], 0
    for table in tables:
        rows = -(-table.shape[0] // 16) * 16
        extra = ((0, rows - table.shape[0]), (0, 384 - table.shape[1]))
        pieces.append(np.pad(table.astype(np.float32), extra))
        places.append((at, rows, table.shape[1]))
        at += rows
    return np.concatenate(pieces).astype(jnp.bfloat16), places


TABLES, PLACES = pack_tables(
    [
        np.concatenate([FX_H, FX_H], axis=0),
        FX_L,
        BX_H,
        BX_L,
        wide_const(FY_A),
        wide_const(BY_A),
        wide_const(FY_B),
        wide_const(BY_B),
        wide_const(FY_I),
        wide_const(BY_I),
    ]
)


def roll_table():
    table = np.zeros((2, 8, 8, LANES))
    for kind, matrix in enumerate((DERIV, DERIV.T)):
        for k in range(8):
            for i in range(8):
                table[kind, k, i, :] = matrix[i, (i + k) % 8]
    return table.reshape(2 * 64, LANES)


WY = np.tile(WEIGHT, WIDE // 8)
WX = np.tile(WEIGHT, EX)


def inner_count(count):
    mult = np.ones(8 * count)
    position = np.arange(8 * count)
    mult[(position % 8 == 0) & (position > 0)] += 1.0
    mult[(position % 8 == 7) & (position < 8 * count - 1)] += 1.0
    return mult


END_MASS = np.where(np.arange(WIDE) % 8 % 7 == 0, 2.0, 1.0)
INV_MASS = (8.0 / (WY * END_MASS)[:, None] / (WX * inner_count(EX))[None, :]).astype(np.float32)

AT_ROLLS = WIDE
AT_DX = AT_ROLLS + 128
AT_DXT = AT_DX + LANES
AT_SQUARE = AT_DXT + LANES
AT_MASS = AT_SQUARE + 16
AT_SPREAD = AT_MASS + WIDE
AT_EIGEN_Y = AT_SPREAD + EX
AT_EIGEN_X = AT_EIGEN_Y + STEP_A
LAM_Y = np.resize(EIGEN, STEP_A)
LAM_X = np.resize(EIGEN, 8 * LANES).reshape(8, LANES)
PACKED = np.concatenate(
    [
        WY[:, None] * WX[None, :],
        roll_table(),
        np.kron(np.eye(EX), DERIV.T),
        np.kron(np.eye(EX), DERIV),
        np.repeat(DERIV[:, :1] ** 2, LANES, axis=1),
        np.repeat(DERIV[:, 7:] ** 2, LANES, axis=1),
        INV_MASS,
        np.kron(np.eye(EX), np.ones((1, 8))),
        np.repeat(LAM_Y[:, None], LANES, axis=1),
        LAM_X,
    ]
).astype(np.float32)


def parts(values):
    high = values.astype(BF16)
    low = (values - high.astype(F32)).astype(BF16)
    return high, low


def dot(left, right):
    return jnp.dot(left, right, preferred_element_type=F32)


def left_pairs(table, planes):
    results = []
    for i in range(0, len(planes), 2):
        high, low = parts(jnp.concatenate([planes[i], planes[i + 1]], axis=1))
        both = dot(table, jnp.concatenate([high, low, high], axis=0))
        results += [both[:, 0:LANES], both[:, LANES : 2 * LANES]]
    return results


def along_z(values, matrix):
    rows = []
    for i in range(matrix.shape[0]):
        total = None
        for j in range(matrix.shape[1]):
            if matrix[i, j] == 0.0:
                continue
            term = float(matrix[i, j]) * values[j]
            total = term if total is None else total + term
        rows.append(total)
    return rows


def along_y(values, packed, kind):
    count, rows = values.shape[:2]
    grouped = values.reshape(count * rows // 8, 8, LANES)
    start = AT_ROLLS + 64 * kind
    total = packed[start : start + 8][None] * grouped
    for k in range(1, 8):
        total = total + packed[start + 8 * k : start + 8 * k + 8][None] * pltpu.roll(grouped, 8 - k, 1)
    return total.reshape(count, rows, LANES)


def along_x(values, packed, kind):
    start = AT_DXT if kind else AT_DX
    high, low = parts(packed[start : start + LANES])
    first, rest = parts(values.reshape(values.shape[0] * values.shape[1], LANES))
    total = dot(
        jnp.concatenate([first, rest], axis=1), jnp.concatenate([high, high], axis=0)
    ) + dot(first, low)
    return total.reshape(values.shape)


def stack(planes):
    return jnp.concatenate([plane[None] for plane in planes], axis=0)


def edge_rows(rows, low, high):
    position = lax.broadcasted_iota(jnp.int32, (rows, LANES), 0)
    return jnp.where(position == 0, low, jnp.where(position == rows - 1, high, 1.0))


def local_operator(values, flux, packed):
    plane_w = packed[0 : values.shape[1]]
    gz = along_z([values[i] for i in range(8)], DERIV)
    fz = along_z([flux[i] * gz[i] for i in range(8)], DERIV.T)
    total = along_y(flux * along_y(values, packed, 0), packed, 1)
    total = total + along_x(flux * along_x(values, packed, 0), packed, 1)
    planes = [
        total[i] + fz[i] + (HELM_COEF * 0.125 * float(WEIGHT[i])) * (plane_w * values[i])
        for i in range(8)
    ]
    return stack(planes)


def add_planes(own, low_z, high_z):
    planes = [own[i] for i in range(8)]
    planes[0] = planes[0] + low_z
    planes[7] = planes[7] + high_z
    return stack(planes)


def solve_elements(planes, packed, tables, kind):
    def table(index):
        at, rows, width = PLACES[index]
        return tables[at : at + rows, 0:width]

    fxhh, fxl, bxh, bxl = (table(index) for index in range(4))
    spectral = left_pairs(table(4 + 2 * kind), along_z(planes, FZ))
    high, low = parts(jnp.concatenate(spectral, axis=0))
    wide = dot(jnp.concatenate([high, low], axis=1), fxhh) + dot(high, fxl)
    step = PLACES[4 + 2 * kind][1]
    column = packed[AT_EIGEN_Y : AT_EIGEN_Y + step]
    rest = 10 * EX - LANES
    lam = jnp.concatenate(
        [
            column + packed[AT_EIGEN_X : AT_EIGEN_X + 1],
            column[:, 0:rest] + packed[AT_EIGEN_X + 1 : AT_EIGEN_X + 2, 0:rest],
        ],
        axis=1,
    )
    scaled = [
        wide[step * i : step * (i + 1)]
        / (SCHWARZ_SCALE * lam + float(SCHWARZ_SCALE * EIGEN[i] + SCHWARZ_SHIFT))
        for i in range(10)
    ]
    high, low = parts(jnp.concatenate(scaled, axis=0))
    back = dot(high, bxh) + dot(low, bxh) + dot(high, bxl)
    back = left_pairs(table(5 + 2 * kind), [back[step * i : step * (i + 1)] for i in range(10)])
    return along_z(back, BZ)


def store_faces(planes, near, out_ref, low_ref, high_ref):
    planes[0] = planes[0] * near[0]
    planes[7] = planes[7] * near[1]
    for i in range(8):
        out_ref[i] = planes[i]
    low_ref[...] = planes[0]
    high_ref[...] = planes[7]


def ring_rows(near):
    row = lax.broadcasted_iota(jnp.int32, (WIDE, LANES), 0)
    return row, 2.0 - 2.0 * near[2], 2.0 - 2.0 * near[3]


def partition_total(own, low_z, high_z, low_y, high_y, near):
    def planes(array):
        total = near[0] * array[0] + near[1] * array[7]
        for i in range(1, 7):
            total = total + array[i]
        return total

    total = planes(own) + 0.5 * (low_z[1] + high_z[0])
    below = planes(low_y) + 0.5 * (low_y[9] + low_y[10])
    above = planes(high_y) + 0.5 * (high_y[9] + high_y[10])
    faces = 0.5 * (below[REACH - 1 : REACH] + above[0:1])
    return jnp.sum(total * edge_rows(ROWS, near[2], near[3])) + jnp.sum(faces)


def lane_row(entries):
    lane = lax.broadcasted_iota(jnp.int32, (1, LANES), 1)
    row = jnp.zeros((1, LANES), F32)
    for index, value in enumerate(entries):
        row = jnp.where(lane == index, value, row)
    return row


def advect_kernel(
    lev_in, vel_in, src_in, packed_in, solid_in, b_ref, l_ref, zlo, zhi, solid_ref,
    lev, vel, src, packed, solid, sems,
):
    pairs = ((lev_in, lev), (packed_in, packed), (vel_in, vel), (src_in, src), (solid_in, solid))
    copies = [
        pltpu.make_async_copy(source, target, sems.at[index])
        for index, (source, target) in enumerate(pairs)
    ]
    for copy in copies:
        copy.start()
    copies[0].wait()
    level = lev[...]
    gz = stack(along_z([level[i] for i in range(8)], DERIV))
    copies[1].wait()
    gy = along_y(level, packed, 0)
    gx = along_x(level, packed, 0)
    for copy in copies[2:]:
        copy.wait()
    spread = packed[AT_SPREAD : AT_SPREAD + EX].astype(BF16)
    in_solid = dot(solid[...].astype(F32).astype(BF16), spread)
    solid_ref[...] = jnp.concatenate([in_solid, jnp.zeros((8 - EY, LANES), F32)], axis=0)
    v0, v1, v2 = vel[0], vel[1], vel[2]
    moved = level - (2.0 * TIME_STEP) * (v0 * gz + v1 * gy + v2 * gx)
    diverge = stack(along_z([v0[i] for i in range(8)], DERIV))
    diverge = diverge + along_y(v1, packed, 0) + along_x(v2, packed, 0)
    force = src[...] - (2.0 * TIME_STEP) * diverge
    weights = packed[0:ROWS]
    for i in range(8):
        mass = (0.125 * float(WEIGHT[i])) * weights
        term = mass * force[i]
        moved_i = mass * moved[i]
        b_ref[i] = term
        l_ref[i] = moved_i
        if i < 2:
            zlo[i] = term
        if i == 0:
            zlo[2] = moved_i
        if i > 5:
            zhi[i - 6] = term
        if i == 7:
            zhi[2] = moved_i


def rim_kernel(solid, b, l, low_z, high_z, low_y, high_y):
    in_solid = solid[...]
    rest = TILE - REACH - RING - 1

    def rows(planes, at, level, far, extra=None):
        start = ROWS - REACH if far else 0
        pieces = [planes[at, start : start + REACH]]
        if level is None:
            pieces.append(jnp.zeros((RING + 1, LANES), F32))
        else:
            array, index = level
            start = ROWS - RING - 1 if far else 0
            pieces.append(array[index, start : start + RING + 1])
        if extra is None:
            pieces.append(jnp.zeros((rest, LANES), F32))
        else:
            pieces += [extra, jnp.zeros((rest - 2, LANES), F32)]
        return jnp.concatenate(pieces, axis=0)

    for far, out in ((False, low_y), (True, high_y)):
        extra = in_solid[EY - 2 : EY] if far else in_solid[0:2]
        for i in range(8):
            out[i] = rows(b, i, (l, i), far, extra if i == 0 else None)
        for i in range(2):
            out[8 + i] = rows(low_z, i, (low_z, 2) if i == 1 else None, far)
            out[10 + i] = rows(high_z, i, (high_z, 2) if i == 0 else None, far)


def level_kernel(
    near, solid, packed, b, l, zlo, zhi, ylo, yhi, level_ref, flux_ref, stat
):
    row, has_low, has_high = ring_rows(near)
    at = REACH

    def wide_rows(slot, own):
        return jnp.concatenate(
            [ylo[slot, at + 1 : at + 1 + RING], own, yhi[slot, at : at + RING]], axis=0
        )

    planes = []
    for i in range(8):
        plane = wide_rows(i, l[i])
        first = ylo[i, at : at + 1]
        last = yhi[i, at + RING : at + RING + 1]
        if i == 0:
            plane = plane + wide_rows(9, zlo[2])
            first = first + ylo[9, at : at + 1]
            last = last + yhi[9, at + RING : at + RING + 1]
        if i == 7:
            plane = plane + wide_rows(10, zhi[2])
            first = first + ylo[10, at : at + 1]
            last = last + yhi[10, at + RING : at + RING + 1]
        before = jnp.where(row == 0, first, pltpu.roll(plane, 1, 0))
        after = jnp.where(row == WIDE - 1, last, pltpu.roll(plane, WIDE - 1, 0))
        plane = plane + jnp.where(row % 8 == 0, before, jnp.where(row % 8 == 7, after, 0.0))
        planes.append(plane)
    own = stack(planes)
    lane = lax.broadcasted_iota(jnp.int32, (8, WIDE, LANES), 2)
    before = jnp.where((lane % 8 == 0) & (lane > 0), pltpu.roll(own, 1, 2), 0.0)
    after = jnp.where((lane % 8 == 7) & (lane < LANES - 1), pltpu.roll(own, LANES - 1, 2), 0.0)
    own = own + before + after
    ends = jnp.where(row == RING, 2.0 * near[2], jnp.where(row == RING + ROWS - 1, 2.0 * near[3], 1.0))
    inverse = packed[AT_MASS : AT_MASS + WIDE] * ends
    in_solid = solid[...]
    solids = [ylo[0, at + RING + 1 + k : at + RING + 2 + k] for k in range(2)]
    solids += [in_solid[e : e + 1] for e in range(EY)]
    solids += [yhi[0, at + RING + 1 + k : at + RING + 2 + k] for k in range(2)]
    open_part = jnp.concatenate(
        [jnp.broadcast_to(1.0 - (1.0 - SOLID_FACTOR) * rows, (8, LANES)) for rows in solids], axis=0
    )
    in_grid = jnp.where(row < RING, has_low, jnp.where(row >= RING + ROWS, has_high, 1.0))
    flux_w = packed[0:WIDE] * in_grid
    total = jnp.zeros((ROWS, LANES), F32)
    fluxes = []
    for i in range(8):
        scale = 1.0 / float(WEIGHT[i])
        plane = own[i] * (inverse * scale)
        if i == 0:
            plane = plane * near[0]
        if i == 7:
            plane = plane * near[1]
        level_ref[i] = plane[RING : RING + ROWS]
        liquid = jax.nn.sigmoid(plane * (1.0 / LEVEL_WIDTH))
        coef = (GAS_RATIO - (GAS_RATIO - 1.0) * liquid) * open_part
        total = total + coef[RING : RING + ROWS]
        flux = (0.5 * float(WEIGHT[i])) * (coef * flux_w)
        flux_ref[i] = flux
        fluxes.append(flux[RING : RING + ROWS])
    kbar = jnp.sum(total) * (1.0 / (8 * ROWS * LANES))
    entries = [kbar, partition_total(b, zlo, zhi, ylo, yhi, near)] + [0.0] * 9
    for first, second in ((0, 0), (0, 7), (7, 7)):
        slopes = along_z(fluxes, (DERIV[:, first] * DERIV[:, second])[None, :])[0]
        column = jnp.sum(slopes, axis=1, keepdims=True)
        entries += [jnp.sum(column, axis=0, keepdims=True), column[0:1], column[ROWS - 1 : ROWS]]
    inner = fluxes[0] + fluxes[1]
    for i in range(2, 8):
        inner = inner + fluxes[i]
    for at_row, start in ((0, 0), (ROWS - 8, 8)):
        square = packed[AT_SQUARE + start : AT_SQUARE + start + 8]
        entries += [
            jnp.sum(square * plane[at_row : at_row + 8]) for plane in (inner, fluxes[0], fluxes[7])
        ]
    stat[...] = lane_row(entries)


def inner_schwarz_kernel(packed, tables, b, zlo, zhi, out_ref):
    planes = [b[i] for i in range(8)] + [zlo[0], zlo[1], zhi[0], zhi[1]]
    planes = solve_elements(planes, packed, tables, 2)
    for i in range(8):
        out_ref[i] = planes[i]


def first_schwarz_kernel(
    near, packed, tables, inner, b, zlo, zhi, ylo, yhi, w_ref, wlo, whi
):
    own = [b[i] for i in range(8)] + [zlo[0], zlo[1], zhi[0], zhi[1]]
    planes = [
        jnp.concatenate([ylo[i, 0:TILE_B], own[i], yhi[i, 0:TILE_B]], axis=0) for i in range(12)
    ]
    planes = solve_elements(planes, packed, tables, 0)
    row, has_low, has_high = ring_rows(near)
    in_grid = jnp.where(row < RING, has_low, jnp.where(row >= RING + ROWS, has_high, 1.0))
    in_grid = jnp.where(row == RING, has_low, jnp.where(row == RING + ROWS - 1, has_high, in_grid))
    rest = jnp.zeros((RING, LANES), F32)
    for i in range(8):
        first = (1.0 - has_low) * planes[i][WIDE : WIDE + 1]
        last = (1.0 - has_high) * planes[i][WIDE + 1 : WIDE + 2]
        alone = jnp.where(row == RING, first, jnp.where(row == RING + ROWS - 1, last, 0.0))
        planes[i] = planes[i][0:WIDE] * in_grid + alone
        planes[i] = planes[i] + jnp.concatenate([rest, inner[i], rest], axis=0)
    store_faces(planes, near, w_ref, wlo, whi)


def galerkin_kernel(near, packed, stat_in, flux, w, zlo, zhi, zl_ref, y_ref, ylo, yhi, stat):
    local = add_planes(w, zlo[...], zhi[...])
    zl_ref[...] = local
    applied = local_operator(local, flux[...], packed)
    y_ref[...] = applied
    fluxes = [flux[i] for i in range(8)]
    for out, rows in ((ylo, (0, 1)), (yhi, (6, 7))):
        for k, i in enumerate(rows):
            out[k] = applied[i]
            for t, end in enumerate((0, 7)):
                out[2 + 2 * t + k] = along_z(fluxes, (DERIV[:, i] * DERIV[:, end])[None, :])[0]
            out[6 + k] = fluxes[i]
    applied = applied[:, RING : RING + ROWS]
    inner = near[0] * applied[0] + near[1] * applied[7]
    for i in range(1, 7):
        inner = inner + applied[i]
    edge = edge_rows(ROWS, near[2], near[3])
    entries = [0.0, 0.0]
    for plane in ((1.0 - near[0]) * applied[0], inner, (1.0 - near[1]) * applied[7]):
        entries += [
            (1.0 - near[2]) * jnp.sum(plane[0:1]),
            jnp.sum(edge * plane),
            (1.0 - near[3]) * jnp.sum(plane[ROWS - 1 : ROWS]),
        ]
    stat[...] = jnp.broadcast_to(stat_in[...] + lane_row(entries), stat.shape)


def column_kernel(gathered, out_ref):
    values = gathered[...]
    sub = lax.broadcasted_iota(jnp.int32, (8, LANES), 0)
    lane = lax.broadcasted_iota(jnp.int32, (8, LANES), 1)
    after = jnp.where(sub < 7, pltpu.roll(values, 7, 0), 0.0)
    before = jnp.where(sub > 0, pltpu.roll(values, 1, 0), 0.0)
    first = lax.broadcasted_iota(jnp.int32, (8, 1), 0) == 0
    last = lax.broadcasted_iota(jnp.int32, (8, 1), 0) == 7

    def column(array, index):
        return array[:, index : index + 1]

    def slopes(array, pair):
        whole, low, high = (column(array, 11 + 3 * pair + k) for k in range(3))
        return whole - low - high, low, high

    merged = [column(values, 0), column(values, 1)]
    for b in range(3):
        merged.append(column(values, 5 + b) + column(after, 2 + b) + column(before, 8 + b))
    merged += [own + other for own, other in zip(slopes(values, 0), slopes(before, 2), strict=True)]
    merged += list(slopes(values, 1))
    inside, interface = [], []
    for side in range(2):
        whole, low, high = (column(values, 20 + 3 * side + k) for k in range(3))
        ends = jnp.where(first, low, 0.0) + jnp.where(last, high, 0.0)
        inside.append(whole - low - high + ends)
        interface.append(jnp.where(first, 0.0, low) + column(before, 22 + 3 * side))
    rows = jnp.zeros((8, LANES), F32)
    for index, value in enumerate(merged + inside + interface):
        rows = jnp.where(lane == index, value, rows)
    total = rows[0:1]
    for i in range(1, 8):
        total = total + pltpu.roll(rows[i : i + 1], 16 * i, 1)
    out_ref[...] = jnp.broadcast_to(total, out_ref.shape)


def invert(blocks, sub):
    for k in range(0, 8, 2):
        first, second = blocks[k], blocks[k + 1]
        a, b = first[k : k + 1], first[k + 1 : k + 2]
        c, d = second[k : k + 1], second[k + 1 : k + 2]
        scale = 1.0 / (a * d - b * c)
        first = jnp.where(sub == k, 1.0, jnp.where(sub == k + 1, 0.0, first))
        second = jnp.where(sub == k + 1, 1.0, jnp.where(sub == k, 0.0, second))
        low = (d * scale) * first - (b * scale) * second
        high = (a * scale) * second - (c * scale) * first
        pivots = (sub == k) | (sub == k + 1)
        rows = []
        for r in range(8):
            if r == k:
                rows.append(low)
            elif r == k + 1:
                rows.append(high)
            else:
                rest = jnp.where(pivots, 0.0, blocks[r])
                rows.append(rest - blocks[r][k : k + 1] * low - blocks[r][k + 1 : k + 2] * high)
        blocks = rows
    return blocks


def multiply(left, right):
    rows = []
    for r in range(8):
        total = left[r][0:1] * right[0]
        for k in range(1, 8):
            total = total + left[r][k : k + 1] * right[k]
        rows.append(total)
    return rows


def multiply_turned(left, right):
    rows = []
    for r in range(8):
        total = left[0][r : r + 1] * right[0]
        for k in range(1, 8):
            total = total + left[k][r : r + 1] * right[k]
        rows.append(total)
    return rows


def apply_turned(blocks, column):
    total = blocks[0] * column[0:1]
    for k in range(1, 8):
        total = total + blocks[k] * column[k : k + 1]
    return total


def coarse_operator(c, count, sums_z, couplings_z, inside_y, interface_y):
    sub = lax.broadcasted_iota(jnp.int32, c.shape, 0)
    lane = lax.broadcasted_iota(jnp.int32, c.shape, 1)
    has_low = lane > 0
    has_high = lane < count - 1

    def after(array):
        return jnp.where(sub < 7, pltpu.roll(array, 7, 0), 0.0)

    def before(array):
        return jnp.where(sub > 0, pltpu.roll(array, 1, 0), 0.0)

    def right(array):
        return jnp.where(has_high, pltpu.roll(array, LANES - 1, 1), 0.0)

    def left(array):
        return jnp.where(has_low, pltpu.roll(array, 1, 1), 0.0)

    on_low = jnp.where(has_low, 0.5 * (c + left(c)), c)
    on_high = jnp.where(has_high, 0.5 * (c + right(c)), c)
    tested = []
    for place, value in enumerate((c, on_low, on_high)):
        slope = jnp.where(sub > 0, 0.5 * (value - before(value)), 0.0)
        coupling = couplings_z[place]
        force = sums_z[place] * slope - coupling * after(slope) - before(coupling * slope)
        force = jnp.where(sub > 0, force, 0.0)
        tested.append(0.5 * (force - after(force)))
    result = tested[0] + jnp.where(has_low, 0.5, 1.0) * tested[1] + jnp.where(has_high, 0.5, 1.0) * tested[2]
    result = result + 0.5 * right(tested[1]) + 0.5 * left(tested[2])

    interface = jnp.where(sub > 0, 0.5 * (c + before(c)), 0.0)
    for side, (move, there) in enumerate(((left, has_low), (right, has_high))):
        force = inside_y[side] * jnp.where(there, 0.5 * (move(c) - c), 0.0)
        face = interface_y[side] * jnp.where(there, 0.5 * (move(interface) - interface), 0.0)
        force = force + 0.5 * (face + after(face))
        back = right if side == 0 else left
        result = result + 0.5 * (back(force) - force)

    end = float(WEIGHT[0])
    mass = (2.0 - 2.0 * end) * c + end * (interface + after(interface))
    mass = mass + jnp.where((sub == 0) | (sub == 7), end * c, 0.0)
    beside = jnp.where(has_low, 0.5 * (mass + left(mass)), 0.0)
    scaled = (2.0 * EY - 2.0 * end) * mass + end * (beside + right(beside))
    scaled = scaled + jnp.where(has_low, 0.0, end * mass) + jnp.where(has_high, 0.0, end * mass)
    return result + HELM_COEF / 8.0 * float(np.sum(WX)) * scaled


def coarse_kernel(count, near, gathered, out_ref, wide, turned):
    lanes = LANES
    sub = lax.broadcasted_iota(jnp.int32, (8, lanes), 0)
    lane = lax.broadcasted_iota(jnp.int32, (8, lanes), 1)
    wide[...] = jnp.zeros((LANES, LANES), F32)
    wide[0:count] = gathered[...]
    turned[...] = wide[...].T

    def value(index):
        return turned[pl.ds(index, 8, stride=16), :]

    def move(array, dz, dy):
        if dz:
            array = pltpu.roll(array, (-dz) % 8, 0)
        if dy:
            array = pltpu.roll(array, (-dy) % lanes, 1)
        return array

    kbar = jnp.where(lane < count, value(0), 1.0)
    above = move(kbar, 1, 0)
    link_z = jnp.where(sub < 7, 2.0 * kbar * above / (kbar + above) * (EY * EX / EZ), 0.0)
    link_z = jnp.where(lane < count, link_z, 0.0)
    beside = move(kbar, 0, 1)
    link_y = 2.0 * kbar * beside / (kbar + beside) * (EZ * EX / EY)
    link_y = jnp.where(lane < count - 1, link_y, 0.0)
    back_z = move(link_z, -1, 0)
    back_y = move(link_y, 0, -1)
    diagonal = HELM_COEF * EZ * EY * EX + link_z + back_z + link_y + back_y
    blocks = []
    for r in range(8):
        row = jnp.where(sub == r, diagonal, 0.0)
        row = jnp.where(sub == r + 1, -back_z, row)
        row = jnp.where(sub == r - 1, -link_z, row)
        blocks.append(row)

    levels = []
    step = 1
    while step < count:
        inverse = invert(blocks, sub)
        if step == 1:
            up, low = -link_y, -back_y
            solved_up = [row * up for row in inverse]
            solved_low = [row * low for row in inverse]
            pull_up = [up[r : r + 1] * solved_up[r] for r in range(8)]
            pull_low = [low[r : r + 1] * solved_low[r] for r in range(8)]
            new_low = [up[r : r + 1] * solved_low[r] for r in range(8)]
            new_up = [low[r : r + 1] * solved_up[r] for r in range(8)]
        else:
            solved_up, solved_low = multiply(inverse, upper), multiply(inverse, lower)
            pull_up = multiply_turned(solved_up, upper)
            pull_low = multiply_turned(solved_low, lower)
            if 2 * step < count:
                new_low = multiply_turned(solved_up, lower)
                new_up = multiply_turned(solved_low, upper)
        levels.append((step, solved_up, solved_low))
        blocks = [
            blocks[r] - move(pull_up[r], 0, -step) - move(pull_low[r], 0, step) for r in range(8)
        ]
        if 2 * step < count:
            lower = [-move(row, 0, -step) for row in new_low]
            upper = [-move(row, 0, step) for row in new_up]
        step *= 2
    inverse = invert(blocks, sub)

    def solve(column):
        for distance, solved_up, solved_low in levels:
            before = move(apply_turned(solved_up, column), 0, -distance)
            after = move(apply_turned(solved_low, column), 0, distance)
            column = column - before - after
        return apply_turned(inverse, column)

    first = solve(value(1))
    totals = coarse_operator(
        first,
        count,
        [value(5 + k) for k in range(3)],
        [value(8 + k) for k in range(3)],
        [value(11), value(12)],
        [value(13), value(14)],
    )
    totals = totals + value(3)
    totals = totals + jnp.where(lane < count - 1, move(value(2), 0, 1), 0.0)
    totals = totals + jnp.where(lane > 0, move(value(4), 0, -1), 0.0)
    totals = jnp.where(lane < count, totals, 0.0)
    second = solve(totals)
    gx = near[4].astype(jnp.int32)
    gy = near[5].astype(jnp.int32)
    for at, solved in ((0, first), (8, second)):
        turned_z = pltpu.roll(solved, (10 - gx) % 8, 0)
        out_ref[at : at + 8] = pltpu.roll(turned_z, (lanes + 1 - gy) % lanes, 1)


def coarse_columns(near, coarse, start, count):
    row, has_low, has_high = ring_rows(near)
    below = jnp.where(row < RING - 1, 1.0, jnp.where(row <= RING, 0.5, 0.0)) * has_low
    above = jnp.where(row > RING + ROWS, 1.0, jnp.where(row >= RING + ROWS - 1, 0.5, 0.0)) * has_high
    edge = jnp.where((row > RING) & (row < RING + ROWS - 1), 1.0, 0.0)
    edge = jnp.where(row == RING, near[2], jnp.where(row == RING + ROWS - 1, near[3], edge))
    edge = jnp.where(row == RING - 1, 0.5 * has_low, edge)
    edge = jnp.where(row == RING + ROWS, 0.5 * has_high, edge)
    columns = []
    for a in range(start, start + count):
        low, own, high = (coarse[a : a + 1, b : b + 1] for b in range(3))
        columns.append(below * low + edge * own + above * high)
    return columns


def coarse_planes(columns, low, high):
    before, inside, after = columns
    return inside, low * (before - inside), high * (after - inside)


def add_coarse(local, columns):
    inside, first, last = columns
    planes = [local[i] + inside for i in range(8)]
    planes[0] = planes[0] + first
    planes[7] = planes[7] + last
    return stack(planes)


def coarse_applied(columns, flux, packed):
    inside, first, last = columns
    slopes = [
        flux[i] * (float(DERIV[i, 0]) * first + float(DERIV[i, 7]) * last) for i in range(8)
    ]
    fz = along_z(slopes, DERIV.T)
    three = stack([inside + first, inside, inside + last])
    gy = along_y(three, packed, 0)
    fy = along_y(
        stack([flux[i] * gy[0 if i == 0 else 2 if i == 7 else 1] for i in range(8)]), packed, 1
    )
    plane_w = packed[0:WIDE]
    planes = []
    for i in range(8):
        plane = three[0 if i == 0 else 2 if i == 7 else 1]
        planes.append(fz[i] + fy[i] + (HELM_COEF * 0.125 * float(WEIGHT[i])) * (plane_w * plane))
    return stack(planes)


def face_applied(planes, payload, packed, rows, in_grid):
    inside, first, last = planes
    fields = [inside + (first if i == 0 else last if i == 7 else 0.0) for i in rows]
    gy = along_y(stack(fields), packed, 0)
    fy = along_y(stack([payload[6 + k] * gy[k] for k in range(2)]), packed, 1)
    plane_w = packed[0:WIDE]
    result = []
    for k, i in enumerate(rows):
        slopes = payload[2 + k] * first + payload[4 + k] * last
        mass = (HELM_COEF * 0.125 * float(WEIGHT[i])) * in_grid * (plane_w * fields[k])
        result.append(payload[k] + slopes + fy[k] + mass)
    return result


def apply_kernel(
    near, packed, tables, coarse, flux, zl, yl, ylo, yhi,
    z_ref, y_ref, w_ref, wlo, whi,
):
    columns = coarse_columns(near, coarse, 0, 5)
    own = coarse_planes(columns[1:4], 1.0 - near[0], 1.0 - near[1])
    field = add_coarse(zl[...], own)[:, RING : RING + ROWS]
    z_ref[...] = field
    applied = yl[...] + coarse_applied(own, flux[...], packed)
    y_ref[...] = applied[:, RING : RING + ROWS]
    lower = coarse_planes(columns[0:3], 1.0 - near[7], 0.5)
    upper = coarse_planes(columns[2:5], 0.5, 1.0 - near[6])
    planes = [applied[i] for i in range(8)]
    planes += face_applied(lower, ylo, packed, (6, 7), 2.0 - 2.0 * near[0])
    planes += face_applied(upper, yhi, packed, (0, 1), 2.0 - 2.0 * near[1])
    planes = solve_elements(planes, packed, tables, 1)
    row = lax.broadcasted_iota(jnp.int32, (ROWS, LANES), 0)
    _, has_low, has_high = ring_rows(near)
    in_grid = jnp.where(row == 0, has_low, jnp.where(row == ROWS - 1, has_high, 1.0))
    for i in range(8):
        first = (1.0 - has_low) * planes[i][ROWS : ROWS + 1]
        last = (1.0 - has_high) * planes[i][ROWS + 1 : ROWS + 2]
        alone = jnp.where(row == 0, first, jnp.where(row == ROWS - 1, last, 0.0))
        planes[i] = planes[i][0:ROWS] * in_grid + alone
    store_faces(planes, near, w_ref, wlo, whi)


def second_kernel(near, packed, coarse, flux, b, y, z, w, x_ref, kx_ref, stat):
    columns = [column[RING : RING + ROWS] for column in coarse_columns(near, coarse, 9, 3)]
    field = add_coarse(w[...], coarse_planes(columns, 1.0 - near[0], 1.0 - near[1]))
    x_ref[...] = field
    fluxes = flux[:, RING : RING + ROWS]
    gz = along_z([field[i] for i in range(8)], DERIV)
    gy = along_y(field, packed, 0)
    gx = along_x(field, packed, 0)
    slopes = [fluxes[i] * gz[i] for i in range(8)]
    ends = (0, 7)
    back = along_z(slopes, DERIV.T[[0, 7]])
    back_y = along_y(stack([fluxes[i] * gy[i] for i in ends]), packed, 1)
    back_x = along_x(stack([fluxes[i] * gx[i] for i in ends]), packed, 1)
    plane_w = packed[0:ROWS]
    mass = HELM_COEF * 0.125
    for k, i in enumerate(ends):
        weighted = (mass * float(WEIGHT[i])) * (plane_w * field[i])
        kx_ref[k] = back[k] + back_y[k] + back_x[k] + weighted
    energy = None
    for i in range(8):
        term = slopes[i] * gz[i] + fluxes[i] * (gy[i] * gy[i] + gx[i] * gx[i])
        term = term + (mass * float(WEIGHT[i])) * (plane_w * field[i] * field[i])
        energy = term if energy is None else energy + term
    first, right = z[...], b[...]
    sums = [right * first, y[...] * first, right * field, y[...] * field]
    stat[...] = lane_row([jnp.sum(term) for term in sums] + [jnp.sum(energy)])


def face_kernel(packed, flux, b, y, kx, zlo, zhi, stat_in, stat):
    faces = stack([zlo[...], zhi[...]])
    fluxes = flux[:, RING : RING + ROWS]
    gy = along_y(faces, packed, 0)
    gx = along_x(faces, packed, 0)
    plane_w = packed[0:ROWS]
    energy = 2.0 * (kx[0] * faces[0] + kx[1] * faces[1])
    for k, i in enumerate((0, 7)):
        mass = (HELM_COEF * 0.125 * float(WEIGHT[i])) * (plane_w * faces[k] * faces[k])
        energy = energy + mass + fluxes[i] * (gy[k] * gy[k] + gx[k] * gx[k])
    for i in range(8):
        slope = float(DERIV[i, 0]) * faces[0] + float(DERIV[i, 7]) * faces[1]
        energy = energy + fluxes[i] * slope * slope
    sums = [
        0.0,
        0.0,
        jnp.sum(b[0] * faces[0] + b[7] * faces[1]),
        jnp.sum(y[0] * faces[0] + y[7] * faces[1]),
        jnp.sum(energy),
    ]
    stat[...] = jnp.broadcast_to(stat_in[...] + lane_row(sums), stat.shape)


def combine_kernel(sums, z, x, zlo, zhi, p_ref):
    total = jnp.sum(sums[...], axis=0, keepdims=True)
    rz, pap, rq, aq, qhq = (total[:, k : k + 1] for k in range(5))
    step = rz / pap
    rz_next = step * (step * aq - rq)
    beta = rz_next / rz
    grown = 1.0 + beta
    curved = grown * grown * pap - 2.0 * step * grown * aq + step * step * qhq
    step_next = rz_next / curved
    on_z = step + step_next * grown
    on_q = step_next * step
    for i in range(8):
        plane = x[i]
        if i == 0:
            plane = plane + zlo[...]
        if i == 7:
            plane = plane + zhi[...]
        p_ref[i] = on_z * z[i] - on_q * plane


def run(kernel, outs, smem, args, scratch=(), flops=1000000, place=VMEM, limit=LIMIT):
    nbytes = sum(4 * int(np.prod(out)) for out in outs) * 2
    return pl.pallas_call(
        kernel,
        out_shape=[jax.ShapeDtypeStruct(out, F32) for out in outs],
        in_specs=[pl.BlockSpec(memory_space=SMEM) for _ in smem]
        + [pl.BlockSpec(memory_space=place) for _ in args],
        out_specs=[pl.BlockSpec(memory_space=VMEM) for _ in outs],
        scratch_shapes=list(scratch),
        compiler_params=pltpu.CompilerParams(vmem_limit_bytes=limit),
        cost_estimate=pl.CostEstimate(flops=flops, bytes_accessed=nbytes, transcendentals=0),
    )(*smem, *args)


def shift(axis, low_face, high_face):
    count = lax.axis_size(axis)
    forward = [(i, i + 1) for i in range(count - 1)]
    backward = [(target, source) for source, target in forward]
    return lax.ppermute(high_face, axis, forward), lax.ppermute(low_face, axis, backward)


def body(level_set, velocity, source, wick_solid):
    block = level_set.shape
    count_gx = lax.axis_size("gx")
    count_gy = lax.axis_size("gy")
    index_gx = lax.axis_index("gx")
    index_gy = lax.axis_index("gy")

    def ends(index, count):
        return [jnp.where(index > 0, 0.5, 1.0), jnp.where(index < count - 1, 0.5, 1.0)]

    place = [index_gx.astype(F32), index_gy.astype(F32)]
    beyond = [
        jnp.where(index_gx < count_gx - 2, 0.5, 1.0),
        jnp.where(index_gx > 1, 0.5, 1.0),
    ]
    near = jnp.stack(ends(index_gx, count_gx) + ends(index_gy, count_gy) + place + beyond)
    near = near.astype(F32)
    packed = jnp.asarray(PACKED)
    tables = jnp.asarray(TABLES)
    face = (ROWS, LANES)
    wide_block = (8, WIDE, LANES)
    wide_face = (WIDE, LANES)
    rim = (12, TILE, LANES)

    b, l, zlo, zhi, solid = run(
        advect_kernel,
        [block, block, (3, *face), (3, *face), (8, LANES)],
        [],
        [
            pltpu.with_memory_space_constraint(array, pltpu.HBM)
            for array in (level_set, velocity, source, packed, wick_solid.reshape(EY, EX))
        ],
        [VMEM(block, F32), VMEM((3, *block), F32), VMEM(block, F32), VMEM(PACKED.shape, F32)]
        + [VMEM((EY, EX), jnp.int32), pltpu.SemaphoreType.DMA((5,))],
        place=pltpu.HBM,
    )
    zlo, zhi = shift("gx", zlo, zhi)
    ylo, yhi = run(rim_kernel, [rim, rim], [], [solid, b, l, zlo, zhi])
    ylo, yhi = shift("gy", ylo, yhi)
    (inner,) = run(
        inner_schwarz_kernel, [block], [], [packed, tables, b, zlo, zhi], flops=20000000
    )
    w, wlo, whi = run(
        first_schwarz_kernel,
        [wide_block, wide_face, wide_face],
        [near],
        [packed, tables, inner, b, zlo, zhi, ylo, yhi],
    )
    wlo, whi = shift("gx", wlo, whi)
    level_new, flux, stat = run(
        level_kernel,
        [block, wide_block, (1, LANES)],
        [near],
        [solid, packed, b, l, zlo, zhi, ylo, yhi],
        flops=20000000,
    )
    zl, yl, zlo, zhi, stat = run(
        galerkin_kernel,
        [wide_block, wide_block, wide_block, wide_block, (count_gx, LANES)],
        [near],
        [packed, stat, flux, w, wlo, whi],
    )
    zlo, zhi = shift("gx", zlo, zhi)
    gathered = lax.all_to_all(stat, "gx", 0, 0, tiled=True)
    (column,) = run(column_kernel, [(count_gy, LANES)], [], [gathered])
    gathered = lax.all_to_all(column, "gy", 0, 0, tiled=True)
    (coarse,) = run(
        functools.partial(coarse_kernel, count_gy),
        [(16, LANES)],
        [near],
        [gathered],
        [VMEM((LANES, LANES), F32), VMEM((LANES, LANES), F32)],
    )
    z, y, w, wlo, whi = run(
        apply_kernel,
        [block, block, block, face, face],
        [near],
        [packed, tables, coarse, flux, zl, yl, zlo, zhi],
    )
    zlo, zhi = shift("gx", wlo, whi)
    x, kx, sums = run(
        second_kernel,
        [block, (2, *face), (1, LANES)],
        [near],
        [packed, coarse, flux, b, y, z, w],
        flops=20000000,
    )
    (sums,) = run(
        face_kernel, [(count_gx, LANES)], [], [packed, flux, b, y, kx, zlo, zhi, sums]
    )
    tile = lax.all_to_all(sums, "gx", 0, 0, tiled=True)
    wide = jnp.broadcast_to(jnp.sum(tile, axis=0, keepdims=True), (count_gy, LANES))
    wide = lax.all_to_all(wide, "gy", 0, 0, tiled=True)
    (pressure,) = run(combine_kernel, [block], [], [wide, z, x, zlo, zhi])
    return (level_new, pressure)


def solution(mesh):
    placed = (
        P("gx", "gy", None),
        P(None, "gx", "gy", None),
        P("gx", "gy", None),
        P("gx", "gy", None),
    )
    return jax.shard_map(
        body,
        mesh=mesh,
        in_specs=placed,
        out_specs=(P("gx", "gy", None), P("gx", "gy", None)),
        check_vma=False,
    )
```

```python
import functools

import jax
import jax.numpy as jnp
import numpy as np
from jax import lax
from jax.experimental import pallas as pl
from jax.experimental.pallas import tpu as pltpu
from jax.sharding import PartitionSpec as P

EZ = 1
EY = 4
EX = 16
ROWS = 8 * EY
LANES = 8 * EX

TIME_STEP = 0.02
HELM_COEF = 0.25
LEVEL_WIDTH = 0.25
GAS_RATIO = 10.0
SOLID_FACTOR = 0.25
SCHWARZ_SCALE = 0.5
SCHWARZ_SHIFT = 0.05

F32 = jnp.float32
BF16 = jnp.bfloat16
VMEM = pltpu.VMEM
SMEM = pltpu.SMEM
LIMIT = 24 * 1024 * 1024


def gll_tables():
    gll_nodes = np.array(
        [
            -1.0,
            -0.8717401485096066,
            -0.5917001814331423,
            -0.2092992179024789,
            0.2092992179024789,
            0.5917001814331423,
            0.8717401485096066,
            1.0,
        ]
    )
    weight_np = np.array(
        [
            1.0 / 28.0,
            0.21070422714350603,
            0.3411226924835044,
            0.4124587946587038,
            0.4124587946587038,
            0.3411226924835044,
            0.21070422714350603,
            1.0 / 28.0,
        ]
    )
    bary_weights = np.array(
        [1.0 / np.prod([gll_nodes[i] - gll_nodes[j] for j in range(8) if j != i]) for i in range(8)]
    )
    derivative = np.zeros((8, 8))
    for i in range(8):
        for j in range(8):
            if i != j:
                derivative[i, j] = bary_weights[j] / bary_weights[i] / (gll_nodes[i] - gll_nodes[j])
        derivative[i, i] = -np.sum(derivative[i])
    return (weight_np, derivative)


def sine_tables():
    indices = np.arange(10) + 1.0
    sine_basis = np.sqrt(2.0 / 11.0) * np.sin(np.pi * np.outer(indices, indices) / 11.0)
    eigen_vals = 2.0 - 2.0 * np.cos(np.pi * indices / 11.0)
    return (sine_basis, eigen_vals)


WEIGHT, DERIV = gll_tables()
SINE, EIGEN = sine_tables()


def split_const(matrix):
    single = matrix.astype(np.float32)
    high = single.astype(jnp.bfloat16)
    low = (single - high.astype(np.float32)).astype(jnp.bfloat16)
    return high, low


def line_maps(count):
    length = 8 * count
    total = length + 4

    def column(position):
        if 0 <= position < length:
            return position
        return {-2: length, -1: length + 1, length: length + 2, length + 1: length + 3}[position]

    assembled = {}
    for position in range(-2, length + 2):
        row = np.zeros(total)
        row[column(position)] = 1.0
        if 0 <= position < length:
            if position % 8 == 0:
                row[column(position - 1)] += 1.0
            if position % 8 == 7:
                row[column(position + 1)] += 1.0
        assembled[position] = row
    forward = np.zeros((10 * count, total))
    for element in range(count):
        places = [8 * element - 2] + list(range(8 * element, 8 * element + 8)) + [8 * element + 9]
        forward[10 * element : 10 * element + 10] = SINE @ np.stack([assembled[p] for p in places])
    backward = np.zeros((length, 10 * count))
    for element in range(count):
        backward[8 * element : 8 * element + 8, 10 * element : 10 * element + 10] = SINE[1:9]
    for element in range(count - 1):
        first, second = 8 * element + 7, 8 * element + 8
        mean = 0.5 * (backward[first] + backward[second])
        backward[first] = mean
        backward[second] = mean
    return forward, backward


RING = 16
WIDE = ROWS + 2 * RING
REACH = 26
TILE = 48
TILE_B = 32


def ring_maps(reach, depth, inside):
    count = EY + 2 * depth
    forward, _ = line_maps(count)
    length = 8 * count
    columns = np.zeros((10 * count, len(inside)))
    for at, position in enumerate(inside):
        place = None if position is None else position + 8 * depth
        if place is None or place < -2 or place > length + 1:
            continue
        source = place if 0 <= place < length else {-2: 0, -1: 1}.get(place, place - length + 2) + length
        columns[:, at] = forward[:, source]
    _, backward = line_maps(count)
    own = 8 * depth
    rows = np.concatenate(
        [
            backward[own - reach : own + ROWS + reach],
            np.zeros((8, 10 * count)),
        ]
    )
    rows[ROWS + 2 * reach, 10 * depth : 10 * depth + 10] = SINE[1]
    rows[ROWS + 2 * reach + 1, 10 * (depth + EY - 1) : 10 * (depth + EY)] = SINE[8]
    return columns, rows


FZ, BZ = line_maps(1)
TILES = list(range(-REACH, 0)) + [None] * (TILE_B - REACH) + list(range(ROWS))
TILES += list(range(ROWS, ROWS + REACH)) + [None] * (TILE_B - REACH)
FY_A, BY_A = ring_maps(RING, 3, TILES)
FY_B, BY_B = ring_maps(0, 1, list(range(-RING, ROWS + RING)))
INNER = np.arange(40, 60)
OUTER = np.concatenate([np.arange(0, 40), np.arange(60, 100)])
FY_I, BY_I = FY_A[INNER, TILE_B : TILE_B + ROWS], BY_A[RING : RING + ROWS, INNER]
FY_A, BY_A = FY_A[OUTER], BY_A[:, OUTER]
STEP_A = 80
STEP_B = 64
STEP_I = 32


def padded(forward, backward, step):
    forward = np.pad(forward, ((0, step - forward.shape[0]), (0, 0)))
    return forward, np.pad(backward, ((0, 0), (0, step - backward.shape[1])))


FY_A, BY_A = padded(FY_A, BY_A, STEP_A)
FY_B, BY_B = padded(FY_B, BY_B, STEP_B)
FY_I, BY_I = padded(FY_I, BY_I, STEP_I)
FX, BX = line_maps(EX)
FX = FX[:, :LANES]


FX_H, FX_L = split_const(FX.T.copy())
BX_H, BX_L = split_const(BX.T.copy())


def wide_const(table):
    high, low = split_const(table)
    return np.concatenate([high, high, low], axis=1)


def pack_tables(tables):
    places, pieces, at = [], [], 0
    for table in tables:
        rows = -(-table.shape[0] // 16) * 16
        extra = ((0, rows - table.shape[0]), (0, 384 - table.shape[1]))
        pieces.append(np.pad(table.astype(np.float32), extra))
        places.append((at, rows, table.shape[1]))
        at += rows
    return np.concatenate(pieces).astype(jnp.bfloat16), places


TABLES, PLACES = pack_tables(
    [
        np.concatenate([FX_H, FX_H], axis=0),
        FX_L,
        BX_H,
        BX_L,
        wide_const(FY_A),
        wide_const(BY_A),
        wide_const(FY_B),
        wide_const(BY_B),
        wide_const(FY_I),
        wide_const(BY_I),
    ]
)


def roll_table():
    table = np.zeros((2, 8, 8, LANES))
    for kind, matrix in enumerate((DERIV, DERIV.T)):
        for k in range(8):
            for i in range(8):
                table[kind, k, i, :] = matrix[i, (i + k) % 8]
    return table.reshape(2 * 64, LANES)


WY = np.tile(WEIGHT, WIDE // 8)
WX = np.tile(WEIGHT, EX)


def inner_count(count):
    mult = np.ones(8 * count)
    position = np.arange(8 * count)
    mult[(position % 8 == 0) & (position > 0)] += 1.0
    mult[(position % 8 == 7) & (position < 8 * count - 1)] += 1.0
    return mult


END_MASS = np.where(np.arange(WIDE) % 8 % 7 == 0, 2.0, 1.0)
INV_MASS = (8.0 / (WY * END_MASS)[:, None] / (WX * inner_count(EX))[None, :]).astype(np.float32)

AT_ROLLS = WIDE
AT_DX = AT_ROLLS + 128
AT_DXT = AT_DX + LANES
AT_SQUARE = AT_DXT + LANES
AT_MASS = AT_SQUARE + 16
AT_SPREAD = AT_MASS + WIDE
AT_EIGEN_Y = AT_SPREAD + EX
AT_EIGEN_X = AT_EIGEN_Y + STEP_A
LAM_Y = np.resize(EIGEN, STEP_A)
LAM_X = np.resize(EIGEN, 8 * LANES).reshape(8, LANES)
PACKED = np.concatenate(
    [
        WY[:, None] * WX[None, :],
        roll_table(),
        np.kron(np.eye(EX), DERIV.T),
        np.kron(np.eye(EX), DERIV),
        np.repeat(DERIV[:, :1] ** 2, LANES, axis=1),
        np.repeat(DERIV[:, 7:] ** 2, LANES, axis=1),
        INV_MASS,
        np.kron(np.eye(EX), np.ones((1, 8))),
        np.repeat(LAM_Y[:, None], LANES, axis=1),
        LAM_X,
    ]
).astype(np.float32)


def parts(values):
    high = values.astype(BF16)
    low = (values - high.astype(F32)).astype(BF16)
    return high, low


def dot(left, right):
    return jnp.dot(left, right, preferred_element_type=F32)


def left_pairs(table, planes):
    results = []
    for i in range(0, len(planes), 2):
        high, low = parts(jnp.concatenate([planes[i], planes[i + 1]], axis=1))
        both = dot(table, jnp.concatenate([high, low, high], axis=0))
        results += [both[:, 0:LANES], both[:, LANES : 2 * LANES]]
    return results


def along_z(values, matrix):
    rows = []
    for i in range(matrix.shape[0]):
        total = None
        for j in range(matrix.shape[1]):
            if matrix[i, j] == 0.0:
                continue
            term = float(matrix[i, j]) * values[j]
            total = term if total is None else total + term
        rows.append(total)
    return rows


def along_y(values, packed, kind):
    count, rows = values.shape[:2]
    grouped = values.reshape(count * rows // 8, 8, LANES)
    start = AT_ROLLS + 64 * kind
    total = packed[start : start + 8][None] * grouped
    for k in range(1, 8):
        total = total + packed[start + 8 * k : start + 8 * k + 8][None] * pltpu.roll(grouped, 8 - k, 1)
    return total.reshape(count, rows, LANES)


def along_x(values, packed, kind):
    start = AT_DXT if kind else AT_DX
    high, low = parts(packed[start : start + LANES])
    first, rest = parts(values.reshape(values.shape[0] * values.shape[1], LANES))
    total = dot(
        jnp.concatenate([first, rest], axis=1), jnp.concatenate([high, high], axis=0)
    ) + dot(first, low)
    return total.reshape(values.shape)


def stack(planes):
    return jnp.concatenate([plane[None] for plane in planes], axis=0)


def edge_rows(rows, low, high):
    position = lax.broadcasted_iota(jnp.int32, (rows, LANES), 0)
    return jnp.where(position == 0, low, jnp.where(position == rows - 1, high, 1.0))


def local_operator(values, flux, packed):
    plane_w = packed[0 : values.shape[1]]
    gz = along_z([values[i] for i in range(8)], DERIV)
    fz = along_z([flux[i] * gz[i] for i in range(8)], DERIV.T)
    total = along_y(flux * along_y(values, packed, 0), packed, 1)
    total = total + along_x(flux * along_x(values, packed, 0), packed, 1)
    planes = [
        total[i] + fz[i] + (HELM_COEF * 0.125 * float(WEIGHT[i])) * (plane_w * values[i])
        for i in range(8)
    ]
    return stack(planes)


def add_planes(own, low_z, high_z):
    planes = [own[i] for i in range(8)]
    planes[0] = planes[0] + low_z
    planes[7] = planes[7] + high_z
    return stack(planes)


def solve_elements(planes, packed, tables, kind):
    def table(index):
        at, rows, width = PLACES[index]
        return tables[at : at + rows, 0:width]

    fxhh, fxl, bxh, bxl = (table(index) for index in range(4))
    spectral = left_pairs(table(4 + 2 * kind), along_z(planes, FZ))
    high, low = parts(jnp.concatenate(spectral, axis=0))
    wide = dot(jnp.concatenate([high, low], axis=1), fxhh) + dot(high, fxl)
    step = PLACES[4 + 2 * kind][1]
    column = packed[AT_EIGEN_Y : AT_EIGEN_Y + step]
    rest = 10 * EX - LANES
    lam = jnp.concatenate(
        [
            column + packed[AT_EIGEN_X : AT_EIGEN_X + 1],
            column[:, 0:rest] + packed[AT_EIGEN_X + 1 : AT_EIGEN_X + 2, 0:rest],
        ],
        axis=1,
    )
    scaled = [
        wide[step * i : step * (i + 1)]
        / (SCHWARZ_SCALE * lam + float(SCHWARZ_SCALE * EIGEN[i] + SCHWARZ_SHIFT))
        for i in range(10)
    ]
    high, low = parts(jnp.concatenate(scaled, axis=0))
    back = dot(high, bxh) + dot(low, bxh) + dot(high, bxl)
    back = left_pairs(table(5 + 2 * kind), [back[step * i : step * (i + 1)] for i in range(10)])
    return along_z(back, BZ)


def store_faces(planes, near, out_ref, low_ref, high_ref):
    planes[0] = planes[0] * near[0]
    planes[7] = planes[7] * near[1]
    for i in range(8):
        out_ref[i] = planes[i]
    low_ref[...] = planes[0]
    high_ref[...] = planes[7]


def ring_rows(near):
    row = lax.broadcasted_iota(jnp.int32, (WIDE, LANES), 0)
    return row, 2.0 - 2.0 * near[2], 2.0 - 2.0 * near[3]


def partition_total(own, low_z, high_z, low_y, high_y, near):
    def planes(array):
        total = near[0] * array[0] + near[1] * array[7]
        for i in range(1, 7):
            total = total + array[i]
        return total

    total = planes(own) + 0.5 * (low_z[1] + high_z[0])
    below = planes(low_y) + 0.5 * (low_y[9] + low_y[10])
    above = planes(high_y) + 0.5 * (high_y[9] + high_y[10])
    faces = 0.5 * (below[REACH - 1 : REACH] + above[0:1])
    return jnp.sum(total * edge_rows(ROWS, near[2], near[3])) + jnp.sum(faces)


def lane_row(entries):
    lane = lax.broadcasted_iota(jnp.int32, (1, LANES), 1)
    row = jnp.zeros((1, LANES), F32)
    for index, value in enumerate(entries):
        row = jnp.where(lane == index, value, row)
    return row


def advect_kernel(
    lev_in, vel_in, src_in, packed_in, solid_in, b_ref, l_ref, zlo, zhi, solid_ref,
    lev, vel, src, packed, solid, sems,
):
    pairs = ((lev_in, lev), (packed_in, packed), (vel_in, vel), (src_in, src), (solid_in, solid))
    copies = [
        pltpu.make_async_copy(source, target, sems.at[index])
        for index, (source, target) in enumerate(pairs)
    ]
    for copy in copies:
        copy.start()
    copies[0].wait()
    level = lev[...]
    gz = stack(along_z([level[i] for i in range(8)], DERIV))
    copies[1].wait()
    gy = along_y(level, packed, 0)
    gx = along_x(level, packed, 0)
    for copy in copies[2:]:
        copy.wait()
    spread = packed[AT_SPREAD : AT_SPREAD + EX].astype(BF16)
    in_solid = dot(solid[...].astype(F32).astype(BF16), spread)
    solid_ref[...] = jnp.concatenate([in_solid, jnp.zeros((8 - EY, LANES), F32)], axis=0)
    v0, v1, v2 = vel[0], vel[1], vel[2]
    moved = level - (2.0 * TIME_STEP) * (v0 * gz + v1 * gy + v2 * gx)
    diverge = stack(along_z([v0[i] for i in range(8)], DERIV))
    diverge = diverge + along_y(v1, packed, 0) + along_x(v2, packed, 0)
    force = src[...] - (2.0 * TIME_STEP) * diverge
    weights = packed[0:ROWS]
    for i in range(8):
        mass = (0.125 * float(WEIGHT[i])) * weights
        term = mass * force[i]
        moved_i = mass * moved[i]
        b_ref[i] = term
        l_ref[i] = moved_i
        if i < 2:
            zlo[i] = term
        if i == 0:
            zlo[2] = moved_i
        if i > 5:
            zhi[i - 6] = term
        if i == 7:
            zhi[2] = moved_i


def rim_kernel(solid, b, l, low_z, high_z, low_y, high_y):
    in_solid = solid[...]
    rest = TILE - REACH - RING - 1

    def rows(planes, at, level, far, extra=None):
        start = ROWS - REACH if far else 0
        pieces = [planes[at, start : start + REACH]]
        if level is None:
            pieces.append(jnp.zeros((RING + 1, LANES), F32))
        else:
            array, index = level
            start = ROWS - RING - 1 if far else 0
            pieces.append(array[index, start : start + RING + 1])
        if extra is None:
            pieces.append(jnp.zeros((rest, LANES), F32))
        else:
            pieces += [extra, jnp.zeros((rest - 2, LANES), F32)]
        return jnp.concatenate(pieces, axis=0)

    for far, out in ((False, low_y), (True, high_y)):
        extra = in_solid[EY - 2 : EY] if far else in_solid[0:2]
        for i in range(8):
            out[i] = rows(b, i, (l, i), far, extra if i == 0 else None)
        for i in range(2):
            out[8 + i] = rows(low_z, i, (low_z, 2) if i == 1 else None, far)
            out[10 + i] = rows(high_z, i, (high_z, 2) if i == 0 else None, far)


def level_kernel(
    near, solid, packed, b, l, zlo, zhi, ylo, yhi, level_ref, flux_ref, stat
):
    row, has_low, has_high = ring_rows(near)
    at = REACH

    def wide_rows(slot, own):
        return jnp.concatenate(
            [ylo[slot, at + 1 : at + 1 + RING], own, yhi[slot, at : at + RING]], axis=0
        )

    planes = []
    for i in range(8):
        plane = wide_rows(i, l[i])
        first = ylo[i, at : at + 1]
        last = yhi[i, at + RING : at + RING + 1]
        if i == 0:
            plane = plane + wide_rows(9, zlo[2])
            first = first + ylo[9, at : at + 1]
            last = last + yhi[9, at + RING : at + RING + 1]
        if i == 7:
            plane = plane + wide_rows(10, zhi[2])
            first = first + ylo[10, at : at + 1]
            last = last + yhi[10, at + RING : at + RING + 1]
        before = jnp.where(row == 0, first, pltpu.roll(plane, 1, 0))
        after = jnp.where(row == WIDE - 1, last, pltpu.roll(plane, WIDE - 1, 0))
        plane = plane + jnp.where(row % 8 == 0, before, jnp.where(row % 8 == 7, after, 0.0))
        planes.append(plane)
    own = stack(planes)
    lane = lax.broadcasted_iota(jnp.int32, (8, WIDE, LANES), 2)
    before = jnp.where((lane % 8 == 0) & (lane > 0), pltpu.roll(own, 1, 2), 0.0)
    after = jnp.where((lane % 8 == 7) & (lane < LANES - 1), pltpu.roll(own, LANES - 1, 2), 0.0)
    own = own + before + after
    ends = jnp.where(row == RING, 2.0 * near[2], jnp.where(row == RING + ROWS - 1, 2.0 * near[3], 1.0))
    inverse = packed[AT_MASS : AT_MASS + WIDE] * ends
    in_solid = solid[...]
    solids = [ylo[0, at + RING + 1 + k : at + RING + 2 + k] for k in range(2)]
    solids += [in_solid[e : e + 1] for e in range(EY)]
    solids += [yhi[0, at + RING + 1 + k : at + RING + 2 + k] for k in range(2)]
    open_part = jnp.concatenate(
        [jnp.broadcast_to(1.0 - (1.0 - SOLID_FACTOR) * rows, (8, LANES)) for rows in solids], axis=0
    )
    in_grid = jnp.where(row < RING, has_low, jnp.where(row >= RING + ROWS, has_high, 1.0))
    flux_w = packed[0:WIDE] * in_grid
    total = jnp.zeros((ROWS, LANES), F32)
    fluxes = []
    for i in range(8):
        scale = 1.0 / float(WEIGHT[i])
        plane = own[i] * (inverse * scale)
        if i == 0:
            plane = plane * near[0]
        if i == 7:
            plane = plane * near[1]
        level_ref[i] = plane[RING : RING + ROWS]
        liquid = jax.nn.sigmoid(plane * (1.0 / LEVEL_WIDTH))
        coef = (GAS_RATIO - (GAS_RATIO - 1.0) * liquid) * open_part
        total = total + coef[RING : RING + ROWS]
        flux = (0.5 * float(WEIGHT[i])) * (coef * flux_w)
        flux_ref[i] = flux
        fluxes.append(flux[RING : RING + ROWS])
    kbar = jnp.sum(total) * (1.0 / (8 * ROWS * LANES))
    entries = [kbar, partition_total(b, zlo, zhi, ylo, yhi, near)] + [0.0] * 9
    for first, second in ((0, 0), (0, 7), (7, 7)):
        slopes = along_z(fluxes, (DERIV[:, first] * DERIV[:, second])[None, :])[0]
        column = jnp.sum(slopes, axis=1, keepdims=True)
        entries += [jnp.sum(column, axis=0, keepdims=True), column[0:1], column[ROWS - 1 : ROWS]]
    inner = fluxes[0] + fluxes[1]
    for i in range(2, 8):
        inner = inner + fluxes[i]
    for at_row, start in ((0, 0), (ROWS - 8, 8)):
        square = packed[AT_SQUARE + start : AT_SQUARE + start + 8]
        entries += [
            jnp.sum(square * plane[at_row : at_row + 8]) for plane in (inner, fluxes[0], fluxes[7])
        ]
    stat[...] = lane_row(entries)


def inner_schwarz_kernel(packed, tables, b, zlo, zhi, out_ref):
    planes = [b[i] for i in range(8)] + [zlo[0], zlo[1], zhi[0], zhi[1]]
    planes = solve_elements(planes, packed, tables, 2)
    for i in range(8):
        out_ref[i] = planes[i]


def first_schwarz_kernel(
    near, packed, tables, inner, b, zlo, zhi, ylo, yhi, w_ref, wlo, whi
):
    own = [b[i] for i in range(8)] + [zlo[0], zlo[1], zhi[0], zhi[1]]
    planes = [
        jnp.concatenate([ylo[i, 0:TILE_B], own[i], yhi[i, 0:TILE_B]], axis=0) for i in range(12)
    ]
    planes = solve_elements(planes, packed, tables, 0)
    row, has_low, has_high = ring_rows(near)
    in_grid = jnp.where(row < RING, has_low, jnp.where(row >= RING + ROWS, has_high, 1.0))
    in_grid = jnp.where(row == RING, has_low, jnp.where(row == RING + ROWS - 1, has_high, in_grid))
    rest = jnp.zeros((RING, LANES), F32)
    for i in range(8):
        first = (1.0 - has_low) * planes[i][WIDE : WIDE + 1]
        last = (1.0 - has_high) * planes[i][WIDE + 1 : WIDE + 2]
        alone = jnp.where(row == RING, first, jnp.where(row == RING + ROWS - 1, last, 0.0))
        planes[i] = planes[i][0:WIDE] * in_grid + alone
        planes[i] = planes[i] + jnp.concatenate([rest, inner[i], rest], axis=0)
    store_faces(planes, near, w_ref, wlo, whi)


def galerkin_kernel(near, packed, stat_in, flux, w, zlo, zhi, zl_ref, y_ref, ylo, yhi, stat):
    local = add_planes(w, zlo[...], zhi[...])
    zl_ref[...] = local
    applied = local_operator(local, flux[...], packed)
    y_ref[...] = applied
    fluxes = [flux[i] for i in range(8)]
    for out, rows in ((ylo, (0, 1)), (yhi, (6, 7))):
        for k, i in enumerate(rows):
            out[k] = applied[i]
            for t, end in enumerate((0, 7)):
                out[2 + 2 * t + k] = along_z(fluxes, (DERIV[:, i] * DERIV[:, end])[None, :])[0]
            out[6 + k] = fluxes[i]
    applied = applied[:, RING : RING + ROWS]
    inner = near[0] * applied[0] + near[1] * applied[7]
    for i in range(1, 7):
        inner = inner + applied[i]
    edge = edge_rows(ROWS, near[2], near[3])
    entries = [0.0, 0.0]
    for plane in ((1.0 - near[0]) * applied[0], inner, (1.0 - near[1]) * applied[7]):
        entries += [
            (1.0 - near[2]) * jnp.sum(plane[0:1]),
            jnp.sum(edge * plane),
            (1.0 - near[3]) * jnp.sum(plane[ROWS - 1 : ROWS]),
        ]
    stat[...] = jnp.broadcast_to(stat_in[...] + lane_row(entries), stat.shape)


def column_kernel(gathered, out_ref):
    values = gathered[...]
    sub = lax.broadcasted_iota(jnp.int32, (8, LANES), 0)
    lane = lax.broadcasted_iota(jnp.int32, (8, LANES), 1)
    after = jnp.where(sub < 7, pltpu.roll(values, 7, 0), 0.0)
    before = jnp.where(sub > 0, pltpu.roll(values, 1, 0), 0.0)
    first = lax.broadcasted_iota(jnp.int32, (8, 1), 0) == 0
    last = lax.broadcasted_iota(jnp.int32, (8, 1), 0) == 7

    def column(array, index):
        return array[:, index : index + 1]

    def slopes(array, pair):
        whole, low, high = (column(array, 11 + 3 * pair + k) for k in range(3))
        return whole - low - high, low, high

    merged = [column(values, 0), column(values, 1)]
    for b in range(3):
        merged.append(column(values, 5 + b) + column(after, 2 + b) + column(before, 8 + b))
    merged += [own + other for own, other in zip(slopes(values, 0), slopes(before, 2), strict=True)]
    merged += list(slopes(values, 1))
    inside, interface = [], []
    for side in range(2):
        whole, low, high = (column(values, 20 + 3 * side + k) for k in range(3))
        ends = jnp.where(first, low, 0.0) + jnp.where(last, high, 0.0)
        inside.append(whole - low - high + ends)
        interface.append(jnp.where(first, 0.0, low) + column(before, 22 + 3 * side))
    rows = jnp.zeros((8, LANES), F32)
    for index, value in enumerate(merged + inside + interface):
        rows = jnp.where(lane == index, value, rows)
    total = rows[0:1]
    for i in range(1, 8):
        total = total + pltpu.roll(rows[i : i + 1], 16 * i, 1)
    out_ref[...] = jnp.broadcast_to(total, out_ref.shape)


def invert(blocks, sub):
    for k in range(0, 8, 2):
        first, second = blocks[k], blocks[k + 1]
        a, b = first[k : k + 1], first[k + 1 : k + 2]
        c, d = second[k : k + 1], second[k + 1 : k + 2]
        scale = 1.0 / (a * d - b * c)
        first = jnp.where(sub == k, 1.0, jnp.where(sub == k + 1, 0.0, first))
        second = jnp.where(sub == k + 1, 1.0, jnp.where(sub == k, 0.0, second))
        low = (d * scale) * first - (b * scale) * second
        high = (a * scale) * second - (c * scale) * first
        pivots = (sub == k) | (sub == k + 1)
        rows = []
        for r in range(8):
            if r == k:
                rows.append(low)
            elif r == k + 1:
                rows.append(high)
            else:
                rest = jnp.where(pivots, 0.0, blocks[r])
                rows.append(rest - blocks[r][k : k + 1] * low - blocks[r][k + 1 : k + 2] * high)
        blocks = rows
    return blocks


def multiply(left, right):
    rows = []
    for r in range(8):
        total = left[r][0:1] * right[0]
        for k in range(1, 8):
            total = total + left[r][k : k + 1] * right[k]
        rows.append(total)
    return rows


def multiply_turned(left, right):
    rows = []
    for r in range(8):
        total = left[0][r : r + 1] * right[0]
        for k in range(1, 8):
            total = total + left[k][r : r + 1] * right[k]
        rows.append(total)
    return rows


def apply_turned(blocks, column):
    total = blocks[0] * column[0:1]
    for k in range(1, 8):
        total = total + blocks[k] * column[k : k + 1]
    return total


def coarse_operator(c, count, sums_z, couplings_z, inside_y, interface_y):
    sub = lax.broadcasted_iota(jnp.int32, c.shape, 0)
    lane = lax.broadcasted_iota(jnp.int32, c.shape, 1)
    has_low = lane > 0
    has_high = lane < count - 1

    def after(array):
        return jnp.where(sub < 7, pltpu.roll(array, 7, 0), 0.0)

    def before(array):
        return jnp.where(sub > 0, pltpu.roll(array, 1, 0), 0.0)

    def right(array):
        return jnp.where(has_high, pltpu.roll(array, LANES - 1, 1), 0.0)

    def left(array):
        return jnp.where(has_low, pltpu.roll(array, 1, 1), 0.0)

    on_low = jnp.where(has_low, 0.5 * (c + left(c)), c)
    on_high = jnp.where(has_high, 0.5 * (c + right(c)), c)
    tested = []
    for place, value in enumerate((c, on_low, on_high)):
        slope = jnp.where(sub > 0, 0.5 * (value - before(value)), 0.0)
        coupling = couplings_z[place]
        force = sums_z[place] * slope - coupling * after(slope) - before(coupling * slope)
        force = jnp.where(sub > 0, force, 0.0)
        tested.append(0.5 * (force - after(force)))
    result = tested[0] + jnp.where(has_low, 0.5, 1.0) * tested[1] + jnp.where(has_high, 0.5, 1.0) * tested[2]
    result = result + 0.5 * right(tested[1]) + 0.5 * left(tested[2])

    interface = jnp.where(sub > 0, 0.5 * (c + before(c)), 0.0)
    for side, (move, there) in enumerate(((left, has_low), (right, has_high))):
        force = inside_y[side] * jnp.where(there, 0.5 * (move(c) - c), 0.0)
        face = interface_y[side] * jnp.where(there, 0.5 * (move(interface) - interface), 0.0)
        force = force + 0.5 * (face + after(face))
        back = right if side == 0 else left
        result = result + 0.5 * (back(force) - force)

    end = float(WEIGHT[0])
    mass = (2.0 - 2.0 * end) * c + end * (interface + after(interface))
    mass = mass + jnp.where((sub == 0) | (sub == 7), end * c, 0.0)
    beside = jnp.where(has_low, 0.5 * (mass + left(mass)), 0.0)
    scaled = (2.0 * EY - 2.0 * end) * mass + end * (beside + right(beside))
    scaled = scaled + jnp.where(has_low, 0.0, end * mass) + jnp.where(has_high, 0.0, end * mass)
    return result + HELM_COEF / 8.0 * float(np.sum(WX)) * scaled


def coarse_kernel(count, near, gathered, out_ref, wide, turned):
    lanes = LANES
    sub = lax.broadcasted_iota(jnp.int32, (8, lanes), 0)
    lane = lax.broadcasted_iota(jnp.int32, (8, lanes), 1)
    wide[...] = jnp.zeros((LANES, LANES), F32)
    wide[0:count] = gathered[...]
    turned[...] = wide[...].T

    def value(index):
        return turned[pl.ds(index, 8, stride=16), :]

    def move(array, dz, dy):
        if dz:
            array = pltpu.roll(array, (-dz) % 8, 0)
        if dy:
            array = pltpu.roll(array, (-dy) % lanes, 1)
        return array

    kbar = jnp.where(lane < count, value(0), 1.0)
    above = move(kbar, 1, 0)
    link_z = jnp.where(sub < 7, 2.0 * kbar * above / (kbar + above) * (EY * EX / EZ), 0.0)
    link_z = jnp.where(lane < count, link_z, 0.0)
    beside = move(kbar, 0, 1)
    link_y = 2.0 * kbar * beside / (kbar + beside) * (EZ * EX / EY)
    link_y = jnp.where(lane < count - 1, link_y, 0.0)
    back_z = move(link_z, -1, 0)
    back_y = move(link_y, 0, -1)
    diagonal = HELM_COEF * EZ * EY * EX + link_z + back_z + link_y + back_y
    blocks = []
    for r in range(8):
        row = jnp.where(sub == r, diagonal, 0.0)
        row = jnp.where(sub == r + 1, -back_z, row)
        row = jnp.where(sub == r - 1, -link_z, row)
        blocks.append(row)

    levels = []
    step = 1
    while step < count:
        inverse = invert(blocks, sub)
        if step == 1:
            up, low = -link_y, -back_y
            solved_up = [row * up for row in inverse]
            solved_low = [row * low for row in inverse]
            pull_up = [up[r : r + 1] * solved_up[r] for r in range(8)]
            pull_low = [low[r : r + 1] * solved_low[r] for r in range(8)]
            new_low = [up[r : r + 1] * solved_low[r] for r in range(8)]
            new_up = [low[r : r + 1] * solved_up[r] for r in range(8)]
        else:
            solved_up, solved_low = multiply(inverse, upper), multiply(inverse, lower)
            pull_up = multiply_turned(solved_up, upper)
            pull_low = multiply_turned(solved_low, lower)
            if 2 * step < count:
                new_low = multiply_turned(solved_up, lower)
                new_up = multiply_turned(solved_low, upper)
        levels.append((step, solved_up, solved_low))
        blocks = [
            blocks[r] - move(pull_up[r], 0, -step) - move(pull_low[r], 0, step) for r in range(8)
        ]
        if 2 * step < count:
            lower = [-move(row, 0, -step) for row in new_low]
            upper = [-move(row, 0, step) for row in new_up]
        step *= 2
    inverse = invert(blocks, sub)

    def solve(column):
        for distance, solved_up, solved_low in levels:
            before = move(apply_turned(solved_up, column), 0, -distance)
            after = move(apply_turned(solved_low, column), 0, distance)
            column = column - before - after
        return apply_turned(inverse, column)

    first = solve(value(1))
    totals = coarse_operator(
        first,
        count,
        [value(5 + k) for k in range(3)],
        [value(8 + k) for k in range(3)],
        [value(11), value(12)],
        [value(13), value(14)],
    )
    totals = totals + value(3)
    totals = totals + jnp.where(lane < count - 1, move(value(2), 0, 1), 0.0)
    totals = totals + jnp.where(lane > 0, move(value(4), 0, -1), 0.0)
    totals = jnp.where(lane < count, totals, 0.0)
    second = solve(totals)
    gx = near[4].astype(jnp.int32)
    gy = near[5].astype(jnp.int32)
    for at, solved in ((0, first), (8, second)):
        turned_z = pltpu.roll(solved, (10 - gx) % 8, 0)
        out_ref[at : at + 8] = pltpu.roll(turned_z, (lanes + 1 - gy) % lanes, 1)


def coarse_columns(near, coarse, start, count):
    row, has_low, has_high = ring_rows(near)
    below = jnp.where(row < RING - 1, 1.0, jnp.where(row <= RING, 0.5, 0.0)) * has_low
    above = jnp.where(row > RING + ROWS, 1.0, jnp.where(row >= RING + ROWS - 1, 0.5, 0.0)) * has_high
    edge = jnp.where((row > RING) & (row < RING + ROWS - 1), 1.0, 0.0)
    edge = jnp.where(row == RING, near[2], jnp.where(row == RING + ROWS - 1, near[3], edge))
    edge = jnp.where(row == RING - 1, 0.5 * has_low, edge)
    edge = jnp.where(row == RING + ROWS, 0.5 * has_high, edge)
    columns = []
    for a in range(start, start + count):
        low, own, high = (coarse[a : a + 1, b : b + 1] for b in range(3))
        columns.append(below * low + edge * own + above * high)
    return columns


def coarse_planes(columns, low, high):
    before, inside, after = columns
    return inside, low * (before - inside), high * (after - inside)


def add_coarse(local, columns):
    inside, first, last = columns
    planes = [local[i] + inside for i in range(8)]
    planes[0] = planes[0] + first
    planes[7] = planes[7] + last
    return stack(planes)


def coarse_applied(columns, flux, packed):
    inside, first, last = columns
    slopes = [
        flux[i] * (float(DERIV[i, 0]) * first + float(DERIV[i, 7]) * last) for i in range(8)
    ]
    fz = along_z(slopes, DERIV.T)
    three = stack([inside + first, inside, inside + last])
    gy = along_y(three, packed, 0)
    fy = along_y(
        stack([flux[i] * gy[0 if i == 0 else 2 if i == 7 else 1] for i in range(8)]), packed, 1
    )
    plane_w = packed[0:WIDE]
    planes = []
    for i in range(8):
        plane = three[0 if i == 0 else 2 if i == 7 else 1]
        planes.append(fz[i] + fy[i] + (HELM_COEF * 0.125 * float(WEIGHT[i])) * (plane_w * plane))
    return stack(planes)


def face_applied(planes, payload, packed, rows, in_grid):
    inside, first, last = planes
    fields = [inside + (first if i == 0 else last if i == 7 else 0.0) for i in rows]
    gy = along_y(stack(fields), packed, 0)
    fy = along_y(stack([payload[6 + k] * gy[k] for k in range(2)]), packed, 1)
    plane_w = packed[0:WIDE]
    result = []
    for k, i in enumerate(rows):
        slopes = payload[2 + k] * first + payload[4 + k] * last
        mass = (HELM_COEF * 0.125 * float(WEIGHT[i])) * in_grid * (plane_w * fields[k])
        result.append(payload[k] + slopes + fy[k] + mass)
    return result


def apply_kernel(
    near, packed, tables, coarse, flux, zl, yl, ylo, yhi,
    z_ref, y_ref, w_ref, wlo, whi,
):
    columns = coarse_columns(near, coarse, 0, 5)
    own = coarse_planes(columns[1:4], 1.0 - near[0], 1.0 - near[1])
    field = add_coarse(zl[...], own)[:, RING : RING + ROWS]
    z_ref[...] = field
    applied = yl[...] + coarse_applied(own, flux[...], packed)
    y_ref[...] = applied[:, RING : RING + ROWS]
    lower = coarse_planes(columns[0:3], 1.0 - near[7], 0.5)
    upper = coarse_planes(columns[2:5], 0.5, 1.0 - near[6])
    planes = [applied[i] for i in range(8)]
    planes += face_applied(lower, ylo, packed, (6, 7), 2.0 - 2.0 * near[0])
    planes += face_applied(upper, yhi, packed, (0, 1), 2.0 - 2.0 * near[1])
    planes = solve_elements(planes, packed, tables, 1)
    row = lax.broadcasted_iota(jnp.int32, (ROWS, LANES), 0)
    _, has_low, has_high = ring_rows(near)
    in_grid = jnp.where(row == 0, has_low, jnp.where(row == ROWS - 1, has_high, 1.0))
    for i in range(8):
        first = (1.0 - has_low) * planes[i][ROWS : ROWS + 1]
        last = (1.0 - has_high) * planes[i][ROWS + 1 : ROWS + 2]
        alone = jnp.where(row == 0, first, jnp.where(row == ROWS - 1, last, 0.0))
        planes[i] = planes[i][0:ROWS] * in_grid + alone
    store_faces(planes, near, w_ref, wlo, whi)


def second_kernel(near, packed, coarse, flux, b, y, z, w, x_ref, kx_ref, stat):
    columns = [column[RING : RING + ROWS] for column in coarse_columns(near, coarse, 9, 3)]
    field = add_coarse(w[...], coarse_planes(columns, 1.0 - near[0], 1.0 - near[1]))
    x_ref[...] = field
    fluxes = flux[:, RING : RING + ROWS]
    gz = along_z([field[i] for i in range(8)], DERIV)
    gy = along_y(field, packed, 0)
    gx = along_x(field, packed, 0)
    slopes = [fluxes[i] * gz[i] for i in range(8)]
    ends = (0, 7)
    back = along_z(slopes, DERIV.T[[0, 7]])
    back_y = along_y(stack([fluxes[i] * gy[i] for i in ends]), packed, 1)
    back_x = along_x(stack([fluxes[i] * gx[i] for i in ends]), packed, 1)
    plane_w = packed[0:ROWS]
    mass = HELM_COEF * 0.125
    for k, i in enumerate(ends):
        weighted = (mass * float(WEIGHT[i])) * (plane_w * field[i])
        kx_ref[k] = back[k] + back_y[k] + back_x[k] + weighted
    energy = None
    for i in range(8):
        term = slopes[i] * gz[i] + fluxes[i] * (gy[i] * gy[i] + gx[i] * gx[i])
        term = term + (mass * float(WEIGHT[i])) * (plane_w * field[i] * field[i])
        energy = term if energy is None else energy + term
    first, right = z[...], b[...]
    sums = [right * first, y[...] * first, right * field, y[...] * field]
    stat[...] = lane_row([jnp.sum(term) for term in sums] + [jnp.sum(energy)])


def face_kernel(packed, flux, b, y, kx, zlo, zhi, stat_in, stat):
    faces = stack([zlo[...], zhi[...]])
    fluxes = flux[:, RING : RING + ROWS]
    gy = along_y(faces, packed, 0)
    gx = along_x(faces, packed, 0)
    plane_w = packed[0:ROWS]
    energy = 2.0 * (kx[0] * faces[0] + kx[1] * faces[1])
    for k, i in enumerate((0, 7)):
        mass = (HELM_COEF * 0.125 * float(WEIGHT[i])) * (plane_w * faces[k] * faces[k])
        energy = energy + mass + fluxes[i] * (gy[k] * gy[k] + gx[k] * gx[k])
    for i in range(8):
        slope = float(DERIV[i, 0]) * faces[0] + float(DERIV[i, 7]) * faces[1]
        energy = energy + fluxes[i] * slope * slope
    sums = [
        0.0,
        0.0,
        jnp.sum(b[0] * faces[0] + b[7] * faces[1]),
        jnp.sum(y[0] * faces[0] + y[7] * faces[1]),
        jnp.sum(energy),
    ]
    stat[...] = jnp.broadcast_to(stat_in[...] + lane_row(sums), stat.shape)


def combine_kernel(sums, z, x, zlo, zhi, p_ref):
    total = jnp.sum(sums[...], axis=0, keepdims=True)
    rz, pap, rq, aq, qhq = (total[:, k : k + 1] for k in range(5))
    step = rz / pap
    rz_next = step * (step * aq - rq)
    beta = rz_next / rz
    grown = 1.0 + beta
    curved = grown * grown * pap - 2.0 * step * grown * aq + step * step * qhq
    step_next = rz_next / curved
    on_z = step + step_next * grown
    on_q = step_next * step
    for i in range(8):
        plane = x[i]
        if i == 0:
            plane = plane + zlo[...]
        if i == 7:
            plane = plane + zhi[...]
        p_ref[i] = on_z * z[i] - on_q * plane


def run(kernel, outs, smem, args, scratch=(), flops=1000000, place=VMEM, limit=LIMIT):
    nbytes = sum(4 * int(np.prod(out)) for out in outs) * 2
    return pl.pallas_call(
        kernel,
        out_shape=[jax.ShapeDtypeStruct(out, F32) for out in outs],
        in_specs=[pl.BlockSpec(memory_space=SMEM) for _ in smem]
        + [pl.BlockSpec(memory_space=place) for _ in args],
        out_specs=[pl.BlockSpec(memory_space=VMEM) for _ in outs],
        scratch_shapes=list(scratch),
        compiler_params=pltpu.CompilerParams(vmem_limit_bytes=limit),
        cost_estimate=pl.CostEstimate(flops=flops, bytes_accessed=nbytes, transcendentals=0),
    )(*smem, *args)


def shift(axis, low_face, high_face):
    count = lax.axis_size(axis)
    forward = [(i, i + 1) for i in range(count - 1)]
    backward = [(target, source) for source, target in forward]
    return lax.ppermute(high_face, axis, forward), lax.ppermute(low_face, axis, backward)


def body(level_set, velocity, source, wick_solid):
    block = level_set.shape
    count_gx = lax.axis_size("gx")
    count_gy = lax.axis_size("gy")
    index_gx = lax.axis_index("gx")
    index_gy = lax.axis_index("gy")

    def ends(index, count):
        return [jnp.where(index > 0, 0.5, 1.0), jnp.where(index < count - 1, 0.5, 1.0)]

    place = [index_gx.astype(F32), index_gy.astype(F32)]
    beyond = [
        jnp.where(index_gx < count_gx - 2, 0.5, 1.0),
        jnp.where(index_gx > 1, 0.5, 1.0),
    ]
    near = jnp.stack(ends(index_gx, count_gx) + ends(index_gy, count_gy) + place + beyond)
    near = near.astype(F32)
    packed = jnp.asarray(PACKED)
    tables = jnp.asarray(TABLES)
    face = (ROWS, LANES)
    wide_block = (8, WIDE, LANES)
    wide_face = (WIDE, LANES)
    rim = (12, TILE, LANES)

    b, l, zlo, zhi, solid = run(
        advect_kernel,
        [block, block, (3, *face), (3, *face), (8, LANES)],
        [],
        [
            pltpu.with_memory_space_constraint(array, pltpu.HBM)
            for array in (level_set, velocity, source, packed, wick_solid.reshape(EY, EX))
        ],
        [VMEM(block, F32), VMEM((3, *block), F32), VMEM(block, F32), VMEM(PACKED.shape, F32)]
        + [VMEM((EY, EX), jnp.int32), pltpu.SemaphoreType.DMA((5,))],
        place=pltpu.HBM,
    )
    zlo, zhi = shift("gx", zlo, zhi)
    ylo, yhi = run(rim_kernel, [rim, rim], [], [solid, b, l, zlo, zhi])
    ylo, yhi = shift("gy", ylo, yhi)
    (inner,) = run(
        inner_schwarz_kernel, [block], [], [packed, tables, b, zlo, zhi], flops=20000000
    )
    w, wlo, whi = run(
        first_schwarz_kernel,
        [wide_block, wide_face, wide_face],
        [near],
        [packed, tables, inner, b, zlo, zhi, ylo, yhi],
    )
    wlo, whi = shift("gx", wlo, whi)
    level_new, flux, stat = run(
        level_kernel,
        [block, wide_block, (1, LANES)],
        [near],
        [solid, packed, b, l, zlo, zhi, ylo, yhi],
        flops=20000000,
    )
    zl, yl, zlo, zhi, stat = run(
        galerkin_kernel,
        [wide_block, wide_block, wide_block, wide_block, (count_gx, LANES)],
        [near],
        [packed, stat, flux, w, wlo, whi],
    )
    zlo, zhi = shift("gx", zlo, zhi)
    gathered = lax.all_to_all(stat, "gx", 0, 0, tiled=True)
    (column,) = run(column_kernel, [(count_gy, LANES)], [], [gathered])
    gathered = lax.all_to_all(column, "gy", 0, 0, tiled=True)
    (coarse,) = run(
        functools.partial(coarse_kernel, count_gy),
        [(16, LANES)],
        [near],
        [gathered],
        [VMEM((LANES, LANES), F32), VMEM((LANES, LANES), F32)],
    )
    z, y, w, wlo, whi = run(
        apply_kernel,
        [block, block, block, face, face],
        [near],
        [packed, tables, coarse, flux, zl, yl, zlo, zhi],
    )
    zlo, zhi = shift("gx", wlo, whi)
    x, kx, sums = run(
        second_kernel,
        [block, (2, *face), (1, LANES)],
        [near],
        [packed, coarse, flux, b, y, z, w],
        flops=20000000,
    )
    (sums,) = run(
        face_kernel, [(2 * count_gx, LANES)], [], [packed, flux, b, y, kx, zlo, zhi, sums]
    )
    pairs = count_gy // 2
    columns = [
        [z * count_gy + 2 * m + c for z in range(count_gx) for c in range(2)] for m in range(pairs)
    ]
    layers = [
        [z * count_gy + 2 * m + c for m in range(pairs)] for z in range(count_gx) for c in range(2)
    ]
    axes = ("gx", "gy")
    tile = lax.all_to_all(sums, axes, 0, 0, axis_index_groups=columns, tiled=True)
    wide = jnp.broadcast_to(jnp.sum(tile, axis=0, keepdims=True), (pairs, LANES))
    wide = lax.all_to_all(wide, axes, 0, 0, axis_index_groups=layers, tiled=True)
    (pressure,) = run(combine_kernel, [block], [], [wide, z, x, zlo, zhi])
    return (level_new, pressure)


def solution(mesh):
    placed = (
        P("gx", "gy", None),
        P(None, "gx", "gy", None),
        P("gx", "gy", None),
        P("gx", "gy", None),
    )
    return jax.shard_map(
        body,
        mesh=mesh,
        in_specs=placed,
        out_specs=(P("gx", "gy", None), P("gx", "gy", None)),
        check_vma=False,
    )
```

```python
import functools

import jax
import jax.numpy as jnp
import numpy as np
from jax import lax
from jax.experimental import pallas as pl
from jax.experimental.pallas import tpu as pltpu
from jax.sharding import PartitionSpec as P

EZ = 1
EY = 4
EX = 16
ROWS = 8 * EY
LANES = 8 * EX

TIME_STEP = 0.02
HELM_COEF = 0.25
LEVEL_WIDTH = 0.25
GAS_RATIO = 10.0
SOLID_FACTOR = 0.25
SCHWARZ_SCALE = 0.5
SCHWARZ_SHIFT = 0.05

F32 = jnp.float32
BF16 = jnp.bfloat16
VMEM = pltpu.VMEM
SMEM = pltpu.SMEM
LIMIT = 24 * 1024 * 1024


def gll_tables():
    gll_nodes = np.array(
        [
            -1.0,
            -0.8717401485096066,
            -0.5917001814331423,
            -0.2092992179024789,
            0.2092992179024789,
            0.5917001814331423,
            0.8717401485096066,
            1.0,
        ]
    )
    weight_np = np.array(
        [
            1.0 / 28.0,
            0.21070422714350603,
            0.3411226924835044,
            0.4124587946587038,
            0.4124587946587038,
            0.3411226924835044,
            0.21070422714350603,
            1.0 / 28.0,
        ]
    )
    bary_weights = np.array(
        [1.0 / np.prod([gll_nodes[i] - gll_nodes[j] for j in range(8) if j != i]) for i in range(8)]
    )
    derivative = np.zeros((8, 8))
    for i in range(8):
        for j in range(8):
            if i != j:
                derivative[i, j] = bary_weights[j] / bary_weights[i] / (gll_nodes[i] - gll_nodes[j])
        derivative[i, i] = -np.sum(derivative[i])
    return (weight_np, derivative)


def sine_tables():
    indices = np.arange(10) + 1.0
    sine_basis = np.sqrt(2.0 / 11.0) * np.sin(np.pi * np.outer(indices, indices) / 11.0)
    eigen_vals = 2.0 - 2.0 * np.cos(np.pi * indices / 11.0)
    return (sine_basis, eigen_vals)


WEIGHT, DERIV = gll_tables()
SINE, EIGEN = sine_tables()


def split_const(matrix):
    single = matrix.astype(np.float32)
    high = single.astype(jnp.bfloat16)
    low = (single - high.astype(np.float32)).astype(jnp.bfloat16)
    return high, low


def line_maps(count):
    length = 8 * count
    total = length + 4

    def column(position):
        if 0 <= position < length:
            return position
        return {-2: length, -1: length + 1, length: length + 2, length + 1: length + 3}[position]

    assembled = {}
    for position in range(-2, length + 2):
        row = np.zeros(total)
        row[column(position)] = 1.0
        if 0 <= position < length:
            if position % 8 == 0:
                row[column(position - 1)] += 1.0
            if position % 8 == 7:
                row[column(position + 1)] += 1.0
        assembled[position] = row
    forward = np.zeros((10 * count, total))
    for element in range(count):
        places = [8 * element - 2] + list(range(8 * element, 8 * element + 8)) + [8 * element + 9]
        forward[10 * element : 10 * element + 10] = SINE @ np.stack([assembled[p] for p in places])
    backward = np.zeros((length, 10 * count))
    for element in range(count):
        backward[8 * element : 8 * element + 8, 10 * element : 10 * element + 10] = SINE[1:9]
    for element in range(count - 1):
        first, second = 8 * element + 7, 8 * element + 8
        mean = 0.5 * (backward[first] + backward[second])
        backward[first] = mean
        backward[second] = mean
    return forward, backward


RING = 16
WIDE = ROWS + 2 * RING
REACH = 26
TILE = 48
TILE_B = 32


def ring_maps(reach, depth, inside):
    count = EY + 2 * depth
    forward, _ = line_maps(count)
    length = 8 * count
    columns = np.zeros((10 * count, len(inside)))
    for at, position in enumerate(inside):
        place = None if position is None else position + 8 * depth
        if place is None or place < -2 or place > length + 1:
            continue
        source = place if 0 <= place < length else {-2: 0, -1: 1}.get(place, place - length + 2) + length
        columns[:, at] = forward[:, source]
    _, backward = line_maps(count)
    own = 8 * depth
    rows = np.concatenate(
        [
            backward[own - reach : own + ROWS + reach],
            np.zeros((8, 10 * count)),
        ]
    )
    rows[ROWS + 2 * reach, 10 * depth : 10 * depth + 10] = SINE[1]
    rows[ROWS + 2 * reach + 1, 10 * (depth + EY - 1) : 10 * (depth + EY)] = SINE[8]
    return columns, rows


FZ, BZ = line_maps(1)
TILES = list(range(-REACH, 0)) + [None] * (TILE_B - REACH) + list(range(ROWS))
TILES += list(range(ROWS, ROWS + REACH)) + [None] * (TILE_B - REACH)
FY_A, BY_A = ring_maps(RING, 3, TILES)
FY_B, BY_B = ring_maps(0, 1, list(range(-RING, ROWS + RING)))
INNER = np.arange(40, 60)
OUTER = np.concatenate([np.arange(0, 40), np.arange(60, 100)])
FY_I, BY_I = FY_A[INNER, TILE_B : TILE_B + ROWS], BY_A[RING : RING + ROWS, INNER]
FY_A, BY_A = FY_A[OUTER], BY_A[:, OUTER]
STEP_A = 80
STEP_B = 64
STEP_I = 32


def padded(forward, backward, step):
    forward = np.pad(forward, ((0, step - forward.shape[0]), (0, 0)))
    return forward, np.pad(backward, ((0, 0), (0, step - backward.shape[1])))


FY_A, BY_A = padded(FY_A, BY_A, STEP_A)
FY_B, BY_B = padded(FY_B, BY_B, STEP_B)
FY_I, BY_I = padded(FY_I, BY_I, STEP_I)
FX, BX = line_maps(EX)
FX = FX[:, :LANES]


FX_H, FX_L = split_const(FX.T.copy())
BX_H, BX_L = split_const(BX.T.copy())


def wide_const(table):
    high, low = split_const(table)
    return np.concatenate([high, high, low], axis=1)


def pack_tables(tables):
    places, pieces, at = [], [], 0
    for table in tables:
        rows = -(-table.shape[0] // 16) * 16
        extra = ((0, rows - table.shape[0]), (0, 384 - table.shape[1]))
        pieces.append(np.pad(table.astype(np.float32), extra))
        places.append((at, rows, table.shape[1]))
        at += rows
    return np.concatenate(pieces).astype(jnp.bfloat16), places


TABLES, PLACES = pack_tables(
    [
        np.concatenate([FX_H, FX_H], axis=0),
        FX_L,
        BX_H,
        BX_L,
        wide_const(FY_A),
        wide_const(BY_A),
        wide_const(FY_B),
        wide_const(BY_B),
        wide_const(FY_I),
        wide_const(BY_I),
    ]
)


def roll_table():
    table = np.zeros((2, 8, 8, LANES))
    for kind, matrix in enumerate((DERIV, DERIV.T)):
        for k in range(8):
            for i in range(8):
                table[kind, k, i, :] = matrix[i, (i + k) % 8]
    return table.reshape(2 * 64, LANES)


WY = np.tile(WEIGHT, WIDE // 8)
WX = np.tile(WEIGHT, EX)


def inner_count(count):
    mult = np.ones(8 * count)
    position = np.arange(8 * count)
    mult[(position % 8 == 0) & (position > 0)] += 1.0
    mult[(position % 8 == 7) & (position < 8 * count - 1)] += 1.0
    return mult


END_MASS = np.where(np.arange(WIDE) % 8 % 7 == 0, 2.0, 1.0)
INV_MASS = (8.0 / (WY * END_MASS)[:, None] / (WX * inner_count(EX))[None, :]).astype(np.float32)

AT_ROLLS = WIDE
AT_DX = AT_ROLLS + 128
AT_DXT = AT_DX + LANES
AT_SQUARE = AT_DXT + LANES
AT_MASS = AT_SQUARE + 16
AT_SPREAD = AT_MASS + WIDE
AT_EIGEN_Y = AT_SPREAD + EX
AT_EIGEN_X = AT_EIGEN_Y + STEP_A
LAM_Y = np.resize(EIGEN, STEP_A)
LAM_X = np.resize(EIGEN, 8 * LANES).reshape(8, LANES)
PACKED = np.concatenate(
    [
        WY[:, None] * WX[None, :],
        roll_table(),
        np.kron(np.eye(EX), DERIV.T),
        np.kron(np.eye(EX), DERIV),
        np.repeat(DERIV[:, :1] ** 2, LANES, axis=1),
        np.repeat(DERIV[:, 7:] ** 2, LANES, axis=1),
        INV_MASS,
        np.kron(np.eye(EX), np.ones((1, 8))),
        np.repeat(LAM_Y[:, None], LANES, axis=1),
        LAM_X,
    ]
).astype(np.float32)


def parts(values):
    high = values.astype(BF16)
    low = (values - high.astype(F32)).astype(BF16)
    return high, low


def dot(left, right):
    return jnp.dot(left, right, preferred_element_type=F32)


def left_pairs(table, planes):
    results = []
    for i in range(0, len(planes), 2):
        high, low = parts(jnp.concatenate([planes[i], planes[i + 1]], axis=1))
        both = dot(table, jnp.concatenate([high, low, high], axis=0))
        results += [both[:, 0:LANES], both[:, LANES : 2 * LANES]]
    return results


def along_z(values, matrix):
    rows = []
    for i in range(matrix.shape[0]):
        total = None
        for j in range(matrix.shape[1]):
            if matrix[i, j] == 0.0:
                continue
            term = float(matrix[i, j]) * values[j]
            total = term if total is None else total + term
        rows.append(total)
    return rows


def along_y(values, packed, kind):
    count, rows = values.shape[:2]
    grouped = values.reshape(count * rows // 8, 8, LANES)
    start = AT_ROLLS + 64 * kind
    total = packed[start : start + 8][None] * grouped
    for k in range(1, 8):
        total = total + packed[start + 8 * k : start + 8 * k + 8][None] * pltpu.roll(grouped, 8 - k, 1)
    return total.reshape(count, rows, LANES)


def along_x(values, packed, kind):
    start = AT_DXT if kind else AT_DX
    high, low = parts(packed[start : start + LANES])
    first, rest = parts(values.reshape(values.shape[0] * values.shape[1], LANES))
    total = dot(
        jnp.concatenate([first, rest], axis=1), jnp.concatenate([high, high], axis=0)
    ) + dot(first, low)
    return total.reshape(values.shape)


def stack(planes):
    return jnp.concatenate([plane[None] for plane in planes], axis=0)


def edge_rows(rows, low, high):
    position = lax.broadcasted_iota(jnp.int32, (rows, LANES), 0)
    return jnp.where(position == 0, low, jnp.where(position == rows - 1, high, 1.0))


def local_operator(values, flux, packed):
    plane_w = packed[0 : values.shape[1]]
    gz = along_z([values[i] for i in range(8)], DERIV)
    fz = along_z([flux[i] * gz[i] for i in range(8)], DERIV.T)
    total = along_y(flux * along_y(values, packed, 0), packed, 1)
    total = total + along_x(flux * along_x(values, packed, 0), packed, 1)
    planes = [
        total[i] + fz[i] + (HELM_COEF * 0.125 * float(WEIGHT[i])) * (plane_w * values[i])
        for i in range(8)
    ]
    return stack(planes)


def add_planes(own, low_z, high_z):
    planes = [own[i] for i in range(8)]
    planes[0] = planes[0] + low_z
    planes[7] = planes[7] + high_z
    return stack(planes)


def solve_elements(planes, packed, tables, kind):
    def table(index):
        at, rows, width = PLACES[index]
        return tables[at : at + rows, 0:width]

    fxhh, fxl, bxh, bxl = (table(index) for index in range(4))
    spectral = left_pairs(table(4 + 2 * kind), along_z(planes, FZ))
    high, low = parts(jnp.concatenate(spectral, axis=0))
    wide = dot(jnp.concatenate([high, low], axis=1), fxhh) + dot(high, fxl)
    step = PLACES[4 + 2 * kind][1]
    column = packed[AT_EIGEN_Y : AT_EIGEN_Y + step]
    rest = 10 * EX - LANES
    lam = jnp.concatenate(
        [
            column + packed[AT_EIGEN_X : AT_EIGEN_X + 1],
            column[:, 0:rest] + packed[AT_EIGEN_X + 1 : AT_EIGEN_X + 2, 0:rest],
        ],
        axis=1,
    )
    scaled = [
        wide[step * i : step * (i + 1)]
        / (SCHWARZ_SCALE * lam + float(SCHWARZ_SCALE * EIGEN[i] + SCHWARZ_SHIFT))
        for i in range(10)
    ]
    high, low = parts(jnp.concatenate(scaled, axis=0))
    back = dot(high, bxh) + dot(low, bxh) + dot(high, bxl)
    back = left_pairs(table(5 + 2 * kind), [back[step * i : step * (i + 1)] for i in range(10)])
    return along_z(back, BZ)


def store_faces(planes, near, out_ref, low_ref, high_ref):
    planes[0] = planes[0] * near[0]
    planes[7] = planes[7] * near[1]
    for i in range(8):
        out_ref[i] = planes[i]
    low_ref[...] = planes[0]
    high_ref[...] = planes[7]


def ring_rows(near):
    row = lax.broadcasted_iota(jnp.int32, (WIDE, LANES), 0)
    return row, 2.0 - 2.0 * near[2], 2.0 - 2.0 * near[3]


def partition_total(own, low_z, high_z, low_y, high_y, near):
    def planes(array):
        total = near[0] * array[0] + near[1] * array[7]
        for i in range(1, 7):
            total = total + array[i]
        return total

    total = planes(own) + 0.5 * (low_z[1] + high_z[0])
    below = planes(low_y) + 0.5 * (low_y[9] + low_y[10])
    above = planes(high_y) + 0.5 * (high_y[9] + high_y[10])
    faces = 0.5 * (below[REACH - 1 : REACH] + above[0:1])
    return jnp.sum(total * edge_rows(ROWS, near[2], near[3])) + jnp.sum(faces)


def lane_row(entries):
    lane = lax.broadcasted_iota(jnp.int32, (1, LANES), 1)
    row = jnp.zeros((1, LANES), F32)
    for index, value in enumerate(entries):
        row = jnp.where(lane == index, value, row)
    return row


def advect_kernel(
    lev_in, vel_in, src_in, packed_in, solid_in, b_ref, l_ref, zlo, zhi, solid_ref,
    lev, vel, src, packed, solid, sems,
):
    pairs = ((lev_in, lev), (packed_in, packed), (vel_in, vel), (src_in, src), (solid_in, solid))
    copies = [
        pltpu.make_async_copy(source, target, sems.at[index])
        for index, (source, target) in enumerate(pairs)
    ]
    for copy in copies:
        copy.start()
    copies[0].wait()
    level = lev[...]
    gz = stack(along_z([level[i] for i in range(8)], DERIV))
    copies[1].wait()
    gy = along_y(level, packed, 0)
    gx = along_x(level, packed, 0)
    for copy in copies[2:]:
        copy.wait()
    spread = packed[AT_SPREAD : AT_SPREAD + EX].astype(BF16)
    in_solid = dot(solid[...].astype(F32).astype(BF16), spread)
    solid_ref[...] = jnp.concatenate([in_solid, jnp.zeros((8 - EY, LANES), F32)], axis=0)
    v0, v1, v2 = vel[0], vel[1], vel[2]
    moved = level - (2.0 * TIME_STEP) * (v0 * gz + v1 * gy + v2 * gx)
    diverge = stack(along_z([v0[i] for i in range(8)], DERIV))
    diverge = diverge + along_y(v1, packed, 0) + along_x(v2, packed, 0)
    force = src[...] - (2.0 * TIME_STEP) * diverge
    weights = packed[0:ROWS]
    for i in range(8):
        mass = (0.125 * float(WEIGHT[i])) * weights
        term = mass * force[i]
        moved_i = mass * moved[i]
        b_ref[i] = term
        l_ref[i] = moved_i
        if i < 2:
            zlo[i] = term
        if i == 0:
            zlo[2] = moved_i
        if i > 5:
            zhi[i - 6] = term
        if i == 7:
            zhi[2] = moved_i


def rim_kernel(solid, b, l, low_z, high_z, low_y, high_y):
    in_solid = solid[...]
    rest = TILE - REACH - RING - 1

    def rows(planes, at, level, far, extra=None):
        start = ROWS - REACH if far else 0
        pieces = [planes[at, start : start + REACH]]
        if level is None:
            pieces.append(jnp.zeros((RING + 1, LANES), F32))
        else:
            array, index = level
            start = ROWS - RING - 1 if far else 0
            pieces.append(array[index, start : start + RING + 1])
        if extra is None:
            pieces.append(jnp.zeros((rest, LANES), F32))
        else:
            pieces += [extra, jnp.zeros((rest - 2, LANES), F32)]
        return jnp.concatenate(pieces, axis=0)

    for far, out in ((False, low_y), (True, high_y)):
        extra = in_solid[EY - 2 : EY] if far else in_solid[0:2]
        for i in range(8):
            out[i] = rows(b, i, (l, i), far, extra if i == 0 else None)
        for i in range(2):
            out[8 + i] = rows(low_z, i, (low_z, 2) if i == 1 else None, far)
            out[10 + i] = rows(high_z, i, (high_z, 2) if i == 0 else None, far)


def level_kernel(
    near, solid, packed, b, l, zlo, zhi, ylo, yhi, level_ref, flux_ref, stat
):
    row, has_low, has_high = ring_rows(near)
    at = REACH

    def wide_rows(slot, own):
        return jnp.concatenate(
            [ylo[slot, at + 1 : at + 1 + RING], own, yhi[slot, at : at + RING]], axis=0
        )

    planes = []
    for i in range(8):
        plane = wide_rows(i, l[i])
        first = ylo[i, at : at + 1]
        last = yhi[i, at + RING : at + RING + 1]
        if i == 0:
            plane = plane + wide_rows(9, zlo[2])
            first = first + ylo[9, at : at + 1]
            last = last + yhi[9, at + RING : at + RING + 1]
        if i == 7:
            plane = plane + wide_rows(10, zhi[2])
            first = first + ylo[10, at : at + 1]
            last = last + yhi[10, at + RING : at + RING + 1]
        before = jnp.where(row == 0, first, pltpu.roll(plane, 1, 0))
        after = jnp.where(row == WIDE - 1, last, pltpu.roll(plane, WIDE - 1, 0))
        plane = plane + jnp.where(row % 8 == 0, before, jnp.where(row % 8 == 7, after, 0.0))
        planes.append(plane)
    own = stack(planes)
    lane = lax.broadcasted_iota(jnp.int32, (8, WIDE, LANES), 2)
    before = jnp.where((lane % 8 == 0) & (lane > 0), pltpu.roll(own, 1, 2), 0.0)
    after = jnp.where((lane % 8 == 7) & (lane < LANES - 1), pltpu.roll(own, LANES - 1, 2), 0.0)
    own = own + before + after
    ends = jnp.where(row == RING, 2.0 * near[2], jnp.where(row == RING + ROWS - 1, 2.0 * near[3], 1.0))
    inverse = packed[AT_MASS : AT_MASS + WIDE] * ends
    in_solid = solid[...]
    solids = [ylo[0, at + RING + 1 + k : at + RING + 2 + k] for k in range(2)]
    solids += [in_solid[e : e + 1] for e in range(EY)]
    solids += [yhi[0, at + RING + 1 + k : at + RING + 2 + k] for k in range(2)]
    open_part = jnp.concatenate(
        [jnp.broadcast_to(1.0 - (1.0 - SOLID_FACTOR) * rows, (8, LANES)) for rows in solids], axis=0
    )
    in_grid = jnp.where(row < RING, has_low, jnp.where(row >= RING + ROWS, has_high, 1.0))
    flux_w = packed[0:WIDE] * in_grid
    total = jnp.zeros((ROWS, LANES), F32)
    fluxes = []
    for i in range(8):
        scale = 1.0 / float(WEIGHT[i])
        plane = own[i] * (inverse * scale)
        if i == 0:
            plane = plane * near[0]
        if i == 7:
            plane = plane * near[1]
        level_ref[i] = plane[RING : RING + ROWS]
        liquid = jax.nn.sigmoid(plane * (1.0 / LEVEL_WIDTH))
        coef = (GAS_RATIO - (GAS_RATIO - 1.0) * liquid) * open_part
        total = total + coef[RING : RING + ROWS]
        flux = (0.5 * float(WEIGHT[i])) * (coef * flux_w)
        flux_ref[i] = flux
        fluxes.append(flux[RING : RING + ROWS])
    kbar = jnp.sum(total) * (1.0 / (8 * ROWS * LANES))
    entries = [kbar, partition_total(b, zlo, zhi, ylo, yhi, near)] + [0.0] * 9
    for first, second in ((0, 0), (0, 7), (7, 7)):
        slopes = along_z(fluxes, (DERIV[:, first] * DERIV[:, second])[None, :])[0]
        column = jnp.sum(slopes, axis=1, keepdims=True)
        entries += [jnp.sum(column, axis=0, keepdims=True), column[0:1], column[ROWS - 1 : ROWS]]
    inner = fluxes[0] + fluxes[1]
    for i in range(2, 8):
        inner = inner + fluxes[i]
    for at_row, start in ((0, 0), (ROWS - 8, 8)):
        square = packed[AT_SQUARE + start : AT_SQUARE + start + 8]
        entries += [
            jnp.sum(square * plane[at_row : at_row + 8]) for plane in (inner, fluxes[0], fluxes[7])
        ]
    stat[...] = lane_row(entries)


def inner_schwarz_kernel(packed, tables, b, zlo, zhi, out_ref):
    planes = [b[i] for i in range(8)] + [zlo[0], zlo[1], zhi[0], zhi[1]]
    planes = solve_elements(planes, packed, tables, 2)
    for i in range(8):
        out_ref[i] = planes[i]


def first_schwarz_kernel(
    near, packed, tables, inner, b, zlo, zhi, ylo, yhi, w_ref, wlo, whi
):
    own = [b[i] for i in range(8)] + [zlo[0], zlo[1], zhi[0], zhi[1]]
    planes = [
        jnp.concatenate([ylo[i, 0:TILE_B], own[i], yhi[i, 0:TILE_B]], axis=0) for i in range(12)
    ]
    planes = solve_elements(planes, packed, tables, 0)
    row, has_low, has_high = ring_rows(near)
    in_grid = jnp.where(row < RING, has_low, jnp.where(row >= RING + ROWS, has_high, 1.0))
    in_grid = jnp.where(row == RING, has_low, jnp.where(row == RING + ROWS - 1, has_high, in_grid))
    rest = jnp.zeros((RING, LANES), F32)
    for i in range(8):
        first = (1.0 - has_low) * planes[i][WIDE : WIDE + 1]
        last = (1.0 - has_high) * planes[i][WIDE + 1 : WIDE + 2]
        alone = jnp.where(row == RING, first, jnp.where(row == RING + ROWS - 1, last, 0.0))
        planes[i] = planes[i][0:WIDE] * in_grid + alone
        planes[i] = planes[i] + jnp.concatenate([rest, inner[i], rest], axis=0)
    store_faces(planes, near, w_ref, wlo, whi)


def galerkin_kernel(near, packed, stat_in, flux, w, zlo, zhi, zl_ref, y_ref, ylo, yhi, stat):
    local = add_planes(w, zlo[...], zhi[...])
    zl_ref[...] = local
    applied = local_operator(local, flux[...], packed)
    y_ref[...] = applied
    fluxes = [flux[i] for i in range(8)]
    for out, rows in ((ylo, (0, 1)), (yhi, (6, 7))):
        for k, i in enumerate(rows):
            out[k] = applied[i]
            for t, end in enumerate((0, 7)):
                out[2 + 2 * t + k] = along_z(fluxes, (DERIV[:, i] * DERIV[:, end])[None, :])[0]
            out[6 + k] = fluxes[i]
    applied = applied[:, RING : RING + ROWS]
    inner = near[0] * applied[0] + near[1] * applied[7]
    for i in range(1, 7):
        inner = inner + applied[i]
    edge = edge_rows(ROWS, near[2], near[3])
    entries = [0.0, 0.0]
    for plane in ((1.0 - near[0]) * applied[0], inner, (1.0 - near[1]) * applied[7]):
        entries += [
            (1.0 - near[2]) * jnp.sum(plane[0:1]),
            jnp.sum(edge * plane),
            (1.0 - near[3]) * jnp.sum(plane[ROWS - 1 : ROWS]),
        ]
    stat[...] = jnp.broadcast_to(stat_in[...] + lane_row(entries), stat.shape)


def merged_row(values):
    sub = lax.broadcasted_iota(jnp.int32, (8, LANES), 0)
    lane = lax.broadcasted_iota(jnp.int32, (8, LANES), 1)
    after = jnp.where(sub < 7, pltpu.roll(values, 7, 0), 0.0)
    before = jnp.where(sub > 0, pltpu.roll(values, 1, 0), 0.0)
    first = lax.broadcasted_iota(jnp.int32, (8, 1), 0) == 0
    last = lax.broadcasted_iota(jnp.int32, (8, 1), 0) == 7

    def column(array, index):
        return array[:, index : index + 1]

    def slopes(array, pair):
        whole, low, high = (column(array, 11 + 3 * pair + k) for k in range(3))
        return whole - low - high, low, high

    merged = [column(values, 0), column(values, 1)]
    for b in range(3):
        merged.append(column(values, 5 + b) + column(after, 2 + b) + column(before, 8 + b))
    merged += [own + other for own, other in zip(slopes(values, 0), slopes(before, 2), strict=True)]
    merged += list(slopes(values, 1))
    inside, interface = [], []
    for side in range(2):
        whole, low, high = (column(values, 20 + 3 * side + k) for k in range(3))
        ends = jnp.where(first, low, 0.0) + jnp.where(last, high, 0.0)
        inside.append(whole - low - high + ends)
        interface.append(jnp.where(first, 0.0, low) + column(before, 22 + 3 * side))
    rows = jnp.zeros((8, LANES), F32)
    for index, value in enumerate(merged + inside + interface):
        rows = jnp.where(lane == index, value, rows)
    total = rows[0:1]
    for i in range(1, 8):
        total = total + pltpu.roll(rows[i : i + 1], 16 * i, 1)
    return total


def column_kernel(gathered, out_ref):
    even, odd = (merged_row(gathered[pl.ds(c, 8, stride=2), :]) for c in range(2))
    row = lax.broadcasted_iota(jnp.int32, out_ref.shape, 0)
    out_ref[...] = jnp.where(row % 2 == 0, even, odd)


def invert(blocks, sub):
    for k in range(0, 8, 2):
        first, second = blocks[k], blocks[k + 1]
        a, b = first[k : k + 1], first[k + 1 : k + 2]
        c, d = second[k : k + 1], second[k + 1 : k + 2]
        scale = 1.0 / (a * d - b * c)
        first = jnp.where(sub == k, 1.0, jnp.where(sub == k + 1, 0.0, first))
        second = jnp.where(sub == k + 1, 1.0, jnp.where(sub == k, 0.0, second))
        low = (d * scale) * first - (b * scale) * second
        high = (a * scale) * second - (c * scale) * first
        pivots = (sub == k) | (sub == k + 1)
        rows = []
        for r in range(8):
            if r == k:
                rows.append(low)
            elif r == k + 1:
                rows.append(high)
            else:
                rest = jnp.where(pivots, 0.0, blocks[r])
                rows.append(rest - blocks[r][k : k + 1] * low - blocks[r][k + 1 : k + 2] * high)
        blocks = rows
    return blocks


def multiply(left, right):
    rows = []
    for r in range(8):
        total = left[r][0:1] * right[0]
        for k in range(1, 8):
            total = total + left[r][k : k + 1] * right[k]
        rows.append(total)
    return rows


def multiply_turned(left, right):
    rows = []
    for r in range(8):
        total = left[0][r : r + 1] * right[0]
        for k in range(1, 8):
            total = total + left[k][r : r + 1] * right[k]
        rows.append(total)
    return rows


def apply_turned(blocks, column):
    total = blocks[0] * column[0:1]
    for k in range(1, 8):
        total = total + blocks[k] * column[k : k + 1]
    return total


def coarse_operator(c, count, sums_z, couplings_z, inside_y, interface_y):
    sub = lax.broadcasted_iota(jnp.int32, c.shape, 0)
    lane = lax.broadcasted_iota(jnp.int32, c.shape, 1)
    has_low = lane > 0
    has_high = lane < count - 1

    def after(array):
        return jnp.where(sub < 7, pltpu.roll(array, 7, 0), 0.0)

    def before(array):
        return jnp.where(sub > 0, pltpu.roll(array, 1, 0), 0.0)

    def right(array):
        return jnp.where(has_high, pltpu.roll(array, LANES - 1, 1), 0.0)

    def left(array):
        return jnp.where(has_low, pltpu.roll(array, 1, 1), 0.0)

    on_low = jnp.where(has_low, 0.5 * (c + left(c)), c)
    on_high = jnp.where(has_high, 0.5 * (c + right(c)), c)
    tested = []
    for place, value in enumerate((c, on_low, on_high)):
        slope = jnp.where(sub > 0, 0.5 * (value - before(value)), 0.0)
        coupling = couplings_z[place]
        force = sums_z[place] * slope - coupling * after(slope) - before(coupling * slope)
        force = jnp.where(sub > 0, force, 0.0)
        tested.append(0.5 * (force - after(force)))
    result = tested[0] + jnp.where(has_low, 0.5, 1.0) * tested[1] + jnp.where(has_high, 0.5, 1.0) * tested[2]
    result = result + 0.5 * right(tested[1]) + 0.5 * left(tested[2])

    interface = jnp.where(sub > 0, 0.5 * (c + before(c)), 0.0)
    for side, (move, there) in enumerate(((left, has_low), (right, has_high))):
        force = inside_y[side] * jnp.where(there, 0.5 * (move(c) - c), 0.0)
        face = interface_y[side] * jnp.where(there, 0.5 * (move(interface) - interface), 0.0)
        force = force + 0.5 * (face + after(face))
        back = right if side == 0 else left
        result = result + 0.5 * (back(force) - force)

    end = float(WEIGHT[0])
    mass = (2.0 - 2.0 * end) * c + end * (interface + after(interface))
    mass = mass + jnp.where((sub == 0) | (sub == 7), end * c, 0.0)
    beside = jnp.where(has_low, 0.5 * (mass + left(mass)), 0.0)
    scaled = (2.0 * EY - 2.0 * end) * mass + end * (beside + right(beside))
    scaled = scaled + jnp.where(has_low, 0.0, end * mass) + jnp.where(has_high, 0.0, end * mass)
    return result + HELM_COEF / 8.0 * float(np.sum(WX)) * scaled


def coarse_kernel(count, near, gathered, out_ref, wide, turned):
    lanes = LANES
    sub = lax.broadcasted_iota(jnp.int32, (8, lanes), 0)
    lane = lax.broadcasted_iota(jnp.int32, (8, lanes), 1)
    wide[...] = jnp.zeros((LANES, LANES), F32)
    wide[0:count] = gathered[...]
    turned[...] = wide[...].T

    def value(index):
        return turned[pl.ds(index, 8, stride=16), :]

    def move(array, dz, dy):
        if dz:
            array = pltpu.roll(array, (-dz) % 8, 0)
        if dy:
            array = pltpu.roll(array, (-dy) % lanes, 1)
        return array

    kbar = jnp.where(lane < count, value(0), 1.0)
    above = move(kbar, 1, 0)
    link_z = jnp.where(sub < 7, 2.0 * kbar * above / (kbar + above) * (EY * EX / EZ), 0.0)
    link_z = jnp.where(lane < count, link_z, 0.0)
    beside = move(kbar, 0, 1)
    link_y = 2.0 * kbar * beside / (kbar + beside) * (EZ * EX / EY)
    link_y = jnp.where(lane < count - 1, link_y, 0.0)
    back_z = move(link_z, -1, 0)
    back_y = move(link_y, 0, -1)
    diagonal = HELM_COEF * EZ * EY * EX + link_z + back_z + link_y + back_y
    blocks = []
    for r in range(8):
        row = jnp.where(sub == r, diagonal, 0.0)
        row = jnp.where(sub == r + 1, -back_z, row)
        row = jnp.where(sub == r - 1, -link_z, row)
        blocks.append(row)

    levels = []
    step = 1
    while step < count:
        inverse = invert(blocks, sub)
        if step == 1:
            up, low = -link_y, -back_y
            solved_up = [row * up for row in inverse]
            solved_low = [row * low for row in inverse]
            pull_up = [up[r : r + 1] * solved_up[r] for r in range(8)]
            pull_low = [low[r : r + 1] * solved_low[r] for r in range(8)]
            new_low = [up[r : r + 1] * solved_low[r] for r in range(8)]
            new_up = [low[r : r + 1] * solved_up[r] for r in range(8)]
        else:
            solved_up, solved_low = multiply(inverse, upper), multiply(inverse, lower)
            pull_up = multiply_turned(solved_up, upper)
            pull_low = multiply_turned(solved_low, lower)
            if 2 * step < count:
                new_low = multiply_turned(solved_up, lower)
                new_up = multiply_turned(solved_low, upper)
        levels.append((step, solved_up, solved_low))
        blocks = [
            blocks[r] - move(pull_up[r], 0, -step) - move(pull_low[r], 0, step) for r in range(8)
        ]
        if 2 * step < count:
            lower = [-move(row, 0, -step) for row in new_low]
            upper = [-move(row, 0, step) for row in new_up]
        step *= 2
    inverse = invert(blocks, sub)

    def solve(column):
        for distance, solved_up, solved_low in levels:
            before = move(apply_turned(solved_up, column), 0, -distance)
            after = move(apply_turned(solved_low, column), 0, distance)
            column = column - before - after
        return apply_turned(inverse, column)

    first = solve(value(1))
    totals = coarse_operator(
        first,
        count,
        [value(5 + k) for k in range(3)],
        [value(8 + k) for k in range(3)],
        [value(11), value(12)],
        [value(13), value(14)],
    )
    totals = totals + value(3)
    totals = totals + jnp.where(lane < count - 1, move(value(2), 0, 1), 0.0)
    totals = totals + jnp.where(lane > 0, move(value(4), 0, -1), 0.0)
    totals = jnp.where(lane < count, totals, 0.0)
    second = solve(totals)
    gx = near[4].astype(jnp.int32)
    gy = near[5].astype(jnp.int32)
    for at, solved in ((0, first), (8, second)):
        turned_z = pltpu.roll(solved, (10 - gx) % 8, 0)
        out_ref[at : at + 8] = pltpu.roll(turned_z, (lanes + 1 - gy) % lanes, 1)


def coarse_columns(near, coarse, start, count):
    row, has_low, has_high = ring_rows(near)
    below = jnp.where(row < RING - 1, 1.0, jnp.where(row <= RING, 0.5, 0.0)) * has_low
    above = jnp.where(row > RING + ROWS, 1.0, jnp.where(row >= RING + ROWS - 1, 0.5, 0.0)) * has_high
    edge = jnp.where((row > RING) & (row < RING + ROWS - 1), 1.0, 0.0)
    edge = jnp.where(row == RING, near[2], jnp.where(row == RING + ROWS - 1, near[3], edge))
    edge = jnp.where(row == RING - 1, 0.5 * has_low, edge)
    edge = jnp.where(row == RING + ROWS, 0.5 * has_high, edge)
    columns = []
    for a in range(start, start + count):
        low, own, high = (coarse[a : a + 1, b : b + 1] for b in range(3))
        columns.append(below * low + edge * own + above * high)
    return columns


def coarse_planes(columns, low, high):
    before, inside, after = columns
    return inside, low * (before - inside), high * (after - inside)


def add_coarse(local, columns):
    inside, first, last = columns
    planes = [local[i] + inside for i in range(8)]
    planes[0] = planes[0] + first
    planes[7] = planes[7] + last
    return stack(planes)


def coarse_applied(columns, flux, packed):
    inside, first, last = columns
    slopes = [
        flux[i] * (float(DERIV[i, 0]) * first + float(DERIV[i, 7]) * last) for i in range(8)
    ]
    fz = along_z(slopes, DERIV.T)
    three = stack([inside + first, inside, inside + last])
    gy = along_y(three, packed, 0)
    fy = along_y(
        stack([flux[i] * gy[0 if i == 0 else 2 if i == 7 else 1] for i in range(8)]), packed, 1
    )
    plane_w = packed[0:WIDE]
    planes = []
    for i in range(8):
        plane = three[0 if i == 0 else 2 if i == 7 else 1]
        planes.append(fz[i] + fy[i] + (HELM_COEF * 0.125 * float(WEIGHT[i])) * (plane_w * plane))
    return stack(planes)


def face_applied(planes, payload, packed, rows, in_grid):
    inside, first, last = planes
    fields = [inside + (first if i == 0 else last if i == 7 else 0.0) for i in rows]
    gy = along_y(stack(fields), packed, 0)
    fy = along_y(stack([payload[6 + k] * gy[k] for k in range(2)]), packed, 1)
    plane_w = packed[0:WIDE]
    result = []
    for k, i in enumerate(rows):
        slopes = payload[2 + k] * first + payload[4 + k] * last
        mass = (HELM_COEF * 0.125 * float(WEIGHT[i])) * in_grid * (plane_w * fields[k])
        result.append(payload[k] + slopes + fy[k] + mass)
    return result


def apply_kernel(
    near, packed, tables, coarse, flux, zl, yl, ylo, yhi,
    z_ref, y_ref, w_ref, wlo, whi,
):
    columns = coarse_columns(near, coarse, 0, 5)
    own = coarse_planes(columns[1:4], 1.0 - near[0], 1.0 - near[1])
    field = add_coarse(zl[...], own)[:, RING : RING + ROWS]
    z_ref[...] = field
    applied = yl[...] + coarse_applied(own, flux[...], packed)
    y_ref[...] = applied[:, RING : RING + ROWS]
    lower = coarse_planes(columns[0:3], 1.0 - near[7], 0.5)
    upper = coarse_planes(columns[2:5], 0.5, 1.0 - near[6])
    planes = [applied[i] for i in range(8)]
    planes += face_applied(lower, ylo, packed, (6, 7), 2.0 - 2.0 * near[0])
    planes += face_applied(upper, yhi, packed, (0, 1), 2.0 - 2.0 * near[1])
    planes = solve_elements(planes, packed, tables, 1)
    row = lax.broadcasted_iota(jnp.int32, (ROWS, LANES), 0)
    _, has_low, has_high = ring_rows(near)
    in_grid = jnp.where(row == 0, has_low, jnp.where(row == ROWS - 1, has_high, 1.0))
    for i in range(8):
        first = (1.0 - has_low) * planes[i][ROWS : ROWS + 1]
        last = (1.0 - has_high) * planes[i][ROWS + 1 : ROWS + 2]
        alone = jnp.where(row == 0, first, jnp.where(row == ROWS - 1, last, 0.0))
        planes[i] = planes[i][0:ROWS] * in_grid + alone
    store_faces(planes, near, w_ref, wlo, whi)


def second_kernel(near, packed, coarse, flux, b, y, z, w, x_ref, kx_ref, stat):
    columns = [column[RING : RING + ROWS] for column in coarse_columns(near, coarse, 9, 3)]
    field = add_coarse(w[...], coarse_planes(columns, 1.0 - near[0], 1.0 - near[1]))
    x_ref[...] = field
    fluxes = flux[:, RING : RING + ROWS]
    gz = along_z([field[i] for i in range(8)], DERIV)
    gy = along_y(field, packed, 0)
    gx = along_x(field, packed, 0)
    slopes = [fluxes[i] * gz[i] for i in range(8)]
    ends = (0, 7)
    back = along_z(slopes, DERIV.T[[0, 7]])
    back_y = along_y(stack([fluxes[i] * gy[i] for i in ends]), packed, 1)
    back_x = along_x(stack([fluxes[i] * gx[i] for i in ends]), packed, 1)
    plane_w = packed[0:ROWS]
    mass = HELM_COEF * 0.125
    for k, i in enumerate(ends):
        weighted = (mass * float(WEIGHT[i])) * (plane_w * field[i])
        kx_ref[k] = back[k] + back_y[k] + back_x[k] + weighted
    energy = None
    for i in range(8):
        term = slopes[i] * gz[i] + fluxes[i] * (gy[i] * gy[i] + gx[i] * gx[i])
        term = term + (mass * float(WEIGHT[i])) * (plane_w * field[i] * field[i])
        energy = term if energy is None else energy + term
    first, right = z[...], b[...]
    sums = [right * first, y[...] * first, right * field, y[...] * field]
    stat[...] = lane_row([jnp.sum(term) for term in sums] + [jnp.sum(energy)])


def face_kernel(packed, flux, b, y, kx, zlo, zhi, stat_in, stat):
    faces = stack([zlo[...], zhi[...]])
    fluxes = flux[:, RING : RING + ROWS]
    gy = along_y(faces, packed, 0)
    gx = along_x(faces, packed, 0)
    plane_w = packed[0:ROWS]
    energy = 2.0 * (kx[0] * faces[0] + kx[1] * faces[1])
    for k, i in enumerate((0, 7)):
        mass = (HELM_COEF * 0.125 * float(WEIGHT[i])) * (plane_w * faces[k] * faces[k])
        energy = energy + mass + fluxes[i] * (gy[k] * gy[k] + gx[k] * gx[k])
    for i in range(8):
        slope = float(DERIV[i, 0]) * faces[0] + float(DERIV[i, 7]) * faces[1]
        energy = energy + fluxes[i] * slope * slope
    sums = [
        0.0,
        0.0,
        jnp.sum(b[0] * faces[0] + b[7] * faces[1]),
        jnp.sum(y[0] * faces[0] + y[7] * faces[1]),
        jnp.sum(energy),
    ]
    stat[...] = jnp.broadcast_to(stat_in[...] + lane_row(sums), stat.shape)


def combine_kernel(sums, z, x, zlo, zhi, p_ref):
    total = jnp.sum(sums[...], axis=0, keepdims=True)
    rz, pap, rq, aq, qhq = (total[:, k : k + 1] for k in range(5))
    step = rz / pap
    rz_next = step * (step * aq - rq)
    beta = rz_next / rz
    grown = 1.0 + beta
    curved = grown * grown * pap - 2.0 * step * grown * aq + step * step * qhq
    step_next = rz_next / curved
    on_z = step + step_next * grown
    on_q = step_next * step
    for i in range(8):
        plane = x[i]
        if i == 0:
            plane = plane + zlo[...]
        if i == 7:
            plane = plane + zhi[...]
        p_ref[i] = on_z * z[i] - on_q * plane


def run(kernel, outs, smem, args, scratch=(), flops=1000000, place=VMEM, limit=LIMIT):
    nbytes = sum(4 * int(np.prod(out)) for out in outs) * 2
    return pl.pallas_call(
        kernel,
        out_shape=[jax.ShapeDtypeStruct(out, F32) for out in outs],
        in_specs=[pl.BlockSpec(memory_space=SMEM) for _ in smem]
        + [pl.BlockSpec(memory_space=place) for _ in args],
        out_specs=[pl.BlockSpec(memory_space=VMEM) for _ in outs],
        scratch_shapes=list(scratch),
        compiler_params=pltpu.CompilerParams(vmem_limit_bytes=limit),
        cost_estimate=pl.CostEstimate(flops=flops, bytes_accessed=nbytes, transcendentals=0),
    )(*smem, *args)


def shift(axis, low_face, high_face):
    count = lax.axis_size(axis)
    forward = [(i, i + 1) for i in range(count - 1)]
    backward = [(target, source) for source, target in forward]
    return lax.ppermute(high_face, axis, forward), lax.ppermute(low_face, axis, backward)


def body(level_set, velocity, source, wick_solid):
    block = level_set.shape
    count_gx = lax.axis_size("gx")
    count_gy = lax.axis_size("gy")
    index_gx = lax.axis_index("gx")
    index_gy = lax.axis_index("gy")

    def ends(index, count):
        return [jnp.where(index > 0, 0.5, 1.0), jnp.where(index < count - 1, 0.5, 1.0)]

    place = [index_gx.astype(F32), index_gy.astype(F32)]
    beyond = [
        jnp.where(index_gx < count_gx - 2, 0.5, 1.0),
        jnp.where(index_gx > 1, 0.5, 1.0),
    ]
    near = jnp.stack(ends(index_gx, count_gx) + ends(index_gy, count_gy) + place + beyond)
    near = near.astype(F32)
    packed = jnp.asarray(PACKED)
    tables = jnp.asarray(TABLES)
    face = (ROWS, LANES)
    wide_block = (8, WIDE, LANES)
    wide_face = (WIDE, LANES)
    rim = (12, TILE, LANES)

    pairs = count_gy // 2
    columns = [
        [z * count_gy + 2 * m + c for z in range(count_gx) for c in range(2)] for m in range(pairs)
    ]
    layers = [
        [z * count_gy + 2 * m + c for m in range(pairs)] for z in range(count_gx) for c in range(2)
    ]
    axes = ("gx", "gy")

    b, l, zlo, zhi, solid = run(
        advect_kernel,
        [block, block, (3, *face), (3, *face), (8, LANES)],
        [],
        [
            pltpu.with_memory_space_constraint(array, pltpu.HBM)
            for array in (level_set, velocity, source, packed, wick_solid.reshape(EY, EX))
        ],
        [VMEM(block, F32), VMEM((3, *block), F32), VMEM(block, F32), VMEM(PACKED.shape, F32)]
        + [VMEM((EY, EX), jnp.int32), pltpu.SemaphoreType.DMA((5,))],
        place=pltpu.HBM,
    )
    zlo, zhi = shift("gx", zlo, zhi)
    ylo, yhi = run(rim_kernel, [rim, rim], [], [solid, b, l, zlo, zhi])
    ylo, yhi = shift("gy", ylo, yhi)
    (inner,) = run(
        inner_schwarz_kernel, [block], [], [packed, tables, b, zlo, zhi], flops=20000000
    )
    w, wlo, whi = run(
        first_schwarz_kernel,
        [wide_block, wide_face, wide_face],
        [near],
        [packed, tables, inner, b, zlo, zhi, ylo, yhi],
    )
    wlo, whi = shift("gx", wlo, whi)
    level_new, flux, stat = run(
        level_kernel,
        [block, wide_block, (1, LANES)],
        [near],
        [solid, packed, b, l, zlo, zhi, ylo, yhi],
        flops=20000000,
    )
    zl, yl, zlo, zhi, stat = run(
        galerkin_kernel,
        [wide_block, wide_block, wide_block, wide_block, (2 * count_gx, LANES)],
        [near],
        [packed, stat, flux, w, wlo, whi],
    )
    zlo, zhi = shift("gx", zlo, zhi)
    gathered = lax.all_to_all(stat, axes, 0, 0, axis_index_groups=columns, tiled=True)
    (column,) = run(column_kernel, [(count_gy, LANES)], [], [gathered])
    gathered = lax.all_to_all(column, axes, 0, 0, axis_index_groups=layers, tiled=True)
    (coarse,) = run(
        functools.partial(coarse_kernel, count_gy),
        [(16, LANES)],
        [near],
        [gathered],
        [VMEM((LANES, LANES), F32), VMEM((LANES, LANES), F32)],
    )
    z, y, w, wlo, whi = run(
        apply_kernel,
        [block, block, block, face, face],
        [near],
        [packed, tables, coarse, flux, zl, yl, zlo, zhi],
    )
    zlo, zhi = shift("gx", wlo, whi)
    x, kx, sums = run(
        second_kernel,
        [block, (2, *face), (1, LANES)],
        [near],
        [packed, coarse, flux, b, y, z, w],
        flops=20000000,
    )
    (sums,) = run(
        face_kernel, [(2 * count_gx, LANES)], [], [packed, flux, b, y, kx, zlo, zhi, sums]
    )
    tile = lax.all_to_all(sums, axes, 0, 0, axis_index_groups=columns, tiled=True)
    wide = jnp.broadcast_to(jnp.sum(tile, axis=0, keepdims=True), (pairs, LANES))
    wide = lax.all_to_all(wide, axes, 0, 0, axis_index_groups=layers, tiled=True)
    (pressure,) = run(combine_kernel, [block], [], [wide, z, x, zlo, zhi])
    return (level_new, pressure)


def solution(mesh):
    placed = (
        P("gx", "gy", None),
        P(None, "gx", "gy", None),
        P("gx", "gy", None),
        P("gx", "gy", None),
    )
    return jax.shard_map(
        body,
        mesh=mesh,
        in_specs=placed,
        out_specs=(P("gx", "gy", None), P("gx", "gy", None)),
        check_vma=False,
    )
```

```python
import functools

import jax
import jax.numpy as jnp
import numpy as np
from jax import lax
from jax.experimental import pallas as pl
from jax.experimental.pallas import tpu as pltpu
from jax.sharding import PartitionSpec as P

EZ = 1
EY = 4
EX = 16
ROWS = 8 * EY
LANES = 8 * EX

TIME_STEP = 0.02
HELM_COEF = 0.25
LEVEL_WIDTH = 0.25
GAS_RATIO = 10.0
SOLID_FACTOR = 0.25
SCHWARZ_SCALE = 0.5
SCHWARZ_SHIFT = 0.05

F32 = jnp.float32
BF16 = jnp.bfloat16
VMEM = pltpu.VMEM
SMEM = pltpu.SMEM
LIMIT = 24 * 1024 * 1024


def gll_tables():
    gll_nodes = np.array(
        [
            -1.0,
            -0.8717401485096066,
            -0.5917001814331423,
            -0.2092992179024789,
            0.2092992179024789,
            0.5917001814331423,
            0.8717401485096066,
            1.0,
        ]
    )
    weight_np = np.array(
        [
            1.0 / 28.0,
            0.21070422714350603,
            0.3411226924835044,
            0.4124587946587038,
            0.4124587946587038,
            0.3411226924835044,
            0.21070422714350603,
            1.0 / 28.0,
        ]
    )
    bary_weights = np.array(
        [1.0 / np.prod([gll_nodes[i] - gll_nodes[j] for j in range(8) if j != i]) for i in range(8)]
    )
    derivative = np.zeros((8, 8))
    for i in range(8):
        for j in range(8):
            if i != j:
                derivative[i, j] = bary_weights[j] / bary_weights[i] / (gll_nodes[i] - gll_nodes[j])
        derivative[i, i] = -np.sum(derivative[i])
    return (weight_np, derivative)


def sine_tables():
    indices = np.arange(10) + 1.0
    sine_basis = np.sqrt(2.0 / 11.0) * np.sin(np.pi * np.outer(indices, indices) / 11.0)
    eigen_vals = 2.0 - 2.0 * np.cos(np.pi * indices / 11.0)
    return (sine_basis, eigen_vals)


WEIGHT, DERIV = gll_tables()
SINE, EIGEN = sine_tables()


def split_const(matrix):
    single = matrix.astype(np.float32)
    high = single.astype(jnp.bfloat16)
    low = (single - high.astype(np.float32)).astype(jnp.bfloat16)
    return high, low


def line_maps(count):
    length = 8 * count
    total = length + 4

    def column(position):
        if 0 <= position < length:
            return position
        return {-2: length, -1: length + 1, length: length + 2, length + 1: length + 3}[position]

    assembled = {}
    for position in range(-2, length + 2):
        row = np.zeros(total)
        row[column(position)] = 1.0
        if 0 <= position < length:
            if position % 8 == 0:
                row[column(position - 1)] += 1.0
            if position % 8 == 7:
                row[column(position + 1)] += 1.0
        assembled[position] = row
    forward = np.zeros((10 * count, total))
    for element in range(count):
        places = [8 * element - 2] + list(range(8 * element, 8 * element + 8)) + [8 * element + 9]
        forward[10 * element : 10 * element + 10] = SINE @ np.stack([assembled[p] for p in places])
    backward = np.zeros((length, 10 * count))
    for element in range(count):
        backward[8 * element : 8 * element + 8, 10 * element : 10 * element + 10] = SINE[1:9]
    for element in range(count - 1):
        first, second = 8 * element + 7, 8 * element + 8
        mean = 0.5 * (backward[first] + backward[second])
        backward[first] = mean
        backward[second] = mean
    return forward, backward


RING = 16
WIDE = ROWS + 2 * RING
REACH = 26
TILE = 48
TILE_B = 32


def ring_maps(reach, depth, inside):
    count = EY + 2 * depth
    forward, _ = line_maps(count)
    length = 8 * count
    columns = np.zeros((10 * count, len(inside)))
    for at, position in enumerate(inside):
        place = None if position is None else position + 8 * depth
        if place is None or place < -2 or place > length + 1:
            continue
        source = place if 0 <= place < length else {-2: 0, -1: 1}.get(place, place - length + 2) + length
        columns[:, at] = forward[:, source]
    _, backward = line_maps(count)
    own = 8 * depth
    rows = np.concatenate(
        [
            backward[own - reach : own + ROWS + reach],
            np.zeros((8, 10 * count)),
        ]
    )
    rows[ROWS + 2 * reach, 10 * depth : 10 * depth + 10] = SINE[1]
    rows[ROWS + 2 * reach + 1, 10 * (depth + EY - 1) : 10 * (depth + EY)] = SINE[8]
    return columns, rows


FZ, BZ = line_maps(1)
TILES = list(range(-REACH, 0)) + [None] * (TILE_B - REACH) + list(range(ROWS))
TILES += list(range(ROWS, ROWS + REACH)) + [None] * (TILE_B - REACH)
FY_A, BY_A = ring_maps(RING, 3, TILES)
FY_B, BY_B = ring_maps(0, 1, list(range(-RING, ROWS + RING)))
INNER = np.arange(40, 60)
OUTER = np.concatenate([np.arange(0, 40), np.arange(60, 100)])
FY_I, BY_I = FY_A[INNER, TILE_B : TILE_B + ROWS], BY_A[RING : RING + ROWS, INNER]
FY_A, BY_A = FY_A[OUTER], BY_A[:, OUTER]
STEP_A = 80
STEP_B = 64
STEP_I = 32


def padded(forward, backward, step):
    forward = np.pad(forward, ((0, step - forward.shape[0]), (0, 0)))
    return forward, np.pad(backward, ((0, 0), (0, step - backward.shape[1])))


FY_A, BY_A = padded(FY_A, BY_A, STEP_A)
FY_B, BY_B = padded(FY_B, BY_B, STEP_B)
FY_I, BY_I = padded(FY_I, BY_I, STEP_I)
FX, BX = line_maps(EX)
FX = FX[:, :LANES]


FX_H, FX_L = split_const(FX.T.copy())
BX_H, BX_L = split_const(BX.T.copy())


def wide_const(table):
    high, low = split_const(table)
    return np.concatenate([high, high, low], axis=1)


def pack_tables(tables):
    places, pieces, at = [], [], 0
    for table in tables:
        rows = -(-table.shape[0] // 16) * 16
        extra = ((0, rows - table.shape[0]), (0, 384 - table.shape[1]))
        pieces.append(np.pad(table.astype(np.float32), extra))
        places.append((at, rows, table.shape[1]))
        at += rows
    return np.concatenate(pieces).astype(jnp.bfloat16), places


TABLES, PLACES = pack_tables(
    [
        np.concatenate([FX_H, FX_H], axis=0),
        FX_L,
        BX_H,
        BX_L,
        wide_const(FY_A),
        wide_const(BY_A),
        wide_const(FY_B),
        wide_const(BY_B),
        wide_const(FY_I),
        wide_const(BY_I),
    ]
)


def roll_table():
    table = np.zeros((2, 8, 8, LANES))
    for kind, matrix in enumerate((DERIV, DERIV.T)):
        for k in range(8):
            for i in range(8):
                table[kind, k, i, :] = matrix[i, (i + k) % 8]
    return table.reshape(2 * 64, LANES)


WY = np.tile(WEIGHT, WIDE // 8)
WX = np.tile(WEIGHT, EX)


def inner_count(count):
    mult = np.ones(8 * count)
    position = np.arange(8 * count)
    mult[(position % 8 == 0) & (position > 0)] += 1.0
    mult[(position % 8 == 7) & (position < 8 * count - 1)] += 1.0
    return mult


END_MASS = np.where(np.arange(WIDE) % 8 % 7 == 0, 2.0, 1.0)
INV_MASS = (8.0 / (WY * END_MASS)[:, None] / (WX * inner_count(EX))[None, :]).astype(np.float32)

AT_ROLLS = WIDE
AT_DX = AT_ROLLS + 128
AT_DXT = AT_DX + LANES
AT_SQUARE = AT_DXT + LANES
AT_MASS = AT_SQUARE + 16
AT_SPREAD = AT_MASS + WIDE
AT_EIGEN_Y = AT_SPREAD + EX
AT_EIGEN_X = AT_EIGEN_Y + STEP_A
LAM_Y = np.resize(EIGEN, STEP_A)
LAM_X = np.resize(EIGEN, 8 * LANES).reshape(8, LANES)
PACKED = np.concatenate(
    [
        WY[:, None] * WX[None, :],
        roll_table(),
        np.kron(np.eye(EX), DERIV.T),
        np.kron(np.eye(EX), DERIV),
        np.repeat(DERIV[:, :1] ** 2, LANES, axis=1),
        np.repeat(DERIV[:, 7:] ** 2, LANES, axis=1),
        INV_MASS,
        np.kron(np.eye(EX), np.ones((1, 8))),
        np.repeat(LAM_Y[:, None], LANES, axis=1),
        LAM_X,
    ]
).astype(np.float32)


def parts(values):
    high = values.astype(BF16)
    low = (values - high.astype(F32)).astype(BF16)
    return high, low


def dot(left, right):
    return jnp.dot(left, right, preferred_element_type=F32)


def left_pairs(table, planes):
    results = []
    for i in range(0, len(planes), 2):
        high, low = parts(jnp.concatenate([planes[i], planes[i + 1]], axis=1))
        both = dot(table, jnp.concatenate([high, low, high], axis=0))
        results += [both[:, 0:LANES], both[:, LANES : 2 * LANES]]
    return results


def along_z(values, matrix):
    rows = []
    for i in range(matrix.shape[0]):
        total = None
        for j in range(matrix.shape[1]):
            if matrix[i, j] == 0.0:
                continue
            term = float(matrix[i, j]) * values[j]
            total = term if total is None else total + term
        rows.append(total)
    return rows


def along_y(values, packed, kind):
    count, rows = values.shape[:2]
    grouped = values.reshape(count * rows // 8, 8, LANES)
    start = AT_ROLLS + 64 * kind
    total = packed[start : start + 8][None] * grouped
    for k in range(1, 8):
        total = total + packed[start + 8 * k : start + 8 * k + 8][None] * pltpu.roll(grouped, 8 - k, 1)
    return total.reshape(count, rows, LANES)


def along_x(values, packed, kind):
    start = AT_DXT if kind else AT_DX
    high, low = parts(packed[start : start + LANES])
    first, rest = parts(values.reshape(values.shape[0] * values.shape[1], LANES))
    total = dot(
        jnp.concatenate([first, rest], axis=1), jnp.concatenate([high, high], axis=0)
    ) + dot(first, low)
    return total.reshape(values.shape)


def stack(planes):
    return jnp.concatenate([plane[None] for plane in planes], axis=0)


def edge_rows(rows, low, high):
    position = lax.broadcasted_iota(jnp.int32, (rows, LANES), 0)
    return jnp.where(position == 0, low, jnp.where(position == rows - 1, high, 1.0))


def local_operator(values, flux, packed):
    plane_w = packed[0 : values.shape[1]]
    gz = along_z([values[i] for i in range(8)], DERIV)
    fz = along_z([flux[i] * gz[i] for i in range(8)], DERIV.T)
    total = along_y(flux * along_y(values, packed, 0), packed, 1)
    total = total + along_x(flux * along_x(values, packed, 0), packed, 1)
    planes = [
        total[i] + fz[i] + (HELM_COEF * 0.125 * float(WEIGHT[i])) * (plane_w * values[i])
        for i in range(8)
    ]
    return stack(planes)


def add_planes(own, low_z, high_z):
    planes = [own[i] for i in range(8)]
    planes[0] = planes[0] + low_z
    planes[7] = planes[7] + high_z
    return stack(planes)


def solve_elements(planes, packed, tables, kind):
    def table(index):
        at, rows, width = PLACES[index]
        return tables[at : at + rows, 0:width]

    fxhh, fxl, bxh, bxl = (table(index) for index in range(4))
    spectral = left_pairs(table(4 + 2 * kind), along_z(planes, FZ))
    high, low = parts(jnp.concatenate(spectral, axis=0))
    wide = dot(jnp.concatenate([high, low], axis=1), fxhh) + dot(high, fxl)
    step = PLACES[4 + 2 * kind][1]
    column = packed[AT_EIGEN_Y : AT_EIGEN_Y + step]
    rest = 10 * EX - LANES
    lam = jnp.concatenate(
        [
            column + packed[AT_EIGEN_X : AT_EIGEN_X + 1],
            column[:, 0:rest] + packed[AT_EIGEN_X + 1 : AT_EIGEN_X + 2, 0:rest],
        ],
        axis=1,
    )
    scaled = [
        wide[step * i : step * (i + 1)]
        / (SCHWARZ_SCALE * lam + float(SCHWARZ_SCALE * EIGEN[i] + SCHWARZ_SHIFT))
        for i in range(10)
    ]
    high, low = parts(jnp.concatenate(scaled, axis=0))
    back = dot(high, bxh) + dot(low, bxh) + dot(high, bxl)
    back = left_pairs(table(5 + 2 * kind), [back[step * i : step * (i + 1)] for i in range(10)])
    return along_z(back, BZ)


def store_faces(planes, near, out_ref, low_ref, high_ref):
    planes[0] = planes[0] * near[0]
    planes[7] = planes[7] * near[1]
    for i in range(8):
        out_ref[i] = planes[i]
    low_ref[...] = planes[0]
    high_ref[...] = planes[7]


def ring_rows(near):
    row = lax.broadcasted_iota(jnp.int32, (WIDE, LANES), 0)
    return row, 2.0 - 2.0 * near[2], 2.0 - 2.0 * near[3]


def partition_total(own, low_z, high_z, low_y, high_y, near):
    def planes(array):
        total = near[0] * array[0] + near[1] * array[7]
        for i in range(1, 7):
            total = total + array[i]
        return total

    total = planes(own) + 0.5 * (low_z[1] + high_z[0])
    below = planes(low_y) + 0.5 * (low_y[9] + low_y[10])
    above = planes(high_y) + 0.5 * (high_y[9] + high_y[10])
    faces = 0.5 * (below[REACH - 1 : REACH] + above[0:1])
    return jnp.sum(total * edge_rows(ROWS, near[2], near[3])) + jnp.sum(faces)


def lane_row(entries):
    lane = lax.broadcasted_iota(jnp.int32, (1, LANES), 1)
    row = jnp.zeros((1, LANES), F32)
    for index, value in enumerate(entries):
        row = jnp.where(lane == index, value, row)
    return row


def advect_kernel(
    lev_in, vel_in, src_in, packed_in, solid_in, b_ref, l_ref, zlo, zhi, solid_ref,
    lev, vel, src, packed, solid, sems,
):
    pairs = ((lev_in, lev), (packed_in, packed), (vel_in, vel), (src_in, src), (solid_in, solid))
    copies = [
        pltpu.make_async_copy(source, target, sems.at[index])
        for index, (source, target) in enumerate(pairs)
    ]
    for copy in copies:
        copy.start()
    copies[0].wait()
    level = lev[...]
    gz = stack(along_z([level[i] for i in range(8)], DERIV))
    copies[1].wait()
    gy = along_y(level, packed, 0)
    gx = along_x(level, packed, 0)
    for copy in copies[2:]:
        copy.wait()
    spread = packed[AT_SPREAD : AT_SPREAD + EX].astype(BF16)
    in_solid = dot(solid[...].astype(F32).astype(BF16), spread)
    solid_ref[...] = jnp.concatenate([in_solid, jnp.zeros((8 - EY, LANES), F32)], axis=0)
    v0, v1, v2 = vel[0], vel[1], vel[2]
    moved = level - (2.0 * TIME_STEP) * (v0 * gz + v1 * gy + v2 * gx)
    diverge = stack(along_z([v0[i] for i in range(8)], DERIV))
    diverge = diverge + along_y(v1, packed, 0) + along_x(v2, packed, 0)
    force = src[...] - (2.0 * TIME_STEP) * diverge
    weights = packed[0:ROWS]
    for i in range(8):
        mass = (0.125 * float(WEIGHT[i])) * weights
        term = mass * force[i]
        moved_i = mass * moved[i]
        b_ref[i] = term
        l_ref[i] = moved_i
        if i < 2:
            zlo[i] = term
        if i == 0:
            zlo[2] = moved_i
        if i > 5:
            zhi[i - 6] = term
        if i == 7:
            zhi[2] = moved_i


def rim_kernel(solid, b, l, low_z, high_z, low_y, high_y):
    in_solid = solid[...]
    rest = TILE - REACH - RING - 1

    def rows(planes, at, level, far, extra=None):
        start = ROWS - REACH if far else 0
        pieces = [planes[at, start : start + REACH]]
        if level is None:
            pieces.append(jnp.zeros((RING + 1, LANES), F32))
        else:
            array, index = level
            start = ROWS - RING - 1 if far else 0
            pieces.append(array[index, start : start + RING + 1])
        if extra is None:
            pieces.append(jnp.zeros((rest, LANES), F32))
        else:
            pieces += [extra, jnp.zeros((rest - 2, LANES), F32)]
        return jnp.concatenate(pieces, axis=0)

    for far, out in ((False, low_y), (True, high_y)):
        extra = in_solid[EY - 2 : EY] if far else in_solid[0:2]
        for i in range(8):
            out[i] = rows(b, i, (l, i), far, extra if i == 0 else None)
        for i in range(2):
            out[8 + i] = rows(low_z, i, (low_z, 2) if i == 1 else None, far)
            out[10 + i] = rows(high_z, i, (high_z, 2) if i == 0 else None, far)


def level_kernel(
    near, solid, packed, b, l, zlo, zhi, ylo, yhi, level_ref, flux_ref, stat
):
    row, has_low, has_high = ring_rows(near)
    at = REACH

    def wide_rows(slot, own):
        return jnp.concatenate(
            [ylo[slot, at + 1 : at + 1 + RING], own, yhi[slot, at : at + RING]], axis=0
        )

    planes = []
    for i in range(8):
        plane = wide_rows(i, l[i])
        first = ylo[i, at : at + 1]
        last = yhi[i, at + RING : at + RING + 1]
        if i == 0:
            plane = plane + wide_rows(9, zlo[2])
            first = first + ylo[9, at : at + 1]
            last = last + yhi[9, at + RING : at + RING + 1]
        if i == 7:
            plane = plane + wide_rows(10, zhi[2])
            first = first + ylo[10, at : at + 1]
            last = last + yhi[10, at + RING : at + RING + 1]
        before = jnp.where(row == 0, first, pltpu.roll(plane, 1, 0))
        after = jnp.where(row == WIDE - 1, last, pltpu.roll(plane, WIDE - 1, 0))
        plane = plane + jnp.where(row % 8 == 0, before, jnp.where(row % 8 == 7, after, 0.0))
        planes.append(plane)
    own = stack(planes)
    lane = lax.broadcasted_iota(jnp.int32, (8, WIDE, LANES), 2)
    before = jnp.where((lane % 8 == 0) & (lane > 0), pltpu.roll(own, 1, 2), 0.0)
    after = jnp.where((lane % 8 == 7) & (lane < LANES - 1), pltpu.roll(own, LANES - 1, 2), 0.0)
    own = own + before + after
    ends = jnp.where(row == RING, 2.0 * near[2], jnp.where(row == RING + ROWS - 1, 2.0 * near[3], 1.0))
    inverse = packed[AT_MASS : AT_MASS + WIDE] * ends
    in_solid = solid[...]
    solids = [ylo[0, at + RING + 1 + k : at + RING + 2 + k] for k in range(2)]
    solids += [in_solid[e : e + 1] for e in range(EY)]
    solids += [yhi[0, at + RING + 1 + k : at + RING + 2 + k] for k in range(2)]
    open_part = jnp.concatenate(
        [jnp.broadcast_to(1.0 - (1.0 - SOLID_FACTOR) * rows, (8, LANES)) for rows in solids], axis=0
    )
    in_grid = jnp.where(row < RING, has_low, jnp.where(row >= RING + ROWS, has_high, 1.0))
    flux_w = packed[0:WIDE] * in_grid
    total = jnp.zeros((ROWS, LANES), F32)
    fluxes = []
    for i in range(8):
        scale = 1.0 / float(WEIGHT[i])
        plane = own[i] * (inverse * scale)
        if i == 0:
            plane = plane * near[0]
        if i == 7:
            plane = plane * near[1]
        level_ref[i] = plane[RING : RING + ROWS]
        liquid = jax.nn.sigmoid(plane * (1.0 / LEVEL_WIDTH))
        coef = (GAS_RATIO - (GAS_RATIO - 1.0) * liquid) * open_part
        total = total + coef[RING : RING + ROWS]
        flux = (0.5 * float(WEIGHT[i])) * (coef * flux_w)
        flux_ref[i] = flux
        fluxes.append(flux[RING : RING + ROWS])
    kbar = jnp.sum(total) * (1.0 / (8 * ROWS * LANES))
    entries = [kbar, partition_total(b, zlo, zhi, ylo, yhi, near)] + [0.0] * 9
    for first, second in ((0, 0), (0, 7), (7, 7)):
        slopes = along_z(fluxes, (DERIV[:, first] * DERIV[:, second])[None, :])[0]
        column = jnp.sum(slopes, axis=1, keepdims=True)
        entries += [jnp.sum(column, axis=0, keepdims=True), column[0:1], column[ROWS - 1 : ROWS]]
    inner = fluxes[0] + fluxes[1]
    for i in range(2, 8):
        inner = inner + fluxes[i]
    for at_row, start in ((0, 0), (ROWS - 8, 8)):
        square = packed[AT_SQUARE + start : AT_SQUARE + start + 8]
        entries += [
            jnp.sum(square * plane[at_row : at_row + 8]) for plane in (inner, fluxes[0], fluxes[7])
        ]
    stat[...] = lane_row(entries)


def inner_schwarz_kernel(packed, tables, b, zlo, zhi, out_ref):
    planes = [b[i] for i in range(8)] + [zlo[0], zlo[1], zhi[0], zhi[1]]
    planes = solve_elements(planes, packed, tables, 2)
    for i in range(8):
        out_ref[i] = planes[i]


def first_schwarz_kernel(
    near, packed, tables, inner, b, zlo, zhi, ylo, yhi, w_ref, wlo, whi
):
    own = [b[i] for i in range(8)] + [zlo[0], zlo[1], zhi[0], zhi[1]]
    planes = [
        jnp.concatenate([ylo[i, 0:TILE_B], own[i], yhi[i, 0:TILE_B]], axis=0) for i in range(12)
    ]
    planes = solve_elements(planes, packed, tables, 0)
    row, has_low, has_high = ring_rows(near)
    in_grid = jnp.where(row < RING, has_low, jnp.where(row >= RING + ROWS, has_high, 1.0))
    in_grid = jnp.where(row == RING, has_low, jnp.where(row == RING + ROWS - 1, has_high, in_grid))
    rest = jnp.zeros((RING, LANES), F32)
    for i in range(8):
        first = (1.0 - has_low) * planes[i][WIDE : WIDE + 1]
        last = (1.0 - has_high) * planes[i][WIDE + 1 : WIDE + 2]
        alone = jnp.where(row == RING, first, jnp.where(row == RING + ROWS - 1, last, 0.0))
        planes[i] = planes[i][0:WIDE] * in_grid + alone
        planes[i] = planes[i] + jnp.concatenate([rest, inner[i], rest], axis=0)
    store_faces(planes, near, w_ref, wlo, whi)


def galerkin_kernel(near, packed, stat_in, flux, w, zlo, zhi, zl_ref, y_ref, ylo, yhi, stat):
    local = add_planes(w, zlo[...], zhi[...])
    zl_ref[...] = local
    applied = local_operator(local, flux[...], packed)
    y_ref[...] = applied
    fluxes = [flux[i] for i in range(8)]
    for out, rows in ((ylo, (0, 1)), (yhi, (6, 7))):
        for k, i in enumerate(rows):
            out[k] = applied[i]
            for t, end in enumerate((0, 7)):
                out[2 + 2 * t + k] = along_z(fluxes, (DERIV[:, i] * DERIV[:, end])[None, :])[0]
            out[6 + k] = fluxes[i]
    applied = applied[:, RING : RING + ROWS]
    inner = near[0] * applied[0] + near[1] * applied[7]
    for i in range(1, 7):
        inner = inner + applied[i]
    edge = edge_rows(ROWS, near[2], near[3])
    entries = [0.0, 0.0]
    for plane in ((1.0 - near[0]) * applied[0], inner, (1.0 - near[1]) * applied[7]):
        entries += [
            (1.0 - near[2]) * jnp.sum(plane[0:1]),
            jnp.sum(edge * plane),
            (1.0 - near[3]) * jnp.sum(plane[ROWS - 1 : ROWS]),
        ]
    stat[...] = jnp.broadcast_to(stat_in[...] + lane_row(entries), stat.shape)


def column_kernel(gathered, out_ref):
    values = gathered[...]
    sub = lax.broadcasted_iota(jnp.int32, (8, LANES), 0)
    lane = lax.broadcasted_iota(jnp.int32, (8, LANES), 1)
    after = jnp.where(sub < 7, pltpu.roll(values, 7, 0), 0.0)
    before = jnp.where(sub > 0, pltpu.roll(values, 1, 0), 0.0)
    first = lax.broadcasted_iota(jnp.int32, (8, 1), 0) == 0
    last = lax.broadcasted_iota(jnp.int32, (8, 1), 0) == 7

    def column(array, index):
        return array[:, index : index + 1]

    def slopes(array, pair):
        whole, low, high = (column(array, 11 + 3 * pair + k) for k in range(3))
        return whole - low - high, low, high

    merged = [column(values, 0), column(values, 1)]
    for b in range(3):
        merged.append(column(values, 5 + b) + column(after, 2 + b) + column(before, 8 + b))
    merged += [own + other for own, other in zip(slopes(values, 0), slopes(before, 2), strict=True)]
    merged += list(slopes(values, 1))
    inside, interface = [], []
    for side in range(2):
        whole, low, high = (column(values, 20 + 3 * side + k) for k in range(3))
        ends = jnp.where(first, low, 0.0) + jnp.where(last, high, 0.0)
        inside.append(whole - low - high + ends)
        interface.append(jnp.where(first, 0.0, low) + column(before, 22 + 3 * side))
    rows = jnp.zeros((8, LANES), F32)
    for index, value in enumerate(merged + inside + interface):
        rows = jnp.where(lane == index, value, rows)
    total = rows[0:1]
    for i in range(1, 8):
        total = total + pltpu.roll(rows[i : i + 1], 16 * i, 1)
    out_ref[...] = jnp.broadcast_to(total, out_ref.shape)


def invert(blocks, sub):
    for k in range(0, 8, 2):
        first, second = blocks[k], blocks[k + 1]
        a, b = first[k : k + 1], first[k + 1 : k + 2]
        c, d = second[k : k + 1], second[k + 1 : k + 2]
        scale = 1.0 / (a * d - b * c)
        first = jnp.where(sub == k, 1.0, jnp.where(sub == k + 1, 0.0, first))
        second = jnp.where(sub == k + 1, 1.0, jnp.where(sub == k, 0.0, second))
        low = (d * scale) * first - (b * scale) * second
        high = (a * scale) * second - (c * scale) * first
        pivots = (sub == k) | (sub == k + 1)
        rows = []
        for r in range(8):
            if r == k:
                rows.append(low)
            elif r == k + 1:
                rows.append(high)
            else:
                rest = jnp.where(pivots, 0.0, blocks[r])
                rows.append(rest - blocks[r][k : k + 1] * low - blocks[r][k + 1 : k + 2] * high)
        blocks = rows
    return blocks


def multiply(left, right):
    rows = []
    for r in range(8):
        total = left[r][0:1] * right[0]
        for k in range(1, 8):
            total = total + left[r][k : k + 1] * right[k]
        rows.append(total)
    return rows


def multiply_turned(left, right):
    rows = []
    for r in range(8):
        total = left[0][r : r + 1] * right[0]
        for k in range(1, 8):
            total = total + left[k][r : r + 1] * right[k]
        rows.append(total)
    return rows


def apply_turned(blocks, column):
    total = blocks[0] * column[0:1]
    for k in range(1, 8):
        total = total + blocks[k] * column[k : k + 1]
    return total


def coarse_operator(c, count, sums_z, couplings_z, inside_y, interface_y):
    sub = lax.broadcasted_iota(jnp.int32, c.shape, 0)
    lane = lax.broadcasted_iota(jnp.int32, c.shape, 1)
    has_low = lane > 0
    has_high = lane < count - 1

    def after(array):
        return jnp.where(sub < 7, pltpu.roll(array, 7, 0), 0.0)

    def before(array):
        return jnp.where(sub > 0, pltpu.roll(array, 1, 0), 0.0)

    def right(array):
        return jnp.where(has_high, pltpu.roll(array, LANES - 1, 1), 0.0)

    def left(array):
        return jnp.where(has_low, pltpu.roll(array, 1, 1), 0.0)

    on_low = jnp.where(has_low, 0.5 * (c + left(c)), c)
    on_high = jnp.where(has_high, 0.5 * (c + right(c)), c)
    tested = []
    for place, value in enumerate((c, on_low, on_high)):
        slope = jnp.where(sub > 0, 0.5 * (value - before(value)), 0.0)
        coupling = couplings_z[place]
        force = sums_z[place] * slope - coupling * after(slope) - before(coupling * slope)
        force = jnp.where(sub > 0, force, 0.0)
        tested.append(0.5 * (force - after(force)))
    result = tested[0] + jnp.where(has_low, 0.5, 1.0) * tested[1] + jnp.where(has_high, 0.5, 1.0) * tested[2]
    result = result + 0.5 * right(tested[1]) + 0.5 * left(tested[2])

    interface = jnp.where(sub > 0, 0.5 * (c + before(c)), 0.0)
    for side, (move, there) in enumerate(((left, has_low), (right, has_high))):
        force = inside_y[side] * jnp.where(there, 0.5 * (move(c) - c), 0.0)
        face = interface_y[side] * jnp.where(there, 0.5 * (move(interface) - interface), 0.0)
        force = force + 0.5 * (face + after(face))
        back = right if side == 0 else left
        result = result + 0.5 * (back(force) - force)

    end = float(WEIGHT[0])
    mass = (2.0 - 2.0 * end) * c + end * (interface + after(interface))
    mass = mass + jnp.where((sub == 0) | (sub == 7), end * c, 0.0)
    beside = jnp.where(has_low, 0.5 * (mass + left(mass)), 0.0)
    scaled = (2.0 * EY - 2.0 * end) * mass + end * (beside + right(beside))
    scaled = scaled + jnp.where(has_low, 0.0, end * mass) + jnp.where(has_high, 0.0, end * mass)
    return result + HELM_COEF / 8.0 * float(np.sum(WX)) * scaled


def coarse_kernel(count, near, gathered, out_ref, wide, turned):
    lanes = LANES
    sub = lax.broadcasted_iota(jnp.int32, (8, lanes), 0)
    lane = lax.broadcasted_iota(jnp.int32, (8, lanes), 1)
    wide[...] = jnp.zeros((LANES, LANES), F32)
    wide[0:count] = gathered[...]
    turned[...] = wide[...].T

    def value(index):
        return turned[pl.ds(index, 8, stride=16), :]

    def move(array, dz, dy):
        if dz:
            array = pltpu.roll(array, (-dz) % 8, 0)
        if dy:
            array = pltpu.roll(array, (-dy) % lanes, 1)
        return array

    kbar = jnp.where(lane < count, value(0), 1.0)
    above = move(kbar, 1, 0)
    link_z = jnp.where(sub < 7, 2.0 * kbar * above / (kbar + above) * (EY * EX / EZ), 0.0)
    link_z = jnp.where(lane < count, link_z, 0.0)
    beside = move(kbar, 0, 1)
    link_y = 2.0 * kbar * beside / (kbar + beside) * (EZ * EX / EY)
    link_y = jnp.where(lane < count - 1, link_y, 0.0)
    back_z = move(link_z, -1, 0)
    back_y = move(link_y, 0, -1)
    diagonal = HELM_COEF * EZ * EY * EX + link_z + back_z + link_y + back_y
    blocks = []
    for r in range(8):
        row = jnp.where(sub == r, diagonal, 0.0)
        row = jnp.where(sub == r + 1, -back_z, row)
        row = jnp.where(sub == r - 1, -link_z, row)
        blocks.append(row)

    levels = []
    step = 1
    while step < count:
        inverse = invert(blocks, sub)
        if step == 1:
            up, low = -link_y, -back_y
            solved_up = [row * up for row in inverse]
            solved_low = [row * low for row in inverse]
            pull_up = [up[r : r + 1] * solved_up[r] for r in range(8)]
            pull_low = [low[r : r + 1] * solved_low[r] for r in range(8)]
            new_low = [up[r : r + 1] * solved_low[r] for r in range(8)]
            new_up = [low[r : r + 1] * solved_up[r] for r in range(8)]
        else:
            solved_up, solved_low = multiply(inverse, upper), multiply(inverse, lower)
            pull_up = multiply_turned(solved_up, upper)
            pull_low = multiply_turned(solved_low, lower)
            if 2 * step < count:
                new_low = multiply_turned(solved_up, lower)
                new_up = multiply_turned(solved_low, upper)
        levels.append((step, solved_up, solved_low))
        blocks = [
            blocks[r] - move(pull_up[r], 0, -step) - move(pull_low[r], 0, step) for r in range(8)
        ]
        if 2 * step < count:
            lower = [-move(row, 0, -step) for row in new_low]
            upper = [-move(row, 0, step) for row in new_up]
        step *= 2
    inverse = invert(blocks, sub)

    def solve(column):
        for distance, solved_up, solved_low in levels:
            before = move(apply_turned(solved_up, column), 0, -distance)
            after = move(apply_turned(solved_low, column), 0, distance)
            column = column - before - after
        return apply_turned(inverse, column)

    first = solve(value(1))
    totals = coarse_operator(
        first,
        count,
        [value(5 + k) for k in range(3)],
        [value(8 + k) for k in range(3)],
        [value(11), value(12)],
        [value(13), value(14)],
    )
    totals = totals + value(3)
    totals = totals + jnp.where(lane < count - 1, move(value(2), 0, 1), 0.0)
    totals = totals + jnp.where(lane > 0, move(value(4), 0, -1), 0.0)
    totals = jnp.where(lane < count, totals, 0.0)
    second = solve(totals)
    gx = near[4].astype(jnp.int32)
    gy = near[5].astype(jnp.int32)
    for at, solved in ((0, first), (8, second)):
        turned_z = pltpu.roll(solved, (10 - gx) % 8, 0)
        out_ref[at : at + 8] = pltpu.roll(turned_z, (lanes + 1 - gy) % lanes, 1)


def coarse_columns(near, coarse, start, count):
    row, has_low, has_high = ring_rows(near)
    below = jnp.where(row < RING - 1, 1.0, jnp.where(row <= RING, 0.5, 0.0)) * has_low
    above = jnp.where(row > RING + ROWS, 1.0, jnp.where(row >= RING + ROWS - 1, 0.5, 0.0)) * has_high
    edge = jnp.where((row > RING) & (row < RING + ROWS - 1), 1.0, 0.0)
    edge = jnp.where(row == RING, near[2], jnp.where(row == RING + ROWS - 1, near[3], edge))
    edge = jnp.where(row == RING - 1, 0.5 * has_low, edge)
    edge = jnp.where(row == RING + ROWS, 0.5 * has_high, edge)
    columns = []
    for a in range(start, start + count):
        low, own, high = (coarse[a : a + 1, b : b + 1] for b in range(3))
        columns.append(below * low + edge * own + above * high)
    return columns


def coarse_planes(columns, low, high):
    before, inside, after = columns
    return inside, low * (before - inside), high * (after - inside)


def add_coarse(local, columns):
    inside, first, last = columns
    planes = [local[i] + inside for i in range(8)]
    planes[0] = planes[0] + first
    planes[7] = planes[7] + last
    return stack(planes)


def coarse_applied(columns, flux, packed):
    inside, first, last = columns
    slopes = [
        flux[i] * (float(DERIV[i, 0]) * first + float(DERIV[i, 7]) * last) for i in range(8)
    ]
    fz = along_z(slopes, DERIV.T)
    three = stack([inside + first, inside, inside + last])
    gy = along_y(three, packed, 0)
    fy = along_y(
        stack([flux[i] * gy[0 if i == 0 else 2 if i == 7 else 1] for i in range(8)]), packed, 1
    )
    plane_w = packed[0:WIDE]
    planes = []
    for i in range(8):
        plane = three[0 if i == 0 else 2 if i == 7 else 1]
        planes.append(fz[i] + fy[i] + (HELM_COEF * 0.125 * float(WEIGHT[i])) * (plane_w * plane))
    return stack(planes)


def face_applied(planes, payload, packed, rows, in_grid):
    inside, first, last = planes
    fields = [inside + (first if i == 0 else last if i == 7 else 0.0) for i in rows]
    gy = along_y(stack(fields), packed, 0)
    fy = along_y(stack([payload[6 + k] * gy[k] for k in range(2)]), packed, 1)
    plane_w = packed[0:WIDE]
    result = []
    for k, i in enumerate(rows):
        slopes = payload[2 + k] * first + payload[4 + k] * last
        mass = (HELM_COEF * 0.125 * float(WEIGHT[i])) * in_grid * (plane_w * fields[k])
        result.append(payload[k] + slopes + fy[k] + mass)
    return result


def apply_kernel(
    near, packed, tables, coarse, flux, zl, yl, ylo, yhi,
    z_ref, y_ref, w_ref, wlo, whi,
):
    columns = coarse_columns(near, coarse, 0, 5)
    own = coarse_planes(columns[1:4], 1.0 - near[0], 1.0 - near[1])
    field = add_coarse(zl[...], own)[:, RING : RING + ROWS]
    z_ref[...] = field
    applied = yl[...] + coarse_applied(own, flux[...], packed)
    y_ref[...] = applied[:, RING : RING + ROWS]
    lower = coarse_planes(columns[0:3], 1.0 - near[7], 0.5)
    upper = coarse_planes(columns[2:5], 0.5, 1.0 - near[6])
    planes = [applied[i] for i in range(8)]
    planes += face_applied(lower, ylo, packed, (6, 7), 2.0 - 2.0 * near[0])
    planes += face_applied(upper, yhi, packed, (0, 1), 2.0 - 2.0 * near[1])
    planes = solve_elements(planes, packed, tables, 1)
    row = lax.broadcasted_iota(jnp.int32, (ROWS, LANES), 0)
    _, has_low, has_high = ring_rows(near)
    in_grid = jnp.where(row == 0, has_low, jnp.where(row == ROWS - 1, has_high, 1.0))
    for i in range(8):
        first = (1.0 - has_low) * planes[i][ROWS : ROWS + 1]
        last = (1.0 - has_high) * planes[i][ROWS + 1 : ROWS + 2]
        alone = jnp.where(row == 0, first, jnp.where(row == ROWS - 1, last, 0.0))
        planes[i] = planes[i][0:ROWS] * in_grid + alone
    store_faces(planes, near, w_ref, wlo, whi)


def solve_apply_kernel(
    count, near, gathered, packed, tables, flux, zl, yl, ylo, yhi,
    coarse, z_ref, y_ref, w_ref, wlo, whi, wide, turned,
):
    coarse_kernel(count, near, gathered, coarse, wide, turned)
    apply_kernel(
        near, packed, tables, coarse, flux, zl, yl, ylo, yhi, z_ref, y_ref, w_ref, wlo, whi
    )


def second_kernel(near, packed, coarse, flux, b, y, z, w, x_ref, kx_ref, stat):
    columns = [column[RING : RING + ROWS] for column in coarse_columns(near, coarse, 9, 3)]
    field = add_coarse(w[...], coarse_planes(columns, 1.0 - near[0], 1.0 - near[1]))
    x_ref[...] = field
    fluxes = flux[:, RING : RING + ROWS]
    gz = along_z([field[i] for i in range(8)], DERIV)
    gy = along_y(field, packed, 0)
    gx = along_x(field, packed, 0)
    slopes = [fluxes[i] * gz[i] for i in range(8)]
    ends = (0, 7)
    back = along_z(slopes, DERIV.T[[0, 7]])
    back_y = along_y(stack([fluxes[i] * gy[i] for i in ends]), packed, 1)
    back_x = along_x(stack([fluxes[i] * gx[i] for i in ends]), packed, 1)
    plane_w = packed[0:ROWS]
    mass = HELM_COEF * 0.125
    for k, i in enumerate(ends):
        weighted = (mass * float(WEIGHT[i])) * (plane_w * field[i])
        kx_ref[k] = back[k] + back_y[k] + back_x[k] + weighted
    energy = None
    for i in range(8):
        term = slopes[i] * gz[i] + fluxes[i] * (gy[i] * gy[i] + gx[i] * gx[i])
        term = term + (mass * float(WEIGHT[i])) * (plane_w * field[i] * field[i])
        energy = term if energy is None else energy + term
    first, right = z[...], b[...]
    sums = [right * first, y[...] * first, right * field, y[...] * field]
    stat[...] = lane_row([jnp.sum(term) for term in sums] + [jnp.sum(energy)])


def face_kernel(packed, flux, b, y, kx, zlo, zhi, stat_in, stat):
    faces = stack([zlo[...], zhi[...]])
    fluxes = flux[:, RING : RING + ROWS]
    gy = along_y(faces, packed, 0)
    gx = along_x(faces, packed, 0)
    plane_w = packed[0:ROWS]
    energy = 2.0 * (kx[0] * faces[0] + kx[1] * faces[1])
    for k, i in enumerate((0, 7)):
        mass = (HELM_COEF * 0.125 * float(WEIGHT[i])) * (plane_w * faces[k] * faces[k])
        energy = energy + mass + fluxes[i] * (gy[k] * gy[k] + gx[k] * gx[k])
    for i in range(8):
        slope = float(DERIV[i, 0]) * faces[0] + float(DERIV[i, 7]) * faces[1]
        energy = energy + fluxes[i] * slope * slope
    sums = [
        0.0,
        0.0,
        jnp.sum(b[0] * faces[0] + b[7] * faces[1]),
        jnp.sum(y[0] * faces[0] + y[7] * faces[1]),
        jnp.sum(energy),
    ]
    stat[...] = jnp.broadcast_to(stat_in[...] + lane_row(sums), stat.shape)


def combine_kernel(sums, z, x, zlo, zhi, p_ref):
    total = jnp.sum(sums[...], axis=0, keepdims=True)
    rz, pap, rq, aq, qhq = (total[:, k : k + 1] for k in range(5))
    step = rz / pap
    rz_next = step * (step * aq - rq)
    beta = rz_next / rz
    grown = 1.0 + beta
    curved = grown * grown * pap - 2.0 * step * grown * aq + step * step * qhq
    step_next = rz_next / curved
    on_z = step + step_next * grown
    on_q = step_next * step
    for i in range(8):
        plane = x[i]
        if i == 0:
            plane = plane + zlo[...]
        if i == 7:
            plane = plane + zhi[...]
        p_ref[i] = on_z * z[i] - on_q * plane


def run(kernel, outs, smem, args, scratch=(), flops=1000000, place=VMEM, limit=LIMIT):
    nbytes = sum(4 * int(np.prod(out)) for out in outs) * 2
    return pl.pallas_call(
        kernel,
        out_shape=[jax.ShapeDtypeStruct(out, F32) for out in outs],
        in_specs=[pl.BlockSpec(memory_space=SMEM) for _ in smem]
        + [pl.BlockSpec(memory_space=place) for _ in args],
        out_specs=[pl.BlockSpec(memory_space=VMEM) for _ in outs],
        scratch_shapes=list(scratch),
        compiler_params=pltpu.CompilerParams(vmem_limit_bytes=limit),
        cost_estimate=pl.CostEstimate(flops=flops, bytes_accessed=nbytes, transcendentals=0),
    )(*smem, *args)


def shift(axis, low_face, high_face):
    count = lax.axis_size(axis)
    forward = [(i, i + 1) for i in range(count - 1)]
    backward = [(target, source) for source, target in forward]
    return lax.ppermute(high_face, axis, forward), lax.ppermute(low_face, axis, backward)


def body(level_set, velocity, source, wick_solid):
    block = level_set.shape
    count_gx = lax.axis_size("gx")
    count_gy = lax.axis_size("gy")
    index_gx = lax.axis_index("gx")
    index_gy = lax.axis_index("gy")

    def ends(index, count):
        return [jnp.where(index > 0, 0.5, 1.0), jnp.where(index < count - 1, 0.5, 1.0)]

    place = [index_gx.astype(F32), index_gy.astype(F32)]
    beyond = [
        jnp.where(index_gx < count_gx - 2, 0.5, 1.0),
        jnp.where(index_gx > 1, 0.5, 1.0),
    ]
    near = jnp.stack(ends(index_gx, count_gx) + ends(index_gy, count_gy) + place + beyond)
    near = near.astype(F32)
    packed = jnp.asarray(PACKED)
    tables = jnp.asarray(TABLES)
    face = (ROWS, LANES)
    wide_block = (8, WIDE, LANES)
    wide_face = (WIDE, LANES)
    rim = (12, TILE, LANES)

    b, l, zlo, zhi, solid = run(
        advect_kernel,
        [block, block, (3, *face), (3, *face), (8, LANES)],
        [],
        [
            pltpu.with_memory_space_constraint(array, pltpu.HBM)
            for array in (level_set, velocity, source, packed, wick_solid.reshape(EY, EX))
        ],
        [VMEM(block, F32), VMEM((3, *block), F32), VMEM(block, F32), VMEM(PACKED.shape, F32)]
        + [VMEM((EY, EX), jnp.int32), pltpu.SemaphoreType.DMA((5,))],
        place=pltpu.HBM,
    )
    zlo, zhi = shift("gx", zlo, zhi)
    ylo, yhi = run(rim_kernel, [rim, rim], [], [solid, b, l, zlo, zhi])
    ylo, yhi = shift("gy", ylo, yhi)
    (inner,) = run(
        inner_schwarz_kernel, [block], [], [packed, tables, b, zlo, zhi], flops=20000000
    )
    w, wlo, whi = run(
        first_schwarz_kernel,
        [wide_block, wide_face, wide_face],
        [near],
        [packed, tables, inner, b, zlo, zhi, ylo, yhi],
    )
    wlo, whi = shift("gx", wlo, whi)
    level_new, flux, stat = run(
        level_kernel,
        [block, wide_block, (1, LANES)],
        [near],
        [solid, packed, b, l, zlo, zhi, ylo, yhi],
        flops=20000000,
    )
    zl, yl, zlo, zhi, stat = run(
        galerkin_kernel,
        [wide_block, wide_block, wide_block, wide_block, (count_gx, LANES)],
        [near],
        [packed, stat, flux, w, wlo, whi],
    )
    zlo, zhi = shift("gx", zlo, zhi)
    gathered = lax.all_to_all(stat, "gx", 0, 0, tiled=True)
    (column,) = run(column_kernel, [(count_gy, LANES)], [], [gathered])
    gathered = lax.all_to_all(column, "gy", 0, 0, tiled=True)
    coarse, z, y, w, wlo, whi = run(
        functools.partial(solve_apply_kernel, count_gy),
        [(16, LANES), block, block, block, face, face],
        [near],
        [gathered, packed, tables, flux, zl, yl, zlo, zhi],
        [VMEM((LANES, LANES), F32), VMEM((LANES, LANES), F32)],
    )
    zlo, zhi = shift("gx", wlo, whi)
    x, kx, sums = run(
        second_kernel,
        [block, (2, *face), (1, LANES)],
        [near],
        [packed, coarse, flux, b, y, z, w],
        flops=20000000,
    )
    (sums,) = run(
        face_kernel, [(2 * count_gx, LANES)], [], [packed, flux, b, y, kx, zlo, zhi, sums]
    )
    pairs = count_gy // 2
    columns = [
        [z * count_gy + 2 * m + c for z in range(count_gx) for c in range(2)] for m in range(pairs)
    ]
    layers = [
        [z * count_gy + 2 * m + c for m in range(pairs)] for z in range(count_gx) for c in range(2)
    ]
    axes = ("gx", "gy")
    tile = lax.all_to_all(sums, axes, 0, 0, axis_index_groups=columns, tiled=True)
    wide = jnp.broadcast_to(jnp.sum(tile, axis=0, keepdims=True), (pairs, LANES))
    wide = lax.all_to_all(wide, axes, 0, 0, axis_index_groups=layers, tiled=True)
    (pressure,) = run(combine_kernel, [block], [], [wide, z, x, zlo, zhi])
    return (level_new, pressure)


def solution(mesh):
    placed = (
        P("gx", "gy", None),
        P(None, "gx", "gy", None),
        P("gx", "gy", None),
        P("gx", "gy", None),
    )
    return jax.shard_map(
        body,
        mesh=mesh,
        in_specs=placed,
        out_specs=(P("gx", "gy", None), P("gx", "gy", None)),
        check_vma=False,
    )
```

```python
import functools

import jax
import jax.numpy as jnp
import numpy as np
from jax import lax
from jax.experimental import pallas as pl
from jax.experimental.pallas import tpu as pltpu
from jax.sharding import PartitionSpec as P

EZ = 1
EY = 4
EX = 16
ROWS = 8 * EY
LANES = 8 * EX

TIME_STEP = 0.02
HELM_COEF = 0.25
LEVEL_WIDTH = 0.25
GAS_RATIO = 10.0
SOLID_FACTOR = 0.25
SCHWARZ_SCALE = 0.5
SCHWARZ_SHIFT = 0.05

F32 = jnp.float32
BF16 = jnp.bfloat16
VMEM = pltpu.VMEM
SMEM = pltpu.SMEM
LIMIT = 24 * 1024 * 1024


def gll_tables():
    gll_nodes = np.array(
        [
            -1.0,
            -0.8717401485096066,
            -0.5917001814331423,
            -0.2092992179024789,
            0.2092992179024789,
            0.5917001814331423,
            0.8717401485096066,
            1.0,
        ]
    )
    weight_np = np.array(
        [
            1.0 / 28.0,
            0.21070422714350603,
            0.3411226924835044,
            0.4124587946587038,
            0.4124587946587038,
            0.3411226924835044,
            0.21070422714350603,
            1.0 / 28.0,
        ]
    )
    bary_weights = np.array(
        [1.0 / np.prod([gll_nodes[i] - gll_nodes[j] for j in range(8) if j != i]) for i in range(8)]
    )
    derivative = np.zeros((8, 8))
    for i in range(8):
        for j in range(8):
            if i != j:
                derivative[i, j] = bary_weights[j] / bary_weights[i] / (gll_nodes[i] - gll_nodes[j])
        derivative[i, i] = -np.sum(derivative[i])
    return (weight_np, derivative)


def sine_tables():
    indices = np.arange(10) + 1.0
    sine_basis = np.sqrt(2.0 / 11.0) * np.sin(np.pi * np.outer(indices, indices) / 11.0)
    eigen_vals = 2.0 - 2.0 * np.cos(np.pi * indices / 11.0)
    return (sine_basis, eigen_vals)


WEIGHT, DERIV = gll_tables()
SINE, EIGEN = sine_tables()


def split_const(matrix):
    single = matrix.astype(np.float32)
    high = single.astype(jnp.bfloat16)
    low = (single - high.astype(np.float32)).astype(jnp.bfloat16)
    return high, low


def line_maps(count):
    length = 8 * count
    total = length + 4

    def column(position):
        if 0 <= position < length:
            return position
        return {-2: length, -1: length + 1, length: length + 2, length + 1: length + 3}[position]

    assembled = {}
    for position in range(-2, length + 2):
        row = np.zeros(total)
        row[column(position)] = 1.0
        if 0 <= position < length:
            if position % 8 == 0:
                row[column(position - 1)] += 1.0
            if position % 8 == 7:
                row[column(position + 1)] += 1.0
        assembled[position] = row
    forward = np.zeros((10 * count, total))
    for element in range(count):
        places = [8 * element - 2] + list(range(8 * element, 8 * element + 8)) + [8 * element + 9]
        forward[10 * element : 10 * element + 10] = SINE @ np.stack([assembled[p] for p in places])
    backward = np.zeros((length, 10 * count))
    for element in range(count):
        backward[8 * element : 8 * element + 8, 10 * element : 10 * element + 10] = SINE[1:9]
    for element in range(count - 1):
        first, second = 8 * element + 7, 8 * element + 8
        mean = 0.5 * (backward[first] + backward[second])
        backward[first] = mean
        backward[second] = mean
    return forward, backward


RING = 16
WIDE = ROWS + 2 * RING
REACH = 26
TILE = 48
TILE_B = 32


def ring_maps(reach, depth, inside):
    count = EY + 2 * depth
    forward, _ = line_maps(count)
    length = 8 * count
    columns = np.zeros((10 * count, len(inside)))
    for at, position in enumerate(inside):
        place = None if position is None else position + 8 * depth
        if place is None or place < -2 or place > length + 1:
            continue
        source = place if 0 <= place < length else {-2: 0, -1: 1}.get(place, place - length + 2) + length
        columns[:, at] = forward[:, source]
    _, backward = line_maps(count)
    own = 8 * depth
    rows = np.concatenate(
        [
            backward[own - reach : own + ROWS + reach],
            np.zeros((8, 10 * count)),
        ]
    )
    rows[ROWS + 2 * reach, 10 * depth : 10 * depth + 10] = SINE[1]
    rows[ROWS + 2 * reach + 1, 10 * (depth + EY - 1) : 10 * (depth + EY)] = SINE[8]
    return columns, rows


FZ, BZ = line_maps(1)
TILES = list(range(-REACH, 0)) + [None] * (TILE_B - REACH) + list(range(ROWS))
TILES += list(range(ROWS, ROWS + REACH)) + [None] * (TILE_B - REACH)
FY_A, BY_A = ring_maps(RING, 3, TILES)
FY_B, BY_B = ring_maps(0, 1, list(range(-RING, ROWS + RING)))
INNER = np.arange(40, 60)
OUTER = np.concatenate([np.arange(0, 40), np.arange(60, 100)])
FY_I, BY_I = FY_A[INNER, TILE_B : TILE_B + ROWS], BY_A[RING : RING + ROWS, INNER]
FY_A, BY_A = FY_A[OUTER], BY_A[:, OUTER]
STEP_A = 80
STEP_B = 64
STEP_I = 32


def padded(forward, backward, step):
    forward = np.pad(forward, ((0, step - forward.shape[0]), (0, 0)))
    return forward, np.pad(backward, ((0, 0), (0, step - backward.shape[1])))


FY_A, BY_A = padded(FY_A, BY_A, STEP_A)
FY_B, BY_B = padded(FY_B, BY_B, STEP_B)
FY_I, BY_I = padded(FY_I, BY_I, STEP_I)
FX, BX = line_maps(EX)
FX = FX[:, :LANES]


FX_H, FX_L = split_const(FX.T.copy())
BX_H, BX_L = split_const(BX.T.copy())


def wide_const(table):
    high, low = split_const(table)
    return np.concatenate([high, high, low], axis=1)


def pack_tables(tables):
    places, pieces, at = [], [], 0
    for table in tables:
        rows = -(-table.shape[0] // 16) * 16
        extra = ((0, rows - table.shape[0]), (0, 384 - table.shape[1]))
        pieces.append(np.pad(table.astype(np.float32), extra))
        places.append((at, rows, table.shape[1]))
        at += rows
    return np.concatenate(pieces).astype(jnp.bfloat16), places


TABLES, PLACES = pack_tables(
    [
        np.concatenate([FX_H, FX_H], axis=0),
        FX_L,
        BX_H,
        BX_L,
        wide_const(FY_A),
        wide_const(BY_A),
        wide_const(FY_B),
        wide_const(BY_B),
        wide_const(FY_I),
        wide_const(BY_I),
    ]
)


def roll_table():
    table = np.zeros((2, 8, 8, LANES))
    for kind, matrix in enumerate((DERIV, DERIV.T)):
        for k in range(8):
            for i in range(8):
                table[kind, k, i, :] = matrix[i, (i + k) % 8]
    return table.reshape(2 * 64, LANES)


WY = np.tile(WEIGHT, WIDE // 8)
WX = np.tile(WEIGHT, EX)


def inner_count(count):
    mult = np.ones(8 * count)
    position = np.arange(8 * count)
    mult[(position % 8 == 0) & (position > 0)] += 1.0
    mult[(position % 8 == 7) & (position < 8 * count - 1)] += 1.0
    return mult


END_MASS = np.where(np.arange(WIDE) % 8 % 7 == 0, 2.0, 1.0)
INV_MASS = (8.0 / (WY * END_MASS)[:, None] / (WX * inner_count(EX))[None, :]).astype(np.float32)

AT_ROLLS = WIDE
AT_DX = AT_ROLLS + 128
AT_DXT = AT_DX + LANES
AT_SQUARE = AT_DXT + LANES
AT_MASS = AT_SQUARE + 16
AT_SPREAD = AT_MASS + WIDE
AT_EIGEN_Y = AT_SPREAD + EX
AT_EIGEN_X = AT_EIGEN_Y + STEP_A
LAM_Y = np.resize(EIGEN, STEP_A)
LAM_X = np.resize(EIGEN, 8 * LANES).reshape(8, LANES)
PACKED = np.concatenate(
    [
        WY[:, None] * WX[None, :],
        roll_table(),
        np.kron(np.eye(EX), DERIV.T),
        np.kron(np.eye(EX), DERIV),
        np.repeat(DERIV[:, :1] ** 2, LANES, axis=1),
        np.repeat(DERIV[:, 7:] ** 2, LANES, axis=1),
        INV_MASS,
        np.kron(np.eye(EX), np.ones((1, 8))),
        np.repeat(LAM_Y[:, None], LANES, axis=1),
        LAM_X,
    ]
).astype(np.float32)


def parts(values):
    high = values.astype(BF16)
    low = (values - high.astype(F32)).astype(BF16)
    return high, low


def dot(left, right):
    return jnp.dot(left, right, preferred_element_type=F32)


def left_pairs(table, planes):
    results = []
    for i in range(0, len(planes), 2):
        high, low = parts(jnp.concatenate([planes[i], planes[i + 1]], axis=1))
        both = dot(table, jnp.concatenate([high, low, high], axis=0))
        results += [both[:, 0:LANES], both[:, LANES : 2 * LANES]]
    return results


def along_z(values, matrix):
    rows = []
    for i in range(matrix.shape[0]):
        total = None
        for j in range(matrix.shape[1]):
            if matrix[i, j] == 0.0:
                continue
            term = float(matrix[i, j]) * values[j]
            total = term if total is None else total + term
        rows.append(total)
    return rows


def along_y(values, packed, kind):
    count, rows = values.shape[:2]
    grouped = values.reshape(count * rows // 8, 8, LANES)
    start = AT_ROLLS + 64 * kind
    total = packed[start : start + 8][None] * grouped
    for k in range(1, 8):
        total = total + packed[start + 8 * k : start + 8 * k + 8][None] * pltpu.roll(grouped, 8 - k, 1)
    return total.reshape(count, rows, LANES)


def along_x(values, packed, kind):
    start = AT_DXT if kind else AT_DX
    high, low = parts(packed[start : start + LANES])
    first, rest = parts(values.reshape(values.shape[0] * values.shape[1], LANES))
    total = dot(
        jnp.concatenate([first, rest], axis=1), jnp.concatenate([high, high], axis=0)
    ) + dot(first, low)
    return total.reshape(values.shape)


def stack(planes):
    return jnp.concatenate([plane[None] for plane in planes], axis=0)


def edge_rows(rows, low, high):
    position = lax.broadcasted_iota(jnp.int32, (rows, LANES), 0)
    return jnp.where(position == 0, low, jnp.where(position == rows - 1, high, 1.0))


def local_operator(values, flux, packed):
    plane_w = packed[0 : values.shape[1]]
    gz = along_z([values[i] for i in range(8)], DERIV)
    fz = along_z([flux[i] * gz[i] for i in range(8)], DERIV.T)
    total = along_y(flux * along_y(values, packed, 0), packed, 1)
    total = total + along_x(flux * along_x(values, packed, 0), packed, 1)
    planes = [
        total[i] + fz[i] + (HELM_COEF * 0.125 * float(WEIGHT[i])) * (plane_w * values[i])
        for i in range(8)
    ]
    return stack(planes)


def add_planes(own, low_z, high_z):
    planes = [own[i] for i in range(8)]
    planes[0] = planes[0] + low_z
    planes[7] = planes[7] + high_z
    return stack(planes)


def inverse_denominators(packed, step):
    column = packed[AT_EIGEN_Y : AT_EIGEN_Y + step]
    rest = 10 * EX - LANES
    lam = jnp.concatenate(
        [
            column + packed[AT_EIGEN_X : AT_EIGEN_X + 1],
            column[:, 0:rest] + packed[AT_EIGEN_X + 1 : AT_EIGEN_X + 2, 0:rest],
        ],
        axis=1,
    )
    shifts = [float(SCHWARZ_SCALE * value + SCHWARZ_SHIFT) for value in EIGEN]
    return [1.0 / (SCHWARZ_SCALE * lam + shift) for shift in shifts]


def solve_elements(planes, packed, tables, kind, inverse=None):
    def table(index):
        at, rows, width = PLACES[index]
        return tables[at : at + rows, 0:width]

    fxhh, fxl, bxh, bxl = (table(index) for index in range(4))
    spectral = left_pairs(table(4 + 2 * kind), along_z(planes, FZ))
    high, low = parts(jnp.concatenate(spectral, axis=0))
    wide = dot(jnp.concatenate([high, low], axis=1), fxhh) + dot(high, fxl)
    step = PLACES[4 + 2 * kind][1]
    if inverse is None:
        scales = inverse_denominators(packed, step)
    else:
        scales = [inverse[STEP_A * i : STEP_A * i + step] for i in range(10)]
    scaled = [wide[step * i : step * (i + 1)] * scales[i] for i in range(10)]
    high, low = parts(jnp.concatenate(scaled, axis=0))
    back = dot(high, bxh) + dot(low, bxh) + dot(high, bxl)
    back = left_pairs(table(5 + 2 * kind), [back[step * i : step * (i + 1)] for i in range(10)])
    return along_z(back, BZ)


def store_faces(planes, near, out_ref, low_ref, high_ref):
    planes[0] = planes[0] * near[0]
    planes[7] = planes[7] * near[1]
    for i in range(8):
        out_ref[i] = planes[i]
    low_ref[...] = planes[0]
    high_ref[...] = planes[7]


def ring_rows(near):
    row = lax.broadcasted_iota(jnp.int32, (WIDE, LANES), 0)
    return row, 2.0 - 2.0 * near[2], 2.0 - 2.0 * near[3]


def partition_total(own, low_z, high_z, low_y, high_y, near):
    def planes(array):
        total = near[0] * array[0] + near[1] * array[7]
        for i in range(1, 7):
            total = total + array[i]
        return total

    total = planes(own) + 0.5 * (low_z[1] + high_z[0])
    below = planes(low_y) + 0.5 * (low_y[9] + low_y[10])
    above = planes(high_y) + 0.5 * (high_y[9] + high_y[10])
    faces = 0.5 * (below[REACH - 1 : REACH] + above[0:1])
    return jnp.sum(total * edge_rows(ROWS, near[2], near[3])) + jnp.sum(faces)


def lane_row(entries):
    lane = lax.broadcasted_iota(jnp.int32, (1, LANES), 1)
    row = jnp.zeros((1, LANES), F32)
    for index, value in enumerate(entries):
        row = jnp.where(lane == index, value, row)
    return row


def advect_kernel(
    lev_in, vel_in, src_in, packed_in, solid_in, b_ref, l_ref, zlo, zhi, solid_ref,
    lev, vel, src, packed, solid, sems,
):
    pairs = ((lev_in, lev), (packed_in, packed), (vel_in, vel), (src_in, src), (solid_in, solid))
    copies = [
        pltpu.make_async_copy(source, target, sems.at[index])
        for index, (source, target) in enumerate(pairs)
    ]
    for copy in copies:
        copy.start()
    copies[0].wait()
    level = lev[...]
    gz = stack(along_z([level[i] for i in range(8)], DERIV))
    copies[1].wait()
    gy = along_y(level, packed, 0)
    gx = along_x(level, packed, 0)
    for copy in copies[2:]:
        copy.wait()
    spread = packed[AT_SPREAD : AT_SPREAD + EX].astype(BF16)
    in_solid = dot(solid[...].astype(F32).astype(BF16), spread)
    solid_ref[...] = jnp.concatenate([in_solid, jnp.zeros((8 - EY, LANES), F32)], axis=0)
    v0, v1, v2 = vel[0], vel[1], vel[2]
    moved = level - (2.0 * TIME_STEP) * (v0 * gz + v1 * gy + v2 * gx)
    diverge = stack(along_z([v0[i] for i in range(8)], DERIV))
    diverge = diverge + along_y(v1, packed, 0) + along_x(v2, packed, 0)
    force = src[...] - (2.0 * TIME_STEP) * diverge
    weights = packed[0:ROWS]
    for i in range(8):
        mass = (0.125 * float(WEIGHT[i])) * weights
        term = mass * force[i]
        moved_i = mass * moved[i]
        b_ref[i] = term
        l_ref[i] = moved_i
        if i < 2:
            zlo[i] = term
        if i == 0:
            zlo[2] = moved_i
        if i > 5:
            zhi[i - 6] = term
        if i == 7:
            zhi[2] = moved_i


def rim_kernel(solid, b, l, low_z, high_z, low_y, high_y):
    in_solid = solid[...]
    rest = TILE - REACH - RING - 1

    def rows(planes, at, level, far, extra=None):
        start = ROWS - REACH if far else 0
        pieces = [planes[at, start : start + REACH]]
        if level is None:
            pieces.append(jnp.zeros((RING + 1, LANES), F32))
        else:
            array, index = level
            start = ROWS - RING - 1 if far else 0
            pieces.append(array[index, start : start + RING + 1])
        if extra is None:
            pieces.append(jnp.zeros((rest, LANES), F32))
        else:
            pieces += [extra, jnp.zeros((rest - 2, LANES), F32)]
        return jnp.concatenate(pieces, axis=0)

    for far, out in ((False, low_y), (True, high_y)):
        extra = in_solid[EY - 2 : EY] if far else in_solid[0:2]
        for i in range(8):
            out[i] = rows(b, i, (l, i), far, extra if i == 0 else None)
        for i in range(2):
            out[8 + i] = rows(low_z, i, (low_z, 2) if i == 1 else None, far)
            out[10 + i] = rows(high_z, i, (high_z, 2) if i == 0 else None, far)


def level_kernel(
    near, solid, packed, b, l, zlo, zhi, ylo, yhi, level_ref, flux_ref, stat
):
    row, has_low, has_high = ring_rows(near)
    at = REACH

    def wide_rows(slot, own):
        return jnp.concatenate(
            [ylo[slot, at + 1 : at + 1 + RING], own, yhi[slot, at : at + RING]], axis=0
        )

    planes = []
    for i in range(8):
        plane = wide_rows(i, l[i])
        first = ylo[i, at : at + 1]
        last = yhi[i, at + RING : at + RING + 1]
        if i == 0:
            plane = plane + wide_rows(9, zlo[2])
            first = first + ylo[9, at : at + 1]
            last = last + yhi[9, at + RING : at + RING + 1]
        if i == 7:
            plane = plane + wide_rows(10, zhi[2])
            first = first + ylo[10, at : at + 1]
            last = last + yhi[10, at + RING : at + RING + 1]
        before = jnp.where(row == 0, first, pltpu.roll(plane, 1, 0))
        after = jnp.where(row == WIDE - 1, last, pltpu.roll(plane, WIDE - 1, 0))
        plane = plane + jnp.where(row % 8 == 0, before, jnp.where(row % 8 == 7, after, 0.0))
        planes.append(plane)
    own = stack(planes)
    lane = lax.broadcasted_iota(jnp.int32, (8, WIDE, LANES), 2)
    before = jnp.where((lane % 8 == 0) & (lane > 0), pltpu.roll(own, 1, 2), 0.0)
    after = jnp.where((lane % 8 == 7) & (lane < LANES - 1), pltpu.roll(own, LANES - 1, 2), 0.0)
    own = own + before + after
    ends = jnp.where(row == RING, 2.0 * near[2], jnp.where(row == RING + ROWS - 1, 2.0 * near[3], 1.0))
    inverse = packed[AT_MASS : AT_MASS + WIDE] * ends
    in_solid = solid[...]
    solids = [ylo[0, at + RING + 1 + k : at + RING + 2 + k] for k in range(2)]
    solids += [in_solid[e : e + 1] for e in range(EY)]
    solids += [yhi[0, at + RING + 1 + k : at + RING + 2 + k] for k in range(2)]
    open_part = jnp.concatenate(
        [jnp.broadcast_to(1.0 - (1.0 - SOLID_FACTOR) * rows, (8, LANES)) for rows in solids], axis=0
    )
    in_grid = jnp.where(row < RING, has_low, jnp.where(row >= RING + ROWS, has_high, 1.0))
    flux_w = packed[0:WIDE] * in_grid
    total = jnp.zeros((ROWS, LANES), F32)
    fluxes = []
    for i in range(8):
        scale = 1.0 / float(WEIGHT[i])
        plane = own[i] * (inverse * scale)
        if i == 0:
            plane = plane * near[0]
        if i == 7:
            plane = plane * near[1]
        level_ref[i] = plane[RING : RING + ROWS]
        liquid = jax.nn.sigmoid(plane * (1.0 / LEVEL_WIDTH))
        coef = (GAS_RATIO - (GAS_RATIO - 1.0) * liquid) * open_part
        total = total + coef[RING : RING + ROWS]
        flux = (0.5 * float(WEIGHT[i])) * (coef * flux_w)
        flux_ref[i] = flux
        fluxes.append(flux[RING : RING + ROWS])
    kbar = jnp.sum(total) * (1.0 / (8 * ROWS * LANES))
    entries = [kbar, partition_total(b, zlo, zhi, ylo, yhi, near)] + [0.0] * 9
    for first, second in ((0, 0), (0, 7), (7, 7)):
        slopes = along_z(fluxes, (DERIV[:, first] * DERIV[:, second])[None, :])[0]
        column = jnp.sum(slopes, axis=1, keepdims=True)
        entries += [jnp.sum(column, axis=0, keepdims=True), column[0:1], column[ROWS - 1 : ROWS]]
    inner = fluxes[0] + fluxes[1]
    for i in range(2, 8):
        inner = inner + fluxes[i]
    for at_row, start in ((0, 0), (ROWS - 8, 8)):
        square = packed[AT_SQUARE + start : AT_SQUARE + start + 8]
        entries += [
            jnp.sum(square * plane[at_row : at_row + 8]) for plane in (inner, fluxes[0], fluxes[7])
        ]
    stat[...] = lane_row(entries)


def inner_schwarz_kernel(packed, tables, b, zlo, zhi, out_ref, inverse):
    planes = [b[i] for i in range(8)] + [zlo[0], zlo[1], zhi[0], zhi[1]]
    for i, scale in enumerate(inverse_denominators(packed, STEP_A)):
        inverse[STEP_A * i : STEP_A * (i + 1)] = scale
    planes = solve_elements(planes, packed, tables, 2)
    for i in range(8):
        out_ref[i] = planes[i]


def first_schwarz_kernel(
    near, inverse, packed, tables, inner, b, zlo, zhi, ylo, yhi, w_ref, wlo, whi
):
    own = [b[i] for i in range(8)] + [zlo[0], zlo[1], zhi[0], zhi[1]]
    planes = [
        jnp.concatenate([ylo[i, 0:TILE_B], own[i], yhi[i, 0:TILE_B]], axis=0) for i in range(12)
    ]
    planes = solve_elements(planes, packed, tables, 0, inverse)
    row, has_low, has_high = ring_rows(near)
    in_grid = jnp.where(row < RING, has_low, jnp.where(row >= RING + ROWS, has_high, 1.0))
    in_grid = jnp.where(row == RING, has_low, jnp.where(row == RING + ROWS - 1, has_high, in_grid))
    rest = jnp.zeros((RING, LANES), F32)
    for i in range(8):
        first = (1.0 - has_low) * planes[i][WIDE : WIDE + 1]
        last = (1.0 - has_high) * planes[i][WIDE + 1 : WIDE + 2]
        alone = jnp.where(row == RING, first, jnp.where(row == RING + ROWS - 1, last, 0.0))
        planes[i] = planes[i][0:WIDE] * in_grid + alone
        planes[i] = planes[i] + jnp.concatenate([rest, inner[i], rest], axis=0)
    store_faces(planes, near, w_ref, wlo, whi)


def galerkin_kernel(near, packed, stat_in, flux, w, zlo, zhi, zl_ref, y_ref, ylo, yhi, stat):
    local = add_planes(w, zlo[...], zhi[...])
    zl_ref[...] = local
    applied = local_operator(local, flux[...], packed)
    y_ref[...] = applied
    fluxes = [flux[i] for i in range(8)]
    for out, rows in ((ylo, (0, 1)), (yhi, (6, 7))):
        for k, i in enumerate(rows):
            out[k] = applied[i]
            for t, end in enumerate((0, 7)):
                out[2 + 2 * t + k] = along_z(fluxes, (DERIV[:, i] * DERIV[:, end])[None, :])[0]
            out[6 + k] = fluxes[i]
    applied = applied[:, RING : RING + ROWS]
    inner = near[0] * applied[0] + near[1] * applied[7]
    for i in range(1, 7):
        inner = inner + applied[i]
    edge = edge_rows(ROWS, near[2], near[3])
    entries = [0.0, 0.0]
    for plane in ((1.0 - near[0]) * applied[0], inner, (1.0 - near[1]) * applied[7]):
        entries += [
            (1.0 - near[2]) * jnp.sum(plane[0:1]),
            jnp.sum(edge * plane),
            (1.0 - near[3]) * jnp.sum(plane[ROWS - 1 : ROWS]),
        ]
    stat[...] = jnp.broadcast_to(stat_in[...] + lane_row(entries), stat.shape)


def column_kernel(gathered, out_ref):
    values = gathered[...]
    sub = lax.broadcasted_iota(jnp.int32, (8, LANES), 0)
    lane = lax.broadcasted_iota(jnp.int32, (8, LANES), 1)
    after = jnp.where(sub < 7, pltpu.roll(values, 7, 0), 0.0)
    before = jnp.where(sub > 0, pltpu.roll(values, 1, 0), 0.0)
    first = lax.broadcasted_iota(jnp.int32, (8, 1), 0) == 0
    last = lax.broadcasted_iota(jnp.int32, (8, 1), 0) == 7

    def column(array, index):
        return array[:, index : index + 1]

    def slopes(array, pair):
        whole, low, high = (column(array, 11 + 3 * pair + k) for k in range(3))
        return whole - low - high, low, high

    merged = [column(values, 0), column(values, 1)]
    for b in range(3):
        merged.append(column(values, 5 + b) + column(after, 2 + b) + column(before, 8 + b))
    merged += [own + other for own, other in zip(slopes(values, 0), slopes(before, 2), strict=True)]
    merged += list(slopes(values, 1))
    inside, interface = [], []
    for side in range(2):
        whole, low, high = (column(values, 20 + 3 * side + k) for k in range(3))
        ends = jnp.where(first, low, 0.0) + jnp.where(last, high, 0.0)
        inside.append(whole - low - high + ends)
        interface.append(jnp.where(first, 0.0, low) + column(before, 22 + 3 * side))
    rows = jnp.zeros((8, LANES), F32)
    for index, value in enumerate(merged + inside + interface):
        rows = jnp.where(lane == index, value, rows)
    total = rows[0:1]
    for i in range(1, 8):
        total = total + pltpu.roll(rows[i : i + 1], 16 * i, 1)
    out_ref[...] = jnp.broadcast_to(total, out_ref.shape)


def invert(blocks, sub):
    for k in range(0, 8, 2):
        first, second = blocks[k], blocks[k + 1]
        a, b = first[k : k + 1], first[k + 1 : k + 2]
        c, d = second[k : k + 1], second[k + 1 : k + 2]
        scale = 1.0 / (a * d - b * c)
        first = jnp.where(sub == k, 1.0, jnp.where(sub == k + 1, 0.0, first))
        second = jnp.where(sub == k + 1, 1.0, jnp.where(sub == k, 0.0, second))
        low = (d * scale) * first - (b * scale) * second
        high = (a * scale) * second - (c * scale) * first
        pivots = (sub == k) | (sub == k + 1)
        rows = []
        for r in range(8):
            if r == k:
                rows.append(low)
            elif r == k + 1:
                rows.append(high)
            else:
                rest = jnp.where(pivots, 0.0, blocks[r])
                rows.append(rest - blocks[r][k : k + 1] * low - blocks[r][k + 1 : k + 2] * high)
        blocks = rows
    return blocks


def multiply(left, right):
    rows = []
    for r in range(8):
        total = left[r][0:1] * right[0]
        for k in range(1, 8):
            total = total + left[r][k : k + 1] * right[k]
        rows.append(total)
    return rows


def multiply_turned(left, right):
    rows = []
    for r in range(8):
        total = left[0][r : r + 1] * right[0]
        for k in range(1, 8):
            total = total + left[k][r : r + 1] * right[k]
        rows.append(total)
    return rows


def apply_turned(blocks, column):
    total = blocks[0] * column[0:1]
    for k in range(1, 8):
        total = total + blocks[k] * column[k : k + 1]
    return total


def coarse_operator(c, count, sums_z, couplings_z, inside_y, interface_y):
    sub = lax.broadcasted_iota(jnp.int32, c.shape, 0)
    lane = lax.broadcasted_iota(jnp.int32, c.shape, 1)
    has_low = lane > 0
    has_high = lane < count - 1

    def after(array):
        return jnp.where(sub < 7, pltpu.roll(array, 7, 0), 0.0)

    def before(array):
        return jnp.where(sub > 0, pltpu.roll(array, 1, 0), 0.0)

    def right(array):
        return jnp.where(has_high, pltpu.roll(array, LANES - 1, 1), 0.0)

    def left(array):
        return jnp.where(has_low, pltpu.roll(array, 1, 1), 0.0)

    on_low = jnp.where(has_low, 0.5 * (c + left(c)), c)
    on_high = jnp.where(has_high, 0.5 * (c + right(c)), c)
    tested = []
    for place, value in enumerate((c, on_low, on_high)):
        slope = jnp.where(sub > 0, 0.5 * (value - before(value)), 0.0)
        coupling = couplings_z[place]
        force = sums_z[place] * slope - coupling * after(slope) - before(coupling * slope)
        force = jnp.where(sub > 0, force, 0.0)
        tested.append(0.5 * (force - after(force)))
    result = tested[0] + jnp.where(has_low, 0.5, 1.0) * tested[1] + jnp.where(has_high, 0.5, 1.0) * tested[2]
    result = result + 0.5 * right(tested[1]) + 0.5 * left(tested[2])

    interface = jnp.where(sub > 0, 0.5 * (c + before(c)), 0.0)
    for side, (move, there) in enumerate(((left, has_low), (right, has_high))):
        force = inside_y[side] * jnp.where(there, 0.5 * (move(c) - c), 0.0)
        face = interface_y[side] * jnp.where(there, 0.5 * (move(interface) - interface), 0.0)
        force = force + 0.5 * (face + after(face))
        back = right if side == 0 else left
        result = result + 0.5 * (back(force) - force)

    end = float(WEIGHT[0])
    mass = (2.0 - 2.0 * end) * c + end * (interface + after(interface))
    mass = mass + jnp.where((sub == 0) | (sub == 7), end * c, 0.0)
    beside = jnp.where(has_low, 0.5 * (mass + left(mass)), 0.0)
    scaled = (2.0 * EY - 2.0 * end) * mass + end * (beside + right(beside))
    scaled = scaled + jnp.where(has_low, 0.0, end * mass) + jnp.where(has_high, 0.0, end * mass)
    return result + HELM_COEF / 8.0 * float(np.sum(WX)) * scaled


def coarse_kernel(count, near, gathered, out_ref, wide, turned):
    lanes = LANES
    sub = lax.broadcasted_iota(jnp.int32, (8, lanes), 0)
    lane = lax.broadcasted_iota(jnp.int32, (8, lanes), 1)
    wide[...] = jnp.zeros((LANES, LANES), F32)
    wide[0:count] = gathered[...]
    turned[...] = wide[...].T

    def value(index):
        return turned[pl.ds(index, 8, stride=16), :]

    def move(array, dz, dy):
        if dz:
            array = pltpu.roll(array, (-dz) % 8, 0)
        if dy:
            array = pltpu.roll(array, (-dy) % lanes, 1)
        return array

    kbar = jnp.where(lane < count, value(0), 1.0)
    above = move(kbar, 1, 0)
    link_z = jnp.where(sub < 7, 2.0 * kbar * above / (kbar + above) * (EY * EX / EZ), 0.0)
    link_z = jnp.where(lane < count, link_z, 0.0)
    beside = move(kbar, 0, 1)
    link_y = 2.0 * kbar * beside / (kbar + beside) * (EZ * EX / EY)
    link_y = jnp.where(lane < count - 1, link_y, 0.0)
    back_z = move(link_z, -1, 0)
    back_y = move(link_y, 0, -1)
    diagonal = HELM_COEF * EZ * EY * EX + link_z + back_z + link_y + back_y
    blocks = []
    for r in range(8):
        row = jnp.where(sub == r, diagonal, 0.0)
        row = jnp.where(sub == r + 1, -back_z, row)
        row = jnp.where(sub == r - 1, -link_z, row)
        blocks.append(row)

    levels = []
    step = 1
    while step < count:
        inverse = invert(blocks, sub)
        if step == 1:
            up, low = -link_y, -back_y
            solved_up = [row * up for row in inverse]
            solved_low = [row * low for row in inverse]
            pull_up = [up[r : r + 1] * solved_up[r] for r in range(8)]
            pull_low = [low[r : r + 1] * solved_low[r] for r in range(8)]
            new_low = [up[r : r + 1] * solved_low[r] for r in range(8)]
            new_up = [low[r : r + 1] * solved_up[r] for r in range(8)]
        else:
            solved_up, solved_low = multiply(inverse, upper), multiply(inverse, lower)
            pull_up = multiply_turned(solved_up, upper)
            pull_low = multiply_turned(solved_low, lower)
            if 2 * step < count:
                new_low = multiply_turned(solved_up, lower)
                new_up = multiply_turned(solved_low, upper)
        levels.append((step, solved_up, solved_low))
        blocks = [
            blocks[r] - move(pull_up[r], 0, -step) - move(pull_low[r], 0, step) for r in range(8)
        ]
        if 2 * step < count:
            lower = [-move(row, 0, -step) for row in new_low]
            upper = [-move(row, 0, step) for row in new_up]
        step *= 2
    inverse = invert(blocks, sub)

    def solve(column):
        for distance, solved_up, solved_low in levels:
            before = move(apply_turned(solved_up, column), 0, -distance)
            after = move(apply_turned(solved_low, column), 0, distance)
            column = column - before - after
        return apply_turned(inverse, column)

    first = solve(value(1))
    totals = coarse_operator(
        first,
        count,
        [value(5 + k) for k in range(3)],
        [value(8 + k) for k in range(3)],
        [value(11), value(12)],
        [value(13), value(14)],
    )
    totals = totals + value(3)
    totals = totals + jnp.where(lane < count - 1, move(value(2), 0, 1), 0.0)
    totals = totals + jnp.where(lane > 0, move(value(4), 0, -1), 0.0)
    totals = jnp.where(lane < count, totals, 0.0)
    second = solve(totals)
    gx = near[4].astype(jnp.int32)
    gy = near[5].astype(jnp.int32)
    for at, solved in ((0, first), (8, second)):
        turned_z = pltpu.roll(solved, (10 - gx) % 8, 0)
        out_ref[at : at + 8] = pltpu.roll(turned_z, (lanes + 1 - gy) % lanes, 1)


def coarse_columns(near, coarse, start, count):
    row, has_low, has_high = ring_rows(near)
    below = jnp.where(row < RING - 1, 1.0, jnp.where(row <= RING, 0.5, 0.0)) * has_low
    above = jnp.where(row > RING + ROWS, 1.0, jnp.where(row >= RING + ROWS - 1, 0.5, 0.0)) * has_high
    edge = jnp.where((row > RING) & (row < RING + ROWS - 1), 1.0, 0.0)
    edge = jnp.where(row == RING, near[2], jnp.where(row == RING + ROWS - 1, near[3], edge))
    edge = jnp.where(row == RING - 1, 0.5 * has_low, edge)
    edge = jnp.where(row == RING + ROWS, 0.5 * has_high, edge)
    columns = []
    for a in range(start, start + count):
        low, own, high = (coarse[a : a + 1, b : b + 1] for b in range(3))
        columns.append(below * low + edge * own + above * high)
    return columns


def coarse_planes(columns, low, high):
    before, inside, after = columns
    return inside, low * (before - inside), high * (after - inside)


def add_coarse(local, columns):
    inside, first, last = columns
    planes = [local[i] + inside for i in range(8)]
    planes[0] = planes[0] + first
    planes[7] = planes[7] + last
    return stack(planes)


def coarse_applied(columns, flux, packed):
    inside, first, last = columns
    slopes = [
        flux[i] * (float(DERIV[i, 0]) * first + float(DERIV[i, 7]) * last) for i in range(8)
    ]
    fz = along_z(slopes, DERIV.T)
    three = stack([inside + first, inside, inside + last])
    gy = along_y(three, packed, 0)
    fy = along_y(
        stack([flux[i] * gy[0 if i == 0 else 2 if i == 7 else 1] for i in range(8)]), packed, 1
    )
    plane_w = packed[0:WIDE]
    planes = []
    for i in range(8):
        plane = three[0 if i == 0 else 2 if i == 7 else 1]
        planes.append(fz[i] + fy[i] + (HELM_COEF * 0.125 * float(WEIGHT[i])) * (plane_w * plane))
    return stack(planes)


def face_applied(planes, payload, packed, rows, in_grid):
    inside, first, last = planes
    fields = [inside + (first if i == 0 else last if i == 7 else 0.0) for i in rows]
    gy = along_y(stack(fields), packed, 0)
    fy = along_y(stack([payload[6 + k] * gy[k] for k in range(2)]), packed, 1)
    plane_w = packed[0:WIDE]
    result = []
    for k, i in enumerate(rows):
        slopes = payload[2 + k] * first + payload[4 + k] * last
        mass = (HELM_COEF * 0.125 * float(WEIGHT[i])) * in_grid * (plane_w * fields[k])
        result.append(payload[k] + slopes + fy[k] + mass)
    return result


def apply_kernel(
    near, inverse, packed, tables, coarse, flux, zl, yl, ylo, yhi,
    z_ref, y_ref, w_ref, wlo, whi,
):
    columns = coarse_columns(near, coarse, 0, 5)
    own = coarse_planes(columns[1:4], 1.0 - near[0], 1.0 - near[1])
    field = add_coarse(zl[...], own)[:, RING : RING + ROWS]
    z_ref[...] = field
    applied = yl[...] + coarse_applied(own, flux[...], packed)
    y_ref[...] = applied[:, RING : RING + ROWS]
    lower = coarse_planes(columns[0:3], 1.0 - near[7], 0.5)
    upper = coarse_planes(columns[2:5], 0.5, 1.0 - near[6])
    planes = [applied[i] for i in range(8)]
    planes += face_applied(lower, ylo, packed, (6, 7), 2.0 - 2.0 * near[0])
    planes += face_applied(upper, yhi, packed, (0, 1), 2.0 - 2.0 * near[1])
    planes = solve_elements(planes, packed, tables, 1, inverse)
    row = lax.broadcasted_iota(jnp.int32, (ROWS, LANES), 0)
    _, has_low, has_high = ring_rows(near)
    in_grid = jnp.where(row == 0, has_low, jnp.where(row == ROWS - 1, has_high, 1.0))
    for i in range(8):
        first = (1.0 - has_low) * planes[i][ROWS : ROWS + 1]
        last = (1.0 - has_high) * planes[i][ROWS + 1 : ROWS + 2]
        alone = jnp.where(row == 0, first, jnp.where(row == ROWS - 1, last, 0.0))
        planes[i] = planes[i][0:ROWS] * in_grid + alone
    store_faces(planes, near, w_ref, wlo, whi)


def solve_apply_kernel(
    count, near, gathered, inverse, packed, tables, flux, zl, yl, ylo, yhi,
    coarse, z_ref, y_ref, w_ref, wlo, whi, wide, turned,
):
    coarse_kernel(count, near, gathered, coarse, wide, turned)
    apply_kernel(
        near, inverse, packed, tables, coarse, flux, zl, yl, ylo, yhi,
        z_ref, y_ref, w_ref, wlo, whi,
    )


def second_kernel(near, packed, coarse, flux, b, y, z, w, x_ref, kx_ref, stat):
    columns = [column[RING : RING + ROWS] for column in coarse_columns(near, coarse, 9, 3)]
    field = add_coarse(w[...], coarse_planes(columns, 1.0 - near[0], 1.0 - near[1]))
    x_ref[...] = field
    fluxes = flux[:, RING : RING + ROWS]
    gz = along_z([field[i] for i in range(8)], DERIV)
    gy = along_y(field, packed, 0)
    gx = along_x(field, packed, 0)
    slopes = [fluxes[i] * gz[i] for i in range(8)]
    ends = (0, 7)
    back = along_z(slopes, DERIV.T[[0, 7]])
    back_y = along_y(stack([fluxes[i] * gy[i] for i in ends]), packed, 1)
    back_x = along_x(stack([fluxes[i] * gx[i] for i in ends]), packed, 1)
    plane_w = packed[0:ROWS]
    mass = HELM_COEF * 0.125
    for k, i in enumerate(ends):
        weighted = (mass * float(WEIGHT[i])) * (plane_w * field[i])
        kx_ref[k] = back[k] + back_y[k] + back_x[k] + weighted
    energy = None
    for i in range(8):
        term = slopes[i] * gz[i] + fluxes[i] * (gy[i] * gy[i] + gx[i] * gx[i])
        term = term + (mass * float(WEIGHT[i])) * (plane_w * field[i] * field[i])
        energy = term if energy is None else energy + term
    first, right = z[...], b[...]
    sums = [right * first, y[...] * first, right * field, y[...] * field]
    stat[...] = lane_row([jnp.sum(term) for term in sums] + [jnp.sum(energy)])


def face_kernel(packed, flux, b, y, kx, zlo, zhi, stat_in, stat):
    faces = stack([zlo[...], zhi[...]])
    fluxes = flux[:, RING : RING + ROWS]
    gy = along_y(faces, packed, 0)
    gx = along_x(faces, packed, 0)
    plane_w = packed[0:ROWS]
    energy = 2.0 * (kx[0] * faces[0] + kx[1] * faces[1])
    for k, i in enumerate((0, 7)):
        mass = (HELM_COEF * 0.125 * float(WEIGHT[i])) * (plane_w * faces[k] * faces[k])
        energy = energy + mass + fluxes[i] * (gy[k] * gy[k] + gx[k] * gx[k])
    for i in range(8):
        slope = float(DERIV[i, 0]) * faces[0] + float(DERIV[i, 7]) * faces[1]
        energy = energy + fluxes[i] * slope * slope
    sums = [
        0.0,
        0.0,
        jnp.sum(b[0] * faces[0] + b[7] * faces[1]),
        jnp.sum(y[0] * faces[0] + y[7] * faces[1]),
        jnp.sum(energy),
    ]
    stat[...] = jnp.broadcast_to(stat_in[...] + lane_row(sums), stat.shape)


def combine_kernel(sums, z, x, zlo, zhi, p_ref):
    total = jnp.sum(sums[...], axis=0, keepdims=True)
    rz, pap, rq, aq, qhq = (total[:, k : k + 1] for k in range(5))
    step = rz / pap
    rz_next = step * (step * aq - rq)
    beta = rz_next / rz
    grown = 1.0 + beta
    curved = grown * grown * pap - 2.0 * step * grown * aq + step * step * qhq
    step_next = rz_next / curved
    on_z = step + step_next * grown
    on_q = step_next * step
    for i in range(8):
        plane = x[i]
        if i == 0:
            plane = plane + zlo[...]
        if i == 7:
            plane = plane + zhi[...]
        p_ref[i] = on_z * z[i] - on_q * plane


def run(kernel, outs, smem, args, scratch=(), flops=1000000, place=VMEM, limit=LIMIT):
    nbytes = sum(4 * int(np.prod(out)) for out in outs) * 2
    return pl.pallas_call(
        kernel,
        out_shape=[jax.ShapeDtypeStruct(out, F32) for out in outs],
        in_specs=[pl.BlockSpec(memory_space=SMEM) for _ in smem]
        + [pl.BlockSpec(memory_space=place) for _ in args],
        out_specs=[pl.BlockSpec(memory_space=VMEM) for _ in outs],
        scratch_shapes=list(scratch),
        compiler_params=pltpu.CompilerParams(vmem_limit_bytes=limit),
        cost_estimate=pl.CostEstimate(flops=flops, bytes_accessed=nbytes, transcendentals=0),
    )(*smem, *args)


def shift(axis, low_face, high_face):
    count = lax.axis_size(axis)
    forward = [(i, i + 1) for i in range(count - 1)]
    backward = [(target, source) for source, target in forward]
    return lax.ppermute(high_face, axis, forward), lax.ppermute(low_face, axis, backward)


def body(level_set, velocity, source, wick_solid):
    block = level_set.shape
    count_gx = lax.axis_size("gx")
    count_gy = lax.axis_size("gy")
    index_gx = lax.axis_index("gx")
    index_gy = lax.axis_index("gy")

    def ends(index, count):
        return [jnp.where(index > 0, 0.5, 1.0), jnp.where(index < count - 1, 0.5, 1.0)]

    place = [index_gx.astype(F32), index_gy.astype(F32)]
    beyond = [
        jnp.where(index_gx < count_gx - 2, 0.5, 1.0),
        jnp.where(index_gx > 1, 0.5, 1.0),
    ]
    near = jnp.stack(ends(index_gx, count_gx) + ends(index_gy, count_gy) + place + beyond)
    near = near.astype(F32)
    packed = jnp.asarray(PACKED)
    tables = jnp.asarray(TABLES)
    face = (ROWS, LANES)
    wide_block = (8, WIDE, LANES)
    wide_face = (WIDE, LANES)
    rim = (12, TILE, LANES)

    b, l, zlo, zhi, solid = run(
        advect_kernel,
        [block, block, (3, *face), (3, *face), (8, LANES)],
        [],
        [
            pltpu.with_memory_space_constraint(array, pltpu.HBM)
            for array in (level_set, velocity, source, packed, wick_solid.reshape(EY, EX))
        ],
        [VMEM(block, F32), VMEM((3, *block), F32), VMEM(block, F32), VMEM(PACKED.shape, F32)]
        + [VMEM((EY, EX), jnp.int32), pltpu.SemaphoreType.DMA((5,))],
        place=pltpu.HBM,
    )
    zlo, zhi = shift("gx", zlo, zhi)
    ylo, yhi = run(rim_kernel, [rim, rim], [], [solid, b, l, zlo, zhi])
    ylo, yhi = shift("gy", ylo, yhi)
    inner, inverse = run(
        inner_schwarz_kernel, [block, (10 * STEP_A, 10 * EX)], [], [packed, tables, b, zlo, zhi], flops=20000000
    )
    w, wlo, whi = run(
        first_schwarz_kernel,
        [wide_block, wide_face, wide_face],
        [near],
        [inverse, packed, tables, inner, b, zlo, zhi, ylo, yhi],
    )
    wlo, whi = shift("gx", wlo, whi)
    level_new, flux, stat = run(
        level_kernel,
        [block, wide_block, (1, LANES)],
        [near],
        [solid, packed, b, l, zlo, zhi, ylo, yhi],
        flops=20000000,
    )
    zl, yl, zlo, zhi, stat = run(
        galerkin_kernel,
        [wide_block, wide_block, wide_block, wide_block, (count_gx, LANES)],
        [near],
        [packed, stat, flux, w, wlo, whi],
    )
    zlo, zhi = shift("gx", zlo, zhi)
    gathered = lax.all_to_all(stat, "gx", 0, 0, tiled=True)
    (column,) = run(column_kernel, [(count_gy, LANES)], [], [gathered])
    gathered = lax.all_to_all(column, "gy", 0, 0, tiled=True)
    coarse, z, y, w, wlo, whi = run(
        functools.partial(solve_apply_kernel, count_gy),
        [(16, LANES), block, block, block, face, face],
        [near],
        [gathered, inverse, packed, tables, flux, zl, yl, zlo, zhi],
        [VMEM((LANES, LANES), F32), VMEM((LANES, LANES), F32)],
    )
    zlo, zhi = shift("gx", wlo, whi)
    x, kx, sums = run(
        second_kernel,
        [block, (2, *face), (1, LANES)],
        [near],
        [packed, coarse, flux, b, y, z, w],
        flops=20000000,
    )
    (sums,) = run(
        face_kernel, [(2 * count_gx, LANES)], [], [packed, flux, b, y, kx, zlo, zhi, sums]
    )
    pairs = count_gy // 2
    columns = [
        [z * count_gy + 2 * m + c for z in range(count_gx) for c in range(2)] for m in range(pairs)
    ]
    layers = [
        [z * count_gy + 2 * m + c for m in range(pairs)] for z in range(count_gx) for c in range(2)
    ]
    axes = ("gx", "gy")
    tile = lax.all_to_all(sums, axes, 0, 0, axis_index_groups=columns, tiled=True)
    wide = jnp.broadcast_to(jnp.sum(tile, axis=0, keepdims=True), (pairs, LANES))
    wide = lax.all_to_all(wide, axes, 0, 0, axis_index_groups=layers, tiled=True)
    (pressure,) = run(combine_kernel, [block], [], [wide, z, x, zlo, zhi])
    return (level_new, pressure)


def solution(mesh):
    placed = (
        P("gx", "gy", None),
        P(None, "gx", "gy", None),
        P("gx", "gy", None),
        P("gx", "gy", None),
    )
    return jax.shard_map(
        body,
        mesh=mesh,
        in_specs=placed,
        out_specs=(P("gx", "gy", None), P("gx", "gy", None)),
        check_vma=False,
    )
```
